128 devices in a mesh: dp: 32 (over z_lo, x, y), tensor: 4 (over z_hi, core).
Axes of the slice: x: 4, y: 4, z: 4 (z_hi: 2, z_lo: 2; z = z_hi * 2 + z_lo), core: 2. Of those that a mesh axis runs over, the one named last changes fastest.
Arguments:
- hidden_in: bfloat16 [16384, 2048], P('dp'), may hold values from -6 to 6
- segment_ids: int32 [16384], P('dp'), may hold values from 0 to 3, as said below
- positions: int32 [16384], P('dp'), may hold values from 0 to 508, as said below
- ln1_gain: float32 [2048], replicated, may hold values from 0.1 to 1.9
- ln1_bias: float32 [2048], replicated, may hold values from -3 to 3
- qkv_weight: bfloat16 [2048, 6144], P(None, 'tensor'), may hold values from -0.125 to 0.125
- qkv_bias: float32 [8, 768], P('tensor'), may hold values from -3 to 3
- dense_weight: bfloat16 [2048, 2048], P('tensor'), may hold values from -0.5 to 0.5
- dense_bias: float32 [2048], replicated, may hold values from -3 to 3
- ln2_gain: float32 [2048], replicated, may hold values from 0.1 to 1.9
- ln2_bias: float32 [2048], replicated, may hold values from -3 to 3
- fc1_weight: bfloat16 [2048, 8192], P(None, 'tensor'), may hold values from -0.125 to 0.125
- fc1_bias: float32 [64, 128], P('tensor'), may hold values from -3 to 3
- fc2_weight: bfloat16 [8192, 2048], P('tensor'), may hold values from -0.0625 to 0.0625
- fc2_bias: float32 [2048], replicated, may hold values from -3 to 3
- cotangent: bfloat16 [16384, 2048], P('dp'), may hold values from -6 to 6
Outputs:
- output: float32 [16384, 2048], P('dp')
- input_grad: float32 [16384, 2048], P('dp')
- ln1_gain_grad: float32 [2048], P('dp')
- ln1_bias_grad: float32 [2048], P('dp')
- qkv_weight_grad: float32 [2048, 6144], P('dp', 'tensor')
- qkv_bias_grad: float32 [8, 768], P('tensor', 'dp')
- dense_weight_grad: float32 [2048, 2048], P('tensor', 'dp')
- dense_bias_grad: float32 [2048], P('dp')
- ln2_gain_grad: float32 [2048], P('dp')
- ln2_bias_grad: float32 [2048], P('dp')
- fc1_weight_grad: float32 [2048, 8192], P('dp', 'tensor')
- fc1_bias_grad: float32 [64, 128], P('tensor', 'dp')
- fc2_weight_grad: float32 [8192, 2048], P('tensor', 'dp')
- fc2_bias_grad: float32 [2048], P('dp')
The draws below stay inside these ranges and needn't reach their ends.
Inputs may be any that keep to these rules, and one draw needn't show every extreme that they name: `segment_ids`: within each sequence of 512 tokens the segment numbers start at 0, never fall, and take each of the 4 values. `positions`: A token's index in its sequence minus the index of its document's first token.
All inputs are finite; a program needn't handle non-finite values.
Results may differ from the reference program's by a relative error of at most 0.011.
Values sent between devices are 32-bit elements; how exact they have to be, the bound alone decides.
No kernel may reach another device: no remote copies, remote signals or barrier semaphores. Data moves between devices by JAX's collectives and lax.ppermute only.
A program may use at most 256 MiB of HBM per device.

```python
import math
import jax
import jax.numpy as jnp
from jax import lax

D = 2048
H = 8
HD = 256
ROT = 64
FF = 8192
TOK_DEV = 512
DOCS = 4
TOKENS = 16384
N_DP = 32


def document_layout(key):
    chosen = jax.random.randint(jax.random.fold_in(key, 7), (), 0, N_DP)
    block_keys = jax.random.split(jax.random.fold_in(key, 11), N_DP)
    block_ids = jnp.arange(N_DP, dtype=jnp.int32)

    def one_block(block_key, block_id):
        random_cuts = (jax.random.permutation(block_key, TOK_DEV - 1)[:DOCS - 1] + 1).astype(jnp.int32)
        late_cuts = (TOK_DEV - DOCS + 1 + jnp.arange(DOCS - 1, dtype=jnp.int32)).astype(jnp.int32)
        cuts = jnp.where(block_id == chosen, late_cuts, random_cuts)
        order = jnp.arange(TOK_DEV, dtype=jnp.int32)
        passed = order[:, None] >= cuts[None, :]
        numbers = jnp.sum(passed.astype(jnp.int32), axis=1)
        starts = jnp.max(jnp.where(passed, cuts[None, :], 0), axis=1)
        return (numbers, order - starts)
    numbers, offsets = jax.vmap(one_block)(block_keys, block_ids)
    return (numbers.reshape(-1).astype(jnp.int32), offsets.reshape(-1).astype(jnp.int32))


def draw_segment_ids(key, part):
    return document_layout(key)[0]


def draw_positions(key, part):
    return document_layout(key)[1]


def spiked(result, own_key, source, target, shards_of, factor):
    owner, partner = [(jnp.arange(result.shape[axis_at]) // (result.shape[axis_at] // shards_of)).reshape([-1 if axis == axis_at else 1 for axis in range(result.ndim)]) for axis_at in (source, target)]
    chosen = jax.random.permutation(own_key, shards_of)[partner]
    strong = (owner == chosen) | (owner == (partner + shards_of // 2) % shards_of)
    return jnp.where(strong, factor * result, result)


def block_scale(own_key, dims, shards, low, top_value):
    def one(position, blocks):
        draws = jax.random.uniform(jax.random.fold_in(jax.random.fold_in(own_key, 6), position), (blocks,), jnp.float32, low / len(shards), top_value / len(shards))
        return jnp.repeat(jnp.exp(draws), dims[position] // blocks).reshape((-1,) + (1,) * (len(dims) - position - 1))

    factor_of = one(*shards[0])
    for cut in shards[1:]:
        factor_of = factor_of * one(*cut)
    return factor_of


def noise(stream_key, dims, deviation, reach, pieces=(), held_as=jnp.bfloat16):
    result = deviation * jax.random.normal(stream_key, dims, jnp.float32)
    if pieces:
        result = result * block_scale(stream_key, dims, pieces, -0.22, 0.18)
    return jnp.clip(result, -reach, reach).astype(held_as)


def bell_draw_with(own_key, shape, width, limit, shards, heavy, kind=jnp.bfloat16):
    drawn = width * jax.random.normal(own_key, shape, jnp.float32)
    if shards:
        drawn = drawn * block_scale(own_key, shape, shards, -0.22, 0.18)
    return jnp.clip(spiked(drawn, jax.random.fold_in(own_key, 3), *heavy), -limit, limit).astype(kind)


def setup_inputs(seed: int = 0) -> dict:
    key_list = jax.random.split(jax.random.key(seed), 17)
    hidden_in = bell_draw_with(key_list[0], (TOKENS, D), 1.0, 6.0, ((0, 32),), (0, 1, 32, 2.75))
    segment_ids = draw_segment_ids(jax.random.fold_in(key_list[16], 71), 0)
    positions = draw_positions(jax.random.fold_in(key_list[16], 71), 0)
    ln1_gain = jnp.clip(1.0 + 0.18 * jax.random.normal(key_list[3], (D,), jnp.float32), 0.1, 1.9)
    ln1_bias = noise(key_list[4], (D,), 0.5, 3.0, (), jnp.float32)
    qkv_weight = noise(key_list[5], (D, 3 * H * HD), D ** -0.5, 0.125, ((1, 4),))
    qkv_bias = noise(key_list[6], (H, 3 * HD), 0.5, 3.0, ((0, 4),), jnp.float32)
    dense_weight = noise(key_list[7], (H * HD, D), (H * HD // 16) ** -0.5, 0.5, ((0, 4),))
    dense_bias = noise(key_list[8], (D,), 0.5, 3.0, (), jnp.float32)
    ln2_gain = jnp.clip(1.0 + 0.18 * jax.random.normal(key_list[9], (D,), jnp.float32), 0.1, 1.9)
    ln2_bias = noise(key_list[10], (D,), 0.5, 3.0, (), jnp.float32)
    fc1_weight = noise(key_list[11], (D, FF), D ** -0.5, 0.125, ((1, 4),))
    fc1_bias = noise(key_list[12], (FF // 128, 128), 0.5, 3.0, ((0, 4),), jnp.float32)
    fc2_weight = noise(key_list[13], (FF, D), FF ** -0.5, 0.0625, ((0, 4),))
    fc2_bias = noise(key_list[14], (D,), 0.5, 3.0, (), jnp.float32)
    cotangent = bell_draw_with(key_list[15], (TOKENS, D), 1.0, 6.0, ((0, 32),), (0, 1, 32, 2.75))
    return {"hidden_in": hidden_in, "segment_ids": segment_ids, "positions": positions, "ln1_gain": ln1_gain, "ln1_bias": ln1_bias, "qkv_weight": qkv_weight, "qkv_bias": qkv_bias, "dense_weight": dense_weight, "dense_bias": dense_bias, "ln2_gain": ln2_gain, "ln2_bias": ln2_bias, "fc1_weight": fc1_weight, "fc1_bias": fc1_bias, "fc2_weight": fc2_weight, "fc2_bias": fc2_bias, "cotangent": cotangent}


EPSILON = 1e-05
HIGHEST = lax.Precision.HIGHEST

@jax.custom_vjp
def low(v):
    return lax.optimization_barrier(v.astype(jnp.bfloat16)).astype(jnp.float32)

@jax.custom_vjp
def low_back(v):
    return v

def low_keep(v):
    return (low(v), None)

def low_pass(kept, grad):
    return (grad,)

def back_keep(v):
    return (v, None)

def back_low(kept, grad):
    return (low(grad),)
low.defvjp(low_keep, low_pass)
low_back.defvjp(back_keep, back_low)

def matmul(left, right):
    return jnp.dot(left, right, precision=HIGHEST)

def angle_tables(positions):
    halves = jnp.arange(ROT // 2, dtype=jnp.float32)
    inverse = 10000.0 ** (-2.0 * halves / ROT)
    angles = positions.astype(jnp.float32)[..., None] * inverse
    angles = jnp.concatenate([angles, angles], axis=-1)
    return (jnp.cos(angles), jnp.sin(angles))

def rotate(vectors, cosine, sine):
    turned = vectors[..., :ROT]
    first = turned[..., :ROT // 2]
    second = turned[..., ROT // 2:]
    swapped = jnp.concatenate([-second, first], axis=-1)
    return jnp.concatenate([turned * cosine + swapped * sine, vectors[..., ROT:]], axis=-1)

def attend_one(queries, keys_rot, values_in, segments):
    scores = jnp.einsum('qhd,khd->hqk', queries, keys_rot, precision=HIGHEST) * (1.0 / math.sqrt(HD))
    order = jnp.arange(segments.shape[0])
    allowed = (segments[:, None] == segments[None, :]) & (order[None, :] <= order[:, None])
    scores = low_back(jnp.where(allowed[None], scores, -1000000000.0))
    top = lax.optimization_barrier(jnp.max(scores, axis=-1, keepdims=True))
    weights = jnp.exp(scores - top)
    probs = weights / lax.optimization_barrier(jnp.sum(weights, axis=-1, keepdims=True))
    return jnp.einsum('hqk,khd->qhd', low(probs), values_in, precision=HIGHEST)

def reference(hidden_in, segment_ids, positions, ln1_gain, ln1_bias, qkv_weight, qkv_bias, dense_weight, dense_bias, ln2_gain, ln2_bias, fc1_weight, fc1_bias, fc2_weight, fc2_bias, cotangent):
    cosine, sine = angle_tables(positions.reshape(N_DP, TOK_DEV))
    cosine = cosine[:, :, None, :]
    sine = sine[:, :, None, :]
    seg_blocks = segment_ids.reshape(N_DP, TOK_DEV)

    def forward(hidden, gain_one, shift_one, weight_qkv, bias_qkv, weight_dense, bias_dense, gain_two, shift_two, weight_up, bias_up, weight_down, bias_down):
        average = lax.optimization_barrier(jnp.mean(hidden, axis=-1, keepdims=True))
        centred = hidden - average
        normed = centred * lax.rsqrt(lax.optimization_barrier(jnp.mean(centred * centred, axis=-1, keepdims=True)) + EPSILON)
        first_in = low(normed * gain_one + shift_one)
        second_in = low(normed * gain_two + shift_two)
        packed = low_back(matmul(first_in, weight_qkv) + bias_qkv.reshape(-1))
        packed = packed.reshape(N_DP, TOK_DEV, H, 3, HD)
        queries = low(rotate(packed[:, :, :, 0], cosine, sine))
        keys_rot = low(rotate(packed[:, :, :, 1], cosine, sine))
        values_in = low(packed[:, :, :, 2])
        attend = jax.checkpoint(attend_one)
        mixed = lax.map(lambda members: attend(members[0], members[1], members[2], members[3]), (queries, keys_rot, values_in, seg_blocks))
        mixed = low(low_back(mixed.reshape(N_DP * TOK_DEV, H * HD)))
        upward = low_back(matmul(second_in, weight_up) + bias_up.reshape(-1))
        activated = low(jax.nn.gelu(upward, approximate=False))
        return hidden + matmul(mixed, weight_dense) + matmul(activated, weight_down) + bias_dense + bias_down
    floats = (hidden_in.astype(jnp.float32), ln1_gain.astype(jnp.float32), ln1_bias.astype(jnp.float32), qkv_weight.astype(jnp.float32), qkv_bias.astype(jnp.float32), dense_weight.astype(jnp.float32), dense_bias.astype(jnp.float32), ln2_gain.astype(jnp.float32), ln2_bias.astype(jnp.float32), fc1_weight.astype(jnp.float32), fc1_bias.astype(jnp.float32), fc2_weight.astype(jnp.float32), fc2_bias.astype(jnp.float32))
    output, pullback = jax.vjp(forward, *floats)
    grads = pullback(cotangent.astype(jnp.float32))
    return (output, grads[0], grads[1], grads[2], grads[3], grads[4], grads[5], grads[6], grads[7], grads[8], grads[9], grads[10], grads[11], grads[12])
```

```python
from functools import partial
import math

import jax
import jax.numpy as jnp
from jax import lax
from jax.experimental import pallas as pl
from jax.experimental.pallas import tpu as pltpu
from jax.sharding import Mesh, PartitionSpec as P

HD = 256
ROT = 64
TOK = 512
D = 2048
EPSILON = 1e-05
NEGATIVE = -1000000000.0
SIZES = {"zl": 2, "x": 4, "y": 4, "zh": 2, "c": 2}
DP = ("zl", "x", "y")
TENSOR = ("zh", "c")
F32 = jnp.float32
BF16 = jnp.bfloat16


def send(value, axis, step=1):
    n = SIZES[axis]
    return lax.ppermute(value, axis, [(i, (i + step) % n) for i in range(n)])


def angle_tables(positions):
    halves = jnp.arange(ROT // 2, dtype=F32)
    inverse = 10000.0 ** (-2.0 * halves / ROT)
    angles = positions.astype(F32)[..., None] * inverse
    angles = jnp.concatenate([angles, angles], axis=-1)
    return (jnp.cos(angles), jnp.sin(angles))


def rotate(vectors, cosine, sine):
    turned = vectors[..., :ROT]
    first = turned[..., : ROT // 2]
    second = turned[..., ROT // 2 :]
    swapped = jnp.concatenate([-second, first], axis=-1)
    return jnp.concatenate([turned * cosine + swapped * sine, vectors[..., ROT:]], axis=-1)


def plain_dot(left, right):
    return jnp.dot(left, right, preferred_element_type=F32)


def contract_cols(left, right):
    return lax.dot_general(left, right, (((1,), (1,)), ((), ())), preferred_element_type=F32)


def masked_scores(queries, keys_rot, segments):
    scores = jnp.einsum("qhd,khd->hqk", queries, keys_rot, preferred_element_type=F32) * (
        1.0 / math.sqrt(HD)
    )
    order = jnp.arange(segments.shape[0])
    allowed = (segments[:, None] == segments[None, :]) & (order[None, :] <= order[:, None])
    return jnp.where(allowed[None], scores, NEGATIVE)


def turn_kernel(place, source, target, turned):
    turned[...] = source[...].astype(F32).T.astype(BF16)
    for ky in range(4):
        start = pl.multiple_of(lax.rem(place[2] + ky, 4) * 64, 64)
        target[0, 0, ky] = turned[pl.ds(start, 64), :]


def turned_rows(values, place):
    return pl.pallas_call(
        turn_kernel,
        grid_spec=pltpu.PrefetchScalarGridSpec(
            num_scalar_prefetch=1,
            grid=(2, 4),
            in_specs=[
                pl.BlockSpec(
                    (TOK, 256),
                    lambda kz, kx, at: (0, lax.rem(at[0] + kz, 2) * 4 + lax.rem(at[1] + kx, 4)),
                )
            ],
            out_specs=pl.BlockSpec((1, 1, 4, 64, TOK), lambda kz, kx, at: (kz, kx, 0, 0, 0)),
            scratch_shapes=[pltpu.VMEM((256, TOK), BF16)],
        ),
        out_shape=jax.ShapeDtypeStruct((2, 4, 4, 64, TOK), BF16),
        cost_estimate=pl.CostEstimate(flops=0, bytes_accessed=4 * TOK * D, transcendentals=0),
    )(place, values)


def ring(term, axis):
    ahead = send(term(2, 0), axis, 1)
    behind = send(term(2, 1), axis, -1)
    ahead_one = send(term(1, 1), axis, 1)
    behind_one = send(term(3, 0), axis, -1)
    ahead_sum = send(term(1, 0, ahead), axis, 1)
    behind_sum = send(term(3, 1, behind), axis, -1)
    return term(0, 0, behind_one, ahead_sum), term(0, 1, ahead_one, behind_sum)


def scatter(left, right, first, second):
    def outer(k, h, *more):
        rows = left[h, k] if first == "x" else left[h, :, k]
        total = plain_dot(rows.reshape(256, TOK), right).reshape(4, 64, -1)
        for value in more:
            total = total + value
        return total

    halves = ring(outer, first)

    def inner(k, h, *more):
        total = halves[h][k]
        for value in more:
            total = total + value
        return total

    mine, other = ring(inner, second)
    return mine + send(other, "zl")


def scatter_both(left, right):
    half = right.shape[1] // 2
    return jnp.concatenate(
        [scatter(left, right[:, :half], "x", "y"), scatter(left, right[:, half:], "y", "x")],
        axis=1,
    )


def scatter_small(blocks):
    def outer(k, h, *more):
        total = blocks[h, k]
        for value in more:
            total = total + value
        return total

    halves = ring(outer, "x")

    def inner(k, h, *more):
        total = halves[h][k]
        for value in more:
            total = total + value
        return total

    mine, other = ring(inner, "y")
    return mine + send(other, "zl")


def rolled(blocks, place):
    for axis, at in enumerate(place):
        n = blocks.shape[axis]
        twice = jnp.concatenate([blocks, blocks], axis=axis)
        blocks = lax.dynamic_slice_in_dim(twice, at, n, axis)
    return blocks


def body(
    hidden_in,
    segment_ids,
    positions,
    ln1_gain,
    ln1_bias,
    qkv_weight,
    qkv_bias,
    dense_weight,
    dense_bias,
    ln2_gain,
    ln2_bias,
    fc1_weight,
    fc1_bias,
    fc2_weight,
    fc2_bias,
    cotangent,
):
    place = [lax.axis_index(a) for a in DP]
    where = jnp.stack(place).astype(jnp.int32)
    core = lax.axis_index("c")
    half_rows = TOK // 2

    def of_core(values, which):
        return lax.dynamic_slice_in_dim(values, which * half_rows, half_rows, 0)

    def both_cores(mine):
        theirs = send(mine, "c")
        whole = jnp.zeros((TOK,) + mine.shape[1:], mine.dtype)
        whole = lax.dynamic_update_slice_in_dim(whole, mine, core * half_rows, 0)
        return lax.dynamic_update_slice_in_dim(whole, theirs, (1 - core) * half_rows, 0)

    hidden = hidden_in.astype(F32)
    tokens = TOK
    heads = 2
    cot_rows = turned_rows(cotangent, where)
    average = jnp.mean(hidden, axis=-1, keepdims=True)
    centred = hidden - average
    inv_std = lax.rsqrt(jnp.mean(centred * centred, axis=-1, keepdims=True) + EPSILON)
    normed = centred * inv_std
    first_in = (normed * ln1_gain + ln1_bias).astype(BF16)
    second_in = (normed * ln2_gain + ln2_bias).astype(BF16)

    upward = plain_dot(second_in, fc1_weight) + fc1_bias.reshape(-1)
    act_low = jax.nn.gelu(upward, approximate=False).astype(BF16)
    down_sum = scatter_both(cot_rows, act_low)

    grad_act = contract_cols(cotangent, fc2_weight)
    _, gelu_back = jax.vjp(partial(jax.nn.gelu, approximate=False), upward)
    grad_up = gelu_back(grad_act)[0].astype(BF16)
    second_rows = turned_rows(second_in, where)
    up_sum = scatter_both(second_rows, grad_up)
    up_bias_grad = jnp.sum(grad_up.astype(F32), axis=0)

    packed = (plain_dot(first_in, qkv_weight) + qkv_bias.reshape(-1)).reshape(tokens, heads, 3, HD)
    cosine, sine = angle_tables(positions)
    cosine = cosine[:, None, :]
    sine = sine[:, None, :]
    queries = rotate(packed[:, :, 0], cosine, sine).astype(BF16)
    keys_rot = rotate(packed[:, :, 1], cosine, sine).astype(BF16)
    values_in = packed[:, :, 2].astype(BF16)
    scores = masked_scores(queries, keys_rot, segment_ids)
    top = jnp.max(scores, axis=-1, keepdims=True)
    weights = jnp.exp(scores - top)
    totals = jnp.sum(weights, axis=-1, keepdims=True)
    probs = weights / totals
    probs_low = probs.astype(BF16)
    mixed = jnp.einsum("hqk,khd->qhd", probs_low, values_in, preferred_element_type=F32)
    mixed_low = mixed.reshape(tokens, heads * HD).astype(BF16)

    grad_mixed = contract_cols(cotangent, dense_weight).astype(BF16).reshape(tokens, heads, HD)
    grad_probs = jnp.einsum("qhd,khd->hqk", grad_mixed, values_in, preferred_element_type=F32)
    along = jnp.sum(probs * grad_probs, axis=-1, keepdims=True)
    grad_scores = (probs * (grad_probs - along)).astype(BF16)
    score_scale = 1.0 / math.sqrt(HD)
    grad_query = (
        jnp.einsum("hqk,khd->qhd", grad_scores, keys_rot, preferred_element_type=F32) * score_scale
    )
    grad_key = (
        jnp.einsum("hqk,qhd->khd", grad_scores, queries, preferred_element_type=F32) * score_scale
    )
    grad_value = jnp.einsum("hqk,qhd->khd", probs_low, grad_mixed, preferred_element_type=F32)
    grad_packed = jnp.stack(
        [rotate(grad_query, cosine, -sine), rotate(grad_key, cosine, -sine), grad_value], axis=2
    )
    grad_packed = grad_packed.reshape(tokens, heads * 3 * HD).astype(BF16)
    first_rows = turned_rows(first_in, where)
    dense_sum = scatter_both(cot_rows, mixed_low)
    qkv_sum = scatter_both(first_rows, grad_packed)
    qkv_bias_sum = jnp.sum(grad_packed.astype(F32), axis=0)

    def branch_half(which):
        return plain_dot(of_core(mixed_low, which), dense_weight) + plain_dot(
            of_core(act_low, which), fc2_weight
        )

    branch = branch_half(core) + send(branch_half(1 - core), "c")
    branch = branch + send(branch, "zh")
    output = both_cores(of_core(hidden, core) + branch + dense_bias + fc2_bias)

    first_part = contract_cols(grad_packed, qkv_weight)
    second_part = contract_cols(grad_up, fc1_weight)
    combined = first_part * ln1_gain + second_part * ln2_gain
    combined = of_core(combined, core) + send(of_core(combined, 1 - core), "c")
    combined = combined + send(combined, "zh")
    normed_half = of_core(normed, core)
    grad_out = cotangent.astype(F32)
    input_half = of_core(grad_out, core) + of_core(inv_std, core) * (
        combined
        - jnp.mean(combined, axis=-1, keepdims=True)
        - normed_half * jnp.mean(combined * normed_half, axis=-1, keepdims=True)
    )
    input_grad = both_cores(input_half)

    gain_one_grad = jnp.sum(first_part * normed, axis=0)
    shift_one_grad = jnp.sum(first_part, axis=0)
    gain_two_grad = jnp.sum(second_part * normed, axis=0)
    shift_two_grad = jnp.sum(second_part, axis=0)
    bias_sum = jnp.sum(grad_out, axis=0)
    features = jnp.stack(
        [gain_one_grad, shift_one_grad, gain_two_grad, shift_two_grad, bias_sum]
    ).reshape(5, 32, 64)
    small = jnp.concatenate(
        [
            features.transpose(1, 0, 2).reshape(32, 320),
            qkv_bias_sum.reshape(2, 32, 24).transpose(1, 0, 2).reshape(32, 48),
            up_bias_grad.reshape(16, 32, 4).transpose(1, 0, 2).reshape(32, 64),
            jnp.zeros((32, 80), F32),
        ],
        axis=1,
    )
    small = rolled(small.reshape(2, 4, 4, 512), place)
    small = scatter_small(small)
    norms = small[:256]
    norms = norms + send(norms, "c")
    norms = (norms + send(norms, "zh")).reshape(4, 64)
    bias_total = small[256:320]
    return (
        output,
        input_grad,
        norms[0],
        norms[1],
        qkv_sum,
        small[320:368].reshape(2, 24),
        dense_sum.T,
        bias_total,
        norms[2],
        norms[3],
        up_sum,
        small[368:432].reshape(16, 4),
        down_sum.T,
        bias_total,
    )


def solution(mesh):
    fine = Mesh(mesh.devices.reshape(tuple(SIZES.values())), tuple(SIZES))
    return jax.shard_map(
        body,
        mesh=fine,
        in_specs=(
            P(DP, None),
            P(DP),
            P(DP),
            P(),
            P(),
            P(None, TENSOR),
            P(TENSOR, None),
            P(TENSOR, None),
            P(),
            P(),
            P(),
            P(None, TENSOR),
            P(TENSOR, None),
            P(TENSOR, None),
            P(),
            P(DP, None),
        ),
        out_specs=(
            P(DP, None),
            P(DP, None),
            P(DP),
            P(DP),
            P(DP, TENSOR),
            P(TENSOR, DP),
            P(TENSOR, DP),
            P(DP),
            P(DP),
            P(DP),
            P(DP, TENSOR),
            P(TENSOR, DP),
            P(TENSOR, DP),
            P(DP),
        ),
        check_vma=False,
    )
```

```python
from functools import partial
import math

import jax
import jax.numpy as jnp
from jax import lax
from jax.experimental import pallas as pl
from jax.sharding import Mesh, PartitionSpec as P

HD = 256
ROT = 64
TOK = 512
D = 2048
EPSILON = 1e-05
NEGATIVE = -1000000000.0
SIZES = {"zl": 2, "x": 4, "y": 4, "zh": 2, "c": 2}
DP = ("zl", "x", "y")
TENSOR = ("zh", "c")
F32 = jnp.float32
BF16 = jnp.bfloat16


def send(value, axis, step=1):
    n = SIZES[axis]
    return lax.ppermute(value, axis, [(i, (i + step) % n) for i in range(n)])


def angle_tables(positions):
    halves = jnp.arange(ROT // 2, dtype=F32)
    inverse = 10000.0 ** (-2.0 * halves / ROT)
    angles = positions.astype(F32)[..., None] * inverse
    angles = jnp.concatenate([angles, angles], axis=-1)
    return (jnp.cos(angles), jnp.sin(angles))


def rotate(vectors, cosine, sine):
    turned = vectors[..., :ROT]
    first = turned[..., : ROT // 2]
    second = turned[..., ROT // 2 :]
    swapped = jnp.concatenate([-second, first], axis=-1)
    return jnp.concatenate([turned * cosine + swapped * sine, vectors[..., ROT:]], axis=-1)


def plain_dot(left, right):
    return jnp.dot(left, right, preferred_element_type=F32)


def contract_cols(left, right):
    return lax.dot_general(left, right, (((1,), (1,)), ((), ())), preferred_element_type=F32)


def turn_kernel(source, *targets):
    rows = source[...].astype(F32)
    targets[0][0, :, 0] = rows.T.astype(BF16).reshape(4, 64, TOK)
    if len(targets) > 1:
        targets[1][...] = rows.astype(BF16)


def turned(values, keep=False):
    shapes = [jax.ShapeDtypeStruct((4, 4, 2, 64, TOK), BF16)]
    specs = [pl.BlockSpec((1, 4, 1, 64, TOK), lambda z, x: (x, 0, z, 0, 0))]
    if keep:
        shapes.append(jax.ShapeDtypeStruct((TOK, D), BF16))
        specs.append(pl.BlockSpec((TOK, 256), lambda z, x: (0, z * 4 + x)))
    found = pl.pallas_call(
        turn_kernel,
        grid=(2, 4),
        in_specs=[pl.BlockSpec((TOK, 256), lambda z, x: (0, z * 4 + x))],
        out_specs=specs,
        out_shape=shapes,
        cost_estimate=pl.CostEstimate(flops=0, bytes_accessed=4 * TOK * D, transcendentals=0),
    )(values)
    rows = found[0].reshape(D, TOK)
    return (rows, found[1]) if keep else rows


def normalise(hidden):
    average = jnp.mean(hidden, axis=-1, keepdims=True)
    centred = hidden - average
    inv_std = lax.rsqrt(jnp.mean(centred * centred, axis=-1, keepdims=True) + EPSILON)
    return centred * inv_std, inv_std


def gelu_both(upward, grad_act):
    _, back = jax.vjp(partial(jax.nn.gelu, approximate=False), upward)
    return back(grad_act)[0].astype(BF16)


def attention(first_in, cot, qkv_weight, qkv_bias, dense_weight, segments, positions, order):
    heads = qkv_weight.shape[1] // (3 * HD)
    packed = (plain_dot(first_in, qkv_weight) + qkv_bias.reshape(-1)).reshape(TOK, heads, 3, HD)
    cosine, sine = angle_tables(positions)
    cosine = cosine[:, None, :]
    sine = sine[:, None, :]
    queries = rotate(packed[:, :, 0], cosine, sine).astype(BF16)
    keys_rot = rotate(packed[:, :, 1], cosine, sine).astype(BF16)
    values_in = packed[:, :, 2].astype(BF16)
    score_scale = 1.0 / math.sqrt(HD)
    scores = jnp.einsum("qhd,khd->hqk", queries, keys_rot, preferred_element_type=F32) * score_scale
    allowed = (segments[:, None] == segments[None, :]) & (order[None, :] <= order[:, None])
    scores = jnp.where(allowed[None], scores, NEGATIVE)
    top = jnp.max(scores, axis=-1, keepdims=True)
    weights = jnp.exp(scores - top)
    totals = jnp.sum(weights, axis=-1, keepdims=True)
    probs = weights / totals
    probs_low = probs.astype(BF16)
    mixed = jnp.einsum("hqk,khd->qhd", probs_low, values_in, preferred_element_type=F32)
    mixed_low = mixed.reshape(TOK, heads * HD).astype(BF16)

    grad_mixed = contract_cols(cot, dense_weight).astype(BF16).reshape(TOK, heads, HD)
    grad_probs = jnp.einsum("qhd,khd->hqk", grad_mixed, values_in, preferred_element_type=F32)
    along = jnp.sum(probs * grad_probs, axis=-1, keepdims=True)
    grad_scores = (probs * (grad_probs - along)).astype(BF16)
    grad_query = (
        jnp.einsum("hqk,khd->qhd", grad_scores, keys_rot, preferred_element_type=F32) * score_scale
    )
    grad_key = (
        jnp.einsum("hqk,qhd->khd", grad_scores, queries, preferred_element_type=F32) * score_scale
    )
    grad_value = jnp.einsum("hqk,qhd->khd", probs_low, grad_mixed, preferred_element_type=F32)
    grad_packed = jnp.stack(
        [rotate(grad_query, cosine, -sine), rotate(grad_key, cosine, -sine), grad_value], axis=2
    )
    return mixed_low, grad_packed.reshape(TOK, heads * 3 * HD).astype(BF16)


def body(
    hidden_in,
    segment_ids,
    positions,
    ln1_gain,
    ln1_bias,
    qkv_weight,
    qkv_bias,
    dense_weight,
    dense_bias,
    ln2_gain,
    ln2_bias,
    fc1_weight,
    fc1_bias,
    fc2_weight,
    fc2_bias,
    cotangent,
):
    core = lax.axis_index("c")
    side = lax.axis_index("zl")
    half_rows = TOK // 2
    half_units = fc1_weight.shape[1] // 2
    after = lax.optimization_barrier

    def of_core(values, which):
        return lax.dynamic_slice_in_dim(values, which * half_rows, half_rows, 0)

    def both_cores(mine):
        theirs = send(mine, "c")
        whole = jnp.zeros((TOK,) + mine.shape[1:], mine.dtype)
        whole = lax.dynamic_update_slice_in_dim(whole, mine, core * half_rows, 0)
        return lax.dynamic_update_slice_in_dim(whole, theirs, (1 - core) * half_rows, 0)

    def cut(values, width, axis):
        return lax.dynamic_slice_in_dim(values, side * width, width, axis)

    hidden_got = send(of_core(hidden_in, core).astype(F32), "zl")
    cot_got = send(of_core(cotangent, core).astype(F32), "zl")
    marks_got = send(jnp.stack([segment_ids, positions]), "zl")

    cot_rows = turned(cotangent)
    hidden = hidden_in.astype(F32)
    normed, inv_std = normalise(hidden)
    second_in = (normed * ln2_gain + ln2_bias).astype(BF16)
    upward = plain_dot(second_in, fc1_weight) + fc1_bias.reshape(-1)
    act_low = jax.nn.gelu(upward, approximate=False).astype(BF16)
    down_grad = plain_dot(cot_rows, act_low)
    down_sum = lax.psum_scatter(down_grad, ("x", "y"), scatter_dimension=0, tiled=True)
    _, cotangent, upward, hidden = after((down_grad, cotangent, upward, hidden))

    normed, inv_std = normalise(hidden)
    first_in = (normed * ln1_gain + ln1_bias).astype(BF16)
    second_rows = turned(second_in)
    first_rows = turned(first_in)
    grad_up = gelu_both(upward, contract_cols(cotangent, fc2_weight))
    mixed_low, grad_packed = attention(
        first_in,
        cotangent,
        qkv_weight,
        qkv_bias,
        dense_weight,
        segment_ids,
        positions,
        jnp.arange(TOK),
    )

    _, _, hidden_got, cot_got = after((grad_up, grad_packed, hidden_got, cot_got))
    hidden_far = jnp.concatenate([hidden_got, send(hidden_got, "c")], axis=0)
    cot_far = jnp.concatenate([cot_got, send(cot_got, "c")], axis=0)
    order_far = (jnp.arange(TOK) + core * half_rows) % TOK
    marks_far = jnp.concatenate(
        [lax.dynamic_slice_in_dim(marks_got, w * half_rows, half_rows, 1) for w in (core, 1 - core)],
        axis=1,
    )
    cot_far_rows, cot_far = turned(cot_far, keep=True)
    normed_far, _ = normalise(hidden_far)
    first_far = (normed_far * ln1_gain + ln1_bias).astype(BF16)
    second_far = (normed_far * ln2_gain + ln2_bias).astype(BF16)
    upward_far = plain_dot(second_far, cut(fc1_weight, half_units, 1)) + cut(
        fc1_bias.reshape(-1), half_units, 0
    )
    grad_up_far = gelu_both(upward_far, contract_cols(cot_far, cut(fc2_weight, half_units, 0)))
    mixed_far, grad_packed_far = attention(
        first_far,
        cot_far,
        cut(qkv_weight, 3 * HD, 1),
        cut(qkv_bias, 1, 0),
        cut(dense_weight, HD, 0),
        marks_far[0],
        marks_far[1],
        order_far,
    )
    second_far_rows = turned(second_far)
    first_far_rows = turned(first_far)

    def pair(own, far, width):
        return jnp.concatenate([cut(own, width, 1), far], axis=0)

    def beside(own, far):
        return jnp.concatenate([own, far], axis=1)

    widths = (half_units, HD, 3 * HD)
    joint_grad = jnp.concatenate(
        [
            plain_dot(beside(second_rows, second_far_rows), pair(grad_up, grad_up_far, widths[0])),
            plain_dot(beside(cot_rows, cot_far_rows), pair(mixed_low, mixed_far, widths[1])),
            plain_dot(beside(first_rows, first_far_rows), pair(grad_packed, grad_packed_far, widths[2])),
        ],
        axis=1,
    )
    joint_sum = lax.psum_scatter(joint_grad, ("x", "y"), scatter_dimension=0, tiled=True)
    _, mixed_low, act_low, grad_up, grad_packed = after(
        (joint_grad, mixed_low, act_low, grad_up, grad_packed)
    )

    def branch_half(which):
        return plain_dot(of_core(mixed_low, which), dense_weight) + plain_dot(
            of_core(act_low, which), fc2_weight
        )

    branch = branch_half(core) + send(branch_half(1 - core), "c")
    branch = branch + send(branch, "zh")
    output = both_cores(of_core(hidden, core) + branch + dense_bias + fc2_bias)

    first_part = contract_cols(grad_packed, qkv_weight)
    second_part = contract_cols(grad_up, fc1_weight)
    combined = first_part * ln1_gain + second_part * ln2_gain
    combined = of_core(combined, core) + send(of_core(combined, 1 - core), "c")
    combined = combined + send(combined, "zh")
    normed_half = of_core(normed, core)
    grad_out = cotangent.astype(F32)
    input_half = of_core(grad_out, core) + of_core(inv_std, core) * (
        combined
        - jnp.mean(combined, axis=-1, keepdims=True)
        - normed_half * jnp.mean(combined * normed_half, axis=-1, keepdims=True)
    )
    input_grad = both_cores(input_half)

    gain_one_grad = jnp.sum(first_part * normed, axis=0)
    shift_one_grad = jnp.sum(first_part, axis=0)
    gain_two_grad = jnp.sum(second_part * normed, axis=0)
    shift_two_grad = jnp.sum(second_part, axis=0)
    bias_sum = jnp.sum(grad_out, axis=0)
    qkv_bias_sum = jnp.sum(grad_packed.astype(F32), axis=0)
    up_bias_grad = jnp.sum(grad_up.astype(F32), axis=0)
    features = jnp.stack(
        [gain_one_grad, shift_one_grad, gain_two_grad, shift_two_grad, bias_sum]
    ).reshape(5, 32, 64)
    small = jnp.concatenate(
        [
            features.transpose(1, 0, 2).reshape(32, 320),
            qkv_bias_sum.reshape(2, 32, 24).transpose(1, 0, 2).reshape(32, 48),
            up_bias_grad.reshape(16, 32, 4).transpose(1, 0, 2).reshape(32, 64),
            jnp.zeros((32, 80), F32),
        ],
        axis=1,
    )
    small = lax.psum(small, ("x", "y"))
    block = lax.axis_index("x") * 4 + lax.axis_index("y")
    own_small = lax.dynamic_slice_in_dim(small, side * 16 + block, 1, 0)
    far_small = lax.dynamic_slice_in_dim(small, (1 - side) * 16 + block, 1, 0)
    small = (own_small + send(far_small, "zl")).reshape(-1)
    norms = small[:256]
    norms = norms + send(norms, "c")
    norms = (norms + send(norms, "zh")).reshape(4, 64)
    bias_total = small[256:320]

    def of_side(values, which):
        return lax.dynamic_slice_in_dim(values, which * 64, 64, 0)

    down_sum = of_side(down_sum, side) + send(of_side(down_sum, 1 - side), "zl")
    near = of_side(joint_sum, side)
    far = send(of_side(joint_sum, 1 - side), "zl")
    low = jnp.where(side == 0, near, far)
    high = jnp.where(side == 0, far, near)
    sums = []
    start = 0
    for width in widths:
        sums.append(
            jnp.concatenate([low[:, start : start + width], high[:, start : start + width]], axis=1)
        )
        start += width
    up_sum, dense_sum, qkv_sum = sums
    return (
        output,
        input_grad,
        norms[0],
        norms[1],
        qkv_sum,
        small[320:368].reshape(2, 24),
        dense_sum.T,
        bias_total,
        norms[2],
        norms[3],
        up_sum,
        small[368:432].reshape(16, 4),
        down_sum.T,
        bias_total,
    )


def solution(mesh):
    fine = Mesh(mesh.devices.reshape(tuple(SIZES.values())), tuple(SIZES))
    return jax.shard_map(
        body,
        mesh=fine,
        in_specs=(
            P(DP, None),
            P(DP),
            P(DP),
            P(),
            P(),
            P(None, TENSOR),
            P(TENSOR, None),
            P(TENSOR, None),
            P(),
            P(),
            P(),
            P(None, TENSOR),
            P(TENSOR, None),
            P(TENSOR, None),
            P(),
            P(DP, None),
        ),
        out_specs=(
            P(DP, None),
            P(DP, None),
            P(DP),
            P(DP),
            P(DP, TENSOR),
            P(TENSOR, DP),
            P(TENSOR, DP),
            P(DP),
            P(DP),
            P(DP),
            P(DP, TENSOR),
            P(TENSOR, DP),
            P(TENSOR, DP),
            P(DP),
        ),
        check_vma=False,
    )
```

```python
from functools import partial
import math

import jax
import jax.numpy as jnp
from jax import lax
from jax.experimental import pallas as pl
from jax.experimental.pallas import tpu as pltpu
from jax.sharding import Mesh, PartitionSpec as P

HD = 256
ROT = 64
TOK = 512
D = 2048
EPSILON = 1e-05
NEGATIVE = -1000000000.0
SIZES = {"zl": 2, "x": 4, "y": 4, "zh": 2, "c": 2}
DP = ("zl", "x", "y")
TENSOR = ("zh", "c")
F32 = jnp.float32
BF16 = jnp.bfloat16


def send(value, axis, step=1):
    n = SIZES[axis]
    return lax.ppermute(value, axis, [(i, (i + step) % n) for i in range(n)])


def swap(value, axis, bit):
    return lax.ppermute(value, axis, [(i, i ^ bit) for i in range(SIZES[axis])])


def plain_dot(left, right):
    return jnp.dot(left, right, preferred_element_type=F32)


def contract_cols(left, right):
    return lax.dot_general(left, right, (((1,), (1,)), ((), ())), preferred_element_type=F32)


VMEM = 56 * 1024 * 1024


def whole(shape):
    return pl.BlockSpec(shape, lambda *_: (0,) * len(shape), pipeline_mode=pl.Buffered(1))


def by_destination(rows):
    lane = lax.broadcasted_iota(jnp.int32, (rows.shape[0], 128), 1)
    pieces = []
    for pair in range(8):
        low = rows[:, pair * 128 : pair * 128 + 128]
        high = rows[:, 1024 + pair * 128 : 1024 + pair * 128 + 128]
        pieces.append(jnp.where(lane < 64, low, pltpu.roll(high, 64, 1)))
        pieces.append(jnp.where(lane < 64, pltpu.roll(low, 64, 1), high))
    return jnp.concatenate(pieces, axis=1)


def norm_rows(hidden, cot, gain_one, shift_one, gain_two, shift_two, targets):
    average = jnp.mean(hidden, axis=-1, keepdims=True)
    centred = hidden - average
    inv_std = lax.rsqrt(jnp.mean(centred * centred, axis=-1, keepdims=True) + EPSILON)
    normed = centred * inv_std
    first = normed * gain_one[...] + shift_one[...]
    second = normed * gain_two[...] + shift_two[...]
    targets[0][...] = first.astype(BF16)
    targets[1][...] = second.astype(BF16)
    targets[2][...] = by_destination(first).astype(BF16)
    targets[3][...] = by_destination(second).astype(BF16)
    targets[4][...] = by_destination(cot).astype(BF16)
    if len(targets) > 5:
        targets[5][...] = cot.astype(BF16)


def norm_kernel(hidden, cot, gain_one, shift_one, gain_two, shift_two, *targets):
    norm_rows(
        hidden[...].astype(F32),
        cot[...].astype(F32),
        gain_one,
        shift_one,
        gain_two,
        shift_two,
        targets,
    )


def norm_far_kernel(
    hidden, hidden_too, cot, cot_too, gain_one, shift_one, gain_two, shift_two, *targets
):
    params = (gain_one, shift_one, gain_two, shift_two, targets)

    @pl.when(pl.program_id(0) < 2)
    def _():
        norm_rows(hidden[...], cot[...], *params)

    @pl.when(pl.program_id(0) >= 2)
    def _():
        norm_rows(hidden_too[...], cot_too[...], *params)


def norms_in(hidden, cot, params):
    far = len(hidden) == 2
    rows = 128
    if far:
        picks = (lambda i: (lax.min(i, 1), 0), lambda i: (lax.max(i - 2, 0), 0))
        specs = [pl.BlockSpec((rows, D), p) for p in picks] * 2
    else:
        specs = [pl.BlockSpec((rows, D), lambda i: (i, 0))] * 2
    n = 6 if far else 5
    return pl.pallas_call(
        norm_far_kernel if far else norm_kernel,
        grid=(TOK // rows,),
        in_specs=specs + [whole((1, D))] * 4,
        out_specs=[pl.BlockSpec((rows, D), lambda i: (i, 0))] * n,
        out_shape=[jax.ShapeDtypeStruct((TOK, D), BF16)] * n,
        compiler_params=pltpu.CompilerParams(vmem_limit_bytes=VMEM),
        cost_estimate=pl.CostEstimate(
            flops=20 * TOK * D, bytes_accessed=14 * TOK * D, transcendentals=0
        ),
    )(*hidden, *cot, *(p.reshape(1, D) for p in params))


def feed_kernel(scatter, side, second, cot, *refs):
    if scatter:
        cot_to, up_weight, up_bias, down_weight, act_out, up_grad, down_grad = refs
    else:
        up_weight, up_bias, down_weight, up_grad = refs
    upward = plain_dot(second[...], up_weight[...]) + up_bias[...]
    below = 0.5 * (1.0 + lax.erf(upward * math.sqrt(0.5)))
    if scatter:
        act = (upward * below).astype(BF16)
        act_out[...] = act
        total = plain_dot(act.T, cot_to[...])
        for d in range(16):
            down_grad[d] = total[:, d * 128 : d * 128 + 128]
    slope = below + upward * (jnp.exp(-0.5 * upward * upward) * (1.0 / math.sqrt(2.0 * math.pi)))
    up_grad[...] = (contract_cols(cot[...], down_weight[...]) * slope).astype(BF16)


def feed(side, second, cot, up_weight, up_bias, down_weight, cot_to=None):
    scatter = cot_to is not None
    width = 256
    units = up_weight.shape[1] if scatter else up_weight.shape[1] // 2
    steps = units // width
    at = (lambda j, s: j) if scatter else (lambda j, s: s[0] * steps + j)
    specs = [whole((TOK, D))] * (3 if scatter else 2)
    specs += [
        pl.BlockSpec((D, width), lambda j, s: (0, at(j, s))),
        pl.BlockSpec((1, width), lambda j, s: (0, at(j, s))),
        pl.BlockSpec((width, D), lambda j, s: (at(j, s), 0)),
    ]
    out_specs = [pl.BlockSpec((TOK, width), lambda j, s: (0, j))]
    shapes = [jax.ShapeDtypeStruct((TOK, units), BF16)]
    if scatter:
        out_specs = out_specs * 2 + [pl.BlockSpec((16, width, 128), lambda j, s: (0, j, 0))]
        shapes = shapes * 2 + [jax.ShapeDtypeStruct((16, units, 128), F32)]
    operands = (second, cot) + ((cot_to,) if scatter else ())
    return pl.pallas_call(
        partial(feed_kernel, scatter),
        grid_spec=pltpu.PrefetchScalarGridSpec(
            num_scalar_prefetch=1, grid=(steps,), in_specs=specs, out_specs=out_specs
        ),
        out_shape=shapes,
        compiler_params=pltpu.CompilerParams(vmem_limit_bytes=VMEM),
        cost_estimate=pl.CostEstimate(
            flops=(6 if scatter else 4) * TOK * D * units,
            bytes_accessed=(12 if scatter else 4) * D * units,
            transcendentals=2 * TOK * units,
        ),
    )(side, *operands, up_weight, up_bias.reshape(1, -1), down_weight)


def turn(values, tables, sign):
    first = values[:, :128]
    cosine, rising, falling = tables
    first = (
        first * cosine[...]
        + (pltpu.roll(first, 32, 1) * rising[...] + pltpu.roll(first, 96, 1) * falling[...]) * sign
    )
    return jnp.concatenate([first, values[:, 128:]], axis=1)


def attend_kernel(
    side, first, cot, weight, bias, dense, cosine, rising, falling, marks, marks_too, mixed_out, grad_out
):
    tables = (cosine, rising, falling)
    scale = 1.0 / math.sqrt(HD)
    packed = plain_dot(first[...], weight[...]) + bias[0]
    queries = turn(packed[:, :HD], tables, 1.0).astype(BF16)
    keys = turn(packed[:, HD : 2 * HD], tables, 1.0).astype(BF16)
    values = packed[:, 2 * HD :].astype(BF16)
    scores = contract_cols(queries, keys) * scale
    allowed = (marks[:, 0:1] == marks_too[0:1, :]) & (marks[:, 1:2] >= marks_too[1:2, :])
    scores = jnp.where(allowed, scores, NEGATIVE)
    top = jnp.max(scores, axis=-1, keepdims=True)
    weights = jnp.exp(scores - top)
    probs = weights / jnp.sum(weights, axis=-1, keepdims=True)
    probs_low = probs.astype(BF16)
    mixed_out[...] = plain_dot(probs_low, values).astype(BF16)
    grad_mixed = contract_cols(cot[...], dense[...]).astype(BF16)
    grad_probs = contract_cols(grad_mixed, values)
    along = jnp.sum(probs * grad_probs, axis=-1, keepdims=True)
    grad_scores = (probs * (grad_probs - along)).astype(BF16)
    grad_query = plain_dot(grad_scores, keys) * scale
    grad_key = plain_dot(grad_scores.T, queries) * scale
    grad_value = plain_dot(probs_low.T, grad_mixed)
    grad_out[:, :HD] = turn(grad_query, tables, -1.0).astype(BF16)
    grad_out[:, HD : 2 * HD] = turn(grad_key, tables, -1.0).astype(BF16)
    grad_out[:, 2 * HD :] = grad_value.astype(BF16)


def attend(side, heads, first, cot, weight, bias, dense, segments, positions, order):
    halves = jnp.arange(ROT // 2, dtype=F32)
    inverse = 10000.0 ** (-2.0 * halves / ROT)
    angles = positions.astype(F32)[:, None] * inverse
    cosine, sine = jnp.cos(angles), jnp.sin(angles)
    none, rest = jnp.zeros((TOK, 32), F32), jnp.zeros((TOK, 64), F32)
    tables = (
        jnp.concatenate([cosine, cosine, rest + 1.0], axis=1),
        jnp.concatenate([none, sine, rest], axis=1),
        jnp.concatenate([-sine, none, rest], axis=1),
    )
    marks = jnp.stack([segments, order], axis=1)
    at = (lambda h, s: h) if heads == 2 else (lambda h, s: s[0])
    return pl.pallas_call(
        attend_kernel,
        grid_spec=pltpu.PrefetchScalarGridSpec(
            num_scalar_prefetch=1,
            grid=(heads,),
            in_specs=[
                whole((TOK, D)),
                whole((TOK, D)),
                pl.BlockSpec((D, 3 * HD), lambda h, s: (0, at(h, s))),
                pl.BlockSpec((1, 1, 3 * HD), lambda h, s: (at(h, s), 0, 0)),
                pl.BlockSpec((HD, D), lambda h, s: (at(h, s), 0)),
            ]
            + [whole((TOK, 128))] * 3
            + [whole((TOK, 2)), whole((2, TOK))],
            out_specs=[
                pl.BlockSpec((TOK, HD), lambda h, s: (0, h)),
                pl.BlockSpec((TOK, 3 * HD), lambda h, s: (0, h)),
            ],
        ),
        out_shape=[
            jax.ShapeDtypeStruct((TOK, heads * HD), BF16),
            jax.ShapeDtypeStruct((TOK, heads * 3 * HD), BF16),
        ],
        compiler_params=pltpu.CompilerParams(vmem_limit_bytes=VMEM),
        cost_estimate=pl.CostEstimate(
            flops=heads * (8 * TOK * D * HD + 14 * TOK * TOK * HD),
            bytes_accessed=4 * TOK * D + heads * 8 * D * HD,
            transcendentals=heads * TOK * TOK,
        ),
    )(
        side,
        first,
        cot,
        weight,
        bias.reshape(-1, 1, 3 * HD),
        dense,
        *tables,
        marks,
        marks.T,
    )


def joint_kernel(side, *refs):
    lefts, rights, target = refs[:6], refs[6:12], refs[12]
    step = pl.program_id(0)

    def put(left, right):
        total = plain_dot(right[0][...].T, left[0][...])
        total = total + plain_dot(right[1][...].T, left[1][...])
        for d in range(16):
            target[d] = total[:, d * 128 : d * 128 + 128]

    for k, (start, stop) in enumerate(((0, 4), (4, 5), (5, 8))):

        @pl.when((step >= start) & (step < stop))
        def _(k=k):
            put(lefts[2 * k : 2 * k + 2], rights[2 * k : 2 * k + 2])


def joint(side, lefts, rights):
    width = 256
    specs = [whole((TOK, D))] * 6
    for start, n in ((0, 4), (4, 1), (5, 3)):

        def near(j, s, start=start, n=n):
            return (0, s[0] * n + jnp.clip(j - start, 0, n - 1))

        def far(j, s, start=start, n=n):
            return (0, jnp.clip(j - start, 0, n - 1))

        specs += [pl.BlockSpec((TOK, width), near), pl.BlockSpec((TOK, width), far)]
    return pl.pallas_call(
        joint_kernel,
        grid_spec=pltpu.PrefetchScalarGridSpec(
            num_scalar_prefetch=1,
            grid=(8,),
            in_specs=specs,
            out_specs=pl.BlockSpec((16, width, 128), lambda j, s: (0, j, 0)),
        ),
        out_shape=jax.ShapeDtypeStruct((16, 8 * width, 128), F32),
        compiler_params=pltpu.CompilerParams(vmem_limit_bytes=VMEM),
        cost_estimate=pl.CostEstimate(
            flops=4 * TOK * D * 2048, bytes_accessed=36 * TOK * D, transcendentals=0
        ),
    )(side, *lefts, *rights)


def body(
    hidden_in,
    segment_ids,
    positions,
    ln1_gain,
    ln1_bias,
    qkv_weight,
    qkv_bias,
    dense_weight,
    dense_bias,
    ln2_gain,
    ln2_bias,
    fc1_weight,
    fc1_bias,
    fc2_weight,
    fc2_bias,
    cotangent,
):
    core = lax.axis_index("c")
    side = lax.axis_index("zl")
    at_side = side.astype(jnp.int32).reshape(1)
    half_rows = TOK // 2
    after = lax.optimization_barrier
    params = (ln1_gain, ln1_bias, ln2_gain, ln2_bias)

    def of_core(values, which):
        return lax.dynamic_slice_in_dim(values, which * half_rows, half_rows, 0)

    def both_cores(mine):
        theirs = send(mine, "c")
        filled = jnp.zeros((TOK,) + mine.shape[1:], mine.dtype)
        filled = lax.dynamic_update_slice_in_dim(filled, mine, core * half_rows, 0)
        return lax.dynamic_update_slice_in_dim(filled, theirs, (1 - core) * half_rows, 0)

    hidden_got = send(of_core(hidden_in, core).astype(F32), "zl")
    cot_got = send(of_core(cotangent, core).astype(F32), "zl")
    marks_got = send(jnp.stack([segment_ids, positions]), "zl")

    first_in, second_in, first_to, second_to, cot_to = norms_in((hidden_in,), (cotangent,), params)
    act_low, grad_up, down_grad = feed(
        at_side, second_in, cotangent, fc1_weight, fc1_bias, fc2_weight, cot_to
    )
    down_sum = lax.psum_scatter(down_grad, ("x", "y"), scatter_dimension=0, tiled=True)
    _, first_in = after((down_grad, first_in))
    mixed_low, grad_packed = attend(
        at_side,
        2,
        first_in,
        cotangent,
        qkv_weight,
        qkv_bias,
        dense_weight,
        segment_ids,
        positions,
        jnp.arange(TOK, dtype=jnp.int32),
    )

    _, hidden_got, cot_got = after((grad_packed, hidden_got, cot_got))
    first_far, second_far, first_far_to, second_far_to, cot_far_to, cot_far = norms_in(
        (hidden_got, send(hidden_got, "c")), (cot_got, send(cot_got, "c")), params
    )
    (grad_up_far,) = feed(at_side, second_far, cot_far, fc1_weight, fc1_bias, fc2_weight)
    marks_far = jnp.concatenate(
        [lax.dynamic_slice_in_dim(marks_got, w * half_rows, half_rows, 1) for w in (core, 1 - core)],
        axis=1,
    )
    mixed_far, grad_packed_far = attend(
        at_side,
        1,
        first_far,
        cot_far,
        qkv_weight,
        qkv_bias,
        dense_weight,
        marks_far[0],
        marks_far[1],
        (jnp.arange(TOK, dtype=jnp.int32) + core.astype(jnp.int32) * half_rows) % TOK,
    )
    joint_grad = joint(
        at_side,
        (second_to, second_far_to, cot_to, cot_far_to, first_to, first_far_to),
        (grad_up, grad_up_far, mixed_low, mixed_far, grad_packed, grad_packed_far),
    )
    joint_sum = lax.psum_scatter(joint_grad, ("x", "y"), scatter_dimension=0, tiled=True)
    _, mixed_low, act_low, grad_up, grad_packed, hidden_in, cotangent = after(
        (joint_grad, mixed_low, act_low, grad_up, grad_packed, hidden_in, cotangent)
    )

    def branch_half(which):
        return plain_dot(of_core(mixed_low, which), dense_weight) + plain_dot(
            of_core(act_low, which), fc2_weight
        )

    hidden = hidden_in.astype(F32)
    average = jnp.mean(hidden, axis=-1, keepdims=True)
    centred = hidden - average
    inv_std = lax.rsqrt(jnp.mean(centred * centred, axis=-1, keepdims=True) + EPSILON)
    normed = centred * inv_std
    branch = branch_half(core) + send(branch_half(1 - core), "c")
    branch = branch + send(branch, "zh")
    output = both_cores(of_core(hidden, core) + branch + dense_bias + fc2_bias)

    first_part = contract_cols(grad_packed, qkv_weight)
    second_part = contract_cols(grad_up, fc1_weight)
    combined = first_part * ln1_gain + second_part * ln2_gain
    combined = of_core(combined, core) + send(of_core(combined, 1 - core), "c")
    combined = combined + send(combined, "zh")
    normed_half = of_core(normed, core)
    grad_out = cotangent.astype(F32)
    input_half = of_core(grad_out, core) + of_core(inv_std, core) * (
        combined
        - jnp.mean(combined, axis=-1, keepdims=True)
        - normed_half * jnp.mean(combined * normed_half, axis=-1, keepdims=True)
    )
    input_grad = both_cores(input_half)

    norms = jnp.stack(
        [
            jnp.sum(first_part * normed, axis=0),
            jnp.sum(first_part, axis=0),
            jnp.sum(second_part * normed, axis=0),
            jnp.sum(second_part, axis=0),
        ]
    )
    norms = norms.reshape(4, 32, 64).transpose(1, 0, 2).reshape(32, 256)
    norms = norms + send(norms, "c")
    norms = norms + send(norms, "zh")
    bias_sum = jnp.sum(grad_out, axis=0)
    qkv_bias_sum = jnp.sum(grad_packed.astype(F32), axis=0)
    up_bias_grad = jnp.sum(grad_up.astype(F32), axis=0)
    small = jnp.concatenate(
        [
            norms,
            bias_sum.reshape(32, 64),
            qkv_bias_sum.reshape(2, 32, 24).transpose(1, 0, 2).reshape(32, 48),
            up_bias_grad.reshape(16, 32, 4).transpose(1, 0, 2).reshape(32, 64),
            jnp.zeros((32, 80), F32),
        ],
        axis=1,
    )
    for axis in ("x", "y"):
        small = small + swap(small, axis, 1)
        small = small + swap(small, axis, 2)
    block = lax.axis_index("x") * 4 + lax.axis_index("y")
    own_small = lax.dynamic_slice_in_dim(small, side * 16 + block, 1, 0)
    far_small = lax.dynamic_slice_in_dim(small, (1 - side) * 16 + block, 1, 0)
    small = (own_small + send(far_small, "zl")).reshape(-1)
    norms = small[:256].reshape(4, 64)
    bias_total = small[256:320]

    def of_side(values, which):
        return lax.dynamic_slice_in_dim(values.reshape(-1, 2, 64), which, 1, 1)[:, 0]

    down_sum = of_side(down_sum, side) + send(of_side(down_sum, 1 - side), "zl")
    near = of_side(joint_sum, side)
    far = send(of_side(joint_sum, 1 - side), "zl")
    low = jnp.where(side == 0, near, far)
    high = jnp.where(side == 0, far, near)
    sums = []
    start = 0
    for width in (1024, 256, 768):
        stop = start + width
        sums.append(jnp.concatenate([low[start:stop], high[start:stop]], axis=0))
        start = stop
    up_sum, dense_sum, qkv_sum = sums
    return (
        output,
        input_grad,
        norms[0],
        norms[1],
        qkv_sum.T,
        small[320:368].reshape(2, 24),
        dense_sum,
        bias_total,
        norms[2],
        norms[3],
        up_sum.T,
        small[368:432].reshape(16, 4),
        down_sum,
        bias_total,
    )


def solution(mesh):
    fine = Mesh(mesh.devices.reshape(tuple(SIZES.values())), tuple(SIZES))
    return jax.shard_map(
        body,
        mesh=fine,
        in_specs=(
            P(DP, None),
            P(DP),
            P(DP),
            P(),
            P(),
            P(None, TENSOR),
            P(TENSOR, None),
            P(TENSOR, None),
            P(),
            P(),
            P(),
            P(None, TENSOR),
            P(TENSOR, None),
            P(TENSOR, None),
            P(),
            P(DP, None),
        ),
        out_specs=(
            P(DP, None),
            P(DP, None),
            P(DP),
            P(DP),
            P(DP, TENSOR),
            P(TENSOR, DP),
            P(TENSOR, DP),
            P(DP),
            P(DP),
            P(DP),
            P(DP, TENSOR),
            P(TENSOR, DP),
            P(TENSOR, DP),
            P(DP),
        ),
        check_vma=False,
    )
```

```python
from functools import partial
import math

import jax
import jax.numpy as jnp
from jax import lax
from jax.experimental import pallas as pl
from jax.experimental.pallas import tpu as pltpu
from jax.sharding import Mesh, PartitionSpec as P

HD = 256
ROT = 64
TOK = 512
D = 2048
EPSILON = 1e-05
NEGATIVE = -1000000000.0
SIZES = {"zl": 2, "x": 4, "y": 4, "zh": 2, "c": 2}
DP = ("zl", "x", "y")
TENSOR = ("zh", "c")
F32 = jnp.float32
BF16 = jnp.bfloat16


def send(value, axis, step=1):
    n = SIZES[axis]
    return lax.ppermute(value, axis, [(i, (i + step) % n) for i in range(n)])


def swap(value, axis, bit):
    return lax.ppermute(value, axis, [(i, i ^ bit) for i in range(SIZES[axis])])


def plain_dot(left, right):
    return jnp.dot(left, right, preferred_element_type=F32)


def contract_cols(left, right):
    return lax.dot_general(left, right, (((1,), (1,)), ((), ())), preferred_element_type=F32)


VMEM = 56 * 1024 * 1024
COST = pl.CostEstimate(flops=1000000, bytes_accessed=1000000, transcendentals=0)


def whole(shape):
    return pl.BlockSpec(shape, lambda *_: (0,) * len(shape), pipeline_mode=pl.Buffered(1))


def put_turned(target, rows):
    for z in range(2):
        for pair in range(8):
            start = z * 1024 + pair * 128
            block = rows[:, start : start + 128].T.astype(BF16)
            target[2 * pair, z] = block[:64]
            target[2 * pair + 1, z] = block[64:]


def normalise(hidden):
    average = jnp.mean(hidden, axis=-1, keepdims=True)
    centred = hidden - average
    inv_std = lax.rsqrt(jnp.mean(centred * centred, axis=-1, keepdims=True) + EPSILON)
    return centred * inv_std, inv_std


def second_kernel(hidden, cot, gain, shift, second_out, cot_turned):
    normed, _ = normalise(hidden[...].astype(F32))
    second_out[...] = (normed * gain[...] + shift[...]).astype(BF16)
    put_turned(cot_turned, cot[...].astype(F32))


def first_kernel(hidden, gain, shift, gain_two, shift_two, first_out, first_turned, second_turned):
    normed, _ = normalise(hidden[...].astype(F32))
    first = normed * gain[...] + shift[...]
    first_out[...] = first.astype(BF16)
    put_turned(first_turned, first)
    put_turned(second_turned, normed * gain_two[...] + shift_two[...])


def far_kernel(near, other, gain, shift, gain_two, shift_two, *refs):
    first_out, second_out, cot_out, first_turned, second_turned, cot_turned = refs[3:]

    def step(rows):
        cot = rows[1]
        normed, _ = normalise(rows[0])
        first = normed * gain[...] + shift[...]
        second = normed * gain_two[...] + shift_two[...]
        first_out[...] = first.astype(BF16)
        second_out[...] = second.astype(BF16)
        cot_out[...] = cot.astype(BF16)
        put_turned(first_turned, first)
        put_turned(second_turned, second)
        put_turned(cot_turned, cot)

    @pl.when(pl.program_id(0) < 2)
    def _():
        step(near)

    @pl.when(pl.program_id(0) >= 2)
    def _():
        step(other)


TURNED = (16, 2, 64, 2 * TOK)


def norm_call(kernel, rows, n_rows, n_plain, n_turned, params, far=()):
    steps = TOK // rows
    plain = pl.BlockSpec((rows, D), lambda i: (i, 0))
    shift = steps if far else 0
    turned = pl.BlockSpec((16, 2, 64, rows), lambda i: (0, 0, 0, i + shift))
    if far:
        picks = (lambda i: (0, lax.min(i, 1), 0), lambda i: (0, lax.max(i - 2, 0), 0))
        specs = [pl.BlockSpec((2, rows, D), p) for p in picks]
    else:
        specs = [plain] * len(n_rows)
    operands = list(n_rows) + [p.reshape(1, D) for p in params]
    aliases = {len(operands) + i: n_plain + i for i in range(len(far))}
    return pl.pallas_call(
        kernel,
        grid=(steps,),
        in_specs=specs + [whole((1, D))] * len(params) + [pl.BlockSpec(memory_space=pl.ANY)] * len(far),
        out_specs=[plain] * n_plain + [turned] * n_turned,
        out_shape=[jax.ShapeDtypeStruct((TOK, D), BF16)] * n_plain
        + [jax.ShapeDtypeStruct(TURNED, BF16)] * n_turned,
        input_output_aliases=aliases,
        compiler_params=pltpu.CompilerParams(vmem_limit_bytes=VMEM),
        cost_estimate=COST,
    )(*operands, *far)


def phi(upward):
    return 0.5 * (1.0 + lax.erf(upward * math.sqrt(0.5)))


def gelu_slope(upward, below):
    return below + upward * (jnp.exp(-0.5 * upward * upward) * (1.0 / math.sqrt(2.0 * math.pi)))


def feed_kernel(second, cot_turned, weight, bias, act_out, slope_out, down_grad):
    upward = plain_dot(second[...], weight[...]) + bias[...]
    below = phi(upward)
    act = (upward * below).astype(BF16)
    act_out[...] = act
    slope_out[...] = gelu_slope(upward, below)
    down_grad[...] = plain_dot(cot_turned[...].reshape(D, TOK), act).reshape(16, 128, -1)


def feed(second, cot_turned, weight, bias):
    units, width = weight.shape[1], 512
    column = pl.BlockSpec((TOK, width), lambda j: (0, j))
    return pl.pallas_call(
        feed_kernel,
        grid=(units // width,),
        in_specs=[
            whole((TOK, D)),
            whole((16, 2, 64, TOK)),
            pl.BlockSpec((D, width), lambda j: (0, j)),
            pl.BlockSpec((1, width), lambda j: (0, j)),
        ],
        out_specs=[column, column, pl.BlockSpec((16, 128, width), lambda j: (0, 0, j))],
        out_shape=[
            jax.ShapeDtypeStruct((TOK, units), BF16),
            jax.ShapeDtypeStruct((TOK, units), F32),
            jax.ShapeDtypeStruct((16, 128, units), F32),
        ],
        compiler_params=pltpu.CompilerParams(vmem_limit_bytes=VMEM),
        cost_estimate=COST,
    )(second, cot_turned, weight, bias.reshape(1, -1))


def feed_back_kernel(cot, weight, slope, up_grad):
    up_grad[...] = (contract_cols(cot[...], weight[...]) * slope[...]).astype(BF16)


def feed_back(cot, weight, slope):
    units, width = weight.shape[0], 512
    column = pl.BlockSpec((TOK, width), lambda j: (0, j))
    return pl.pallas_call(
        feed_back_kernel,
        grid=(units // width,),
        in_specs=[whole((TOK, D)), pl.BlockSpec((width, D), lambda j: (j, 0)), column],
        out_specs=column,
        out_shape=jax.ShapeDtypeStruct((TOK, units), BF16),
        compiler_params=pltpu.CompilerParams(vmem_limit_bytes=VMEM),
        cost_estimate=COST,
    )(cot, weight, slope)


def feed_far_kernel(side, second, cot, up_weight, up_bias, down_weight, up_grad):
    upward = plain_dot(second[...], up_weight[...]) + up_bias[...]
    slope = gelu_slope(upward, phi(upward))
    up_grad[...] = (contract_cols(cot[...], down_weight[...]) * slope).astype(BF16)


def feed_far(side, second, cot, up_weight, up_bias, down_weight):
    width = 256
    units = up_weight.shape[1] // 2
    steps = units // width
    return pl.pallas_call(
        feed_far_kernel,
        grid_spec=pltpu.PrefetchScalarGridSpec(
            num_scalar_prefetch=1,
            grid=(steps,),
            in_specs=[
                whole((TOK, D)),
                whole((TOK, D)),
                pl.BlockSpec((D, width), lambda j, s: (0, s[0] * steps + j)),
                pl.BlockSpec((1, width), lambda j, s: (0, s[0] * steps + j)),
                pl.BlockSpec((width, D), lambda j, s: (s[0] * steps + j, 0)),
            ],
            out_specs=pl.BlockSpec((TOK, width), lambda j, s: (0, j)),
        ),
        out_shape=jax.ShapeDtypeStruct((TOK, units), BF16),
        compiler_params=pltpu.CompilerParams(vmem_limit_bytes=VMEM),
        cost_estimate=COST,
    )(side, second, cot, up_weight, up_bias.reshape(1, -1), down_weight)


def turn(values, tables, sign):
    first = values[:, :128]
    cosine, rising, falling = tables
    first = (
        first * cosine[...]
        + (pltpu.roll(first, 32, 1) * rising[...] + pltpu.roll(first, 96, 1) * falling[...]) * sign
    )
    return jnp.concatenate([first, values[:, 128:]], axis=1)


def attend_kernel(
    side, first, cot, weight, bias, dense, cosine, rising, falling, marks, marks_too, mixed_out, grad_out
):
    tables = (cosine, rising, falling)
    scale = 1.0 / math.sqrt(HD)
    packed = plain_dot(first[...], weight[...]) + bias[0]
    queries = turn(packed[:, :HD], tables, 1.0).astype(BF16)
    keys = turn(packed[:, HD : 2 * HD], tables, 1.0).astype(BF16)
    values = packed[:, 2 * HD :].astype(BF16)
    scores = contract_cols(queries, keys) * scale
    allowed = (marks[:, 0:1] == marks_too[0:1, :]) & (marks[:, 1:2] >= marks_too[1:2, :])
    scores = jnp.where(allowed, scores, NEGATIVE)
    top = jnp.max(scores, axis=-1, keepdims=True)
    weights = jnp.exp(scores - top)
    probs = weights / jnp.sum(weights, axis=-1, keepdims=True)
    probs_low = probs.astype(BF16)
    mixed_out[...] = plain_dot(probs_low, values).astype(BF16)
    grad_mixed = contract_cols(cot[...], dense[...]).astype(BF16)
    grad_probs = contract_cols(grad_mixed, values)
    along = jnp.sum(probs * grad_probs, axis=-1, keepdims=True)
    grad_scores = (probs * (grad_probs - along)).astype(BF16)
    grad_query = plain_dot(grad_scores, keys) * scale
    grad_key = plain_dot(grad_scores.T, queries) * scale
    grad_value = plain_dot(probs_low.T, grad_mixed)
    grad_out[:, :HD] = turn(grad_query, tables, -1.0).astype(BF16)
    grad_out[:, HD : 2 * HD] = turn(grad_key, tables, -1.0).astype(BF16)
    grad_out[:, 2 * HD :] = grad_value.astype(BF16)


def attend(side, heads, first, cot, weight, bias, dense, segments, positions, order):
    halves = jnp.arange(ROT // 2, dtype=F32)
    inverse = 10000.0 ** (-2.0 * halves / ROT)
    angles = positions.astype(F32)[:, None] * inverse
    cosine, sine = jnp.cos(angles), jnp.sin(angles)
    none, rest = jnp.zeros((TOK, 32), F32), jnp.zeros((TOK, 64), F32)
    tables = (
        jnp.concatenate([cosine, cosine, rest + 1.0], axis=1),
        jnp.concatenate([none, sine, rest], axis=1),
        jnp.concatenate([-sine, none, rest], axis=1),
    )
    marks = jnp.stack([segments, order], axis=1)
    at = (lambda h, s: h) if heads == 2 else (lambda h, s: s[0])
    return pl.pallas_call(
        attend_kernel,
        grid_spec=pltpu.PrefetchScalarGridSpec(
            num_scalar_prefetch=1,
            grid=(heads,),
            in_specs=[
                whole((TOK, D)),
                whole((TOK, D)),
                pl.BlockSpec((D, 3 * HD), lambda h, s: (0, at(h, s))),
                pl.BlockSpec((1, 1, 3 * HD), lambda h, s: (at(h, s), 0, 0)),
                pl.BlockSpec((HD, D), lambda h, s: (at(h, s), 0)),
            ]
            + [whole((TOK, 128))] * 3
            + [whole((TOK, 2)), whole((2, TOK))],
            out_specs=[
                pl.BlockSpec((TOK, HD), lambda h, s: (0, h)),
                pl.BlockSpec((TOK, 3 * HD), lambda h, s: (0, h)),
            ],
        ),
        out_shape=[
            jax.ShapeDtypeStruct((TOK, heads * HD), BF16),
            jax.ShapeDtypeStruct((TOK, heads * 3 * HD), BF16),
        ],
        compiler_params=pltpu.CompilerParams(vmem_limit_bytes=VMEM),
        cost_estimate=COST,
    )(
        side,
        first,
        cot,
        weight,
        bias.reshape(-1, 1, 3 * HD),
        dense,
        *tables,
        marks,
        marks.T,
    )


def joint_kernel(side, *refs):
    lefts, rights, target = refs[:3], refs[3:9], refs[9]
    step = pl.program_id(0)
    for k, (start, stop) in enumerate(((0, 4), (4, 5), (5, 8))):

        @pl.when((step >= start) & (step < stop))
        def _(k=k):
            right = jnp.concatenate([rights[2 * k][...], rights[2 * k + 1][...]], axis=0)
            total = plain_dot(lefts[k][...].reshape(D, 2 * TOK), right)
            target[...] = total.reshape(16, 128, -1)


def joint(side, lefts, rights):
    width = 256
    specs = [whole(TURNED)] * 3
    for start, n in ((0, 4), (4, 1), (5, 3)):

        def near(j, s, start=start, n=n):
            return (0, s[0] * n + jnp.clip(j - start, 0, n - 1))

        def far(j, s, start=start, n=n):
            return (0, jnp.clip(j - start, 0, n - 1))

        specs += [pl.BlockSpec((TOK, width), near), pl.BlockSpec((TOK, width), far)]
    return pl.pallas_call(
        joint_kernel,
        grid_spec=pltpu.PrefetchScalarGridSpec(
            num_scalar_prefetch=1,
            grid=(8,),
            in_specs=specs,
            out_specs=pl.BlockSpec((16, 128, width), lambda j, s: (0, 0, j)),
        ),
        out_shape=jax.ShapeDtypeStruct((16, 128, 8 * width), F32),
        compiler_params=pltpu.CompilerParams(vmem_limit_bytes=VMEM),
        cost_estimate=COST,
    )(side, *lefts, *rights)


def body(
    hidden_in,
    segment_ids,
    positions,
    ln1_gain,
    ln1_bias,
    qkv_weight,
    qkv_bias,
    dense_weight,
    dense_bias,
    ln2_gain,
    ln2_bias,
    fc1_weight,
    fc1_bias,
    fc2_weight,
    fc2_bias,
    cotangent,
):
    core = lax.axis_index("c")
    side = lax.axis_index("zl")
    at_side = side.astype(jnp.int32).reshape(1)
    half_rows = TOK // 2
    after = lax.optimization_barrier
    params = (ln1_gain, ln1_bias, ln2_gain, ln2_bias)

    def of_core(values, which):
        return lax.dynamic_slice_in_dim(values, which * half_rows, half_rows, 0)

    def both_cores(mine):
        theirs = send(mine, "c")
        filled = jnp.zeros((TOK,) + mine.shape[1:], mine.dtype)
        filled = lax.dynamic_update_slice_in_dim(filled, mine, core * half_rows, 0)
        return lax.dynamic_update_slice_in_dim(filled, theirs, (1 - core) * half_rows, 0)

    sent = jnp.stack([of_core(hidden_in, core).astype(F32), of_core(cotangent, core).astype(F32)])
    pair_rows = lax.all_gather(sent, "zl")

    second_in, cot_turned = norm_call(
        second_kernel, 256, (hidden_in, cotangent), 1, 1, (ln2_gain, ln2_bias)
    )
    act_low, slope, down_grad = feed(second_in, cot_turned, fc1_weight, fc1_bias)
    down_sum = after(lax.psum_scatter(down_grad, ("x", "y"), scatter_dimension=0, tiled=True))
    _, cotangent, hidden_in = after((down_grad, cotangent, hidden_in))

    first_in, first_turned, second_turned = norm_call(
        first_kernel, 256, (hidden_in,), 1, 2, (ln1_gain, ln1_bias, ln2_gain, ln2_bias)
    )
    mixed_low, grad_packed = attend(
        at_side,
        2,
        first_in,
        cotangent,
        qkv_weight,
        qkv_bias,
        dense_weight,
        segment_ids,
        positions,
        jnp.arange(TOK, dtype=jnp.int32),
    )
    grad_up = feed_back(cotangent, fc2_weight, slope)

    def branch_half(which):
        return plain_dot(of_core(mixed_low, which), dense_weight) + plain_dot(
            of_core(act_low, which), fc2_weight
        )

    hidden = hidden_in.astype(F32)
    normed, inv_std = normalise(hidden)
    branch = branch_half(core) + send(branch_half(1 - core), "c")
    first_part = contract_cols(grad_packed, qkv_weight)
    second_part = contract_cols(grad_up, fc1_weight)
    combined = first_part * ln1_gain + second_part * ln2_gain
    combined = of_core(combined, core) + send(of_core(combined, 1 - core), "c")
    norms = jnp.stack(
        [
            jnp.sum(first_part * normed, axis=0),
            jnp.sum(first_part, axis=0),
            jnp.sum(second_part * normed, axis=0),
            jnp.sum(second_part, axis=0),
        ]
    )

    branch, combined, norms, pair_rows = after((branch, combined, norms, pair_rows))
    branch = lax.psum(branch, "zh")
    combined = lax.psum(combined, "zh")
    _, marks = after((pair_rows, jnp.stack([segment_ids, positions])))
    marks_got = send(marks, "zl")
    far_rows = lax.dynamic_index_in_dim(pair_rows, 1 - side, 0, keepdims=False)
    first_far, second_far, cot_far, first_turned, second_turned, cot_turned = norm_call(
        far_kernel,
        128,
        (far_rows, send(far_rows, "c")),
        3,
        3,
        params,
        (first_turned, second_turned, cot_turned),
    )
    grad_up_far = feed_far(at_side, second_far, cot_far, fc1_weight, fc1_bias, fc2_weight)
    marks_far = jnp.concatenate(
        [lax.dynamic_slice_in_dim(marks_got, w * half_rows, half_rows, 1) for w in (core, 1 - core)],
        axis=1,
    )
    mixed_far, grad_packed_far = attend(
        at_side,
        1,
        first_far,
        cot_far,
        qkv_weight,
        qkv_bias,
        dense_weight,
        marks_far[0],
        marks_far[1],
        (jnp.arange(TOK, dtype=jnp.int32) + core.astype(jnp.int32) * half_rows) % TOK,
    )
    joint_grad = joint(
        at_side,
        (second_turned, cot_turned, first_turned),
        (grad_up, grad_up_far, mixed_low, mixed_far, grad_packed, grad_packed_far),
    )
    joint_grad, down_sum = after((joint_grad, down_sum))
    joint_sum = after(lax.psum_scatter(joint_grad, ("x", "y"), scatter_dimension=0, tiled=True))
    _, norms, grad_packed, grad_up, cotangent, down_sum = after(
        (joint_grad, norms, grad_packed, grad_up, cotangent, down_sum)
    )

    norms = norms.reshape(4, 32, 64).transpose(1, 0, 2).reshape(32, 256)
    norms = norms + send(norms, "c")
    norms = norms + send(norms, "zh")
    grad_out = cotangent.astype(F32)
    bias_sum = jnp.sum(grad_out, axis=0)
    qkv_bias_sum = jnp.sum(grad_packed.astype(F32), axis=0)
    up_bias_grad = jnp.sum(grad_up.astype(F32), axis=0)
    small = jnp.concatenate(
        [
            norms,
            bias_sum.reshape(32, 64),
            qkv_bias_sum.reshape(2, 32, 24).transpose(1, 0, 2).reshape(32, 48),
            up_bias_grad.reshape(16, 32, 4).transpose(1, 0, 2).reshape(32, 64),
            jnp.zeros((32, 80), F32),
        ],
        axis=1,
    )
    for axis in ("x", "y"):
        small = small + swap(small, axis, 1)
        small = small + swap(small, axis, 2)
    block = lax.axis_index("x") * 4 + lax.axis_index("y")
    own_small = lax.dynamic_slice_in_dim(small, side * 16 + block, 1, 0)
    far_small = lax.dynamic_slice_in_dim(small, (1 - side) * 16 + block, 1, 0)
    small = (own_small + send(far_small, "zl")).reshape(-1)

    small, branch, combined = after((small, branch, combined))
    norms = small[:256].reshape(4, 64)
    bias_total = small[256:320]
    output = both_cores(of_core(hidden, core) + branch + dense_bias + fc2_bias)
    normed_half = of_core(normed, core)
    input_half = of_core(grad_out, core) + of_core(inv_std, core) * (
        combined
        - jnp.mean(combined, axis=-1, keepdims=True)
        - normed_half * jnp.mean(combined * normed_half, axis=-1, keepdims=True)
    )
    input_grad = both_cores(input_half)

    def of_side(values, which):
        return lax.dynamic_slice_in_dim(values[0], which * 64, 64, 0)

    down_sum = of_side(down_sum, side) + send(of_side(down_sum, 1 - side), "zl")
    near = of_side(joint_sum, side)
    far = send(of_side(joint_sum, 1 - side), "zl")
    low = jnp.where(side == 0, near, far)
    high = jnp.where(side == 0, far, near)
    sums = []
    start = 0
    for width in (1024, 256, 768):
        stop = start + width
        sums.append(jnp.concatenate([low[:, start:stop], high[:, start:stop]], axis=1))
        start = stop
    up_sum, dense_sum, qkv_sum = sums
    return (
        output,
        input_grad,
        norms[0],
        norms[1],
        qkv_sum,
        small[320:368].reshape(2, 24),
        dense_sum.T,
        bias_total,
        norms[2],
        norms[3],
        up_sum,
        small[368:432].reshape(16, 4),
        down_sum.T,
        bias_total,
    )


def solution(mesh):
    fine = Mesh(mesh.devices.reshape(tuple(SIZES.values())), tuple(SIZES))
    return jax.shard_map(
        body,
        mesh=fine,
        in_specs=(
            P(DP, None),
            P(DP),
            P(DP),
            P(),
            P(),
            P(None, TENSOR),
            P(TENSOR, None),
            P(TENSOR, None),
            P(),
            P(),
            P(),
            P(None, TENSOR),
            P(TENSOR, None),
            P(TENSOR, None),
            P(),
            P(DP, None),
        ),
        out_specs=(
            P(DP, None),
            P(DP, None),
            P(DP),
            P(DP),
            P(DP, TENSOR),
            P(TENSOR, DP),
            P(TENSOR, DP),
            P(DP),
            P(DP),
            P(DP),
            P(DP, TENSOR),
            P(TENSOR, DP),
            P(TENSOR, DP),
            P(DP),
        ),
        check_vma=False,
    )
```

```python
from functools import partial
import math

import jax
import jax.numpy as jnp
import numpy as np
from jax import lax
from jax.experimental import pallas as pl
from jax.experimental.pallas import tpu as pltpu
from jax.sharding import Mesh, PartitionSpec as P

HD = 256
ROT = 64
TOK = 512
D = 2048
EPSILON = 1e-05
NEGATIVE = -1000000000.0
SIZES = {"zl": 2, "x": 4, "y": 4, "zh": 2, "c": 2}
DP = ("zl", "x", "y")
TENSOR = ("zh", "c")
F32 = jnp.float32
BF16 = jnp.bfloat16


def send(value, axis, step=1):
    n = SIZES[axis]
    return lax.ppermute(value, axis, [(i, (i + step) % n) for i in range(n)])


def swap(value, axis, bit):
    return lax.ppermute(value, axis, [(i, i ^ bit) for i in range(SIZES[axis])])


def plain_dot(left, right):
    return jnp.dot(left, right, preferred_element_type=F32)


def contract_cols(left, right):
    return lax.dot_general(left, right, (((1,), (1,)), ((), ())), preferred_element_type=F32)


VMEM = 56 * 1024 * 1024
COST = pl.CostEstimate(flops=1000000, bytes_accessed=1000000, transcendentals=0)


def whole(shape):
    return pl.BlockSpec(shape, lambda *_: (0,) * len(shape), pipeline_mode=pl.Buffered(1))


def put_turned(target, rows):
    for z in range(2):
        for pair in range(8):
            start = z * 1024 + pair * 128
            block = rows[:, start : start + 128].T.astype(BF16)
            target[2 * pair, z] = block[:64]
            target[2 * pair + 1, z] = block[64:]


def normalise(hidden):
    average = jnp.mean(hidden, axis=-1, keepdims=True)
    centred = hidden - average
    inv_std = lax.rsqrt(jnp.mean(centred * centred, axis=-1, keepdims=True) + EPSILON)
    return centred * inv_std, inv_std


def second_kernel(hidden, cot, gain, shift, second_out, cot_turned, stats):
    rows = hidden[...].astype(F32)
    average = jnp.mean(rows, axis=-1, keepdims=True)
    centred = rows - average
    inv_std = lax.rsqrt(jnp.mean(centred * centred, axis=-1, keepdims=True) + EPSILON)
    second_out[...] = (centred * inv_std * gain[...] + shift[...]).astype(BF16)
    put_turned(cot_turned, cot[...].astype(F32))
    lane = lax.broadcasted_iota(jnp.int32, (rows.shape[0], 128), 1)
    stats[...] = jnp.where(lane < 64, average, inv_std)


def first_kernel(hidden, gain, shift, gain_two, shift_two, first_out, first_turned, second_turned):
    normed, _ = normalise(hidden[...].astype(F32))
    first = normed * gain[...] + shift[...]
    first_out[...] = first.astype(BF16)
    put_turned(first_turned, first)
    put_turned(second_turned, normed * gain_two[...] + shift_two[...])


def first_far_kernel(near, other, gain, shift, gain_two, shift_two, *refs):
    first_out, second_out, first_turned, second_turned = refs[2:]

    def step(rows):
        normed, _ = normalise(rows)
        first = normed * gain[...] + shift[...]
        second = normed * gain_two[...] + shift_two[...]
        first_out[...] = first.astype(BF16)
        second_out[...] = second.astype(BF16)
        put_turned(first_turned, first)
        put_turned(second_turned, second)

    @pl.when(pl.program_id(0) < 2)
    def _():
        step(near[...])

    @pl.when(pl.program_id(0) >= 2)
    def _():
        step(other[...])


def cot_far_kernel(*refs):
    cot_out, cot_turned = refs[5:]
    for k in range(4):

        @pl.when(pl.program_id(0) == k)
        def _(k=k):
            rows = refs[k][...]
            cot_out[...] = rows.astype(BF16)
            put_turned(cot_turned, rows)


TURNED = (16, 2, 64, 2 * TOK)


def norm_call(kernel, rows, n_rows, n_plain, n_turned, params, far=(), stats=False):
    steps = TOK // rows
    plain = pl.BlockSpec((rows, D), lambda i: (i, 0))
    shift = steps if far else 0
    turned = pl.BlockSpec((16, 2, 64, rows), lambda i: (0, 0, 0, i + shift))
    if len(n_rows) == 4:
        specs = [whole((rows, D))] * 4
    elif far:
        picks = (lambda i: (lax.min(i, 1), 0), lambda i: (lax.max(i - 2, 0), 0))
        specs = [pl.BlockSpec((rows, D), p) for p in picks]
    else:
        specs = [plain] * len(n_rows)
    operands = list(n_rows) + [p.reshape(1, D) for p in params]
    aliases = {len(operands) + i: n_plain + i for i in range(len(far))}
    return pl.pallas_call(
        kernel,
        grid=(steps,),
        in_specs=specs + [whole((1, D))] * len(params) + [pl.BlockSpec(memory_space=pl.ANY)] * len(far),
        out_specs=[plain] * n_plain
        + [turned] * n_turned
        + [pl.BlockSpec((rows, 128), lambda i: (i, 0))] * stats,
        out_shape=[jax.ShapeDtypeStruct((TOK, D), BF16)] * n_plain
        + [jax.ShapeDtypeStruct(TURNED, BF16)] * n_turned
        + [jax.ShapeDtypeStruct((TOK, 128), F32)] * stats,
        input_output_aliases=aliases,
        compiler_params=pltpu.CompilerParams(vmem_limit_bytes=VMEM),
        cost_estimate=COST,
    )(*operands, *far)


def phi(upward):
    return 0.5 * (1.0 + lax.erf(upward * math.sqrt(0.5)))


def gelu_slope(upward, below):
    return below + upward * (jnp.exp(-0.5 * upward * upward) * (1.0 / math.sqrt(2.0 * math.pi)))


def as_row(block):
    return jnp.concatenate([block[i : i + 1, :] for i in range(block.shape[0])], axis=1)


def feed_kernel(second, cot_turned, weight, bias, act_out, slope_out, down_grad):
    upward = plain_dot(second[...], weight[...]) + as_row(bias[0])
    below = phi(upward)
    act = (upward * below).astype(BF16)
    act_out[...] = act
    slope_out[...] = gelu_slope(upward, below)
    down_grad[...] = plain_dot(cot_turned[...].reshape(D, TOK), act).reshape(16, 128, -1)


def feed(second, cot_turned, weight, bias):
    units, width = weight.shape[1], 512
    column = pl.BlockSpec((TOK, width), lambda j: (0, j))
    return pl.pallas_call(
        feed_kernel,
        grid=(units // width,),
        in_specs=[
            whole((TOK, D)),
            whole((16, 2, 64, TOK)),
            pl.BlockSpec((D, width), lambda j: (0, j)),
            pl.BlockSpec((1, width // 128, 128), lambda j: (j, 0, 0)),
        ],
        out_specs=[column, column, pl.BlockSpec((16, 128, width), lambda j: (0, 0, j))],
        out_shape=[
            jax.ShapeDtypeStruct((TOK, units), BF16),
            jax.ShapeDtypeStruct((TOK, units), F32),
            jax.ShapeDtypeStruct((16, 128, units), F32),
        ],
        compiler_params=pltpu.CompilerParams(vmem_limit_bytes=VMEM),
        cost_estimate=COST,
    )(second, cot_turned, weight, bias.reshape(-1, width // 128, 128))


def feed_back_kernel(side, cot, weight, slope, up_grad):
    up_grad[...] = (contract_cols(cot[...], weight[...]) * slope[...]).astype(BF16)


def feed_back(side, cot, weight, slope):
    units, width = slope.shape[1], 512
    steps = units // width
    far = units < weight.shape[0]
    column = pl.BlockSpec((TOK, width), lambda j, s: (0, j))
    return pl.pallas_call(
        feed_back_kernel,
        grid_spec=pltpu.PrefetchScalarGridSpec(
            num_scalar_prefetch=1,
            grid=(steps,),
            in_specs=[
                whole((TOK, D)),
                pl.BlockSpec((width, D), lambda j, s: (s[0] * steps * far + j, 0)),
                column,
            ],
            out_specs=column,
        ),
        out_shape=jax.ShapeDtypeStruct((TOK, units), BF16),
        compiler_params=pltpu.CompilerParams(vmem_limit_bytes=VMEM),
        cost_estimate=COST,
    )(side, cot, weight, slope)


def slope_far_kernel(side, second, weight, bias, slope):
    upward = plain_dot(second[...], weight[...]) + as_row(bias[0])
    slope[...] = gelu_slope(upward, phi(upward))


def slope_far(side, second, weight, bias):
    units, width = weight.shape[1] // 2, 512
    steps = units // width
    return pl.pallas_call(
        slope_far_kernel,
        grid_spec=pltpu.PrefetchScalarGridSpec(
            num_scalar_prefetch=1,
            grid=(steps,),
            in_specs=[
                whole((TOK, D)),
                pl.BlockSpec((D, width), lambda j, s: (0, s[0] * steps + j)),
                pl.BlockSpec((1, width // 128, 128), lambda j, s: (s[0] * steps + j, 0, 0)),
            ],
            out_specs=pl.BlockSpec((TOK, width), lambda j, s: (0, j)),
        ),
        out_shape=jax.ShapeDtypeStruct((TOK, units), F32),
        compiler_params=pltpu.CompilerParams(vmem_limit_bytes=VMEM),
        cost_estimate=COST,
    )(side, second, weight, bias.reshape(-1, width // 128, 128))


def turn(values, tables, sign):
    first = values[:, :128]
    cosine, rising, falling = tables
    first = (
        first * cosine[...]
        + (pltpu.roll(first, 32, 1) * rising[...] + pltpu.roll(first, 96, 1) * falling[...]) * sign
    )
    return jnp.concatenate([first, values[:, 128:]], axis=1)


def as_column(row):
    return jnp.broadcast_to(row, (8, row.shape[1])).T[:, 0:1]


def project_kernel(place, first, weight, bias, marks, inverse, queries, keys, values, *tables):
    @pl.when(pl.program_id(0) == 0)
    def _():
        lane = lax.broadcasted_iota(jnp.int32, (TOK, 128), 1)
        angles = as_column(marks[1:2, :]) * inverse[...]
        sine = jnp.sin(angles)
        tables[0][...] = jnp.where(lane < ROT, jnp.cos(angles), 1.0)
        tables[1][...] = jnp.where((lane >= ROT // 2) & (lane < ROT), sine, 0.0)
        tables[2][...] = jnp.where(lane < ROT // 2, -sine, 0.0)

    head = pl.program_id(0) + place[0] * (2 - pl.num_programs(0))
    packed = plain_dot(first[...], weight[...]) + bias[pl.ds(head, 1), :]
    queries[...] = turn(packed[:, :HD], tables, 1.0).astype(BF16)
    keys[...] = turn(packed[:, HD : 2 * HD], tables, 1.0).astype(BF16)
    values[...] = packed[:, 2 * HD :].astype(BF16)


def project(place, heads, first, weight, bias, marks):
    inverse = (10000.0 ** (-2.0 * (np.arange(128) % (ROT // 2)) / ROT)).astype(np.float32)
    inverse = jnp.asarray(inverse.reshape(1, 128))
    at = (lambda h, s: h) if heads == 2 else (lambda h, s: s[0])
    column = pl.BlockSpec((TOK, HD), lambda h, s: (0, h))
    return pl.pallas_call(
        project_kernel,
        grid_spec=pltpu.PrefetchScalarGridSpec(
            num_scalar_prefetch=1,
            grid=(heads,),
            in_specs=[
                whole((TOK, D)),
                pl.BlockSpec((D, 3 * HD), lambda h, s: (0, at(h, s))),
                whole((2, 3 * HD)),
                whole((2, TOK)),
                whole((1, 128)),
            ],
            out_specs=[column] * 3 + [pl.BlockSpec((TOK, 128), lambda h, s: (0, 0))] * 3,
        ),
        out_shape=[jax.ShapeDtypeStruct((TOK, heads * HD), BF16)] * 3
        + [jax.ShapeDtypeStruct((TOK, 128), F32)] * 3,
        compiler_params=pltpu.CompilerParams(vmem_limit_bytes=VMEM),
        cost_estimate=COST,
    )(place, first, weight, bias, marks, inverse)


def attend_kernel(
    place, queries, keys, values, cosine, rising, falling, cot, dense, marks, mixed_out, grad_out
):
    tables = (cosine, rising, falling)
    scale = 1.0 / math.sqrt(HD)
    queries, keys, values = queries[...], keys[...], values[...]
    segments = marks[0:1, :]

    def order(axis):
        return lax.rem(lax.broadcasted_iota(jnp.int32, (TOK, TOK), axis) + place[1], TOK)

    allowed = (as_column(segments) == segments) & (order(0) >= order(1))
    scores = jnp.where(allowed, contract_cols(queries, keys) * scale, NEGATIVE)
    top = jnp.max(scores, axis=-1, keepdims=True)
    weights = jnp.exp(scores - top)
    probs = weights / jnp.sum(weights, axis=-1, keepdims=True)
    probs_low = probs.astype(BF16)
    mixed_out[...] = plain_dot(probs_low, values).astype(BF16)
    grad_mixed = contract_cols(cot[...], dense[...]).astype(BF16)
    grad_probs = contract_cols(grad_mixed, values)
    along = jnp.sum(probs * grad_probs, axis=-1, keepdims=True)
    grad_scores = (probs * (grad_probs - along)).astype(BF16)
    grad_query = plain_dot(grad_scores, keys) * scale
    grad_key = plain_dot(grad_scores.T, queries) * scale
    grad_value = plain_dot(probs_low.T, grad_mixed)
    grad_out[:, :HD] = turn(grad_query, tables, -1.0).astype(BF16)
    grad_out[:, HD : 2 * HD] = turn(grad_key, tables, -1.0).astype(BF16)
    grad_out[:, 2 * HD :] = grad_value.astype(BF16)


def attend(place, heads, projected, cot, dense, marks):
    at = (lambda h, s: h) if heads == 2 else (lambda h, s: s[0])
    column = pl.BlockSpec((TOK, HD), lambda h, s: (0, h))
    return pl.pallas_call(
        attend_kernel,
        grid_spec=pltpu.PrefetchScalarGridSpec(
            num_scalar_prefetch=1,
            grid=(heads,),
            in_specs=[column] * 3
            + [whole((TOK, 128))] * 3
            + [whole((TOK, D)), pl.BlockSpec((HD, D), lambda h, s: (at(h, s), 0)), whole((2, TOK))],
            out_specs=[column, pl.BlockSpec((TOK, 3 * HD), lambda h, s: (0, h))],
        ),
        out_shape=[
            jax.ShapeDtypeStruct((TOK, heads * HD), BF16),
            jax.ShapeDtypeStruct((TOK, heads * 3 * HD), BF16),
        ],
        compiler_params=pltpu.CompilerParams(vmem_limit_bytes=VMEM),
        cost_estimate=COST,
    )(place, *projected, cot, dense, marks)


def put_halves(core, values, scratch, mine, other):
    scratch[...] = values
    half = TOK // 2
    mine[...] = scratch[pl.ds(pl.multiple_of(core[0] * half, half), half), :]
    other[...] = scratch[pl.ds(pl.multiple_of((1 - core[0]) * half, half), half), :]


def branch_kernel(core, mixed, act, dense, down, mine, other, scratch):
    total = plain_dot(act[...], down[...]) + plain_dot(mixed[...], dense[...])
    put_halves(core, total, scratch, mine, other)


def back_kernel(
    core, packed, up_grad, qkv, up, hidden, stats, gain, gain_two, mine, other, sums, scratch
):
    first = contract_cols(packed[...], qkv[...])
    second = contract_cols(up_grad[...], up[...])
    put_halves(core, first * gain[...] + second * gain_two[...], scratch, mine, other)
    normed = (hidden[...].astype(F32) - stats[:, 0:1]) * stats[:, 64:65]
    rows = [
        jnp.sum(v, axis=0, keepdims=True) for v in (first * normed, first, second * normed, second)
    ]
    sums[...] = jnp.concatenate(rows + [jnp.zeros((4, first.shape[1]), F32)], axis=0)


def halves_call(kernel, core, operands, specs, with_sums):
    width = 512
    half = pl.BlockSpec((TOK // 2, width), lambda j, s: (0, j))
    return pl.pallas_call(
        kernel,
        grid_spec=pltpu.PrefetchScalarGridSpec(
            num_scalar_prefetch=1,
            grid=(D // width,),
            in_specs=specs,
            out_specs=[half, half] + [pl.BlockSpec((8, width), lambda j, s: (0, j))] * with_sums,
            scratch_shapes=[pltpu.VMEM((TOK, width), F32)],
        ),
        out_shape=[jax.ShapeDtypeStruct((TOK // 2, D), F32)] * 2
        + [jax.ShapeDtypeStruct((8, D), F32)] * with_sums,
        compiler_params=pltpu.CompilerParams(vmem_limit_bytes=VMEM),
        cost_estimate=COST,
    )(core, *operands)


def branch_halves(core, mixed, act, dense, down):
    specs = [whole(mixed.shape), whole(act.shape)]
    specs += [pl.BlockSpec((w.shape[0], 512), lambda j, s: (0, j)) for w in (dense, down)]
    return halves_call(branch_kernel, core, (mixed, act, dense, down), specs, False)


def back_halves(core, packed, up_grad, qkv, up, hidden, stats, gain, gain_two):
    specs = [whole(packed.shape), whole(up_grad.shape)]
    specs += [pl.BlockSpec((512, w.shape[1]), lambda j, s: (j, 0)) for w in (qkv, up)]
    specs += [pl.BlockSpec((TOK, 512), lambda j, s: (0, j)), whole((TOK, 128))]
    specs += [pl.BlockSpec((1, 512), lambda j, s: (0, j))] * 2
    operands = (packed, up_grad, qkv, up, hidden, stats, gain.reshape(1, D), gain_two.reshape(1, D))
    return halves_call(back_kernel, core, operands, specs, True)


def joint_kernel(side, *refs):
    lefts, rights, target, held, arrived = refs[:3], refs[3:9], refs[9], refs[10:13], refs[13]
    step = pl.program_id(0)
    copies = [pltpu.make_async_copy(lefts[k], held[k], arrived.at[k]) for k in range(3)]

    @pl.when(step == 0)
    def _():
        for copy in copies:
            copy.start()

    for k, (start, stop) in enumerate(((0, 4), (4, 5), (5, 8))):

        @pl.when(step == start)
        def _(k=k):
            copies[k].wait()

        @pl.when((step >= start) & (step < stop))
        def _(k=k):
            right = jnp.concatenate([rights[2 * k][...], rights[2 * k + 1][...]], axis=0)
            total = plain_dot(held[k][...].reshape(D, 2 * TOK), right)
            target[...] = total.reshape(16, 128, -1)


def joint(side, lefts, rights):
    width = 256
    specs = [pl.BlockSpec(memory_space=pl.ANY)] * 3
    for start, n in ((0, 4), (4, 1), (5, 3)):

        def near(j, s, start=start, n=n):
            return (0, s[0] * n + jnp.clip(j - start, 0, n - 1))

        def far(j, s, start=start, n=n):
            return (0, jnp.clip(j - start, 0, n - 1))

        specs += [pl.BlockSpec((TOK, width), near), pl.BlockSpec((TOK, width), far)]
    return pl.pallas_call(
        joint_kernel,
        grid_spec=pltpu.PrefetchScalarGridSpec(
            num_scalar_prefetch=1,
            grid=(8,),
            in_specs=specs,
            out_specs=pl.BlockSpec((16, 128, width), lambda j, s: (0, 0, j)),
            scratch_shapes=[pltpu.VMEM(TURNED, BF16)] * 3 + [pltpu.SemaphoreType.DMA((3,))],
        ),
        out_shape=jax.ShapeDtypeStruct((16, 128, 8 * width), F32),
        compiler_params=pltpu.CompilerParams(vmem_limit_bytes=VMEM),
        cost_estimate=COST,
    )(side, *lefts, *rights)


def body(
    hidden_in,
    segment_ids,
    positions,
    ln1_gain,
    ln1_bias,
    qkv_weight,
    qkv_bias,
    dense_weight,
    dense_bias,
    ln2_gain,
    ln2_bias,
    fc1_weight,
    fc1_bias,
    fc2_weight,
    fc2_bias,
    cotangent,
):
    core = lax.axis_index("c")
    side = lax.axis_index("zl")
    half_rows = TOK // 2
    at_side = side.astype(jnp.int32).reshape(1)
    at_core = core.astype(jnp.int32).reshape(1)
    own_place = jnp.zeros((2,), jnp.int32)
    far_place = jnp.stack([side, core * half_rows]).astype(jnp.int32)
    after = lax.optimization_barrier
    params = (ln1_gain, ln1_bias, ln2_gain, ln2_bias)

    def of_core(values, which):
        return lax.dynamic_slice_in_dim(values, which * half_rows, half_rows, 0)

    def both_cores(mine):
        theirs = send(mine, "c")
        filled = jnp.zeros((TOK,) + mine.shape[1:], mine.dtype)
        filled = lax.dynamic_update_slice_in_dim(filled, mine, core * half_rows, 0)
        return lax.dynamic_update_slice_in_dim(filled, theirs, (1 - core) * half_rows, 0)

    marks = jnp.concatenate([segment_ids, positions]).astype(F32).reshape(1, 2 * TOK)
    hidden_sent = jnp.concatenate(
        [of_core(hidden_in, core).astype(F32), jnp.pad(marks, ((0, 7), (0, D - 2 * TOK)))], axis=0
    )
    hidden_pair = lax.all_gather(hidden_sent, "zl")

    second_in, cot_turned, stats = norm_call(
        second_kernel, 256, (hidden_in, cotangent), 1, 1, (ln2_gain, ln2_bias), stats=True
    )
    act_low, slope, down_grad = feed(second_in, cot_turned, fc1_weight, fc1_bias)
    down_sum = after(lax.psum_scatter(down_grad, ("x", "y"), scatter_dimension=0, tiled=True))
    _, cotangent, hidden_in = after((down_grad, cotangent, hidden_in))
    cot_sent = of_core(cotangent, core).astype(F32)
    cot_got = send(cot_sent[:128], "zl")

    own_marks = marks.reshape(2, TOK)

    def own_step(hidden_in, cotangent, act_low, slope):
        first_in, first_turned, second_turned = norm_call(
            first_kernel, 256, (hidden_in,), 1, 2, params
        )
        projected = project(own_place, 2, first_in, qkv_weight, qkv_bias, own_marks)
        mixed_low, grad_packed = attend(
            own_place, 2, projected, cotangent, dense_weight, own_marks
        )
        grad_up = feed_back(at_side, cotangent, fc2_weight, slope)
        branches = branch_halves(at_core, mixed_low, act_low, dense_weight, fc2_weight)
        backs = back_halves(
            at_core,
            grad_packed,
            grad_up,
            qkv_weight,
            fc1_weight,
            hidden_in,
            stats,
            ln1_gain,
            ln2_gain,
        )
        return (first_turned, second_turned, mixed_low, grad_packed, grad_up, *branches, *backs)

    (
        first_turned,
        second_turned,
        mixed_low,
        grad_packed,
        grad_up,
        branch,
        branch_other,
        combined,
        combined_other,
        norms,
    ) = lax.cond(core == 0, own_step, own_step, hidden_in, cotangent, act_low, slope)
    hidden_pair, branch_other, combined_other, cot_got, cot_sent = after(
        (hidden_pair, branch_other, combined_other, cot_got, cot_sent)
    )
    cot_got_too = send(cot_sent[128:], "zl")
    branch = branch + send(branch_other, "c")
    combined = combined + send(combined_other, "c")
    hidden_got = lax.dynamic_index_in_dim(hidden_pair, 1 - side, 0, keepdims=False)

    def far_step(hidden_got, hidden_too, first_turned, second_turned):
        first_far, second_far, first_turned, second_turned = norm_call(
            first_far_kernel,
            128,
            (hidden_got, hidden_too),
            2,
            2,
            params,
            (first_turned, second_turned),
        )
        slope_side = slope_far(at_side, second_far, fc1_weight, fc1_bias)
        marks_got = hidden_got[half_rows, : 2 * TOK].reshape(2, 2, half_rows)
        marks_far = jnp.where(core == 0, marks_got, marks_got[:, ::-1]).reshape(2, TOK)
        projected_far = project(far_place, 1, first_far, qkv_weight, qkv_bias, marks_far)
        return first_turned, second_turned, slope_side, marks_far, *projected_far

    first_turned, second_turned, slope_side, marks_far, *projected_far = lax.cond(
        core == 0,
        far_step,
        far_step,
        hidden_got,
        send(hidden_got, "c"),
        first_turned,
        second_turned,
    )

    slope_side, projected_far, cot_got_too, branch, combined = after(
        (slope_side, projected_far, cot_got_too, branch, combined)
    )
    cot_far, cot_turned = norm_call(
        cot_far_kernel,
        128,
        (cot_got, cot_got_too, send(cot_got, "c"), send(cot_got_too, "c")),
        1,
        1,
        (),
        (cot_turned,),
    )
    branch = lax.psum(branch, "zh")
    combined = lax.psum(combined, "zh")
    grad_up_far = feed_back(at_side, cot_far, fc2_weight, slope_side)
    mixed_far, grad_packed_far = attend(
        far_place, 1, projected_far, cot_far, dense_weight, marks_far
    )
    joint_grad = joint(
        at_side,
        (second_turned, cot_turned, first_turned),
        (grad_up, grad_up_far, mixed_low, mixed_far, grad_packed, grad_packed_far),
    )
    joint_grad, down_sum = after((joint_grad, down_sum))
    joint_sum = after(lax.psum_scatter(joint_grad, ("x", "y"), scatter_dimension=0, tiled=True))
    _, norms, grad_packed, grad_up, cotangent, down_sum = after(
        (joint_grad, norms, grad_packed, grad_up, cotangent, down_sum)
    )

    norms = norms[:4].reshape(4, 32, 64).transpose(1, 0, 2).reshape(32, 256)
    norms = norms + send(norms, "c")
    norms = norms + send(norms, "zh")
    grad_out = cotangent.astype(F32)
    bias_sum = jnp.sum(grad_out, axis=0)
    qkv_bias_sum = jnp.sum(grad_packed.astype(F32), axis=0)
    up_bias_grad = jnp.sum(grad_up.astype(F32), axis=0)
    small = jnp.concatenate(
        [
            norms,
            bias_sum.reshape(32, 64),
            qkv_bias_sum.reshape(2, 32, 24).transpose(1, 0, 2).reshape(32, 48),
            up_bias_grad.reshape(16, 32, 4).transpose(1, 0, 2).reshape(32, 64),
            jnp.zeros((32, 80), F32),
        ],
        axis=1,
    )
    for axis in ("x", "y"):
        small = small + swap(small, axis, 1)
        small = small + swap(small, axis, 2)
    block = lax.axis_index("x") * 4 + lax.axis_index("y")
    own_small = lax.dynamic_slice_in_dim(small, side * 16 + block, 1, 0)
    far_small = lax.dynamic_slice_in_dim(small, (1 - side) * 16 + block, 1, 0)
    small = (own_small + send(far_small, "zl")).reshape(-1)

    small, branch, combined = after((small, branch, combined))
    norms = small[:256].reshape(4, 64)
    bias_total = small[256:320]
    hidden = hidden_in.astype(F32)
    output = both_cores(of_core(hidden, core) + branch + dense_bias + fc2_bias)
    own_stats = of_core(stats, core)
    average, inv_std = own_stats[:, 0:1], own_stats[:, 64:65]
    normed_half = (of_core(hidden, core) - average) * inv_std
    input_half = of_core(grad_out, core) + inv_std * (
        combined
        - jnp.mean(combined, axis=-1, keepdims=True)
        - normed_half * jnp.mean(combined * normed_half, axis=-1, keepdims=True)
    )
    input_grad = both_cores(input_half)

    def of_side(values, which):
        return lax.dynamic_slice_in_dim(values[0], which * 64, 64, 0)

    down_sum = of_side(down_sum, side) + send(of_side(down_sum, 1 - side), "zl")
    near = of_side(joint_sum, side)
    far = send(of_side(joint_sum, 1 - side), "zl")
    low = jnp.where(side == 0, near, far)
    high = jnp.where(side == 0, far, near)
    sums = []
    start = 0
    for width in (1024, 256, 768):
        stop = start + width
        sums.append(jnp.concatenate([low[:, start:stop], high[:, start:stop]], axis=1))
        start = stop
    up_sum, dense_sum, qkv_sum = sums
    return (
        output,
        input_grad,
        norms[0],
        norms[1],
        qkv_sum,
        small[320:368].reshape(2, 24),
        dense_sum.T,
        bias_total,
        norms[2],
        norms[3],
        up_sum,
        small[368:432].reshape(16, 4),
        down_sum.T,
        bias_total,
    )


def solution(mesh):
    fine = Mesh(mesh.devices.reshape(tuple(SIZES.values())), tuple(SIZES))
    return jax.shard_map(
        body,
        mesh=fine,
        in_specs=(
            P(DP, None),
            P(DP),
            P(DP),
            P(),
            P(),
            P(None, TENSOR),
            P(TENSOR, None),
            P(TENSOR, None),
            P(),
            P(),
            P(),
            P(None, TENSOR),
            P(TENSOR, None),
            P(TENSOR, None),
            P(),
            P(DP, None),
        ),
        out_specs=(
            P(DP, None),
            P(DP, None),
            P(DP),
            P(DP),
            P(DP, TENSOR),
            P(TENSOR, DP),
            P(TENSOR, DP),
            P(DP),
            P(DP),
            P(DP),
            P(DP, TENSOR),
            P(TENSOR, DP),
            P(TENSOR, DP),
            P(DP),
        ),
        check_vma=False,
    )
```

```python
from functools import partial
import math

import jax
import jax.numpy as jnp
import numpy as np
from jax import lax
from jax.experimental import pallas as pl
from jax.experimental.pallas import tpu as pltpu
from jax.sharding import Mesh, PartitionSpec as P

HD = 256
ROT = 64
TOK = 512
D = 2048
EPSILON = 1e-05
NEGATIVE = -1000000000.0
SIZES = {"zl": 2, "x": 4, "y": 4, "zh": 2, "c": 2}
DP = ("zl", "x", "y")
TENSOR = ("zh", "c")
F32 = jnp.float32
BF16 = jnp.bfloat16


def send(value, axis, step=1):
    n = SIZES[axis]
    return lax.ppermute(value, axis, [(i, (i + step) % n) for i in range(n)])


def swap(value, axis, bit):
    return lax.ppermute(value, axis, [(i, i ^ bit) for i in range(SIZES[axis])])


def plain_dot(left, right):
    return jnp.dot(left, right, preferred_element_type=F32)


def contract_cols(left, right):
    return lax.dot_general(left, right, (((1,), (1,)), ((), ())), preferred_element_type=F32)


VMEM = 56 * 1024 * 1024
COST = pl.CostEstimate(flops=1000000, bytes_accessed=1000000, transcendentals=0)


def whole(shape):
    return pl.BlockSpec(shape, lambda *_: (0,) * len(shape), pipeline_mode=pl.Buffered(1))


def put_turned(target, rows):
    for z in range(2):
        for pair in range(8):
            start = z * 1024 + pair * 128
            block = rows[:, start : start + 128].T.astype(BF16)
            target[2 * pair, z] = block[:64]
            target[2 * pair + 1, z] = block[64:]


def normalise(hidden):
    average = jnp.mean(hidden, axis=-1, keepdims=True)
    centred = hidden - average
    inv_std = lax.rsqrt(jnp.mean(centred * centred, axis=-1, keepdims=True) + EPSILON)
    return centred * inv_std, inv_std


def second_kernel(hidden, cot, gain, shift, second_out, cot_turned, stats):
    rows = hidden[...].astype(F32)
    average = jnp.mean(rows, axis=-1, keepdims=True)
    centred = rows - average
    inv_std = lax.rsqrt(jnp.mean(centred * centred, axis=-1, keepdims=True) + EPSILON)
    second_out[...] = (centred * inv_std * gain[...] + shift[...]).astype(BF16)
    put_turned(cot_turned, cot[...].astype(F32))
    lane = lax.broadcasted_iota(jnp.int32, (rows.shape[0], 128), 1)
    stats[...] = jnp.where(lane < 64, average, inv_std)


def first_kernel(hidden, gain, shift, gain_two, shift_two, first_out, first_turned, second_turned):
    normed, _ = normalise(hidden[...].astype(F32))
    first = normed * gain[...] + shift[...]
    first_out[...] = first.astype(BF16)
    put_turned(first_turned, first)
    put_turned(second_turned, normed * gain_two[...] + shift_two[...])


def first_far_kernel(near, other, gain, shift, gain_two, shift_two, *refs):
    first_out, second_out, first_turned, second_turned = refs[2:]

    def step(rows):
        normed, _ = normalise(rows)
        first = normed * gain[...] + shift[...]
        second = normed * gain_two[...] + shift_two[...]
        first_out[...] = first.astype(BF16)
        second_out[...] = second.astype(BF16)
        put_turned(first_turned, first)
        put_turned(second_turned, second)

    @pl.when(pl.program_id(0) < 2)
    def _():
        step(near[...])

    @pl.when(pl.program_id(0) >= 2)
    def _():
        step(other[...])


def cot_far_kernel(near, other, *refs):
    cot_out, cot_turned = refs[1:]

    def step(rows):
        cot_out[...] = rows.astype(BF16)
        put_turned(cot_turned, rows)

    @pl.when(pl.program_id(0) < 2)
    def _():
        step(near[...])

    @pl.when(pl.program_id(0) >= 2)
    def _():
        step(other[...])


TURNED = (16, 2, 64, 2 * TOK)


def norm_call(kernel, rows, n_rows, n_plain, n_turned, params, far=(), stats=False):
    steps = TOK // rows
    plain = pl.BlockSpec((rows, D), lambda i: (i, 0))
    shift = steps if far else 0
    turned = pl.BlockSpec((16, 2, 64, rows), lambda i: (0, 0, 0, i + shift))
    if far:
        picks = (lambda i: (lax.min(i, 1), 0), lambda i: (lax.max(i - 2, 0), 0))
        specs = [pl.BlockSpec((rows, D), p) for p in picks]
    else:
        specs = [plain] * len(n_rows)
    operands = list(n_rows) + [p.reshape(1, D) for p in params]
    aliases = {len(operands) + i: n_plain + i for i in range(len(far))}
    return pl.pallas_call(
        kernel,
        grid=(steps,),
        in_specs=specs + [whole((1, D))] * len(params) + [pl.BlockSpec(memory_space=pl.ANY)] * len(far),
        out_specs=[plain] * n_plain
        + [turned] * n_turned
        + [pl.BlockSpec((rows, 128), lambda i: (i, 0))] * stats,
        out_shape=[jax.ShapeDtypeStruct((TOK, D), BF16)] * n_plain
        + [jax.ShapeDtypeStruct(TURNED, BF16)] * n_turned
        + [jax.ShapeDtypeStruct((TOK, 128), F32)] * stats,
        input_output_aliases=aliases,
        compiler_params=pltpu.CompilerParams(vmem_limit_bytes=VMEM),
        cost_estimate=COST,
    )(*operands, *far)


def phi(upward):
    return 0.5 * (1.0 + lax.erf(upward * math.sqrt(0.5)))


def gelu_slope(upward, below):
    return below + upward * (jnp.exp(-0.5 * upward * upward) * (1.0 / math.sqrt(2.0 * math.pi)))


def as_row(block):
    return jnp.concatenate([block[i : i + 1, :] for i in range(block.shape[0])], axis=1)


def feed_kernel(second, cot_turned, weight, bias, act_out, slope_out, down_grad):
    upward = plain_dot(second[...], weight[...]) + as_row(bias[0])
    below = phi(upward)
    act = (upward * below).astype(BF16)
    act_out[...] = act
    slope_out[...] = gelu_slope(upward, below)
    down_grad[...] = plain_dot(cot_turned[...].reshape(D, TOK), act).reshape(16, 128, -1)


def feed(second, cot_turned, weight, bias):
    units, width = weight.shape[1], 512
    column = pl.BlockSpec((TOK, width), lambda j: (0, j))
    return pl.pallas_call(
        feed_kernel,
        grid=(units // width,),
        in_specs=[
            whole((TOK, D)),
            whole((16, 2, 64, TOK)),
            pl.BlockSpec((D, width), lambda j: (0, j)),
            pl.BlockSpec((1, width // 128, 128), lambda j: (j, 0, 0)),
        ],
        out_specs=[column, column, pl.BlockSpec((16, 128, width), lambda j: (0, 0, j))],
        out_shape=[
            jax.ShapeDtypeStruct((TOK, units), BF16),
            jax.ShapeDtypeStruct((TOK, units), F32),
            jax.ShapeDtypeStruct((16, 128, units), F32),
        ],
        compiler_params=pltpu.CompilerParams(vmem_limit_bytes=VMEM),
        cost_estimate=COST,
    )(second, cot_turned, weight, bias.reshape(-1, width // 128, 128))


def feed_back_kernel(side, cot, weight, slope, up_grad):
    up_grad[...] = (contract_cols(cot[...], weight[...]) * slope[...]).astype(BF16)


def feed_back(side, cot, weight, slope):
    units, width = slope.shape[1], 512
    steps = units // width
    far = units < weight.shape[0]
    column = pl.BlockSpec((TOK, width), lambda j, s: (0, j))
    return pl.pallas_call(
        feed_back_kernel,
        grid_spec=pltpu.PrefetchScalarGridSpec(
            num_scalar_prefetch=1,
            grid=(steps,),
            in_specs=[
                whole((TOK, D)),
                pl.BlockSpec((width, D), lambda j, s: (s[0] * steps * far + j, 0)),
                column,
            ],
            out_specs=column,
        ),
        out_shape=jax.ShapeDtypeStruct((TOK, units), BF16),
        compiler_params=pltpu.CompilerParams(vmem_limit_bytes=VMEM),
        cost_estimate=COST,
    )(side, cot, weight, slope)


def slope_far_kernel(side, second, weight, bias, slope):
    upward = plain_dot(second[...], weight[...]) + as_row(bias[0])
    slope[...] = gelu_slope(upward, phi(upward))


def slope_far(side, second, weight, bias):
    units, width = weight.shape[1] // 2, 512
    steps = units // width
    return pl.pallas_call(
        slope_far_kernel,
        grid_spec=pltpu.PrefetchScalarGridSpec(
            num_scalar_prefetch=1,
            grid=(steps,),
            in_specs=[
                whole((TOK, D)),
                pl.BlockSpec((D, width), lambda j, s: (0, s[0] * steps + j)),
                pl.BlockSpec((1, width // 128, 128), lambda j, s: (s[0] * steps + j, 0, 0)),
            ],
            out_specs=pl.BlockSpec((TOK, width), lambda j, s: (0, j)),
        ),
        out_shape=jax.ShapeDtypeStruct((TOK, units), F32),
        compiler_params=pltpu.CompilerParams(vmem_limit_bytes=VMEM),
        cost_estimate=COST,
    )(side, second, weight, bias.reshape(-1, width // 128, 128))


def turn(values, tables, sign):
    first = values[:, :128]
    cosine, rising, falling = tables
    first = (
        first * cosine[...]
        + (pltpu.roll(first, 32, 1) * rising[...] + pltpu.roll(first, 96, 1) * falling[...]) * sign
    )
    return jnp.concatenate([first, values[:, 128:]], axis=1)


def as_column(row):
    return jnp.broadcast_to(row, (8, row.shape[1])).T[:, 0:1]


def project_kernel(place, first, weight, bias, marks, inverse, queries, keys, values, *tables):
    @pl.when(pl.program_id(0) == 0)
    def _():
        angles = inverse[...] * marks[1:2, :]
        cosine, sine = jnp.cos(angles), jnp.sin(angles)
        none, rest = jnp.zeros_like(sine), jnp.zeros((64, TOK), F32)
        tables[0][...] = jnp.concatenate([cosine, cosine, rest + 1.0], axis=0).T
        tables[1][...] = jnp.concatenate([none, sine, rest], axis=0).T
        tables[2][...] = jnp.concatenate([-sine, none, rest], axis=0).T

    head = pl.program_id(0) + place[0] * (2 - pl.num_programs(0))
    packed = plain_dot(first[...], weight[...]) + bias[pl.ds(head, 1), :]
    queries[...] = turn(packed[:, :HD], tables, 1.0).astype(BF16)
    keys[...] = turn(packed[:, HD : 2 * HD], tables, 1.0).astype(BF16)
    values[...] = packed[:, 2 * HD :].astype(BF16)


def project(place, heads, first, weight, bias, marks):
    inverse = jnp.asarray((10000.0 ** (-2.0 * np.arange(32) / ROT)).astype(np.float32).reshape(32, 1))
    at = (lambda h, s: h) if heads == 2 else (lambda h, s: s[0])
    column = pl.BlockSpec((TOK, HD), lambda h, s: (0, h))
    return pl.pallas_call(
        project_kernel,
        grid_spec=pltpu.PrefetchScalarGridSpec(
            num_scalar_prefetch=1,
            grid=(heads,),
            in_specs=[
                whole((TOK, D)),
                pl.BlockSpec((D, 3 * HD), lambda h, s: (0, at(h, s))),
                whole((2, 3 * HD)),
                whole((2, TOK)),
                whole((32, 1)),
            ],
            out_specs=[column] * 3 + [pl.BlockSpec((TOK, 128), lambda h, s: (0, 0))] * 3,
        ),
        out_shape=[jax.ShapeDtypeStruct((TOK, heads * HD), BF16)] * 3
        + [jax.ShapeDtypeStruct((TOK, 128), F32)] * 3,
        compiler_params=pltpu.CompilerParams(vmem_limit_bytes=VMEM),
        cost_estimate=COST,
    )(place, first, weight, bias, marks, inverse)


def attend_kernel(
    place, queries, keys, values, cosine, rising, falling, cot, dense, marks, mixed_out, grad_out
):
    tables = (cosine, rising, falling)
    scale = 1.0 / math.sqrt(HD)
    queries, keys, values = queries[...], keys[...], values[...]
    segments = marks[0:1, :]

    def order(axis):
        return lax.rem(lax.broadcasted_iota(jnp.int32, (TOK, TOK), axis) + place[1], TOK)

    allowed = (as_column(segments) == segments) & (order(0) >= order(1))
    scores = jnp.where(allowed, contract_cols(queries, keys) * scale, NEGATIVE)
    top = jnp.max(scores, axis=-1, keepdims=True)
    weights = jnp.exp(scores - top)
    probs = weights / jnp.sum(weights, axis=-1, keepdims=True)
    probs_low = probs.astype(BF16)
    mixed_out[...] = plain_dot(probs_low, values).astype(BF16)
    grad_mixed = contract_cols(cot[...], dense[...]).astype(BF16)
    grad_probs = contract_cols(grad_mixed, values)
    along = jnp.sum(probs * grad_probs, axis=-1, keepdims=True)
    grad_scores = (probs * (grad_probs - along)).astype(BF16)
    grad_query = plain_dot(grad_scores, keys) * scale
    grad_key = plain_dot(grad_scores.T, queries) * scale
    grad_value = plain_dot(probs_low.T, grad_mixed)
    grad_out[:, :HD] = turn(grad_query, tables, -1.0).astype(BF16)
    grad_out[:, HD : 2 * HD] = turn(grad_key, tables, -1.0).astype(BF16)
    grad_out[:, 2 * HD :] = grad_value.astype(BF16)


def attend(place, heads, projected, cot, dense, marks):
    at = (lambda h, s: h) if heads == 2 else (lambda h, s: s[0])
    column = pl.BlockSpec((TOK, HD), lambda h, s: (0, h))
    return pl.pallas_call(
        attend_kernel,
        grid_spec=pltpu.PrefetchScalarGridSpec(
            num_scalar_prefetch=1,
            grid=(heads,),
            in_specs=[column] * 3
            + [whole((TOK, 128))] * 3
            + [whole((TOK, D)), pl.BlockSpec((HD, D), lambda h, s: (at(h, s), 0)), whole((2, TOK))],
            out_specs=[column, pl.BlockSpec((TOK, 3 * HD), lambda h, s: (0, h))],
        ),
        out_shape=[
            jax.ShapeDtypeStruct((TOK, heads * HD), BF16),
            jax.ShapeDtypeStruct((TOK, heads * 3 * HD), BF16),
        ],
        compiler_params=pltpu.CompilerParams(vmem_limit_bytes=VMEM),
        cost_estimate=COST,
    )(place, *projected, cot, dense, marks)


def put_halves(core, values, scratch, mine, other):
    scratch[...] = values
    half = TOK // 2
    mine[...] = scratch[pl.ds(pl.multiple_of(core[0] * half, half), half), :]
    other[...] = scratch[pl.ds(pl.multiple_of((1 - core[0]) * half, half), half), :]


def branch_kernel(core, mixed, act, dense, down, mine, other, scratch):
    total = plain_dot(act[...], down[...]) + plain_dot(mixed[...], dense[...])
    put_halves(core, total, scratch, mine, other)


def back_kernel(
    core, packed, up_grad, qkv, up, hidden, stats, gain, gain_two, mine, other, sums, scratch
):
    first = contract_cols(packed[...], qkv[...])
    second = contract_cols(up_grad[...], up[...])
    put_halves(core, first * gain[...] + second * gain_two[...], scratch, mine, other)
    normed = (hidden[...].astype(F32) - stats[:, 0:1]) * stats[:, 64:65]
    rows = [
        jnp.sum(v, axis=0, keepdims=True) for v in (first * normed, first, second * normed, second)
    ]
    sums[...] = jnp.concatenate(rows + [jnp.zeros((4, first.shape[1]), F32)], axis=0)


def halves_call(kernel, core, operands, specs, with_sums):
    width = 512
    half = pl.BlockSpec((TOK // 2, width), lambda j, s: (0, j))
    return pl.pallas_call(
        kernel,
        grid_spec=pltpu.PrefetchScalarGridSpec(
            num_scalar_prefetch=1,
            grid=(D // width,),
            in_specs=specs,
            out_specs=[half, half] + [pl.BlockSpec((8, width), lambda j, s: (0, j))] * with_sums,
            scratch_shapes=[pltpu.VMEM((TOK, width), F32)],
        ),
        out_shape=[jax.ShapeDtypeStruct((TOK // 2, D), F32)] * 2
        + [jax.ShapeDtypeStruct((8, D), F32)] * with_sums,
        compiler_params=pltpu.CompilerParams(vmem_limit_bytes=VMEM),
        cost_estimate=COST,
    )(core, *operands)


def branch_halves(core, mixed, act, dense, down):
    specs = [whole(mixed.shape), whole(act.shape)]
    specs += [pl.BlockSpec((w.shape[0], 512), lambda j, s: (0, j)) for w in (dense, down)]
    return halves_call(branch_kernel, core, (mixed, act, dense, down), specs, False)


def back_halves(core, packed, up_grad, qkv, up, hidden, stats, gain, gain_two):
    specs = [whole(packed.shape), whole(up_grad.shape)]
    specs += [pl.BlockSpec((512, w.shape[1]), lambda j, s: (j, 0)) for w in (qkv, up)]
    specs += [pl.BlockSpec((TOK, 512), lambda j, s: (0, j)), whole((TOK, 128))]
    specs += [pl.BlockSpec((1, 512), lambda j, s: (0, j))] * 2
    operands = (packed, up_grad, qkv, up, hidden, stats, gain.reshape(1, D), gain_two.reshape(1, D))
    return halves_call(back_kernel, core, operands, specs, True)


def joint_kernel(side, *refs):
    lefts, rights, target, held, arrived = refs[:3], refs[3:9], refs[9], refs[10:13], refs[13]
    step = pl.program_id(0)
    copies = [pltpu.make_async_copy(lefts[k], held[k], arrived.at[k]) for k in range(3)]

    @pl.when(step == 0)
    def _():
        for copy in copies:
            copy.start()

    for k, (start, stop) in enumerate(((0, 4), (4, 5), (5, 8))):

        @pl.when(step == start)
        def _(k=k):
            copies[k].wait()

        @pl.when((step >= start) & (step < stop))
        def _(k=k):
            right = jnp.concatenate([rights[2 * k][...], rights[2 * k + 1][...]], axis=0)
            total = plain_dot(held[k][...].reshape(D, 2 * TOK), right)
            target[...] = total.reshape(16, 128, -1)


def joint(side, lefts, rights):
    width = 256
    specs = [pl.BlockSpec(memory_space=pl.ANY)] * 3
    for start, n in ((0, 4), (4, 1), (5, 3)):

        def near(j, s, start=start, n=n):
            return (0, s[0] * n + jnp.clip(j - start, 0, n - 1))

        def far(j, s, start=start, n=n):
            return (0, jnp.clip(j - start, 0, n - 1))

        specs += [pl.BlockSpec((TOK, width), near), pl.BlockSpec((TOK, width), far)]
    return pl.pallas_call(
        joint_kernel,
        grid_spec=pltpu.PrefetchScalarGridSpec(
            num_scalar_prefetch=1,
            grid=(8,),
            in_specs=specs,
            out_specs=pl.BlockSpec((16, 128, width), lambda j, s: (0, 0, j)),
            scratch_shapes=[pltpu.VMEM(TURNED, BF16)] * 3 + [pltpu.SemaphoreType.DMA((3,))],
        ),
        out_shape=jax.ShapeDtypeStruct((16, 128, 8 * width), F32),
        compiler_params=pltpu.CompilerParams(vmem_limit_bytes=VMEM),
        cost_estimate=COST,
    )(side, *lefts, *rights)


def body(
    hidden_in,
    segment_ids,
    positions,
    ln1_gain,
    ln1_bias,
    qkv_weight,
    qkv_bias,
    dense_weight,
    dense_bias,
    ln2_gain,
    ln2_bias,
    fc1_weight,
    fc1_bias,
    fc2_weight,
    fc2_bias,
    cotangent,
):
    core = lax.axis_index("c")
    side = lax.axis_index("zl")
    half_rows = TOK // 2
    at_side = side.astype(jnp.int32).reshape(1)
    at_core = core.astype(jnp.int32).reshape(1)
    own_place = jnp.zeros((2,), jnp.int32)
    far_place = jnp.stack([side, core * half_rows]).astype(jnp.int32)
    after = lax.optimization_barrier
    params = (ln1_gain, ln1_bias, ln2_gain, ln2_bias)

    def of_core(values, which):
        return lax.dynamic_slice_in_dim(values, which * half_rows, half_rows, 0)

    def both_cores(mine):
        theirs = send(mine, "c")
        filled = jnp.zeros((TOK,) + mine.shape[1:], mine.dtype)
        filled = lax.dynamic_update_slice_in_dim(filled, mine, core * half_rows, 0)
        return lax.dynamic_update_slice_in_dim(filled, theirs, (1 - core) * half_rows, 0)

    marks = jnp.concatenate([segment_ids, positions]).astype(F32).reshape(1, 2 * TOK)
    hidden_sent = jnp.concatenate(
        [of_core(hidden_in, core).astype(F32), jnp.pad(marks, ((0, 7), (0, D - 2 * TOK)))], axis=0
    )
    hidden_pair = lax.all_gather(hidden_sent, "zl")

    second_in, cot_turned, stats = norm_call(
        second_kernel, 256, (hidden_in, cotangent), 1, 1, (ln2_gain, ln2_bias), stats=True
    )
    act_low, slope, down_grad = feed(second_in, cot_turned, fc1_weight, fc1_bias)
    down_sum = after(lax.psum_scatter(down_grad, ("x", "y"), scatter_dimension=0, tiled=True))
    _, cotangent, hidden_in = after((down_grad, cotangent, hidden_in))

    own_marks = marks.reshape(2, TOK)
    first_in, first_turned, second_turned = norm_call(first_kernel, 256, (hidden_in,), 1, 2, params)
    projected = project(own_place, 2, first_in, qkv_weight, qkv_bias, own_marks)
    mixed_low, grad_packed = attend(own_place, 2, projected, cotangent, dense_weight, own_marks)
    grad_up = feed_back(at_side, cotangent, fc2_weight, slope)

    hidden_pair, mixed_low, grad_packed, grad_up, cotangent = after(
        (hidden_pair, mixed_low, grad_packed, grad_up, cotangent)
    )
    cot_got = send(of_core(cotangent, core).astype(F32), "zl")
    hidden_got = lax.dynamic_index_in_dim(hidden_pair, 1 - side, 0, keepdims=False)
    hidden_too = send(hidden_got, "c")

    def beside(hidden_got, hidden_too, first_turned, second_turned, mixed_low, grad_packed, grad_up):
        first_far, second_far, first_turned, second_turned = norm_call(
            first_far_kernel,
            128,
            (hidden_got, hidden_too),
            2,
            2,
            params,
            (first_turned, second_turned),
        )
        slope_side = slope_far(at_side, second_far, fc1_weight, fc1_bias)
        marks_got = hidden_got[half_rows, : 2 * TOK].reshape(2, 2, half_rows)
        marks_far = jnp.where(core == 0, marks_got, marks_got[:, ::-1]).reshape(2, TOK)
        projected_far = project(far_place, 1, first_far, qkv_weight, qkv_bias, marks_far)
        branches = branch_halves(at_core, mixed_low, act_low, dense_weight, fc2_weight)
        backs = back_halves(
            at_core,
            grad_packed,
            grad_up,
            qkv_weight,
            fc1_weight,
            hidden_in,
            stats,
            ln1_gain,
            ln2_gain,
        )
        return first_turned, second_turned, slope_side, marks_far, *branches, *backs, *projected_far

    (
        first_turned,
        second_turned,
        slope_side,
        marks_far,
        branch,
        branch_other,
        combined,
        combined_other,
        norms,
        *projected_far,
    ) = lax.cond(
        core == 0,
        beside,
        beside,
        hidden_got,
        hidden_too,
        first_turned,
        second_turned,
        mixed_low,
        grad_packed,
        grad_up,
    )

    slope_side, projected_far, cot_got, branch_other, combined_other = after(
        (slope_side, projected_far, cot_got, branch_other, combined_other)
    )
    cot_far, cot_turned = norm_call(
        cot_far_kernel,
        128,
        (cot_got, send(cot_got, "c")),
        1,
        1,
        (),
        (cot_turned,),
    )
    grad_up_far = feed_back(at_side, cot_far, fc2_weight, slope_side)
    mixed_far, grad_packed_far = attend(
        far_place, 1, projected_far, cot_far, dense_weight, marks_far
    )
    joint_grad = joint(
        at_side,
        (second_turned, cot_turned, first_turned),
        (grad_up, grad_up_far, mixed_low, mixed_far, grad_packed, grad_packed_far),
    )
    joint_grad, down_sum = after((joint_grad, down_sum))
    joint_sum = after(lax.psum_scatter(joint_grad, ("x", "y"), scatter_dimension=0, tiled=True))
    _, norms, grad_packed, grad_up, cotangent, down_sum, branch, combined = after(
        (joint_grad, norms, grad_packed, grad_up, cotangent, down_sum, branch, combined)
    )
    branch = branch + send(branch_other, "c")
    combined = combined + send(combined_other, "c")
    branch_too, combined_too = send(branch, "zh"), send(combined, "zh")

    norms = norms[:4].reshape(4, 32, 64).transpose(1, 0, 2).reshape(32, 256)
    grad_out = cotangent.astype(F32)
    bias_sum = jnp.sum(grad_out, axis=0)
    qkv_bias_sum = jnp.sum(grad_packed.astype(F32), axis=0)
    up_bias_grad = jnp.sum(grad_up.astype(F32), axis=0)
    small = jnp.concatenate(
        [
            norms,
            bias_sum.reshape(32, 64),
            qkv_bias_sum.reshape(2, 32, 24).transpose(1, 0, 2).reshape(32, 48),
            up_bias_grad.reshape(16, 32, 4).transpose(1, 0, 2).reshape(32, 64),
            jnp.zeros((32, 80), F32),
        ],
        axis=1,
    )
    for axis in ("x", "y"):
        small = small + swap(small, axis, 1)
        small = small + swap(small, axis, 2)
    block = lax.axis_index("x") * 4 + lax.axis_index("y")
    own_small = lax.dynamic_slice_in_dim(small, side * 16 + block, 1, 0)
    far_small = lax.dynamic_slice_in_dim(small, (1 - side) * 16 + block, 1, 0)
    small = (own_small + send(far_small, "zl")).reshape(-1)

    small, branch_too, combined_too = after((small, branch_too, combined_too))
    branch = branch + branch_too
    combined = combined + combined_too
    norms = small[:256]
    norms = norms + send(norms, "c")
    norms = (norms + send(norms, "zh")).reshape(4, 64)
    bias_total = small[256:320]
    hidden = hidden_in.astype(F32)
    output = both_cores(of_core(hidden, core) + branch + dense_bias + fc2_bias)
    own_stats = of_core(stats, core)
    average, inv_std = own_stats[:, 0:1], own_stats[:, 64:65]
    normed_half = (of_core(hidden, core) - average) * inv_std
    input_half = of_core(grad_out, core) + inv_std * (
        combined
        - jnp.mean(combined, axis=-1, keepdims=True)
        - normed_half * jnp.mean(combined * normed_half, axis=-1, keepdims=True)
    )
    input_grad = both_cores(input_half)

    def of_side(values, which):
        return lax.dynamic_slice_in_dim(values[0], which * 64, 64, 0)

    down_sum = of_side(down_sum, side) + send(of_side(down_sum, 1 - side), "zl")
    near = of_side(joint_sum, side)
    far = send(of_side(joint_sum, 1 - side), "zl")
    low = jnp.where(side == 0, near, far)
    high = jnp.where(side == 0, far, near)
    sums = []
    start = 0
    for width in (1024, 256, 768):
        stop = start + width
        sums.append(jnp.concatenate([low[:, start:stop], high[:, start:stop]], axis=1))
        start = stop
    up_sum, dense_sum, qkv_sum = sums
    return (
        output,
        input_grad,
        norms[0],
        norms[1],
        qkv_sum,
        small[320:368].reshape(2, 24),
        dense_sum.T,
        bias_total,
        norms[2],
        norms[3],
        up_sum,
        small[368:432].reshape(16, 4),
        down_sum.T,
        bias_total,
    )


def solution(mesh):
    fine = Mesh(mesh.devices.reshape(tuple(SIZES.values())), tuple(SIZES))
    return jax.shard_map(
        body,
        mesh=fine,
        in_specs=(
            P(DP, None),
            P(DP),
            P(DP),
            P(),
            P(),
            P(None, TENSOR),
            P(TENSOR, None),
            P(TENSOR, None),
            P(),
            P(),
            P(),
            P(None, TENSOR),
            P(TENSOR, None),
            P(TENSOR, None),
            P(),
            P(DP, None),
        ),
        out_specs=(
            P(DP, None),
            P(DP, None),
            P(DP),
            P(DP),
            P(DP, TENSOR),
            P(TENSOR, DP),
            P(TENSOR, DP),
            P(DP),
            P(DP),
            P(DP),
            P(DP, TENSOR),
            P(TENSOR, DP),
            P(TENSOR, DP),
            P(DP),
        ),
        check_vma=False,
    )
```

```python
from functools import partial
import math

import jax
import jax.numpy as jnp
import numpy as np
from jax import lax
from jax.experimental import pallas as pl
from jax.experimental.pallas import tpu as pltpu
from jax.sharding import Mesh, PartitionSpec as P

HD = 256
ROT = 64
TOK = 512
D = 2048
EPSILON = 1e-05
NEGATIVE = -1000000000.0
SIZES = {"zl": 2, "x": 4, "y": 4, "zh": 2, "c": 2}
DP = ("zl", "x", "y")
TENSOR = ("zh", "c")
F32 = jnp.float32
BF16 = jnp.bfloat16


def send(value, axis, step=1):
    n = SIZES[axis]
    return lax.ppermute(value, axis, [(i, (i + step) % n) for i in range(n)])


def swap(value, axis, bit):
    return lax.ppermute(value, axis, [(i, i ^ bit) for i in range(SIZES[axis])])


def plain_dot(left, right):
    return jnp.dot(left, right, preferred_element_type=F32)


def contract_cols(left, right):
    return lax.dot_general(left, right, (((1,), (1,)), ((), ())), preferred_element_type=F32)


VMEM = 56 * 1024 * 1024
COST = pl.CostEstimate(flops=1000000, bytes_accessed=1000000, transcendentals=0)


def whole(shape):
    return pl.BlockSpec(shape, lambda *_: (0,) * len(shape), pipeline_mode=pl.Buffered(1))


def put_turned(target, rows):
    for z in range(2):
        for pair in range(8):
            start = z * 1024 + pair * 128
            block = rows[:, start : start + 128].T.astype(BF16)
            target[2 * pair, z] = block[:64]
            target[2 * pair + 1, z] = block[64:]


def normalise(hidden):
    average = jnp.mean(hidden, axis=-1, keepdims=True)
    centred = hidden - average
    inv_std = lax.rsqrt(jnp.mean(centred * centred, axis=-1, keepdims=True) + EPSILON)
    return centred * inv_std, inv_std


def second_kernel(hidden, cot, gain, shift, second_out, cot_turned, stats):
    rows = hidden[...].astype(F32)
    average = jnp.mean(rows, axis=-1, keepdims=True)
    centred = rows - average
    inv_std = lax.rsqrt(jnp.mean(centred * centred, axis=-1, keepdims=True) + EPSILON)
    second_out[...] = (centred * inv_std * gain[...] + shift[...]).astype(BF16)
    put_turned(cot_turned, cot[...].astype(F32))
    lane = lax.broadcasted_iota(jnp.int32, (rows.shape[0], 128), 1)
    stats[...] = jnp.where(lane < 64, average, inv_std)


def first_kernel(hidden, gain, shift, gain_two, shift_two, first_out, first_turned, second_turned):
    normed, _ = normalise(hidden[...].astype(F32))
    first = normed * gain[...] + shift[...]
    first_out[...] = first.astype(BF16)
    put_turned(first_turned, first)
    put_turned(second_turned, normed * gain_two[...] + shift_two[...])


def first_far_kernel(near, other, gain, shift, gain_two, shift_two, *refs):
    first_out, second_out, first_turned, second_turned = refs[2:]

    def step(rows):
        normed, _ = normalise(rows)
        first = normed * gain[...] + shift[...]
        second = normed * gain_two[...] + shift_two[...]
        first_out[...] = first.astype(BF16)
        second_out[...] = second.astype(BF16)
        put_turned(first_turned, first)
        put_turned(second_turned, second)

    @pl.when(pl.program_id(0) < 2)
    def _():
        step(near[...])

    @pl.when(pl.program_id(0) >= 2)
    def _():
        step(other[...])


TURNED = (16, 2, 64, 2 * TOK)


def norm_call(kernel, rows, n_rows, n_plain, n_turned, params, far=(), stats=False):
    steps = TOK // rows
    plain = pl.BlockSpec((rows, D), lambda i: (i, 0))
    shift = steps if far else 0
    turned = pl.BlockSpec((16, 2, 64, rows), lambda i: (0, 0, 0, i + shift))
    if far:
        picks = (lambda i: (lax.min(i, 1), 0), lambda i: (lax.max(i - 2, 0), 0))
        specs = [pl.BlockSpec((rows, D), p) for p in picks]
    else:
        specs = [plain] * len(n_rows)
    operands = list(n_rows) + [p.reshape(1, D) for p in params]
    aliases = {len(operands) + i: n_plain + i for i in range(len(far))}
    return pl.pallas_call(
        kernel,
        grid=(steps,),
        in_specs=specs + [whole((1, D))] * len(params) + [pl.BlockSpec(memory_space=pl.ANY)] * len(far),
        out_specs=[plain] * n_plain
        + [turned] * n_turned
        + [pl.BlockSpec((rows, 128), lambda i: (i, 0))] * stats,
        out_shape=[jax.ShapeDtypeStruct((TOK, D), BF16)] * n_plain
        + [jax.ShapeDtypeStruct(TURNED, BF16)] * n_turned
        + [jax.ShapeDtypeStruct((TOK, 128), F32)] * stats,
        input_output_aliases=aliases,
        compiler_params=pltpu.CompilerParams(vmem_limit_bytes=VMEM),
        cost_estimate=COST,
    )(*operands, *far)


def phi(upward):
    return 0.5 * (1.0 + lax.erf(upward * math.sqrt(0.5)))


def gelu_slope(upward, below):
    return below + upward * (jnp.exp(-0.5 * upward * upward) * (1.0 / math.sqrt(2.0 * math.pi)))


def as_row(block):
    return jnp.concatenate([block[i : i + 1, :] for i in range(block.shape[0])], axis=1)


def feed_kernel(second, cot_turned, weight, bias, act_out, slope_out, down_grad):
    upward = plain_dot(second[...], weight[...]) + as_row(bias[0])
    below = phi(upward)
    act = (upward * below).astype(BF16)
    act_out[...] = act
    slope_out[...] = gelu_slope(upward, below)
    down_grad[...] = plain_dot(cot_turned[...].reshape(D, TOK), act).reshape(16, 128, -1)


def feed(second, cot_turned, weight, bias):
    units, width = weight.shape[1], 512
    column = pl.BlockSpec((TOK, width), lambda j: (0, j))
    return pl.pallas_call(
        feed_kernel,
        grid=(units // width,),
        in_specs=[
            whole((TOK, D)),
            whole((16, 2, 64, TOK)),
            pl.BlockSpec((D, width), lambda j: (0, j)),
            pl.BlockSpec((1, width // 128, 128), lambda j: (j, 0, 0)),
        ],
        out_specs=[column, column, pl.BlockSpec((16, 128, width), lambda j: (0, 0, j))],
        out_shape=[
            jax.ShapeDtypeStruct((TOK, units), BF16),
            jax.ShapeDtypeStruct((TOK, units), F32),
            jax.ShapeDtypeStruct((16, 128, units), F32),
        ],
        compiler_params=pltpu.CompilerParams(vmem_limit_bytes=VMEM),
        cost_estimate=COST,
    )(second, cot_turned, weight, bias.reshape(-1, width // 128, 128))


def feed_back_kernel(cot, weight, slope, dense, up_grad, grad_mixed):
    up_grad[...] = (contract_cols(cot[...], weight[...]) * slope[...]).astype(BF16)

    @pl.when(pl.program_id(0) == 0)
    def _():
        grad_mixed[...] = contract_cols(cot[...], dense[...]).astype(BF16)


def feed_back(cot, weight, slope, dense):
    units, width = slope.shape[1], 512
    column = pl.BlockSpec((TOK, width), lambda j: (0, j))
    mixed = dense.shape[0]
    return pl.pallas_call(
        feed_back_kernel,
        grid=(units // width,),
        in_specs=[
            whole((TOK, D)),
            pl.BlockSpec((width, D), lambda j: (j, 0)),
            column,
            whole(dense.shape),
        ],
        out_specs=[column, pl.BlockSpec((TOK, mixed), lambda j: (0, 0))],
        out_shape=[
            jax.ShapeDtypeStruct((TOK, units), BF16),
            jax.ShapeDtypeStruct((TOK, mixed), BF16),
        ],
        compiler_params=pltpu.CompilerParams(vmem_limit_bytes=VMEM),
        cost_estimate=COST,
    )(cot, weight, slope, dense)


def cot_far_kernel(n, side, rows, weight, slope, dense, *refs):
    up_grad, grad_mixed, cot_turned, low = refs[n:]

    @pl.when(pl.program_id(0) == 0)
    def _():
        low[...] = rows[...].astype(BF16)
        put_turned(cot_turned, rows[...])
        grad_mixed[...] = contract_cols(low[...], dense[...]).astype(BF16)

    up_grad[...] = (contract_cols(low[...], weight[...]) * slope[...]).astype(BF16)


def cot_far_half(k, side, rows, weight, slope, dense, held):
    half, width = TOK // 2, 256
    steps = slope.shape[1] // width
    first = len(held) == 1
    shapes = [
        jax.ShapeDtypeStruct((TOK, slope.shape[1]), BF16),
        jax.ShapeDtypeStruct((TOK, HD), BF16),
        jax.ShapeDtypeStruct(TURNED, BF16),
    ]
    return pl.pallas_call(
        partial(cot_far_kernel, len(held)),
        grid_spec=pltpu.PrefetchScalarGridSpec(
            num_scalar_prefetch=1,
            grid=(steps,),
            in_specs=[
                whole((half, D)),
                pl.BlockSpec((width, D), lambda j, s: (s[0] * steps + j, 0)),
                pl.BlockSpec((half, width), lambda j, s: (k, j)),
                pl.BlockSpec((HD, D), lambda j, s: (s[0], 0)),
            ]
            + [pl.BlockSpec(memory_space=pl.ANY)] * len(held),
            out_specs=[
                pl.BlockSpec((half, width), lambda j, s: (k, j)),
                pl.BlockSpec((half, HD), lambda j, s: (k, 0)),
                pl.BlockSpec((16, 2, 64, half), lambda j, s: (0, 0, 0, 2 + k)),
            ],
            scratch_shapes=[pltpu.VMEM((half, D), BF16)],
        ),
        out_shape=shapes,
        input_output_aliases={5: 2} if first else {5: 0, 6: 1, 7: 2},
        compiler_params=pltpu.CompilerParams(vmem_limit_bytes=VMEM),
        cost_estimate=COST,
    )(side, rows, weight, slope, dense, *held)


def slope_far_kernel(side, second, weight, bias, slope):
    upward = plain_dot(second[...], weight[...]) + as_row(bias[0])
    slope[...] = gelu_slope(upward, phi(upward))


def slope_far(side, second, weight, bias):
    units, width = weight.shape[1] // 2, 512
    steps = units // width
    return pl.pallas_call(
        slope_far_kernel,
        grid_spec=pltpu.PrefetchScalarGridSpec(
            num_scalar_prefetch=1,
            grid=(steps,),
            in_specs=[
                whole((TOK, D)),
                pl.BlockSpec((D, width), lambda j, s: (0, s[0] * steps + j)),
                pl.BlockSpec((1, width // 128, 128), lambda j, s: (s[0] * steps + j, 0, 0)),
            ],
            out_specs=pl.BlockSpec((TOK, width), lambda j, s: (0, j)),
        ),
        out_shape=jax.ShapeDtypeStruct((TOK, units), F32),
        compiler_params=pltpu.CompilerParams(vmem_limit_bytes=VMEM),
        cost_estimate=COST,
    )(side, second, weight, bias.reshape(-1, width // 128, 128))


def turn(values, tables, sign):
    first = values[:, :128]
    cosine, rising, falling = tables
    first = (
        first * cosine[...]
        + (pltpu.roll(first, 32, 1) * rising[...] + pltpu.roll(first, 96, 1) * falling[...]) * sign
    )
    return jnp.concatenate([first, values[:, 128:]], axis=1)


def as_column(row):
    return jnp.broadcast_to(row, (8, row.shape[1])).T[:, 0:1]


def cosine_and_sine(angles):
    turns = jnp.floor(angles * (2.0 / math.pi) + 0.5)
    rest = ((angles - turns * 1.5703125) - turns * 4.837512969970703e-4) - turns * 7.549789954891882e-8
    square = rest * rest
    sine = ((-1.9515295891e-4 * square + 8.3321608736e-3) * square - 1.6666654611e-1) * square
    sine = sine * rest + rest
    cosine = (2.443315711809948e-5 * square - 1.388731625493765e-3) * square + 4.166664568298827e-2
    cosine = cosine * (square * square) - 0.5 * square + 1.0
    quarter = turns.astype(jnp.int32) & 3
    odd = (quarter & 1) == 1
    flipped = jnp.where(odd, sine, cosine), jnp.where(odd, cosine, sine)
    return (
        jnp.where((quarter == 1) | (quarter == 2), -flipped[0], flipped[0]),
        jnp.where(quarter >= 2, -flipped[1], flipped[1]),
    )


def project_kernel(place, first, weight, bias, marks, inverse, queries, keys, values, *tables):
    @pl.when(pl.program_id(0) == 0)
    def _():
        angles = inverse[...] * marks[1:2, :]
        cosine, sine = cosine_and_sine(angles)
        none, rest = jnp.zeros_like(sine), jnp.zeros((64, TOK), F32)
        tables[0][...] = jnp.concatenate([cosine, cosine, rest + 1.0], axis=0).T
        tables[1][...] = jnp.concatenate([none, sine, rest], axis=0).T
        tables[2][...] = jnp.concatenate([-sine, none, rest], axis=0).T

    head = pl.program_id(0) + place[0] * (2 - pl.num_programs(0))
    packed = plain_dot(first[...], weight[...]) + bias[pl.ds(head, 1), :]
    queries[...] = turn(packed[:, :HD], tables, 1.0).astype(BF16)
    keys[...] = turn(packed[:, HD : 2 * HD], tables, 1.0).astype(BF16)
    values[...] = packed[:, 2 * HD :].astype(BF16)


def project(place, heads, first, weight, bias, marks):
    inverse = jnp.asarray((10000.0 ** (-2.0 * np.arange(32) / ROT)).astype(np.float32).reshape(32, 1))
    at = (lambda h, s: h) if heads == 2 else (lambda h, s: s[0])
    column = pl.BlockSpec((TOK, HD), lambda h, s: (0, h))
    return pl.pallas_call(
        project_kernel,
        grid_spec=pltpu.PrefetchScalarGridSpec(
            num_scalar_prefetch=1,
            grid=(heads,),
            in_specs=[
                whole((TOK, D)),
                pl.BlockSpec((D, 3 * HD), lambda h, s: (0, at(h, s))),
                whole((2, 3 * HD)),
                whole((2, TOK)),
                whole((32, 1)),
            ],
            out_specs=[column] * 3 + [pl.BlockSpec((TOK, 128), lambda h, s: (0, 0))] * 3,
        ),
        out_shape=[jax.ShapeDtypeStruct((TOK, heads * HD), BF16)] * 3
        + [jax.ShapeDtypeStruct((TOK, 128), F32)] * 3,
        compiler_params=pltpu.CompilerParams(vmem_limit_bytes=VMEM),
        cost_estimate=COST,
    )(place, first, weight, bias, marks, inverse)


def attend_kernel(
    place, queries, keys, values, cosine, rising, falling, grad_mixed, marks, mixed_out, grad_out
):
    tables = (cosine, rising, falling)
    scale = 1.0 / math.sqrt(HD)
    queries, keys, values = queries[...], keys[...], values[...]
    segments = marks[0:1, :]

    def order(axis):
        return lax.rem(lax.broadcasted_iota(jnp.int32, (TOK, TOK), axis) + place[1], TOK)

    allowed = (as_column(segments) == segments) & (order(0) >= order(1))
    scores = jnp.where(allowed, contract_cols(queries, keys) * scale, NEGATIVE)
    top = jnp.max(scores, axis=-1, keepdims=True)
    weights = jnp.exp(scores - top)
    probs = weights / jnp.sum(weights, axis=-1, keepdims=True)
    probs_low = probs.astype(BF16)
    mixed_out[...] = plain_dot(probs_low, values).astype(BF16)
    grad_probs = contract_cols(grad_mixed[...], values)
    along = jnp.sum(probs * grad_probs, axis=-1, keepdims=True)
    grad_scores = (probs * (grad_probs - along)).astype(BF16)
    grad_query = plain_dot(grad_scores, keys) * scale
    grad_key = plain_dot(grad_scores.T, queries) * scale
    grad_value = plain_dot(probs_low.T, grad_mixed[...])
    grad_out[:, :HD] = turn(grad_query, tables, -1.0).astype(BF16)
    grad_out[:, HD : 2 * HD] = turn(grad_key, tables, -1.0).astype(BF16)
    grad_out[:, 2 * HD :] = grad_value.astype(BF16)


def attend(place, heads, projected, grad_mixed, marks):
    column = pl.BlockSpec((TOK, HD), lambda h, s: (0, h))
    return pl.pallas_call(
        attend_kernel,
        grid_spec=pltpu.PrefetchScalarGridSpec(
            num_scalar_prefetch=1,
            grid=(heads,),
            in_specs=[column] * 3
            + [whole((TOK, 128))] * 3
            + [column, whole((2, TOK))],
            out_specs=[column, pl.BlockSpec((TOK, 3 * HD), lambda h, s: (0, h))],
        ),
        out_shape=[
            jax.ShapeDtypeStruct((TOK, heads * HD), BF16),
            jax.ShapeDtypeStruct((TOK, heads * 3 * HD), BF16),
        ],
        compiler_params=pltpu.CompilerParams(vmem_limit_bytes=VMEM),
        cost_estimate=COST,
    )(place, *projected, grad_mixed, marks)


def put_halves(core, values, scratch, mine, other):
    scratch[...] = values
    half = TOK // 2
    mine[...] = scratch[pl.ds(pl.multiple_of(core[0] * half, half), half), :]
    other[...] = scratch[pl.ds(pl.multiple_of((1 - core[0]) * half, half), half), :]


def branch_kernel(core, mixed, act, dense, down, mine, other, scratch):
    total = plain_dot(act[...], down[...]) + plain_dot(mixed[...], dense[...])
    put_halves(core, total, scratch, mine, other)


def back_kernel(
    core, packed, up_grad, qkv, up, hidden, stats, gain, gain_two, mine, other, sums, scratch
):
    first = contract_cols(packed[...], qkv[...])
    second = contract_cols(up_grad[...], up[...])
    put_halves(core, first * gain[...] + second * gain_two[...], scratch, mine, other)
    normed = (hidden[...].astype(F32) - stats[:, 0:1]) * stats[:, 64:65]
    rows = [
        jnp.sum(v, axis=0, keepdims=True) for v in (first * normed, first, second * normed, second)
    ]
    sums[...] = jnp.concatenate(rows + [jnp.zeros((4, first.shape[1]), F32)], axis=0)


def halves_call(kernel, core, operands, specs, with_sums):
    width = 512
    half = pl.BlockSpec((TOK // 2, width), lambda j, s: (0, j))
    return pl.pallas_call(
        kernel,
        grid_spec=pltpu.PrefetchScalarGridSpec(
            num_scalar_prefetch=1,
            grid=(D // width,),
            in_specs=specs,
            out_specs=[half, half] + [pl.BlockSpec((8, width), lambda j, s: (0, j))] * with_sums,
            scratch_shapes=[pltpu.VMEM((TOK, width), F32)],
        ),
        out_shape=[jax.ShapeDtypeStruct((TOK // 2, D), F32)] * 2
        + [jax.ShapeDtypeStruct((8, D), F32)] * with_sums,
        compiler_params=pltpu.CompilerParams(vmem_limit_bytes=VMEM),
        cost_estimate=COST,
    )(core, *operands)


def branch_halves(core, mixed, act, dense, down):
    specs = [whole(mixed.shape), whole(act.shape)]
    specs += [pl.BlockSpec((w.shape[0], 512), lambda j, s: (0, j)) for w in (dense, down)]
    return halves_call(branch_kernel, core, (mixed, act, dense, down), specs, False)


def back_halves(core, packed, up_grad, qkv, up, hidden, stats, gain, gain_two):
    specs = [whole(packed.shape), whole(up_grad.shape)]
    specs += [pl.BlockSpec((512, w.shape[1]), lambda j, s: (j, 0)) for w in (qkv, up)]
    specs += [pl.BlockSpec((TOK, 512), lambda j, s: (0, j)), whole((TOK, 128))]
    specs += [pl.BlockSpec((1, 512), lambda j, s: (0, j))] * 2
    operands = (packed, up_grad, qkv, up, hidden, stats, gain.reshape(1, D), gain_two.reshape(1, D))
    return halves_call(back_kernel, core, operands, specs, True)


def joint_kernel(side, *refs):
    lefts, rights, target, held, arrived = refs[:3], refs[3:9], refs[9], refs[10:13], refs[13]
    step = pl.program_id(0)
    copies = [pltpu.make_async_copy(lefts[k], held[k], arrived.at[k]) for k in range(3)]

    @pl.when(step == 0)
    def _():
        for copy in copies:
            copy.start()

    for k, (start, stop) in enumerate(((0, 4), (4, 5), (5, 8))):

        @pl.when(step == start)
        def _(k=k):
            copies[k].wait()

        @pl.when((step >= start) & (step < stop))
        def _(k=k):
            right = jnp.concatenate([rights[2 * k][...], rights[2 * k + 1][...]], axis=0)
            total = plain_dot(held[k][...].reshape(D, 2 * TOK), right)
            target[...] = total.reshape(16, 128, -1)


def joint(side, lefts, rights):
    width = 256
    specs = [pl.BlockSpec(memory_space=pl.ANY)] * 3
    for start, n in ((0, 4), (4, 1), (5, 3)):

        def near(j, s, start=start, n=n):
            return (0, s[0] * n + jnp.clip(j - start, 0, n - 1))

        def far(j, s, start=start, n=n):
            return (0, jnp.clip(j - start, 0, n - 1))

        specs += [pl.BlockSpec((TOK, width), near), pl.BlockSpec((TOK, width), far)]
    return pl.pallas_call(
        joint_kernel,
        grid_spec=pltpu.PrefetchScalarGridSpec(
            num_scalar_prefetch=1,
            grid=(8,),
            in_specs=specs,
            out_specs=pl.BlockSpec((16, 128, width), lambda j, s: (0, 0, j)),
            scratch_shapes=[pltpu.VMEM(TURNED, BF16)] * 3 + [pltpu.SemaphoreType.DMA((3,))],
        ),
        out_shape=jax.ShapeDtypeStruct((16, 128, 8 * width), F32),
        compiler_params=pltpu.CompilerParams(vmem_limit_bytes=VMEM),
        cost_estimate=COST,
    )(side, *lefts, *rights)


def body(
    hidden_in,
    segment_ids,
    positions,
    ln1_gain,
    ln1_bias,
    qkv_weight,
    qkv_bias,
    dense_weight,
    dense_bias,
    ln2_gain,
    ln2_bias,
    fc1_weight,
    fc1_bias,
    fc2_weight,
    fc2_bias,
    cotangent,
):
    core = lax.axis_index("c")
    side = lax.axis_index("zl")
    half_rows = TOK // 2
    at_side = side.astype(jnp.int32).reshape(1)
    at_core = core.astype(jnp.int32).reshape(1)
    own_place = jnp.zeros((2,), jnp.int32)
    far_place = jnp.stack([side, core * half_rows]).astype(jnp.int32)
    after = lax.optimization_barrier
    params = (ln1_gain, ln1_bias, ln2_gain, ln2_bias)

    def of_core(values, which):
        return lax.dynamic_slice_in_dim(values, which * half_rows, half_rows, 0)

    def both_cores(mine):
        theirs = send(mine, "c")
        filled = jnp.zeros((TOK,) + mine.shape[1:], mine.dtype)
        filled = lax.dynamic_update_slice_in_dim(filled, mine, core * half_rows, 0)
        return lax.dynamic_update_slice_in_dim(filled, theirs, (1 - core) * half_rows, 0)

    marks = jnp.concatenate([segment_ids, positions]).astype(F32).reshape(1, 2 * TOK)
    hidden_sent = jnp.concatenate(
        [of_core(hidden_in, core).astype(F32), jnp.pad(marks, ((0, 7), (0, D - 2 * TOK)))], axis=0
    )
    hidden_pair = lax.all_gather(hidden_sent, "zl")

    second_in, cot_turned, stats = norm_call(
        second_kernel, 256, (hidden_in, cotangent), 1, 1, (ln2_gain, ln2_bias), stats=True
    )
    act_low, slope, down_grad = feed(second_in, cot_turned, fc1_weight, fc1_bias)
    down_sum = after(lax.psum_scatter(down_grad, ("x", "y"), scatter_dimension=0, tiled=True))
    _, cotangent, hidden_in = after((down_grad, cotangent, hidden_in))

    own_marks = marks.reshape(2, TOK)
    first_in, first_turned, second_turned = norm_call(first_kernel, 256, (hidden_in,), 1, 2, params)
    projected = project(own_place, 2, first_in, qkv_weight, qkv_bias, own_marks)
    grad_up, grad_mixed = feed_back(cotangent, fc2_weight, slope, dense_weight)
    mixed_low, grad_packed = attend(own_place, 2, projected, grad_mixed, own_marks)
    branch, branch_other = branch_halves(at_core, mixed_low, act_low, dense_weight, fc2_weight)
    cot_sent = of_core(cotangent, core).astype(F32)

    hidden_pair, branch_other, cot_sent, grad_up = after(
        (hidden_pair, branch_other, cot_sent, grad_up)
    )
    cot_got = send(cot_sent, "zl")
    hidden_got = lax.dynamic_index_in_dim(hidden_pair, 1 - side, 0, keepdims=False)
    hidden_too = send(hidden_got, "c")
    branch = branch + send(branch_other, "c")
    hidden_too, branch = after((hidden_too, branch))

    def beside(hidden_got, hidden_too, first_turned, second_turned, grad_packed, grad_up):
        first_far, second_far, first_turned, second_turned = norm_call(
            first_far_kernel,
            128,
            (hidden_got, hidden_too),
            2,
            2,
            params,
            (first_turned, second_turned),
        )
        slope_side = slope_far(at_side, second_far, fc1_weight, fc1_bias)
        marks_got = hidden_got[half_rows, : 2 * TOK].reshape(2, 2, half_rows)
        marks_far = jnp.where(core == 0, marks_got, marks_got[:, ::-1]).reshape(2, TOK)
        projected_far = project(far_place, 1, first_far, qkv_weight, qkv_bias, marks_far)
        backs = back_halves(
            at_core,
            grad_packed,
            grad_up,
            qkv_weight,
            fc1_weight,
            hidden_in,
            stats,
            ln1_gain,
            ln2_gain,
        )
        return first_turned, second_turned, slope_side, marks_far, *backs, *projected_far

    (
        first_turned,
        second_turned,
        slope_side,
        marks_far,
        combined,
        combined_other,
        norms,
        *projected_far,
    ) = lax.cond(
        core == 0,
        beside,
        beside,
        hidden_got,
        hidden_too,
        first_turned,
        second_turned,
        grad_packed,
        grad_up,
    )

    slope_side, cot_got, combined_other = after((slope_side, cot_got, combined_other))
    cot_too = send(cot_got, "c")
    combined_too = send(combined_other, "c")
    held = cot_far_half(0, at_side, cot_got, fc2_weight, slope_side, dense_weight, (cot_turned,))
    *held, cot_too, combined_too = after((*held, cot_too, combined_too))
    combined = combined + combined_too
    branch = lax.psum(branch, "zh")
    combined = lax.psum(combined, "zh")
    grad_up_far, grad_mixed_far, cot_turned = cot_far_half(
        1, at_side, cot_too, fc2_weight, slope_side, dense_weight, held
    )
    mixed_far, grad_packed_far = attend(far_place, 1, projected_far, grad_mixed_far, marks_far)
    joint_grad = joint(
        at_side,
        (second_turned, cot_turned, first_turned),
        (grad_up, grad_up_far, mixed_low, mixed_far, grad_packed, grad_packed_far),
    )
    joint_grad, down_sum = after((joint_grad, down_sum))
    joint_sum = after(lax.psum_scatter(joint_grad, ("x", "y"), scatter_dimension=0, tiled=True))
    _, norms, grad_packed, grad_up, cotangent, down_sum = after(
        (joint_grad, norms, grad_packed, grad_up, cotangent, down_sum)
    )

    norms = norms[:4].reshape(4, 32, 64).transpose(1, 0, 2).reshape(32, 256)
    grad_out = cotangent.astype(F32)
    bias_sum = jnp.sum(grad_out, axis=0)
    qkv_bias_sum = jnp.sum(grad_packed.astype(F32), axis=0)
    up_bias_grad = jnp.sum(grad_up.astype(F32), axis=0)
    small = jnp.concatenate(
        [
            norms,
            bias_sum.reshape(32, 64),
            qkv_bias_sum.reshape(2, 32, 24).transpose(1, 0, 2).reshape(32, 48),
            up_bias_grad.reshape(16, 32, 4).transpose(1, 0, 2).reshape(32, 64),
            jnp.zeros((32, 80), F32),
        ],
        axis=1,
    )
    for axis in ("x", "y"):
        small = small + swap(small, axis, 1)
        small = small + swap(small, axis, 2)
    block = lax.axis_index("x") * 4 + lax.axis_index("y")
    own_small = lax.dynamic_slice_in_dim(small, side * 16 + block, 1, 0)
    far_small = lax.dynamic_slice_in_dim(small, (1 - side) * 16 + block, 1, 0)
    small = (own_small + send(far_small, "zl")).reshape(-1)

    small, branch, combined = after((small, branch, combined))
    norms, joint_sum = after((small[:256], joint_sum))
    norms = norms + send(norms, "c")
    norms = (norms + send(norms, "zh")).reshape(4, 64)
    bias_total = small[256:320]
    hidden = hidden_in.astype(F32)
    output = both_cores(of_core(hidden, core) + branch + dense_bias + fc2_bias)
    own_stats = of_core(stats, core)
    average, inv_std = own_stats[:, 0:1], own_stats[:, 64:65]
    normed_half = (of_core(hidden, core) - average) * inv_std
    input_half = of_core(grad_out, core) + inv_std * (
        combined
        - jnp.mean(combined, axis=-1, keepdims=True)
        - normed_half * jnp.mean(combined * normed_half, axis=-1, keepdims=True)
    )
    input_grad = both_cores(input_half)

    def of_side(values, which):
        return lax.dynamic_slice_in_dim(values[0], which * 64, 64, 0)

    down_sum = of_side(down_sum, side) + send(of_side(down_sum, 1 - side), "zl")
    near = of_side(joint_sum, side)
    far = send(of_side(joint_sum, 1 - side), "zl")
    low = jnp.where(side == 0, near, far)
    high = jnp.where(side == 0, far, near)
    sums = []
    start = 0
    for width in (1024, 256, 768):
        stop = start + width
        sums.append(jnp.concatenate([low[:, start:stop], high[:, start:stop]], axis=1))
        start = stop
    up_sum, dense_sum, qkv_sum = sums
    return (
        output,
        input_grad,
        norms[0],
        norms[1],
        qkv_sum,
        small[320:368].reshape(2, 24),
        dense_sum.T,
        bias_total,
        norms[2],
        norms[3],
        up_sum,
        small[368:432].reshape(16, 4),
        down_sum.T,
        bias_total,
    )


def solution(mesh):
    fine = Mesh(mesh.devices.reshape(tuple(SIZES.values())), tuple(SIZES))
    return jax.shard_map(
        body,
        mesh=fine,
        in_specs=(
            P(DP, None),
            P(DP),
            P(DP),
            P(),
            P(),
            P(None, TENSOR),
            P(TENSOR, None),
            P(TENSOR, None),
            P(),
            P(),
            P(),
            P(None, TENSOR),
            P(TENSOR, None),
            P(TENSOR, None),
            P(),
            P(DP, None),
        ),
        out_specs=(
            P(DP, None),
            P(DP, None),
            P(DP),
            P(DP),
            P(DP, TENSOR),
            P(TENSOR, DP),
            P(TENSOR, DP),
            P(DP),
            P(DP),
            P(DP),
            P(DP, TENSOR),
            P(TENSOR, DP),
            P(TENSOR, DP),
            P(DP),
        ),
        check_vma=False,
    )
```

```python
from functools import partial
import math

import jax
import jax.numpy as jnp
import numpy as np
from jax import lax
from jax.experimental import pallas as pl
from jax.experimental.pallas import tpu as pltpu
from jax.sharding import Mesh, PartitionSpec as P

HD = 256
ROT = 64
TOK = 512
D = 2048
EPSILON = 1e-05
NEGATIVE = -1000000000.0
SIZES = {"zl": 2, "x": 4, "y": 4, "zh": 2, "c": 2}
DP = ("zl", "x", "y")
TENSOR = ("zh", "c")
F32 = jnp.float32
BF16 = jnp.bfloat16


def send(value, axis, step=1):
    n = SIZES[axis]
    return lax.ppermute(value, axis, [(i, (i + step) % n) for i in range(n)])


def swap(value, axis, bit):
    return lax.ppermute(value, axis, [(i, i ^ bit) for i in range(SIZES[axis])])


def plain_dot(left, right):
    return jnp.dot(left, right, preferred_element_type=F32)


def contract_cols(left, right):
    return lax.dot_general(left, right, (((1,), (1,)), ((), ())), preferred_element_type=F32)


VMEM = 56 * 1024 * 1024
COST = pl.CostEstimate(flops=1000000, bytes_accessed=1000000, transcendentals=0)


def whole(shape):
    return pl.BlockSpec(shape, lambda *_: (0,) * len(shape), pipeline_mode=pl.Buffered(1))


def put_turned(target, rows):
    for z in range(2):
        for pair in range(8):
            start = z * 1024 + pair * 128
            block = rows[:, start : start + 128].T.astype(BF16)
            target[2 * pair, z] = block[:64]
            target[2 * pair + 1, z] = block[64:]


def normalise(hidden):
    average = jnp.mean(hidden, axis=-1, keepdims=True)
    centred = hidden - average
    inv_std = lax.rsqrt(jnp.mean(centred * centred, axis=-1, keepdims=True) + EPSILON)
    return centred * inv_std, inv_std


def second_kernel(hidden, cot, gain, shift, second_out, cot_turned, stats):
    rows = hidden[...].astype(F32)
    average = jnp.mean(rows, axis=-1, keepdims=True)
    centred = rows - average
    inv_std = lax.rsqrt(jnp.mean(centred * centred, axis=-1, keepdims=True) + EPSILON)
    second_out[...] = (centred * inv_std * gain[...] + shift[...]).astype(BF16)
    put_turned(cot_turned, cot[...].astype(F32))
    lane = lax.broadcasted_iota(jnp.int32, (rows.shape[0], 128), 1)
    stats[...] = jnp.where(lane < 64, average, inv_std)


def first_kernel(hidden, gain, shift, gain_two, shift_two, first_out, first_turned, second_turned):
    normed, _ = normalise(hidden[...].astype(F32))
    first = normed * gain[...] + shift[...]
    first_out[...] = first.astype(BF16)
    put_turned(first_turned, first)
    put_turned(second_turned, normed * gain_two[...] + shift_two[...])


def first_far_kernel(side, near, other, gain, shift, gain_two, shift_two, *refs):
    first_out, second_out, first_turned, second_turned = refs[2:]

    def step(rows):
        normed, _ = normalise(rows)
        first = normed * gain[...] + shift[...]
        second = normed * gain_two[...] + shift_two[...]
        first_out[...] = first.astype(BF16)
        second_out[...] = second.astype(BF16)
        put_turned(first_turned, first)
        put_turned(second_turned, second)

    @pl.when(pl.program_id(0) < 2)
    def _():
        step(near[0])

    @pl.when(pl.program_id(0) >= 2)
    def _():
        step(other[0])


TURNED = (16, 2, 64, 2 * TOK)


def norm_call(kernel, rows, n_rows, n_plain, n_turned, params, stats=False):
    plain = pl.BlockSpec((rows, D), lambda i: (i, 0))
    return pl.pallas_call(
        kernel,
        grid=(TOK // rows,),
        in_specs=[plain] * len(n_rows) + [whole((1, D))] * len(params),
        out_specs=[plain] * n_plain
        + [pl.BlockSpec((16, 2, 64, rows), lambda i: (0, 0, 0, i))] * n_turned
        + [pl.BlockSpec((rows, 128), lambda i: (i, 0))] * stats,
        out_shape=[jax.ShapeDtypeStruct((TOK, D), BF16)] * n_plain
        + [jax.ShapeDtypeStruct(TURNED, BF16)] * n_turned
        + [jax.ShapeDtypeStruct((TOK, 128), F32)] * stats,
        compiler_params=pltpu.CompilerParams(vmem_limit_bytes=VMEM),
        cost_estimate=COST,
    )(*n_rows, *(p.reshape(1, D) for p in params))


def first_far(side, near, other, params, held):
    rows = 128
    plain = pl.BlockSpec((rows, D), lambda i, s: (i, 0))
    return pl.pallas_call(
        first_far_kernel,
        grid_spec=pltpu.PrefetchScalarGridSpec(
            num_scalar_prefetch=1,
            grid=(TOK // rows,),
            in_specs=[
                pl.BlockSpec((1, rows, D), lambda i, s: (1 - s[0], lax.min(i, 1), 0)),
                pl.BlockSpec((1, rows, D), lambda i, s: (1 - s[0], lax.max(i - 2, 0), 0)),
            ]
            + [whole((1, D))] * 4
            + [pl.BlockSpec(memory_space=pl.ANY)] * 2,
            out_specs=[plain] * 2
            + [pl.BlockSpec((16, 2, 64, rows), lambda i, s: (0, 0, 0, i + TOK // rows))] * 2,
        ),
        out_shape=[jax.ShapeDtypeStruct((TOK, D), BF16)] * 2
        + [jax.ShapeDtypeStruct(TURNED, BF16)] * 2,
        input_output_aliases={7: 2, 8: 3},
        compiler_params=pltpu.CompilerParams(vmem_limit_bytes=VMEM),
        cost_estimate=COST,
    )(side, near, other, *(p.reshape(1, D) for p in params), *held)


def phi(upward):
    return 0.5 * (1.0 + lax.erf(upward * math.sqrt(0.5)))


def gelu_slope(upward, below):
    return below + upward * (jnp.exp(-0.5 * upward * upward) * (1.0 / math.sqrt(2.0 * math.pi)))


def as_row(block):
    return jnp.concatenate([block[i : i + 1, :] for i in range(block.shape[0])], axis=1)


def feed_kernel(second, cot_turned, weight, bias, act_out, slope_out, down_grad):
    upward = plain_dot(second[...], weight[...]) + as_row(bias[0])
    below = phi(upward)
    act = (upward * below).astype(BF16)
    act_out[...] = act
    slope_out[...] = gelu_slope(upward, below)
    down_grad[...] = plain_dot(cot_turned[...].reshape(D, TOK), act).reshape(16, 128, -1)


def feed(second, cot_turned, weight, bias):
    units, width = weight.shape[1], 512
    column = pl.BlockSpec((TOK, width), lambda j: (0, j))
    return pl.pallas_call(
        feed_kernel,
        grid=(units // width,),
        in_specs=[
            whole((TOK, D)),
            whole((16, 2, 64, TOK)),
            pl.BlockSpec((D, width), lambda j: (0, j)),
            pl.BlockSpec((1, width // 128, 128), lambda j: (j, 0, 0)),
        ],
        out_specs=[column, column, pl.BlockSpec((16, 128, width), lambda j: (0, 0, j))],
        out_shape=[
            jax.ShapeDtypeStruct((TOK, units), BF16),
            jax.ShapeDtypeStruct((TOK, units), F32),
            jax.ShapeDtypeStruct((16, 128, units), F32),
        ],
        compiler_params=pltpu.CompilerParams(vmem_limit_bytes=VMEM),
        cost_estimate=COST,
    )(second, cot_turned, weight, bias.reshape(-1, width // 128, 128))


def feed_back_kernel(cot, weight, slope, dense, up_grad, grad_mixed):
    up_grad[...] = (contract_cols(cot[...], weight[...]) * slope[...]).astype(BF16)

    @pl.when(pl.program_id(0) == 0)
    def _():
        grad_mixed[...] = contract_cols(cot[...], dense[...]).astype(BF16)


def feed_back(cot, weight, slope, dense):
    units, width = slope.shape[1], 512
    column = pl.BlockSpec((TOK, width), lambda j: (0, j))
    mixed = dense.shape[0]
    return pl.pallas_call(
        feed_back_kernel,
        grid=(units // width,),
        in_specs=[
            whole((TOK, D)),
            pl.BlockSpec((width, D), lambda j: (j, 0)),
            column,
            whole(dense.shape),
        ],
        out_specs=[column, pl.BlockSpec((TOK, mixed), lambda j: (0, 0))],
        out_shape=[
            jax.ShapeDtypeStruct((TOK, units), BF16),
            jax.ShapeDtypeStruct((TOK, mixed), BF16),
        ],
        compiler_params=pltpu.CompilerParams(vmem_limit_bytes=VMEM),
        cost_estimate=COST,
    )(cot, weight, slope, dense)


def cot_far_kernel(n, side, rows, weight, slope, dense, *refs):
    up_grad, grad_mixed, cot_turned, low = refs[n:]

    @pl.when(pl.program_id(0) == 0)
    def _():
        low[...] = rows[...].astype(BF16)
        put_turned(cot_turned, rows[...])
        grad_mixed[...] = contract_cols(low[...], dense[...]).astype(BF16)

    up_grad[...] = (contract_cols(low[...], weight[...]) * slope[...]).astype(BF16)


def cot_far_half(k, side, rows, weight, slope, dense, held):
    half, width = TOK // 2, 256
    steps = slope.shape[1] // width
    first = len(held) == 1
    shapes = [
        jax.ShapeDtypeStruct((TOK, slope.shape[1]), BF16),
        jax.ShapeDtypeStruct((TOK, HD), BF16),
        jax.ShapeDtypeStruct(TURNED, BF16),
    ]
    return pl.pallas_call(
        partial(cot_far_kernel, len(held)),
        grid_spec=pltpu.PrefetchScalarGridSpec(
            num_scalar_prefetch=1,
            grid=(steps,),
            in_specs=[
                whole((half, D)),
                pl.BlockSpec((width, D), lambda j, s: (s[0] * steps + j, 0)),
                pl.BlockSpec((half, width), lambda j, s: (k, j)),
                pl.BlockSpec((HD, D), lambda j, s: (s[0], 0)),
            ]
            + [pl.BlockSpec(memory_space=pl.ANY)] * len(held),
            out_specs=[
                pl.BlockSpec((half, width), lambda j, s: (k, j)),
                pl.BlockSpec((half, HD), lambda j, s: (k, 0)),
                pl.BlockSpec((16, 2, 64, half), lambda j, s: (0, 0, 0, 2 + k)),
            ],
            scratch_shapes=[pltpu.VMEM((half, D), BF16)],
        ),
        out_shape=shapes,
        input_output_aliases={5: 2} if first else {5: 0, 6: 1, 7: 2},
        compiler_params=pltpu.CompilerParams(vmem_limit_bytes=VMEM),
        cost_estimate=COST,
    )(side, rows, weight, slope, dense, *held)


def slope_far_kernel(side, second, weight, bias, slope):
    upward = plain_dot(second[...], weight[...]) + as_row(bias[0])
    slope[...] = gelu_slope(upward, phi(upward))


def slope_far(side, second, weight, bias):
    units, width = weight.shape[1] // 2, 512
    steps = units // width
    return pl.pallas_call(
        slope_far_kernel,
        grid_spec=pltpu.PrefetchScalarGridSpec(
            num_scalar_prefetch=1,
            grid=(steps,),
            in_specs=[
                whole((TOK, D)),
                pl.BlockSpec((D, width), lambda j, s: (0, s[0] * steps + j)),
                pl.BlockSpec((1, width // 128, 128), lambda j, s: (s[0] * steps + j, 0, 0)),
            ],
            out_specs=pl.BlockSpec((TOK, width), lambda j, s: (0, j)),
        ),
        out_shape=jax.ShapeDtypeStruct((TOK, units), F32),
        compiler_params=pltpu.CompilerParams(vmem_limit_bytes=VMEM),
        cost_estimate=COST,
    )(side, second, weight, bias.reshape(-1, width // 128, 128))


def turn(values, tables, sign):
    first = values[:, :128]
    cosine, rising, falling = tables
    first = (
        first * cosine[...]
        + (pltpu.roll(first, 32, 1) * rising[...] + pltpu.roll(first, 96, 1) * falling[...]) * sign
    )
    return jnp.concatenate([first, values[:, 128:]], axis=1)


def as_column(row):
    return jnp.broadcast_to(row, (8, row.shape[1])).T[:, 0:1]


def cosine_and_sine(angles):
    turns = jnp.floor(angles * (2.0 / math.pi) + 0.5)
    rest = ((angles - turns * 1.5703125) - turns * 4.837512969970703e-4) - turns * 7.549789954891882e-8
    square = rest * rest
    sine = ((-1.9515295891e-4 * square + 8.3321608736e-3) * square - 1.6666654611e-1) * square
    sine = sine * rest + rest
    cosine = (2.443315711809948e-5 * square - 1.388731625493765e-3) * square + 4.166664568298827e-2
    cosine = cosine * (square * square) - 0.5 * square + 1.0
    quarter = turns.astype(jnp.int32) & 3
    odd = (quarter & 1) == 1
    flipped = jnp.where(odd, sine, cosine), jnp.where(odd, cosine, sine)
    return (
        jnp.where((quarter == 1) | (quarter == 2), -flipped[0], flipped[0]),
        jnp.where(quarter >= 2, -flipped[1], flipped[1]),
    )


def project_kernel(place, first, weight, bias, marks, inverse, queries, keys, values, *tables):
    @pl.when(pl.program_id(0) == 0)
    def _():
        angles = inverse[...] * marks[1:2, :]
        cosine, sine = cosine_and_sine(angles)
        none, rest = jnp.zeros_like(sine), jnp.zeros((64, TOK), F32)
        tables[0][...] = jnp.concatenate([cosine, cosine, rest + 1.0], axis=0).T
        tables[1][...] = jnp.concatenate([none, sine, rest], axis=0).T
        tables[2][...] = jnp.concatenate([-sine, none, rest], axis=0).T

    head = pl.program_id(0) + place[0] * (2 - pl.num_programs(0))
    packed = plain_dot(first[...], weight[...]) + bias[pl.ds(head, 1), :]
    queries[...] = turn(packed[:, :HD], tables, 1.0).astype(BF16)
    keys[...] = turn(packed[:, HD : 2 * HD], tables, 1.0).astype(BF16)
    values[...] = packed[:, 2 * HD :].astype(BF16)


def project(place, heads, first, weight, bias, marks):
    inverse = jnp.asarray((10000.0 ** (-2.0 * np.arange(32) / ROT)).astype(np.float32).reshape(32, 1))
    at = (lambda h, s: h) if heads == 2 else (lambda h, s: s[0])
    column = pl.BlockSpec((TOK, HD), lambda h, s: (0, h))
    return pl.pallas_call(
        project_kernel,
        grid_spec=pltpu.PrefetchScalarGridSpec(
            num_scalar_prefetch=1,
            grid=(heads,),
            in_specs=[
                whole((TOK, D)),
                pl.BlockSpec((D, 3 * HD), lambda h, s: (0, at(h, s))),
                whole((2, 3 * HD)),
                whole((2, TOK)),
                whole((32, 1)),
            ],
            out_specs=[column] * 3 + [pl.BlockSpec((TOK, 128), lambda h, s: (0, 0))] * 3,
        ),
        out_shape=[jax.ShapeDtypeStruct((TOK, heads * HD), BF16)] * 3
        + [jax.ShapeDtypeStruct((TOK, 128), F32)] * 3,
        compiler_params=pltpu.CompilerParams(vmem_limit_bytes=VMEM),
        cost_estimate=COST,
    )(place, first, weight, bias, marks, inverse)


def attend_kernel(
    place, queries, keys, values, cosine, rising, falling, grad_mixed, marks, mixed_out, grad_out
):
    tables = (cosine, rising, falling)
    scale = 1.0 / math.sqrt(HD)
    queries, keys, values = queries[...], keys[...], values[...]
    segments = marks[0:1, :]

    def order(axis):
        return lax.rem(lax.broadcasted_iota(jnp.int32, (TOK, TOK), axis) + place[1], TOK)

    allowed = (as_column(segments) == segments) & (order(0) >= order(1))
    scores = jnp.where(allowed, contract_cols(queries, keys) * scale, NEGATIVE)
    top = jnp.max(scores, axis=-1, keepdims=True)
    weights = jnp.exp(scores - top)
    probs = weights / jnp.sum(weights, axis=-1, keepdims=True)
    probs_low = probs.astype(BF16)
    mixed_out[...] = plain_dot(probs_low, values).astype(BF16)
    grad_probs = contract_cols(grad_mixed[...], values)
    along = jnp.sum(probs * grad_probs, axis=-1, keepdims=True)
    grad_scores = (probs * (grad_probs - along)).astype(BF16)
    grad_query = plain_dot(grad_scores, keys) * scale
    grad_key = plain_dot(grad_scores.T, queries) * scale
    grad_value = plain_dot(probs_low.T, grad_mixed[...])
    grad_out[:, :HD] = turn(grad_query, tables, -1.0).astype(BF16)
    grad_out[:, HD : 2 * HD] = turn(grad_key, tables, -1.0).astype(BF16)
    grad_out[:, 2 * HD :] = grad_value.astype(BF16)


def attend(place, heads, projected, grad_mixed, marks):
    column = pl.BlockSpec((TOK, HD), lambda h, s: (0, h))
    return pl.pallas_call(
        attend_kernel,
        grid_spec=pltpu.PrefetchScalarGridSpec(
            num_scalar_prefetch=1,
            grid=(heads,),
            in_specs=[column] * 3
            + [whole((TOK, 128))] * 3
            + [column, whole((2, TOK))],
            out_specs=[column, pl.BlockSpec((TOK, 3 * HD), lambda h, s: (0, h))],
        ),
        out_shape=[
            jax.ShapeDtypeStruct((TOK, heads * HD), BF16),
            jax.ShapeDtypeStruct((TOK, heads * 3 * HD), BF16),
        ],
        compiler_params=pltpu.CompilerParams(vmem_limit_bytes=VMEM),
        cost_estimate=COST,
    )(place, *projected, grad_mixed, marks)


def put_halves(core, values, scratch, mine, other):
    scratch[...] = values
    half = TOK // 2
    mine[...] = scratch[pl.ds(pl.multiple_of(core[0] * half, half), half), :]
    other[...] = scratch[pl.ds(pl.multiple_of((1 - core[0]) * half, half), half), :]


def branch_kernel(core, mixed, act, dense, down, mine, other, scratch):
    total = plain_dot(act[...], down[...]) + plain_dot(mixed[...], dense[...])
    put_halves(core, total, scratch, mine, other)


def back_kernel(
    core, packed, up_grad, qkv, up, hidden, stats, gain, gain_two, mine, other, sums, scratch
):
    first = contract_cols(packed[...], qkv[...])
    second = contract_cols(up_grad[...], up[...])
    put_halves(core, first * gain[...] + second * gain_two[...], scratch, mine, other)
    normed = (hidden[...].astype(F32) - stats[:, 0:1]) * stats[:, 64:65]
    rows = [
        jnp.sum(v, axis=0, keepdims=True) for v in (first * normed, first, second * normed, second)
    ]
    sums[...] = jnp.concatenate(rows + [jnp.zeros((4, first.shape[1]), F32)], axis=0)


def halves_call(kernel, core, operands, specs, with_sums):
    width = 512
    half = pl.BlockSpec((TOK // 2, width), lambda j, s: (0, j))
    return pl.pallas_call(
        kernel,
        grid_spec=pltpu.PrefetchScalarGridSpec(
            num_scalar_prefetch=1,
            grid=(D // width,),
            in_specs=specs,
            out_specs=[half, half] + [pl.BlockSpec((8, width), lambda j, s: (0, j))] * with_sums,
            scratch_shapes=[pltpu.VMEM((TOK, width), F32)],
        ),
        out_shape=[jax.ShapeDtypeStruct((TOK // 2, D), F32)] * 2
        + [jax.ShapeDtypeStruct((8, D), F32)] * with_sums,
        compiler_params=pltpu.CompilerParams(vmem_limit_bytes=VMEM),
        cost_estimate=COST,
    )(core, *operands)


def branch_halves(core, mixed, act, dense, down):
    specs = [whole(mixed.shape), whole(act.shape)]
    specs += [pl.BlockSpec((w.shape[0], 512), lambda j, s: (0, j)) for w in (dense, down)]
    return halves_call(branch_kernel, core, (mixed, act, dense, down), specs, False)


def back_halves(core, packed, up_grad, qkv, up, hidden, stats, gain, gain_two):
    specs = [whole(packed.shape), whole(up_grad.shape)]
    specs += [pl.BlockSpec((512, w.shape[1]), lambda j, s: (j, 0)) for w in (qkv, up)]
    specs += [pl.BlockSpec((TOK, 512), lambda j, s: (0, j)), whole((TOK, 128))]
    specs += [pl.BlockSpec((1, 512), lambda j, s: (0, j))] * 2
    operands = (packed, up_grad, qkv, up, hidden, stats, gain.reshape(1, D), gain_two.reshape(1, D))
    return halves_call(back_kernel, core, operands, specs, True)


def joint_kernel(side, *refs):
    lefts, rights, target, held, arrived = refs[:3], refs[3:9], refs[9], refs[10:13], refs[13]
    step = pl.program_id(0)
    copies = [pltpu.make_async_copy(lefts[k], held[k], arrived.at[k]) for k in range(3)]

    @pl.when(step == 0)
    def _():
        for copy in copies:
            copy.start()

    for k, (start, stop) in enumerate(((0, 4), (4, 5), (5, 8))):

        @pl.when(step == start)
        def _(k=k):
            copies[k].wait()

        @pl.when((step >= start) & (step < stop))
        def _(k=k):
            right = jnp.concatenate([rights[2 * k][...], rights[2 * k + 1][...]], axis=0)
            total = plain_dot(held[k][...].reshape(D, 2 * TOK), right)
            target[...] = total.reshape(16, 128, -1)


def joint(side, lefts, rights):
    width = 256
    specs = [pl.BlockSpec(memory_space=pl.ANY)] * 3
    for start, n in ((0, 4), (4, 1), (5, 3)):

        def near(j, s, start=start, n=n):
            return (0, s[0] * n + jnp.clip(j - start, 0, n - 1))

        def far(j, s, start=start, n=n):
            return (0, jnp.clip(j - start, 0, n - 1))

        specs += [pl.BlockSpec((TOK, width), near), pl.BlockSpec((TOK, width), far)]
    return pl.pallas_call(
        joint_kernel,
        grid_spec=pltpu.PrefetchScalarGridSpec(
            num_scalar_prefetch=1,
            grid=(8,),
            in_specs=specs,
            out_specs=pl.BlockSpec((16, 128, width), lambda j, s: (0, 0, j)),
            scratch_shapes=[pltpu.VMEM(TURNED, BF16)] * 3 + [pltpu.SemaphoreType.DMA((3,))],
        ),
        out_shape=jax.ShapeDtypeStruct((16, 128, 8 * width), F32),
        compiler_params=pltpu.CompilerParams(vmem_limit_bytes=VMEM),
        cost_estimate=COST,
    )(side, *lefts, *rights)


def body(
    hidden_in,
    segment_ids,
    positions,
    ln1_gain,
    ln1_bias,
    qkv_weight,
    qkv_bias,
    dense_weight,
    dense_bias,
    ln2_gain,
    ln2_bias,
    fc1_weight,
    fc1_bias,
    fc2_weight,
    fc2_bias,
    cotangent,
):
    core = lax.axis_index("c")
    side = lax.axis_index("zl")
    half_rows = TOK // 2
    at_side = side.astype(jnp.int32).reshape(1)
    at_core = core.astype(jnp.int32).reshape(1)
    own_place = jnp.zeros((2,), jnp.int32)
    far_place = jnp.stack([side, core * half_rows]).astype(jnp.int32)
    after = lax.optimization_barrier
    params = (ln1_gain, ln1_bias, ln2_gain, ln2_bias)

    def of_core(values, which):
        return lax.dynamic_slice_in_dim(values, which * half_rows, half_rows, 0)

    def both_cores(mine):
        theirs = send(mine, "c")
        filled = jnp.zeros((TOK,) + mine.shape[1:], mine.dtype)
        filled = lax.dynamic_update_slice_in_dim(filled, mine, core * half_rows, 0)
        return lax.dynamic_update_slice_in_dim(filled, theirs, (1 - core) * half_rows, 0)

    marks = jnp.concatenate([segment_ids, positions]).astype(F32).reshape(1, 2 * TOK)
    hidden_sent = jnp.concatenate(
        [of_core(hidden_in, core).astype(F32), jnp.pad(marks, ((0, 7), (0, D - 2 * TOK)))], axis=0
    )
    hidden_pair = lax.all_gather(hidden_sent, "zl")

    second_in, cot_turned, stats = norm_call(
        second_kernel, 256, (hidden_in, cotangent), 1, 1, (ln2_gain, ln2_bias), stats=True
    )
    act_low, slope, down_grad = feed(second_in, cot_turned, fc1_weight, fc1_bias)
    down_sum = after(lax.psum_scatter(down_grad, ("x", "y"), scatter_dimension=0, tiled=True))
    _, cotangent, hidden_in = after((down_grad, cotangent, hidden_in))

    own_marks = marks.reshape(2, TOK)
    first_in, first_turned, second_turned = norm_call(first_kernel, 256, (hidden_in,), 1, 2, params)
    projected = project(own_place, 2, first_in, qkv_weight, qkv_bias, own_marks)
    grad_up, grad_mixed = feed_back(cotangent, fc2_weight, slope, dense_weight)
    mixed_low, grad_packed = attend(own_place, 2, projected, grad_mixed, own_marks)
    act_low, cot_sent = after((act_low, of_core(cotangent, core).astype(F32)))
    branch, branch_other = branch_halves(at_core, mixed_low, act_low, dense_weight, fc2_weight)

    hidden_pair, branch_other, cot_sent, grad_up = after(
        (hidden_pair, branch_other, cot_sent, grad_up)
    )
    cot_got = send(cot_sent, "zl")
    hidden_too = send(hidden_pair, "c")
    branch = branch + send(branch_other, "c")
    hidden_too, branch = after((hidden_too, branch))

    def beside(hidden_pair, hidden_too, first_turned, second_turned, grad_packed, grad_up):
        first_in, second_in, first_turned, second_turned = first_far(
            at_side, hidden_pair, hidden_too, params, (first_turned, second_turned)
        )
        slope_side = slope_far(at_side, second_in, fc1_weight, fc1_bias)
        marks_got = lax.dynamic_slice(hidden_pair, (1 - side, half_rows, 0), (1, 1, 2 * TOK))
        marks_got = marks_got.reshape(2, 2, half_rows)
        marks_far = jnp.where(core == 0, marks_got, marks_got[:, ::-1]).reshape(2, TOK)
        projected_far = project(far_place, 1, first_in, qkv_weight, qkv_bias, marks_far)
        backs = back_halves(
            at_core,
            grad_packed,
            grad_up,
            qkv_weight,
            fc1_weight,
            hidden_in,
            stats,
            ln1_gain,
            ln2_gain,
        )
        return first_turned, second_turned, slope_side, marks_far, *backs, *projected_far

    (
        first_turned,
        second_turned,
        slope_side,
        marks_far,
        combined,
        combined_other,
        norms,
        *projected_far,
    ) = lax.cond(
        core == 0,
        beside,
        beside,
        hidden_pair,
        hidden_too,
        first_turned,
        second_turned,
        grad_packed,
        grad_up,
    )

    slope_side, cot_got, combined_other = after((slope_side, cot_got, combined_other))
    cot_too = send(cot_got, "c")
    combined_too = send(combined_other, "c")
    held = cot_far_half(0, at_side, cot_got, fc2_weight, slope_side, dense_weight, (cot_turned,))
    *held, cot_too, combined_too = after((*held, cot_too, combined_too))
    combined = combined + combined_too
    branch = lax.psum(branch, "zh")
    combined = lax.psum(combined, "zh")
    grad_up_far, grad_mixed_far, cot_turned = cot_far_half(
        1, at_side, cot_too, fc2_weight, slope_side, dense_weight, held
    )
    mixed_far, grad_packed_far = attend(far_place, 1, projected_far, grad_mixed_far, marks_far)
    joint_grad = joint(
        at_side,
        (second_turned, cot_turned, first_turned),
        (grad_up, grad_up_far, mixed_low, mixed_far, grad_packed, grad_packed_far),
    )
    joint_grad, down_sum = after((joint_grad, down_sum))
    joint_sum = after(lax.psum_scatter(joint_grad, ("x", "y"), scatter_dimension=0, tiled=True))
    _, norms, grad_packed, grad_up, cotangent, down_sum = after(
        (joint_grad, norms, grad_packed, grad_up, cotangent, down_sum)
    )

    norms = norms[:4].reshape(4, 32, 64).transpose(1, 0, 2).reshape(32, 256)
    grad_out = cotangent.astype(F32)
    bias_sum = jnp.sum(grad_out, axis=0)
    qkv_bias_sum = jnp.sum(grad_packed.astype(F32), axis=0)
    up_bias_grad = jnp.sum(grad_up.astype(F32), axis=0)
    small = jnp.concatenate(
        [
            norms,
            bias_sum.reshape(32, 64),
            qkv_bias_sum.reshape(2, 32, 24).transpose(1, 0, 2).reshape(32, 48),
            up_bias_grad.reshape(16, 32, 4).transpose(1, 0, 2).reshape(32, 64),
            jnp.zeros((32, 80), F32),
        ],
        axis=1,
    )
    def of_side(values, which):
        return lax.dynamic_slice_in_dim(values[0], which * 64, 64, 0)

    down_far = send(of_side(down_sum, 1 - side), "zl")
    for axis in ("x", "y"):
        small = small + swap(small, axis, 1)
        small = small + swap(small, axis, 2)
        small, down_far = after((small, down_far))
    block = lax.axis_index("x") * 4 + lax.axis_index("y")
    own_small = lax.dynamic_slice_in_dim(small, side * 16 + block, 1, 0)
    far_small = lax.dynamic_slice_in_dim(small, (1 - side) * 16 + block, 1, 0)
    small = (own_small + send(far_small, "zl")).reshape(-1)

    small, branch, combined = after((small, branch, combined))
    norms, joint_sum = after((small[:256], joint_sum))
    norms = norms + send(norms, "c")
    norms = (norms + send(norms, "zh")).reshape(4, 64)
    bias_total = small[256:320]
    hidden = hidden_in.astype(F32)
    output = both_cores(of_core(hidden, core) + branch + dense_bias + fc2_bias)
    own_stats = of_core(stats, core)
    average, inv_std = own_stats[:, 0:1], own_stats[:, 64:65]
    normed_half = (of_core(hidden, core) - average) * inv_std
    input_half = of_core(grad_out, core) + inv_std * (
        combined
        - jnp.mean(combined, axis=-1, keepdims=True)
        - normed_half * jnp.mean(combined * normed_half, axis=-1, keepdims=True)
    )
    input_grad = both_cores(input_half)

    down_sum = of_side(down_sum, side) + down_far
    near = of_side(joint_sum, side)
    far = send(of_side(joint_sum, 1 - side), "zl")
    low = jnp.where(side == 0, near, far)
    high = jnp.where(side == 0, far, near)
    sums = []
    start = 0
    for width in (1024, 256, 768):
        stop = start + width
        sums.append(jnp.concatenate([low[:, start:stop], high[:, start:stop]], axis=1))
        start = stop
    up_sum, dense_sum, qkv_sum = sums
    return (
        output,
        input_grad,
        norms[0],
        norms[1],
        qkv_sum,
        small[320:368].reshape(2, 24),
        dense_sum.T,
        bias_total,
        norms[2],
        norms[3],
        up_sum,
        small[368:432].reshape(16, 4),
        down_sum.T,
        bias_total,
    )


def solution(mesh):
    fine = Mesh(mesh.devices.reshape(tuple(SIZES.values())), tuple(SIZES))
    return jax.shard_map(
        body,
        mesh=fine,
        in_specs=(
            P(DP, None),
            P(DP),
            P(DP),
            P(),
            P(),
            P(None, TENSOR),
            P(TENSOR, None),
            P(TENSOR, None),
            P(),
            P(),
            P(),
            P(None, TENSOR),
            P(TENSOR, None),
            P(TENSOR, None),
            P(),
            P(DP, None),
        ),
        out_specs=(
            P(DP, None),
            P(DP, None),
            P(DP),
            P(DP),
            P(DP, TENSOR),
            P(TENSOR, DP),
            P(TENSOR, DP),
            P(DP),
            P(DP),
            P(DP),
            P(DP, TENSOR),
            P(TENSOR, DP),
            P(TENSOR, DP),
            P(DP),
        ),
        check_vma=False,
    )
```

```python
from functools import partial
import math

import jax
import jax.numpy as jnp
import numpy as np
from jax import lax
from jax.experimental import pallas as pl
from jax.experimental.pallas import tpu as pltpu
from jax.sharding import Mesh, PartitionSpec as P

HD = 256
ROT = 64
TOK = 512
D = 2048
EPSILON = 1e-05
NEGATIVE = -1000000000.0
SIZES = {"zl": 2, "x": 4, "y": 4, "zh": 2, "c": 2}
DP = ("zl", "x", "y")
TENSOR = ("zh", "c")
F32 = jnp.float32
BF16 = jnp.bfloat16


def send(value, axis, step=1):
    n = SIZES[axis]
    return lax.ppermute(value, axis, [(i, (i + step) % n) for i in range(n)])


def swap(value, axis, bit):
    return lax.ppermute(value, axis, [(i, i ^ bit) for i in range(SIZES[axis])])


def plain_dot(left, right):
    return jnp.dot(left, right, preferred_element_type=F32)


def contract_cols(left, right):
    return lax.dot_general(left, right, (((1,), (1,)), ((), ())), preferred_element_type=F32)


VMEM = 56 * 1024 * 1024
COST = pl.CostEstimate(flops=1000000, bytes_accessed=1000000, transcendentals=0)


def whole(shape):
    return pl.BlockSpec(shape, lambda *_: (0,) * len(shape), pipeline_mode=pl.Buffered(1))


def put_turned(target, rows):
    for z in range(2):
        for pair in range(8):
            start = z * 1024 + pair * 128
            block = rows[:, start : start + 128].T.astype(BF16)
            target[2 * pair, z] = block[:64]
            target[2 * pair + 1, z] = block[64:]


def normalise(hidden):
    average = jnp.mean(hidden, axis=-1, keepdims=True)
    centred = hidden - average
    inv_std = lax.rsqrt(jnp.mean(centred * centred, axis=-1, keepdims=True) + EPSILON)
    return centred * inv_std, inv_std


def second_kernel(hidden, cot, gain, shift, second_out, cot_turned, stats):
    rows = hidden[...].astype(F32)
    average = jnp.mean(rows, axis=-1, keepdims=True)
    centred = rows - average
    inv_std = lax.rsqrt(jnp.mean(centred * centred, axis=-1, keepdims=True) + EPSILON)
    second_out[...] = (centred * inv_std * gain[...] + shift[...]).astype(BF16)
    put_turned(cot_turned, cot[...].astype(F32))
    lane = lax.broadcasted_iota(jnp.int32, (rows.shape[0], 128), 1)
    stats[...] = jnp.where(lane < 64, average, inv_std)


def first_kernel(hidden, gain, shift, gain_two, shift_two, first_out, first_turned, second_turned):
    normed, _ = normalise(hidden[...].astype(F32))
    first = normed * gain[...] + shift[...]
    first_out[...] = first.astype(BF16)
    put_turned(first_turned, first)
    put_turned(second_turned, normed * gain_two[...] + shift_two[...])


def first_far_kernel(near, other, gain, shift, gain_two, shift_two, *refs):
    first_out, second_out, first_turned, second_turned = refs[2:]

    def step(rows):
        normed, _ = normalise(rows)
        first = normed * gain[...] + shift[...]
        second = normed * gain_two[...] + shift_two[...]
        first_out[...] = first.astype(BF16)
        second_out[...] = second.astype(BF16)
        put_turned(first_turned, first)
        put_turned(second_turned, second)

    @pl.when(pl.program_id(0) < 2)
    def _():
        step(near[0])

    @pl.when(pl.program_id(0) >= 2)
    def _():
        step(other[0])


TURNED = (16, 2, 64, 2 * TOK)


def norm_call(kernel, rows, n_rows, n_plain, n_turned, params, stats=False):
    plain = pl.BlockSpec((rows, D), lambda i: (i, 0))
    return pl.pallas_call(
        kernel,
        grid=(TOK // rows,),
        in_specs=[plain] * len(n_rows) + [whole((1, D))] * len(params),
        out_specs=[plain] * n_plain
        + [pl.BlockSpec((16, 2, 64, rows), lambda i: (0, 0, 0, i))] * n_turned
        + [pl.BlockSpec((rows, 128), lambda i: (i, 0))] * stats,
        out_shape=[jax.ShapeDtypeStruct((TOK, D), BF16)] * n_plain
        + [jax.ShapeDtypeStruct(TURNED, BF16)] * n_turned
        + [jax.ShapeDtypeStruct((TOK, 128), F32)] * stats,
        compiler_params=pltpu.CompilerParams(vmem_limit_bytes=VMEM),
        cost_estimate=COST,
    )(*n_rows, *(p.reshape(1, D) for p in params))


def first_far(near, other, params, held):
    rows = 128
    plain = pl.BlockSpec((rows, D), lambda i: (i, 0))
    return pl.pallas_call(
        first_far_kernel,
        grid=(TOK // rows,),
        in_specs=[
            pl.BlockSpec((1, rows, D), lambda i: (0, lax.min(i, 1), 0)),
            pl.BlockSpec((1, rows, D), lambda i: (0, lax.max(i - 2, 0), 0)),
        ]
        + [whole((1, D))] * 4
        + [pl.BlockSpec(memory_space=pl.ANY)] * 2,
        out_specs=[plain] * 2
        + [pl.BlockSpec((16, 2, 64, rows), lambda i: (0, 0, 0, i + TOK // rows))] * 2,
        out_shape=[jax.ShapeDtypeStruct((TOK, D), BF16)] * 2
        + [jax.ShapeDtypeStruct(TURNED, BF16)] * 2,
        input_output_aliases={6: 2, 7: 3},
        compiler_params=pltpu.CompilerParams(vmem_limit_bytes=VMEM),
        cost_estimate=COST,
    )(near, other, *(p.reshape(1, D) for p in params), *held)


def phi(upward):
    return 0.5 * (1.0 + lax.erf(upward * math.sqrt(0.5)))


def gelu_slope(upward, below):
    return below + upward * (jnp.exp(-0.5 * upward * upward) * (1.0 / math.sqrt(2.0 * math.pi)))


def as_row(block):
    return jnp.concatenate([block[i : i + 1, :] for i in range(block.shape[0])], axis=1)


def feed_kernel(second, cot_turned, weight, bias, act_out, slope_out, down_grad):
    upward = plain_dot(second[...], weight[...]) + as_row(bias[0])
    below = phi(upward)
    act = (upward * below).astype(BF16)
    act_out[...] = act
    slope_out[...] = gelu_slope(upward, below)
    down_grad[...] = plain_dot(cot_turned[...].reshape(D, TOK), act).reshape(16, 128, -1)


def feed(second, cot_turned, weight, bias):
    units, width = weight.shape[1], 512
    column = pl.BlockSpec((TOK, width), lambda j: (0, j))
    return pl.pallas_call(
        feed_kernel,
        grid=(units // width,),
        in_specs=[
            whole((TOK, D)),
            whole((16, 2, 64, TOK)),
            pl.BlockSpec((D, width), lambda j: (0, j)),
            pl.BlockSpec((1, width // 128, 128), lambda j: (j, 0, 0)),
        ],
        out_specs=[column, column, pl.BlockSpec((16, 128, width), lambda j: (0, 0, j))],
        out_shape=[
            jax.ShapeDtypeStruct((TOK, units), BF16),
            jax.ShapeDtypeStruct((TOK, units), F32),
            jax.ShapeDtypeStruct((16, 128, units), F32),
        ],
        compiler_params=pltpu.CompilerParams(vmem_limit_bytes=VMEM),
        cost_estimate=COST,
    )(second, cot_turned, weight, bias.reshape(-1, width // 128, 128))


def feed_back_kernel(cot, weight, slope, dense, up_grad, grad_mixed):
    up_grad[...] = (contract_cols(cot[...], weight[...]) * slope[...]).astype(BF16)

    @pl.when(pl.program_id(0) == 0)
    def _():
        grad_mixed[...] = contract_cols(cot[...], dense[...]).astype(BF16)


def feed_back(cot, weight, slope, dense):
    units, width = slope.shape[1], 512
    column = pl.BlockSpec((TOK, width), lambda j: (0, j))
    mixed = dense.shape[0]
    return pl.pallas_call(
        feed_back_kernel,
        grid=(units // width,),
        in_specs=[
            whole((TOK, D)),
            pl.BlockSpec((width, D), lambda j: (j, 0)),
            column,
            whole(dense.shape),
        ],
        out_specs=[column, pl.BlockSpec((TOK, mixed), lambda j: (0, 0))],
        out_shape=[
            jax.ShapeDtypeStruct((TOK, units), BF16),
            jax.ShapeDtypeStruct((TOK, mixed), BF16),
        ],
        compiler_params=pltpu.CompilerParams(vmem_limit_bytes=VMEM),
        cost_estimate=COST,
    )(cot, weight, slope, dense)


def cot_far_kernel(n, side, rows, weight, slope, dense, *refs):
    up_grad, grad_mixed, cot_turned, low = refs[n:]

    @pl.when(pl.program_id(0) == 0)
    def _():
        low[...] = rows[...].astype(BF16)
        put_turned(cot_turned, rows[...])
        grad_mixed[...] = contract_cols(low[...], dense[...]).astype(BF16)

    up_grad[...] = (contract_cols(low[...], weight[...]) * slope[...]).astype(BF16)


def cot_far_half(k, side, rows, weight, slope, dense, held):
    half, width = TOK // 2, 256
    steps = slope.shape[1] // width
    first = len(held) == 1
    shapes = [
        jax.ShapeDtypeStruct((TOK, slope.shape[1]), BF16),
        jax.ShapeDtypeStruct((TOK, HD), BF16),
        jax.ShapeDtypeStruct(TURNED, BF16),
    ]
    return pl.pallas_call(
        partial(cot_far_kernel, len(held)),
        grid_spec=pltpu.PrefetchScalarGridSpec(
            num_scalar_prefetch=1,
            grid=(steps,),
            in_specs=[
                whole((half, D)),
                pl.BlockSpec((width, D), lambda j, s: (s[0] * steps + j, 0)),
                pl.BlockSpec((half, width), lambda j, s: (k, j)),
                pl.BlockSpec((HD, D), lambda j, s: (s[0], 0)),
            ]
            + [pl.BlockSpec(memory_space=pl.ANY)] * len(held),
            out_specs=[
                pl.BlockSpec((half, width), lambda j, s: (k, j)),
                pl.BlockSpec((half, HD), lambda j, s: (k, 0)),
                pl.BlockSpec((16, 2, 64, half), lambda j, s: (0, 0, 0, 2 + k)),
            ],
            scratch_shapes=[pltpu.VMEM((half, D), BF16)],
        ),
        out_shape=shapes,
        input_output_aliases={5: 2} if first else {5: 0, 6: 1, 7: 2},
        compiler_params=pltpu.CompilerParams(vmem_limit_bytes=VMEM),
        cost_estimate=COST,
    )(side, rows, weight, slope, dense, *held)


def slope_far_kernel(side, second, weight, bias, slope):
    upward = plain_dot(second[...], weight[...]) + as_row(bias[0])
    slope[...] = gelu_slope(upward, phi(upward))


def slope_far(side, second, weight, bias):
    units, width = weight.shape[1] // 2, 512
    steps = units // width
    return pl.pallas_call(
        slope_far_kernel,
        grid_spec=pltpu.PrefetchScalarGridSpec(
            num_scalar_prefetch=1,
            grid=(steps,),
            in_specs=[
                whole((TOK, D)),
                pl.BlockSpec((D, width), lambda j, s: (0, s[0] * steps + j)),
                pl.BlockSpec((1, width // 128, 128), lambda j, s: (s[0] * steps + j, 0, 0)),
            ],
            out_specs=pl.BlockSpec((TOK, width), lambda j, s: (0, j)),
        ),
        out_shape=jax.ShapeDtypeStruct((TOK, units), F32),
        compiler_params=pltpu.CompilerParams(vmem_limit_bytes=VMEM),
        cost_estimate=COST,
    )(side, second, weight, bias.reshape(-1, width // 128, 128))


def turn(values, tables, sign):
    first = values[:, :128]
    cosine, rising, falling = tables
    first = (
        first * cosine[...]
        + (pltpu.roll(first, 32, 1) * rising[...] + pltpu.roll(first, 96, 1) * falling[...]) * sign
    )
    return jnp.concatenate([first, values[:, 128:]], axis=1)


def as_column(row):
    return jnp.broadcast_to(row, (8, row.shape[1])).T[:, 0:1]


def cosine_and_sine(angles):
    turns = jnp.floor(angles * (2.0 / math.pi) + 0.5)
    rest = ((angles - turns * 1.5703125) - turns * 4.837512969970703e-4) - turns * 7.549789954891882e-8
    square = rest * rest
    sine = ((-1.9515295891e-4 * square + 8.3321608736e-3) * square - 1.6666654611e-1) * square
    sine = sine * rest + rest
    cosine = (2.443315711809948e-5 * square - 1.388731625493765e-3) * square + 4.166664568298827e-2
    cosine = cosine * (square * square) - 0.5 * square + 1.0
    quarter = turns.astype(jnp.int32) & 3
    odd = (quarter & 1) == 1
    flipped = jnp.where(odd, sine, cosine), jnp.where(odd, cosine, sine)
    return (
        jnp.where((quarter == 1) | (quarter == 2), -flipped[0], flipped[0]),
        jnp.where(quarter >= 2, -flipped[1], flipped[1]),
    )


def project_kernel(place, first, weight, bias, marks, inverse, queries, keys, values, *tables):
    @pl.when(pl.program_id(0) == 0)
    def _():
        angles = inverse[...] * marks[1:2, :]
        cosine, sine = cosine_and_sine(angles)
        none, rest = jnp.zeros_like(sine), jnp.zeros((64, TOK), F32)
        tables[0][...] = jnp.concatenate([cosine, cosine, rest + 1.0], axis=0).T
        tables[1][...] = jnp.concatenate([none, sine, rest], axis=0).T
        tables[2][...] = jnp.concatenate([-sine, none, rest], axis=0).T

    head = pl.program_id(0) + place[0] * (2 - pl.num_programs(0))
    packed = plain_dot(first[...], weight[...]) + bias[pl.ds(head, 1), :]
    queries[...] = turn(packed[:, :HD], tables, 1.0).astype(BF16)
    keys[...] = turn(packed[:, HD : 2 * HD], tables, 1.0).astype(BF16)
    values[...] = packed[:, 2 * HD :].astype(BF16)


def project(place, heads, first, weight, bias, marks):
    inverse = jnp.asarray((10000.0 ** (-2.0 * np.arange(32) / ROT)).astype(np.float32).reshape(32, 1))
    at = (lambda h, s: h) if heads == 2 else (lambda h, s: s[0])
    column = pl.BlockSpec((TOK, HD), lambda h, s: (0, h))
    return pl.pallas_call(
        project_kernel,
        grid_spec=pltpu.PrefetchScalarGridSpec(
            num_scalar_prefetch=1,
            grid=(heads,),
            in_specs=[
                whole((TOK, D)),
                pl.BlockSpec((D, 3 * HD), lambda h, s: (0, at(h, s))),
                whole((2, 3 * HD)),
                whole((2, TOK)),
                whole((32, 1)),
            ],
            out_specs=[column] * 3 + [pl.BlockSpec((TOK, 128), lambda h, s: (0, 0))] * 3,
        ),
        out_shape=[jax.ShapeDtypeStruct((TOK, heads * HD), BF16)] * 3
        + [jax.ShapeDtypeStruct((TOK, 128), F32)] * 3,
        compiler_params=pltpu.CompilerParams(vmem_limit_bytes=VMEM),
        cost_estimate=COST,
    )(place, first, weight, bias, marks, inverse)


def attend_kernel(
    place, queries, keys, values, cosine, rising, falling, grad_mixed, marks, mixed_out, grad_out
):
    tables = (cosine, rising, falling)
    scale = 1.0 / math.sqrt(HD)
    queries, keys, values = queries[...], keys[...], values[...]
    segments = marks[0:1, :]

    def order(axis):
        return lax.rem(lax.broadcasted_iota(jnp.int32, (TOK, TOK), axis) + place[1], TOK)

    allowed = (as_column(segments) == segments) & (order(0) >= order(1))
    scores = jnp.where(allowed, contract_cols(queries, keys) * scale, NEGATIVE)
    top = jnp.max(scores, axis=-1, keepdims=True)
    weights = jnp.exp(scores - top)
    probs = weights / jnp.sum(weights, axis=-1, keepdims=True)
    probs_low = probs.astype(BF16)
    mixed_out[...] = plain_dot(probs_low, values).astype(BF16)
    grad_probs = contract_cols(grad_mixed[...], values)
    along = jnp.sum(probs * grad_probs, axis=-1, keepdims=True)
    grad_scores = (probs * (grad_probs - along)).astype(BF16)
    grad_query = plain_dot(grad_scores, keys) * scale
    grad_key = plain_dot(grad_scores.T, queries) * scale
    grad_value = plain_dot(probs_low.T, grad_mixed[...])
    grad_out[:, :HD] = turn(grad_query, tables, -1.0).astype(BF16)
    grad_out[:, HD : 2 * HD] = turn(grad_key, tables, -1.0).astype(BF16)
    grad_out[:, 2 * HD :] = grad_value.astype(BF16)


def attend(place, heads, projected, grad_mixed, marks):
    column = pl.BlockSpec((TOK, HD), lambda h, s: (0, h))
    return pl.pallas_call(
        attend_kernel,
        grid_spec=pltpu.PrefetchScalarGridSpec(
            num_scalar_prefetch=1,
            grid=(heads,),
            in_specs=[column] * 3
            + [whole((TOK, 128))] * 3
            + [column, whole((2, TOK))],
            out_specs=[column, pl.BlockSpec((TOK, 3 * HD), lambda h, s: (0, h))],
        ),
        out_shape=[
            jax.ShapeDtypeStruct((TOK, heads * HD), BF16),
            jax.ShapeDtypeStruct((TOK, heads * 3 * HD), BF16),
        ],
        compiler_params=pltpu.CompilerParams(vmem_limit_bytes=VMEM),
        cost_estimate=COST,
    )(place, *projected, grad_mixed, marks)


def put_halves(core, values, scratch, mine, other):
    scratch[...] = values
    half = TOK // 2
    mine[...] = scratch[pl.ds(pl.multiple_of(core[0] * half, half), half), :]
    other[...] = scratch[pl.ds(pl.multiple_of((1 - core[0]) * half, half), half), :]


def branch_kernel(core, mixed, act, dense, down, mine, other, scratch):
    total = plain_dot(act[...], down[...]) + plain_dot(mixed[...], dense[...])
    put_halves(core, total, scratch, mine, other)


def back_kernel(
    core, packed, up_grad, qkv, up, hidden, stats, gain, gain_two, mine, other, sums, scratch
):
    first = contract_cols(packed[...], qkv[...])
    second = contract_cols(up_grad[...], up[...])
    put_halves(core, first * gain[...] + second * gain_two[...], scratch, mine, other)
    normed = (hidden[...].astype(F32) - stats[:, 0:1]) * stats[:, 64:65]
    rows = [
        jnp.sum(v, axis=0, keepdims=True) for v in (first * normed, first, second * normed, second)
    ]
    sums[...] = jnp.concatenate(rows + [jnp.zeros((4, first.shape[1]), F32)], axis=0)


def halves_call(kernel, core, operands, specs, with_sums):
    width = 512
    half = pl.BlockSpec((TOK // 2, width), lambda j, s: (0, j))
    return pl.pallas_call(
        kernel,
        grid_spec=pltpu.PrefetchScalarGridSpec(
            num_scalar_prefetch=1,
            grid=(D // width,),
            in_specs=specs,
            out_specs=[half, half] + [pl.BlockSpec((8, width), lambda j, s: (0, j))] * with_sums,
            scratch_shapes=[pltpu.VMEM((TOK, width), F32)],
        ),
        out_shape=[jax.ShapeDtypeStruct((TOK // 2, D), F32)] * 2
        + [jax.ShapeDtypeStruct((8, D), F32)] * with_sums,
        compiler_params=pltpu.CompilerParams(vmem_limit_bytes=VMEM),
        cost_estimate=COST,
    )(core, *operands)


def branch_halves(core, mixed, act, dense, down):
    specs = [whole(mixed.shape), whole(act.shape)]
    specs += [pl.BlockSpec((w.shape[0], 512), lambda j, s: (0, j)) for w in (dense, down)]
    return halves_call(branch_kernel, core, (mixed, act, dense, down), specs, False)


def back_halves(core, packed, up_grad, qkv, up, hidden, stats, gain, gain_two):
    specs = [whole(packed.shape), whole(up_grad.shape)]
    specs += [pl.BlockSpec((512, w.shape[1]), lambda j, s: (j, 0)) for w in (qkv, up)]
    specs += [pl.BlockSpec((TOK, 512), lambda j, s: (0, j)), whole((TOK, 128))]
    specs += [pl.BlockSpec((1, 512), lambda j, s: (0, j))] * 2
    operands = (packed, up_grad, qkv, up, hidden, stats, gain.reshape(1, D), gain_two.reshape(1, D))
    return halves_call(back_kernel, core, operands, specs, True)


def final_kernel(n, half, branch, combined, hidden, cot, stats, bias, bias_too, *refs):
    output, input_grad = refs[n:]
    rows = hidden[...].astype(F32)
    output[...] = rows + branch[...] + bias[...] + bias_too[...]
    e = combined[...]
    inv_std = stats[:, 64:65]
    normed = (rows - stats[:, 0:1]) * inv_std
    input_grad[...] = cot[...].astype(F32) + inv_std * (
        e
        - jnp.mean(e, axis=-1, keepdims=True)
        - normed * jnp.mean(e * normed, axis=-1, keepdims=True)
    )


def final_half(half, branch, combined, hidden, cot, stats, biases, held):
    rows = 128
    steps = TOK // 2 // rows
    given = pl.BlockSpec((rows, D), lambda i, s: (i, 0))
    placed = pl.BlockSpec((rows, D), lambda i, s: (s[0] * steps + i, 0))
    return pl.pallas_call(
        partial(final_kernel, len(held)),
        grid_spec=pltpu.PrefetchScalarGridSpec(
            num_scalar_prefetch=1,
            grid=(steps,),
            in_specs=[given, given, placed, placed]
            + [pl.BlockSpec((rows, 128), lambda i, s: (s[0] * steps + i, 0))]
            + [whole((1, D))] * 2
            + [pl.BlockSpec(memory_space=pl.ANY)] * len(held),
            out_specs=[placed, placed],
        ),
        out_shape=[jax.ShapeDtypeStruct((TOK, D), F32)] * 2,
        input_output_aliases={8: 0, 9: 1} if held else {},
        compiler_params=pltpu.CompilerParams(vmem_limit_bytes=VMEM),
        cost_estimate=COST,
    )(half, branch, combined, hidden, cot, stats, *(b.reshape(1, D) for b in biases), *held)


def joint_kernel(side, *refs):
    lefts, rights, target, held, arrived = refs[:3], refs[3:9], refs[9], refs[10:13], refs[13]
    step = pl.program_id(0)
    copies = [pltpu.make_async_copy(lefts[k], held[k], arrived.at[k]) for k in range(3)]

    @pl.when(step == 0)
    def _():
        for copy in copies:
            copy.start()

    for k, (start, stop) in enumerate(((0, 4), (4, 5), (5, 8))):

        @pl.when(step == start)
        def _(k=k):
            copies[k].wait()

        @pl.when((step >= start) & (step < stop))
        def _(k=k):
            right = jnp.concatenate([rights[2 * k][...], rights[2 * k + 1][...]], axis=0)
            total = plain_dot(held[k][...].reshape(D, 2 * TOK), right)
            target[...] = total.reshape(16, 128, -1)


def joint(side, lefts, rights):
    width = 256
    specs = [pl.BlockSpec(memory_space=pl.ANY)] * 3
    for start, n in ((0, 4), (4, 1), (5, 3)):

        def near(j, s, start=start, n=n):
            return (0, s[0] * n + jnp.clip(j - start, 0, n - 1))

        def far(j, s, start=start, n=n):
            return (0, jnp.clip(j - start, 0, n - 1))

        specs += [pl.BlockSpec((TOK, width), near), pl.BlockSpec((TOK, width), far)]
    return pl.pallas_call(
        joint_kernel,
        grid_spec=pltpu.PrefetchScalarGridSpec(
            num_scalar_prefetch=1,
            grid=(8,),
            in_specs=specs,
            out_specs=pl.BlockSpec((16, 128, width), lambda j, s: (0, 0, j)),
            scratch_shapes=[pltpu.VMEM(TURNED, BF16)] * 3 + [pltpu.SemaphoreType.DMA((3,))],
        ),
        out_shape=jax.ShapeDtypeStruct((16, 128, 8 * width), F32),
        compiler_params=pltpu.CompilerParams(vmem_limit_bytes=VMEM),
        cost_estimate=COST,
    )(side, *lefts, *rights)


def body(
    hidden_in,
    segment_ids,
    positions,
    ln1_gain,
    ln1_bias,
    qkv_weight,
    qkv_bias,
    dense_weight,
    dense_bias,
    ln2_gain,
    ln2_bias,
    fc1_weight,
    fc1_bias,
    fc2_weight,
    fc2_bias,
    cotangent,
):
    core = lax.axis_index("c")
    side = lax.axis_index("zl")
    half_rows = TOK // 2
    at_side = side.astype(jnp.int32).reshape(1)
    at_core = core.astype(jnp.int32).reshape(1)
    own_place = jnp.zeros((2,), jnp.int32)
    far_place = jnp.stack([side, core * half_rows]).astype(jnp.int32)
    after = lax.optimization_barrier
    params = (ln1_gain, ln1_bias, ln2_gain, ln2_bias)

    def of_core(values, which):
        return lax.dynamic_slice_in_dim(values, which * half_rows, half_rows, 0)

    marks = jnp.concatenate([segment_ids, positions]).astype(F32).reshape(1, 2 * TOK)
    hidden_sent = jnp.concatenate(
        [of_core(hidden_in, core).astype(F32), jnp.pad(marks, ((0, 7), (0, D - 2 * TOK)))], axis=0
    )
    hidden_pair = lax.all_gather(hidden_sent, "zl")

    second_in, cot_turned, stats = norm_call(
        second_kernel, 256, (hidden_in, cotangent), 1, 1, (ln2_gain, ln2_bias), stats=True
    )
    act_low, slope, down_grad = feed(second_in, cot_turned, fc1_weight, fc1_bias)
    down_sum = after(lax.psum_scatter(down_grad, ("x", "y"), scatter_dimension=0, tiled=True))
    _, cotangent, hidden_in = after((down_grad, cotangent, hidden_in))

    own_marks = marks.reshape(2, TOK)
    first_in, first_turned, second_turned = norm_call(first_kernel, 256, (hidden_in,), 1, 2, params)
    projected = project(own_place, 2, first_in, qkv_weight, qkv_bias, own_marks)
    grad_up, grad_mixed = feed_back(cotangent, fc2_weight, slope, dense_weight)
    mixed_low, grad_packed = attend(own_place, 2, projected, grad_mixed, own_marks)
    mixed_low, cot_sent = after((mixed_low, of_core(cotangent, core).astype(F32)))

    hidden_pair, mixed_low, cot_sent, grad_up = after((hidden_pair, mixed_low, cot_sent, grad_up))
    cot_got = send(cot_sent, "zl")
    hidden_got = lax.dynamic_slice_in_dim(hidden_pair, 1 - side, 1, 0)
    hidden_too = send(hidden_got, "c")

    def beside(hidden_got, hidden_too, first_turned, second_turned, mixed_low, grad_packed, grad_up):
        first_in, second_in, first_turned, second_turned = first_far(
            hidden_got, hidden_too, params, (first_turned, second_turned)
        )
        slope_side = slope_far(at_side, second_in, fc1_weight, fc1_bias)
        marks_got = hidden_got[0, half_rows, : 2 * TOK].reshape(2, 2, half_rows)
        marks_far = jnp.where(core == 0, marks_got, marks_got[:, ::-1]).reshape(2, TOK)
        projected_far = project(far_place, 1, first_in, qkv_weight, qkv_bias, marks_far)
        branches = branch_halves(at_core, mixed_low, act_low, dense_weight, fc2_weight)
        backs = back_halves(
            at_core,
            grad_packed,
            grad_up,
            qkv_weight,
            fc1_weight,
            hidden_in,
            stats,
            ln1_gain,
            ln2_gain,
        )
        return first_turned, second_turned, slope_side, marks_far, *branches, *backs, *projected_far

    (
        first_turned,
        second_turned,
        slope_side,
        marks_far,
        branch,
        branch_other,
        combined,
        combined_other,
        norms,
        *projected_far,
    ) = lax.cond(
        core == 0,
        beside,
        beside,
        hidden_got,
        hidden_too,
        first_turned,
        second_turned,
        mixed_low,
        grad_packed,
        grad_up,
    )

    slope_side, cot_got, branch_other, combined_other = after(
        (slope_side, cot_got, branch_other, combined_other)
    )
    cot_too = send(cot_got, "c")
    branch_too, combined_too = send(branch_other, "c"), send(combined_other, "c")
    held = cot_far_half(0, at_side, cot_got, fc2_weight, slope_side, dense_weight, (cot_turned,))
    *held, cot_too, branch_too, combined_too = after((*held, cot_too, branch_too, combined_too))
    branch = lax.psum(branch + branch_too, "zh")
    combined = lax.psum(combined + combined_too, "zh")
    grad_up_far, grad_mixed_far, cot_turned = cot_far_half(
        1, at_side, cot_too, fc2_weight, slope_side, dense_weight, held
    )
    mixed_far, grad_packed_far = attend(far_place, 1, projected_far, grad_mixed_far, marks_far)
    joint_grad = joint(
        at_side,
        (second_turned, cot_turned, first_turned),
        (grad_up, grad_up_far, mixed_low, mixed_far, grad_packed, grad_packed_far),
    )
    joint_grad, down_sum = after((joint_grad, down_sum))
    joint_sum = after(lax.psum_scatter(joint_grad, ("x", "y"), scatter_dimension=0, tiled=True))
    _, norms, grad_packed, grad_up, cotangent, down_sum = after(
        (joint_grad, norms, grad_packed, grad_up, cotangent, down_sum)
    )

    norms = norms[:4].reshape(4, 32, 64).transpose(1, 0, 2).reshape(32, 256)
    grad_out = cotangent.astype(F32)
    bias_sum = jnp.sum(grad_out, axis=0)
    qkv_bias_sum = jnp.sum(grad_packed.astype(F32), axis=0)
    up_bias_grad = jnp.sum(grad_up.astype(F32), axis=0)
    small = jnp.concatenate(
        [
            norms,
            bias_sum.reshape(32, 64),
            qkv_bias_sum.reshape(2, 32, 24).transpose(1, 0, 2).reshape(32, 48),
            up_bias_grad.reshape(16, 32, 4).transpose(1, 0, 2).reshape(32, 64),
            jnp.zeros((32, 80), F32),
        ],
        axis=1,
    )
    def of_side(values, which):
        return lax.dynamic_slice_in_dim(values[0], which * 64, 64, 0)

    down_far = send(of_side(down_sum, 1 - side), "zl")
    for axis in ("x", "y"):
        small = small + swap(small, axis, 1)
        small = small + swap(small, axis, 2)
        small, down_far = after((small, down_far))
    block = lax.axis_index("x") * 4 + lax.axis_index("y")
    own_small = lax.dynamic_slice_in_dim(small, side * 16 + block, 1, 0)
    far_small = lax.dynamic_slice_in_dim(small, (1 - side) * 16 + block, 1, 0)
    small = (own_small + send(far_small, "zl")).reshape(-1)

    small, branch, combined = after((small, branch, combined))
    norms, joint_sum = after((small[:256], joint_sum))
    norms = norms + send(norms, "c")
    norms = (norms + send(norms, "zh")).reshape(4, 64)
    bias_total = small[256:320]
    biases = (dense_bias, fc2_bias)
    own = (hidden_in, cotangent, stats, biases)
    branch_too, combined_too = send(branch, "c"), send(combined, "c")
    finals = final_half(at_core, branch, combined, *own, ())
    output, input_grad = final_half(1 - at_core, branch_too, combined_too, *own, finals)

    down_sum = of_side(down_sum, side) + down_far
    near = of_side(joint_sum, side)
    far = send(of_side(joint_sum, 1 - side), "zl")
    low = jnp.where(side == 0, near, far)
    high = jnp.where(side == 0, far, near)
    sums = []
    start = 0
    for width in (1024, 256, 768):
        stop = start + width
        sums.append(jnp.concatenate([low[:, start:stop], high[:, start:stop]], axis=1))
        start = stop
    up_sum, dense_sum, qkv_sum = sums
    return (
        output,
        input_grad,
        norms[0],
        norms[1],
        qkv_sum,
        small[320:368].reshape(2, 24),
        dense_sum.T,
        bias_total,
        norms[2],
        norms[3],
        up_sum,
        small[368:432].reshape(16, 4),
        down_sum.T,
        bias_total,
    )


def solution(mesh):
    fine = Mesh(mesh.devices.reshape(tuple(SIZES.values())), tuple(SIZES))
    return jax.shard_map(
        body,
        mesh=fine,
        in_specs=(
            P(DP, None),
            P(DP),
            P(DP),
            P(),
            P(),
            P(None, TENSOR),
            P(TENSOR, None),
            P(TENSOR, None),
            P(),
            P(),
            P(),
            P(None, TENSOR),
            P(TENSOR, None),
            P(TENSOR, None),
            P(),
            P(DP, None),
        ),
        out_specs=(
            P(DP, None),
            P(DP, None),
            P(DP),
            P(DP),
            P(DP, TENSOR),
            P(TENSOR, DP),
            P(TENSOR, DP),
            P(DP),
            P(DP),
            P(DP),
            P(DP, TENSOR),
            P(TENSOR, DP),
            P(TENSOR, DP),
            P(DP),
        ),
        check_vma=False,
    )
```

```python
from functools import partial
import math

import jax
import jax.numpy as jnp
import numpy as np
from jax import lax
from jax.experimental import pallas as pl
from jax.experimental.pallas import tpu as pltpu
from jax.sharding import Mesh, PartitionSpec as P

HD = 256
ROT = 64
TOK = 512
D = 2048
EPSILON = 1e-05
NEGATIVE = -1000000000.0
SIZES = {"zl": 2, "x": 4, "y": 4, "zh": 2, "c": 2}
DP = ("zl", "x", "y")
TENSOR = ("zh", "c")
F32 = jnp.float32
BF16 = jnp.bfloat16


def send(value, axis, step=1):
    n = SIZES[axis]
    return lax.ppermute(value, axis, [(i, (i + step) % n) for i in range(n)])


def swap(value, axis, bit):
    return lax.ppermute(value, axis, [(i, i ^ bit) for i in range(SIZES[axis])])


def plain_dot(left, right):
    return jnp.dot(left, right, preferred_element_type=F32)


def contract_cols(left, right):
    return lax.dot_general(left, right, (((1,), (1,)), ((), ())), preferred_element_type=F32)


VMEM = 56 * 1024 * 1024
COST = pl.CostEstimate(flops=1000000, bytes_accessed=1000000, transcendentals=0)


def whole(shape):
    return pl.BlockSpec(shape, lambda *_: (0,) * len(shape), pipeline_mode=pl.Buffered(1))


def put_turned(target, rows):
    for z in range(2):
        for pair in range(8):
            start = z * 1024 + pair * 128
            block = rows[:, start : start + 128].T.astype(BF16)
            target[2 * pair, z] = block[:64]
            target[2 * pair + 1, z] = block[64:]


def normalise(hidden):
    average = jnp.mean(hidden, axis=-1, keepdims=True)
    centred = hidden - average
    inv_std = lax.rsqrt(jnp.mean(centred * centred, axis=-1, keepdims=True) + EPSILON)
    return centred * inv_std, inv_std


def second_kernel(hidden, cot, gain, shift, second_out, cot_turned, stats):
    rows = hidden[...].astype(F32)
    average = jnp.mean(rows, axis=-1, keepdims=True)
    centred = rows - average
    inv_std = lax.rsqrt(jnp.mean(centred * centred, axis=-1, keepdims=True) + EPSILON)
    second_out[...] = (centred * inv_std * gain[...] + shift[...]).astype(BF16)
    put_turned(cot_turned, cot[...].astype(F32))
    lane = lax.broadcasted_iota(jnp.int32, (rows.shape[0], 128), 1)
    stats[...] = jnp.where(lane < 64, average, inv_std)


def first_kernel(hidden, gain, shift, gain_two, shift_two, first_out, first_turned, second_turned):
    normed, _ = normalise(hidden[...].astype(F32))
    first = normed * gain[...] + shift[...]
    first_out[...] = first.astype(BF16)
    put_turned(first_turned, first)
    put_turned(second_turned, normed * gain_two[...] + shift_two[...])


def first_far_kernel(near, other, gain, shift, gain_two, shift_two, *refs):
    first_out, second_out, first_turned, second_turned = refs[2:]

    def step(rows):
        normed, _ = normalise(rows)
        first = normed * gain[...] + shift[...]
        second = normed * gain_two[...] + shift_two[...]
        first_out[...] = first.astype(BF16)
        second_out[...] = second.astype(BF16)
        put_turned(first_turned, first)
        put_turned(second_turned, second)

    @pl.when(pl.program_id(0) < 2)
    def _():
        step(near[0])

    @pl.when(pl.program_id(0) >= 2)
    def _():
        step(other[0])


TURNED = (16, 2, 64, 2 * TOK)


def norm_call(kernel, rows, n_rows, n_plain, n_turned, params, stats=False):
    plain = pl.BlockSpec((rows, D), lambda i: (i, 0))
    return pl.pallas_call(
        kernel,
        grid=(TOK // rows,),
        in_specs=[plain] * len(n_rows) + [whole((1, D))] * len(params),
        out_specs=[plain] * n_plain
        + [pl.BlockSpec((16, 2, 64, rows), lambda i: (0, 0, 0, i))] * n_turned
        + [pl.BlockSpec((rows, 128), lambda i: (i, 0))] * stats,
        out_shape=[jax.ShapeDtypeStruct((TOK, D), BF16)] * n_plain
        + [jax.ShapeDtypeStruct(TURNED, BF16)] * n_turned
        + [jax.ShapeDtypeStruct((TOK, 128), F32)] * stats,
        compiler_params=pltpu.CompilerParams(vmem_limit_bytes=VMEM),
        cost_estimate=COST,
    )(*n_rows, *(p.reshape(1, D) for p in params))


def first_far(near, other, params, held):
    rows = 128
    plain = pl.BlockSpec((rows, D), lambda i: (i, 0))
    return pl.pallas_call(
        first_far_kernel,
        grid=(TOK // rows,),
        in_specs=[
            pl.BlockSpec((1, rows, D), lambda i: (0, lax.min(i, 1), 0)),
            pl.BlockSpec((1, rows, D), lambda i: (0, lax.max(i - 2, 0), 0)),
        ]
        + [whole((1, D))] * 4
        + [pl.BlockSpec(memory_space=pl.ANY)] * 2,
        out_specs=[plain] * 2
        + [pl.BlockSpec((16, 2, 64, rows), lambda i: (0, 0, 0, i + TOK // rows))] * 2,
        out_shape=[jax.ShapeDtypeStruct((TOK, D), BF16)] * 2
        + [jax.ShapeDtypeStruct(TURNED, BF16)] * 2,
        input_output_aliases={6: 2, 7: 3},
        compiler_params=pltpu.CompilerParams(vmem_limit_bytes=VMEM),
        cost_estimate=COST,
    )(near, other, *(p.reshape(1, D) for p in params), *held)


def phi(upward):
    return 0.5 * (1.0 + lax.erf(upward * math.sqrt(0.5)))


def gelu_slope(upward, below):
    return below + upward * (jnp.exp(-0.5 * upward * upward) * (1.0 / math.sqrt(2.0 * math.pi)))


def as_row(block):
    return jnp.concatenate([block[i : i + 1, :] for i in range(block.shape[0])], axis=1)


def feed_kernel(second, cot_turned, weight, bias, act_out, slope_out, down_grad):
    upward = plain_dot(second[...], weight[...]) + as_row(bias[0])
    below = phi(upward)
    act = (upward * below).astype(BF16)
    act_out[...] = act
    slope_out[...] = gelu_slope(upward, below)
    down_grad[...] = plain_dot(cot_turned[...].reshape(D, TOK), act).reshape(16, 128, -1)


def feed(second, cot_turned, weight, bias):
    units, width = weight.shape[1], 512
    column = pl.BlockSpec((TOK, width), lambda j: (0, j))
    return pl.pallas_call(
        feed_kernel,
        grid=(units // width,),
        in_specs=[
            whole((TOK, D)),
            whole((16, 2, 64, TOK)),
            pl.BlockSpec((D, width), lambda j: (0, j)),
            pl.BlockSpec((1, width // 128, 128), lambda j: (j, 0, 0)),
        ],
        out_specs=[column, column, pl.BlockSpec((16, 128, width), lambda j: (0, 0, j))],
        out_shape=[
            jax.ShapeDtypeStruct((TOK, units), BF16),
            jax.ShapeDtypeStruct((TOK, units), F32),
            jax.ShapeDtypeStruct((16, 128, units), F32),
        ],
        compiler_params=pltpu.CompilerParams(vmem_limit_bytes=VMEM),
        cost_estimate=COST,
    )(second, cot_turned, weight, bias.reshape(-1, width // 128, 128))


def feed_back_kernel(cot, weight, slope, dense, up_grad, grad_mixed):
    up_grad[...] = (contract_cols(cot[...], weight[...]) * slope[...]).astype(BF16)

    @pl.when(pl.program_id(0) == 0)
    def _():
        grad_mixed[...] = contract_cols(cot[...], dense[...]).astype(BF16)


def feed_back(cot, weight, slope, dense):
    units, width = slope.shape[1], 512
    column = pl.BlockSpec((TOK, width), lambda j: (0, j))
    mixed = dense.shape[0]
    return pl.pallas_call(
        feed_back_kernel,
        grid=(units // width,),
        in_specs=[
            whole((TOK, D)),
            pl.BlockSpec((width, D), lambda j: (j, 0)),
            column,
            whole(dense.shape),
        ],
        out_specs=[column, pl.BlockSpec((TOK, mixed), lambda j: (0, 0))],
        out_shape=[
            jax.ShapeDtypeStruct((TOK, units), BF16),
            jax.ShapeDtypeStruct((TOK, mixed), BF16),
        ],
        compiler_params=pltpu.CompilerParams(vmem_limit_bytes=VMEM),
        cost_estimate=COST,
    )(cot, weight, slope, dense)


def cot_far_kernel(n, m, side, rows, weight, slope, dense, *refs):
    sums, (up_grad, grad_mixed, cot_turned), totals, low = (
        refs[:m],
        refs[m + n : m + n + 3],
        refs[m + n + 3 : -1],
        refs[-1],
    )

    @pl.when(pl.program_id(0) == 0)
    def _():
        low[...] = rows[...].astype(BF16)
        put_turned(cot_turned, rows[...])
        grad_mixed[...] = contract_cols(low[...], dense[...]).astype(BF16)

    up_grad[...] = (contract_cols(low[...], weight[...]) * slope[...]).astype(BF16)
    for k, total in enumerate(totals):
        total[...] = sums[2 * k][...] + sums[2 * k + 1][...]


def cot_far_half(k, side, rows, weight, slope, dense, held, sums=()):
    half, width = TOK // 2, 256
    steps = slope.shape[1] // width
    shapes = [
        jax.ShapeDtypeStruct((TOK, slope.shape[1]), BF16),
        jax.ShapeDtypeStruct((TOK, HD), BF16),
        jax.ShapeDtypeStruct(TURNED, BF16),
    ]
    piece = pl.BlockSpec((half, D // steps), lambda j, s: (0, j))
    first = 5 + len(sums)
    return pl.pallas_call(
        partial(cot_far_kernel, len(held), len(sums)),
        grid_spec=pltpu.PrefetchScalarGridSpec(
            num_scalar_prefetch=1,
            grid=(steps,),
            in_specs=[
                whole((half, D)),
                pl.BlockSpec((width, D), lambda j, s: (s[0] * steps + j, 0)),
                pl.BlockSpec((half, width), lambda j, s: (k, j)),
                pl.BlockSpec((HD, D), lambda j, s: (s[0], 0)),
            ]
            + [piece] * len(sums)
            + [pl.BlockSpec(memory_space=pl.ANY)] * len(held),
            out_specs=[
                pl.BlockSpec((half, width), lambda j, s: (k, j)),
                pl.BlockSpec((half, HD), lambda j, s: (k, 0)),
                pl.BlockSpec((16, 2, 64, half), lambda j, s: (0, 0, 0, 2 + k)),
            ]
            + [piece] * (len(sums) // 2),
            scratch_shapes=[pltpu.VMEM((half, D), BF16)],
        ),
        out_shape=shapes + [jax.ShapeDtypeStruct((half, D), F32)] * (len(sums) // 2),
        input_output_aliases={first: 2} if len(held) == 1 else {first + i: i for i in range(3)},
        compiler_params=pltpu.CompilerParams(vmem_limit_bytes=VMEM),
        cost_estimate=COST,
    )(side, rows, weight, slope, dense, *sums, *held)


def slope_far_kernel(side, second, weight, bias, slope):
    upward = plain_dot(second[...], weight[...]) + as_row(bias[0])
    slope[...] = gelu_slope(upward, phi(upward))


def slope_far(side, second, weight, bias):
    units, width = weight.shape[1] // 2, 512
    steps = units // width
    return pl.pallas_call(
        slope_far_kernel,
        grid_spec=pltpu.PrefetchScalarGridSpec(
            num_scalar_prefetch=1,
            grid=(steps,),
            in_specs=[
                whole((TOK, D)),
                pl.BlockSpec((D, width), lambda j, s: (0, s[0] * steps + j)),
                pl.BlockSpec((1, width // 128, 128), lambda j, s: (s[0] * steps + j, 0, 0)),
            ],
            out_specs=pl.BlockSpec((TOK, width), lambda j, s: (0, j)),
        ),
        out_shape=jax.ShapeDtypeStruct((TOK, units), F32),
        compiler_params=pltpu.CompilerParams(vmem_limit_bytes=VMEM),
        cost_estimate=COST,
    )(side, second, weight, bias.reshape(-1, width // 128, 128))


def turn(values, tables, sign):
    first = values[:, :128]
    cosine, rising, falling = tables
    first = (
        first * cosine[...]
        + (pltpu.roll(first, 32, 1) * rising[...] + pltpu.roll(first, 96, 1) * falling[...]) * sign
    )
    return jnp.concatenate([first, values[:, 128:]], axis=1)


def as_column(row):
    return jnp.broadcast_to(row, (8, row.shape[1])).T[:, 0:1]


def cosine_and_sine(angles):
    turns = jnp.floor(angles * (2.0 / math.pi) + 0.5)
    rest = ((angles - turns * 1.5703125) - turns * 4.837512969970703e-4) - turns * 7.549789954891882e-8
    square = rest * rest
    sine = ((-1.9515295891e-4 * square + 8.3321608736e-3) * square - 1.6666654611e-1) * square
    sine = sine * rest + rest
    cosine = (2.443315711809948e-5 * square - 1.388731625493765e-3) * square + 4.166664568298827e-2
    cosine = cosine * (square * square) - 0.5 * square + 1.0
    quarter = turns.astype(jnp.int32) & 3
    odd = (quarter & 1) == 1
    flipped = jnp.where(odd, sine, cosine), jnp.where(odd, cosine, sine)
    return (
        jnp.where((quarter == 1) | (quarter == 2), -flipped[0], flipped[0]),
        jnp.where(quarter >= 2, -flipped[1], flipped[1]),
    )


def project_kernel(place, first, weight, bias, marks, inverse, queries, keys, values, *tables):
    @pl.when(pl.program_id(0) == 0)
    def _():
        angles = inverse[...] * marks[1:2, :]
        cosine, sine = cosine_and_sine(angles)
        none, rest = jnp.zeros_like(sine), jnp.zeros((64, TOK), F32)
        tables[0][...] = jnp.concatenate([cosine, cosine, rest + 1.0], axis=0).T
        tables[1][...] = jnp.concatenate([none, sine, rest], axis=0).T
        tables[2][...] = jnp.concatenate([-sine, none, rest], axis=0).T

    head = pl.program_id(0) + place[0] * (2 - pl.num_programs(0))
    packed = plain_dot(first[...], weight[...]) + bias[pl.ds(head, 1), :]
    queries[...] = turn(packed[:, :HD], tables, 1.0).astype(BF16)
    keys[...] = turn(packed[:, HD : 2 * HD], tables, 1.0).astype(BF16)
    values[...] = packed[:, 2 * HD :].astype(BF16)


def project(place, heads, first, weight, bias, marks):
    inverse = jnp.asarray((10000.0 ** (-2.0 * np.arange(32) / ROT)).astype(np.float32).reshape(32, 1))
    at = (lambda h, s: h) if heads == 2 else (lambda h, s: s[0])
    column = pl.BlockSpec((TOK, HD), lambda h, s: (0, h))
    return pl.pallas_call(
        project_kernel,
        grid_spec=pltpu.PrefetchScalarGridSpec(
            num_scalar_prefetch=1,
            grid=(heads,),
            in_specs=[
                whole((TOK, D)),
                pl.BlockSpec((D, 3 * HD), lambda h, s: (0, at(h, s))),
                whole((2, 3 * HD)),
                whole((2, TOK)),
                whole((32, 1)),
            ],
            out_specs=[column] * 3 + [pl.BlockSpec((TOK, 128), lambda h, s: (0, 0))] * 3,
        ),
        out_shape=[jax.ShapeDtypeStruct((TOK, heads * HD), BF16)] * 3
        + [jax.ShapeDtypeStruct((TOK, 128), F32)] * 3,
        compiler_params=pltpu.CompilerParams(vmem_limit_bytes=VMEM),
        cost_estimate=COST,
    )(place, first, weight, bias, marks, inverse)


def attend_kernel(
    place, queries, keys, values, cosine, rising, falling, grad_mixed, marks, mixed_out, grad_out
):
    tables = (cosine, rising, falling)
    scale = 1.0 / math.sqrt(HD)
    queries, keys, values = queries[...], keys[...], values[...]
    segments = marks[0:1, :]

    def order(axis):
        return lax.rem(lax.broadcasted_iota(jnp.int32, (TOK, TOK), axis) + place[1], TOK)

    allowed = (as_column(segments) == segments) & (order(0) >= order(1))
    scores = jnp.where(allowed, contract_cols(queries, keys) * scale, NEGATIVE)
    top = jnp.max(scores, axis=-1, keepdims=True)
    weights = jnp.exp(scores - top)
    probs = weights / jnp.sum(weights, axis=-1, keepdims=True)
    probs_low = probs.astype(BF16)
    mixed_out[...] = plain_dot(probs_low, values).astype(BF16)
    grad_probs = contract_cols(grad_mixed[...], values)
    along = jnp.sum(probs * grad_probs, axis=-1, keepdims=True)
    grad_scores = (probs * (grad_probs - along)).astype(BF16)
    grad_query = plain_dot(grad_scores, keys) * scale
    grad_key = plain_dot(grad_scores.T, queries) * scale
    grad_value = plain_dot(probs_low.T, grad_mixed[...])
    grad_out[:, :HD] = turn(grad_query, tables, -1.0).astype(BF16)
    grad_out[:, HD : 2 * HD] = turn(grad_key, tables, -1.0).astype(BF16)
    grad_out[:, 2 * HD :] = grad_value.astype(BF16)


def attend(place, heads, projected, grad_mixed, marks):
    column = pl.BlockSpec((TOK, HD), lambda h, s: (0, h))
    return pl.pallas_call(
        attend_kernel,
        grid_spec=pltpu.PrefetchScalarGridSpec(
            num_scalar_prefetch=1,
            grid=(heads,),
            in_specs=[column] * 3
            + [whole((TOK, 128))] * 3
            + [column, whole((2, TOK))],
            out_specs=[column, pl.BlockSpec((TOK, 3 * HD), lambda h, s: (0, h))],
        ),
        out_shape=[
            jax.ShapeDtypeStruct((TOK, heads * HD), BF16),
            jax.ShapeDtypeStruct((TOK, heads * 3 * HD), BF16),
        ],
        compiler_params=pltpu.CompilerParams(vmem_limit_bytes=VMEM),
        cost_estimate=COST,
    )(place, *projected, grad_mixed, marks)


def put_halves(core, values, scratch, mine, other):
    scratch[...] = values
    half = TOK // 2
    mine[...] = scratch[pl.ds(pl.multiple_of(core[0] * half, half), half), :]
    other[...] = scratch[pl.ds(pl.multiple_of((1 - core[0]) * half, half), half), :]


def branch_kernel(core, mixed, act, dense, down, mine, other, scratch):
    total = plain_dot(act[...], down[...]) + plain_dot(mixed[...], dense[...])
    put_halves(core, total, scratch, mine, other)


def back_kernel(
    core, packed, up_grad, qkv, up, hidden, stats, gain, gain_two, mine, other, sums, scratch
):
    first = contract_cols(packed[...], qkv[...])
    second = contract_cols(up_grad[...], up[...])
    put_halves(core, first * gain[...] + second * gain_two[...], scratch, mine, other)
    normed = (hidden[...].astype(F32) - stats[:, 0:1]) * stats[:, 64:65]
    rows = [
        jnp.sum(v, axis=0, keepdims=True) for v in (first * normed, first, second * normed, second)
    ]
    sums[...] = jnp.concatenate(rows + [jnp.zeros((4, first.shape[1]), F32)], axis=0)


def halves_call(kernel, core, operands, specs, with_sums):
    width = 512
    half = pl.BlockSpec((TOK // 2, width), lambda j, s: (0, j))
    return pl.pallas_call(
        kernel,
        grid_spec=pltpu.PrefetchScalarGridSpec(
            num_scalar_prefetch=1,
            grid=(D // width,),
            in_specs=specs,
            out_specs=[half, half] + [pl.BlockSpec((8, width), lambda j, s: (0, j))] * with_sums,
            scratch_shapes=[pltpu.VMEM((TOK, width), F32)],
        ),
        out_shape=[jax.ShapeDtypeStruct((TOK // 2, D), F32)] * 2
        + [jax.ShapeDtypeStruct((8, D), F32)] * with_sums,
        compiler_params=pltpu.CompilerParams(vmem_limit_bytes=VMEM),
        cost_estimate=COST,
    )(core, *operands)


def branch_halves(core, mixed, act, dense, down):
    specs = [whole(mixed.shape), whole(act.shape)]
    specs += [pl.BlockSpec((w.shape[0], 512), lambda j, s: (0, j)) for w in (dense, down)]
    return halves_call(branch_kernel, core, (mixed, act, dense, down), specs, False)


def back_halves(core, packed, up_grad, qkv, up, hidden, stats, gain, gain_two):
    specs = [whole(packed.shape), whole(up_grad.shape)]
    specs += [pl.BlockSpec((512, w.shape[1]), lambda j, s: (j, 0)) for w in (qkv, up)]
    specs += [pl.BlockSpec((TOK, 512), lambda j, s: (0, j)), whole((TOK, 128))]
    specs += [pl.BlockSpec((1, 512), lambda j, s: (0, j))] * 2
    operands = (packed, up_grad, qkv, up, hidden, stats, gain.reshape(1, D), gain_two.reshape(1, D))
    return halves_call(back_kernel, core, operands, specs, True)


def final_kernel(n, half, branch, combined, hidden, cot, stats, bias, bias_too, *refs):
    output, input_grad = refs[n:]
    rows = hidden[...].astype(F32)
    output[...] = rows + branch[...] + bias[...] + bias_too[...]
    e = combined[...]
    inv_std = stats[:, 64:65]
    normed = (rows - stats[:, 0:1]) * inv_std
    input_grad[...] = cot[...].astype(F32) + inv_std * (
        e
        - jnp.mean(e, axis=-1, keepdims=True)
        - normed * jnp.mean(e * normed, axis=-1, keepdims=True)
    )


def final_half(half, branch, combined, hidden, cot, stats, biases, held):
    rows = 128
    steps = TOK // 2 // rows
    given = pl.BlockSpec((rows, D), lambda i, s: (i, 0))
    placed = pl.BlockSpec((rows, D), lambda i, s: (s[0] * steps + i, 0))
    return pl.pallas_call(
        partial(final_kernel, len(held)),
        grid_spec=pltpu.PrefetchScalarGridSpec(
            num_scalar_prefetch=1,
            grid=(steps,),
            in_specs=[given, given, placed, placed]
            + [pl.BlockSpec((rows, 128), lambda i, s: (s[0] * steps + i, 0))]
            + [whole((1, D))] * 2
            + [pl.BlockSpec(memory_space=pl.ANY)] * len(held),
            out_specs=[placed, placed],
        ),
        out_shape=[jax.ShapeDtypeStruct((TOK, D), F32)] * 2,
        input_output_aliases={8: 0, 9: 1} if held else {},
        compiler_params=pltpu.CompilerParams(vmem_limit_bytes=VMEM),
        cost_estimate=COST,
    )(half, branch, combined, hidden, cot, stats, *(b.reshape(1, D) for b in biases), *held)


def joint_kernel(side, *refs):
    lefts, rights, target, held, arrived = refs[:3], refs[3:9], refs[9], refs[10:13], refs[13]
    step = pl.program_id(0)
    copies = [pltpu.make_async_copy(lefts[k], held[k], arrived.at[k]) for k in range(3)]

    @pl.when(step == 0)
    def _():
        for copy in copies:
            copy.start()

    for k, (start, stop) in enumerate(((0, 4), (4, 5), (5, 8))):

        @pl.when(step == start)
        def _(k=k):
            copies[k].wait()

        @pl.when((step >= start) & (step < stop))
        def _(k=k):
            right = jnp.concatenate([rights[2 * k][...], rights[2 * k + 1][...]], axis=0)
            total = plain_dot(held[k][...].reshape(D, 2 * TOK), right)
            target[...] = total.reshape(16, 128, -1)


def joint(side, lefts, rights):
    width = 256
    specs = [pl.BlockSpec(memory_space=pl.ANY)] * 3
    for start, n in ((0, 4), (4, 1), (5, 3)):

        def near(j, s, start=start, n=n):
            return (0, s[0] * n + jnp.clip(j - start, 0, n - 1))

        def far(j, s, start=start, n=n):
            return (0, jnp.clip(j - start, 0, n - 1))

        specs += [pl.BlockSpec((TOK, width), near), pl.BlockSpec((TOK, width), far)]
    return pl.pallas_call(
        joint_kernel,
        grid_spec=pltpu.PrefetchScalarGridSpec(
            num_scalar_prefetch=1,
            grid=(8,),
            in_specs=specs,
            out_specs=pl.BlockSpec((16, 128, width), lambda j, s: (0, 0, j)),
            scratch_shapes=[pltpu.VMEM(TURNED, BF16)] * 3 + [pltpu.SemaphoreType.DMA((3,))],
        ),
        out_shape=jax.ShapeDtypeStruct((16, 128, 8 * width), F32),
        compiler_params=pltpu.CompilerParams(vmem_limit_bytes=VMEM),
        cost_estimate=COST,
    )(side, *lefts, *rights)


def assemble_kernel(side, near, far, up, dense, qkv):
    def put(low, high):
        up[...] = jnp.concatenate([low[:, :1024], high[:, :1024]], axis=1)
        dense[...] = jnp.concatenate([low[:, 1024:1280], high[:, 1024:1280]], axis=1).T
        qkv[...] = jnp.concatenate([low[:, 1280:], high[:, 1280:]], axis=1)

    @pl.when(side[0] == 0)
    def _():
        put(near[0], far[...])

    @pl.when(side[0] != 0)
    def _():
        put(far[...], near[0])


def assemble(side, near, far):
    shapes = ((64, 2048), (512, 64), (64, 1536))
    return pl.pallas_call(
        assemble_kernel,
        grid_spec=pltpu.PrefetchScalarGridSpec(
            num_scalar_prefetch=1,
            grid=(1,),
            in_specs=[
                pl.BlockSpec((1, 64, 2048), lambda i, s: (0, s[0], 0)),
                pl.BlockSpec((64, 2048), lambda i, s: (0, 0)),
            ],
            out_specs=[pl.BlockSpec(shape, lambda i, s: (0, 0)) for shape in shapes],
        ),
        out_shape=[jax.ShapeDtypeStruct(shape, F32) for shape in shapes],
        compiler_params=pltpu.CompilerParams(vmem_limit_bytes=VMEM),
        cost_estimate=COST,
    )(side, near, far)


def body(
    hidden_in,
    segment_ids,
    positions,
    ln1_gain,
    ln1_bias,
    qkv_weight,
    qkv_bias,
    dense_weight,
    dense_bias,
    ln2_gain,
    ln2_bias,
    fc1_weight,
    fc1_bias,
    fc2_weight,
    fc2_bias,
    cotangent,
):
    core = lax.axis_index("c")
    side = lax.axis_index("zl")
    half_rows = TOK // 2
    at_side = side.astype(jnp.int32).reshape(1)
    at_core = core.astype(jnp.int32).reshape(1)
    own_place = jnp.zeros((2,), jnp.int32)
    far_place = jnp.stack([side, core * half_rows]).astype(jnp.int32)
    after = lax.optimization_barrier
    params = (ln1_gain, ln1_bias, ln2_gain, ln2_bias)

    def of_core(values, which):
        return lax.dynamic_slice_in_dim(values, which * half_rows, half_rows, 0)

    marks = jnp.concatenate([segment_ids, positions]).astype(F32).reshape(1, 2 * TOK)
    hidden_sent = jnp.concatenate(
        [of_core(hidden_in, core).astype(F32), jnp.pad(marks, ((0, 7), (0, D - 2 * TOK)))], axis=0
    )
    hidden_pair = lax.all_gather(hidden_sent, "zl")

    second_in, cot_turned, stats = norm_call(
        second_kernel, 256, (hidden_in, cotangent), 1, 1, (ln2_gain, ln2_bias), stats=True
    )
    act_low, slope, down_grad = feed(second_in, cot_turned, fc1_weight, fc1_bias)
    down_sum = after(lax.psum_scatter(down_grad, ("x", "y"), scatter_dimension=0, tiled=True))
    _, cotangent, hidden_in = after((down_grad, cotangent, hidden_in))

    own_marks = marks.reshape(2, TOK)
    first_in, first_turned, second_turned = norm_call(first_kernel, 256, (hidden_in,), 1, 2, params)
    projected = project(own_place, 2, first_in, qkv_weight, qkv_bias, own_marks)
    grad_up, grad_mixed = feed_back(cotangent, fc2_weight, slope, dense_weight)
    mixed_low, grad_packed = attend(own_place, 2, projected, grad_mixed, own_marks)
    mixed_low, cot_sent = after((mixed_low, of_core(cotangent, core).astype(F32)))

    hidden_pair, mixed_low, cot_sent, grad_up = after((hidden_pair, mixed_low, cot_sent, grad_up))
    cot_got = send(cot_sent, "zl")
    hidden_got = lax.dynamic_slice_in_dim(hidden_pair, 1 - side, 1, 0)
    hidden_too = send(hidden_got, "c")

    def beside(hidden_got, hidden_too, first_turned, second_turned, mixed_low, grad_packed, grad_up):
        first_in, second_in, first_turned, second_turned = first_far(
            hidden_got, hidden_too, params, (first_turned, second_turned)
        )
        slope_side = slope_far(at_side, second_in, fc1_weight, fc1_bias)
        marks_got = hidden_got[0, half_rows, : 2 * TOK].reshape(2, 2, half_rows)
        marks_far = jnp.where(core == 0, marks_got, marks_got[:, ::-1]).reshape(2, TOK)
        projected_far = project(far_place, 1, first_in, qkv_weight, qkv_bias, marks_far)
        branches = branch_halves(at_core, mixed_low, act_low, dense_weight, fc2_weight)
        backs = back_halves(
            at_core,
            grad_packed,
            grad_up,
            qkv_weight,
            fc1_weight,
            hidden_in,
            stats,
            ln1_gain,
            ln2_gain,
        )
        return first_turned, second_turned, slope_side, marks_far, *branches, *backs, *projected_far

    (
        first_turned,
        second_turned,
        slope_side,
        marks_far,
        branch,
        branch_other,
        combined,
        combined_other,
        norms,
        *projected_far,
    ) = lax.cond(
        core > 1,
        beside,
        beside,
        hidden_got,
        hidden_too,
        first_turned,
        second_turned,
        mixed_low,
        grad_packed,
        grad_up,
    )

    slope_side, cot_got, branch_other, combined_other = after(
        (slope_side, cot_got, branch_other, combined_other)
    )
    cot_too = send(cot_got, "c")
    branch_too, combined_too = send(branch_other, "c"), send(combined_other, "c")
    held = cot_far_half(0, at_side, cot_got, fc2_weight, slope_side, dense_weight, (cot_turned,))
    *held, cot_too, branch_too, combined_too = after((*held, cot_too, branch_too, combined_too))
    grad_up_far, grad_mixed_far, cot_turned, branch, combined = cot_far_half(
        1,
        at_side,
        cot_too,
        fc2_weight,
        slope_side,
        dense_weight,
        held,
        (branch, branch_too, combined, combined_too),
    )
    branch = lax.psum(branch, "zh")
    combined = lax.psum(combined, "zh")
    mixed_far, grad_packed_far = attend(far_place, 1, projected_far, grad_mixed_far, marks_far)
    joint_grad = joint(
        at_side,
        (second_turned, cot_turned, first_turned),
        (grad_up, grad_up_far, mixed_low, mixed_far, grad_packed, grad_packed_far),
    )
    joint_grad, down_sum = after((joint_grad, down_sum))
    joint_sum = after(lax.psum_scatter(joint_grad, ("x", "y"), scatter_dimension=0, tiled=True))
    _, norms, grad_packed, grad_up, cotangent, down_sum = after(
        (joint_grad, norms, grad_packed, grad_up, cotangent, down_sum)
    )

    norms = norms[:4].reshape(4, 32, 64).transpose(1, 0, 2).reshape(32, 256)
    grad_out = cotangent.astype(F32)
    bias_sum = jnp.sum(grad_out, axis=0)
    qkv_bias_sum = jnp.sum(grad_packed.astype(F32), axis=0)
    up_bias_grad = jnp.sum(grad_up.astype(F32), axis=0)
    small = jnp.concatenate(
        [
            norms,
            bias_sum.reshape(32, 64),
            qkv_bias_sum.reshape(2, 32, 24).transpose(1, 0, 2).reshape(32, 48),
            up_bias_grad.reshape(16, 32, 4).transpose(1, 0, 2).reshape(32, 64),
            jnp.zeros((32, 80), F32),
        ],
        axis=1,
    )
    def of_side(values, which):
        return lax.dynamic_slice_in_dim(values[0], which * 64, 64, 0)

    down_far = send(of_side(down_sum, 1 - side), "zl")
    for axis in ("x", "y"):
        small = small + swap(small, axis, 1)
        small = small + swap(small, axis, 2)
        small, down_far = after((small, down_far))
    block = lax.axis_index("x") * 4 + lax.axis_index("y")
    own_small = lax.dynamic_slice_in_dim(small, side * 16 + block, 1, 0)
    far_small = lax.dynamic_slice_in_dim(small, (1 - side) * 16 + block, 1, 0)
    small = (own_small + send(far_small, "zl")).reshape(-1)

    norms = small[:256]
    norms = norms + send(norms, "c")
    norms = norms + send(norms, "zh")
    norms, branch, combined = after((norms, branch, combined))
    norms = norms.reshape(4, 64)
    bias_total = small[256:320]
    biases = (dense_bias, fc2_bias)
    own = (hidden_in, cotangent, stats, biases)
    branch_too, combined_too = send(branch, "c"), send(combined, "c")
    *finals, joint_sum = after((*final_half(at_core, branch, combined, *own, ()), joint_sum))
    output, input_grad = final_half(1 - at_core, branch_too, combined_too, *own, finals)

    down_sum = of_side(down_sum, side) + down_far
    joint_far = send(of_side(joint_sum, 1 - side), "zl")
    up_sum, dense_sum, qkv_sum = assemble(at_side, joint_sum, joint_far)
    return (
        output,
        input_grad,
        norms[0],
        norms[1],
        qkv_sum,
        small[320:368].reshape(2, 24),
        dense_sum,
        bias_total,
        norms[2],
        norms[3],
        up_sum,
        small[368:432].reshape(16, 4),
        down_sum.T,
        bias_total,
    )


def solution(mesh):
    fine = Mesh(mesh.devices.reshape(tuple(SIZES.values())), tuple(SIZES))
    return jax.shard_map(
        body,
        mesh=fine,
        in_specs=(
            P(DP, None),
            P(DP),
            P(DP),
            P(),
            P(),
            P(None, TENSOR),
            P(TENSOR, None),
            P(TENSOR, None),
            P(),
            P(),
            P(),
            P(None, TENSOR),
            P(TENSOR, None),
            P(TENSOR, None),
            P(),
            P(DP, None),
        ),
        out_specs=(
            P(DP, None),
            P(DP, None),
            P(DP),
            P(DP),
            P(DP, TENSOR),
            P(TENSOR, DP),
            P(TENSOR, DP),
            P(DP),
            P(DP),
            P(DP),
            P(DP, TENSOR),
            P(TENSOR, DP),
            P(TENSOR, DP),
            P(DP),
        ),
        check_vma=False,
    )
```

```python
from functools import partial
import math

import jax
import jax.numpy as jnp
import numpy as np
from jax import lax
from jax.experimental import pallas as pl
from jax.experimental.pallas import tpu as pltpu
from jax.sharding import Mesh, PartitionSpec as P

HD = 256
ROT = 64
TOK = 512
D = 2048
EPSILON = 1e-05
NEGATIVE = -1000000000.0
SIZES = {"zl": 2, "x": 4, "y": 4, "zh": 2, "c": 2}
DP = ("zl", "x", "y")
TENSOR = ("zh", "c")
F32 = jnp.float32
BF16 = jnp.bfloat16


def send(value, axis, step=1):
    n = SIZES[axis]
    return lax.ppermute(value, axis, [(i, (i + step) % n) for i in range(n)])


def swap(value, axis, bit):
    return lax.ppermute(value, axis, [(i, i ^ bit) for i in range(SIZES[axis])])


def plain_dot(left, right):
    return jnp.dot(left, right, preferred_element_type=F32)


def contract_cols(left, right):
    return lax.dot_general(left, right, (((1,), (1,)), ((), ())), preferred_element_type=F32)


VMEM = 56 * 1024 * 1024
COST = pl.CostEstimate(flops=1000000, bytes_accessed=1000000, transcendentals=0)


def whole(shape):
    return pl.BlockSpec(shape, lambda *_: (0,) * len(shape), pipeline_mode=pl.Buffered(1))


def put_turned(target, rows):
    for z in range(2):
        for pair in range(8):
            start = z * 1024 + pair * 128
            block = rows[:, start : start + 128].T.astype(BF16)
            target[2 * pair, z] = block[:64]
            target[2 * pair + 1, z] = block[64:]


def normalise(hidden):
    average = jnp.mean(hidden, axis=-1, keepdims=True)
    centred = hidden - average
    inv_std = lax.rsqrt(jnp.mean(centred * centred, axis=-1, keepdims=True) + EPSILON)
    return centred * inv_std, inv_std


def second_kernel(hidden, cot, gain, shift, second_out, cot_turned, stats):
    rows = hidden[...].astype(F32)
    average = jnp.mean(rows, axis=-1, keepdims=True)
    centred = rows - average
    inv_std = lax.rsqrt(jnp.mean(centred * centred, axis=-1, keepdims=True) + EPSILON)
    second_out[...] = (centred * inv_std * gain[...] + shift[...]).astype(BF16)
    put_turned(cot_turned, cot[...].astype(F32))
    lane = lax.broadcasted_iota(jnp.int32, (rows.shape[0], 128), 1)
    stats[...] = jnp.where(lane < 64, average, inv_std)


def first_kernel(hidden, gain, shift, gain_two, shift_two, first_out, first_turned, second_turned):
    normed, _ = normalise(hidden[...].astype(F32))
    first = normed * gain[...] + shift[...]
    first_out[...] = first.astype(BF16)
    put_turned(first_turned, first)
    put_turned(second_turned, normed * gain_two[...] + shift_two[...])


def first_far_kernel(near, other, gain, shift, gain_two, shift_two, *refs):
    first_out, second_out, first_turned, second_turned = refs[2:]

    def step(rows):
        normed, _ = normalise(rows)
        first = normed * gain[...] + shift[...]
        second = normed * gain_two[...] + shift_two[...]
        first_out[...] = first.astype(BF16)
        second_out[...] = second.astype(BF16)
        put_turned(first_turned, first)
        put_turned(second_turned, second)

    @pl.when(pl.program_id(0) < 2)
    def _():
        step(near[0])

    @pl.when(pl.program_id(0) >= 2)
    def _():
        step(other[0])


TURNED = (16, 2, 64, 2 * TOK)


def norm_call(kernel, rows, n_rows, n_plain, n_turned, params, stats=False):
    plain = pl.BlockSpec((rows, D), lambda i: (i, 0))
    return pl.pallas_call(
        kernel,
        grid=(TOK // rows,),
        in_specs=[plain] * len(n_rows) + [whole((1, D))] * len(params),
        out_specs=[plain] * n_plain
        + [pl.BlockSpec((16, 2, 64, rows), lambda i: (0, 0, 0, i))] * n_turned
        + [pl.BlockSpec((rows, 128), lambda i: (i, 0))] * stats,
        out_shape=[jax.ShapeDtypeStruct((TOK, D), BF16)] * n_plain
        + [jax.ShapeDtypeStruct(TURNED, BF16)] * n_turned
        + [jax.ShapeDtypeStruct((TOK, 128), F32)] * stats,
        compiler_params=pltpu.CompilerParams(vmem_limit_bytes=VMEM),
        cost_estimate=COST,
    )(*n_rows, *(p.reshape(1, D) for p in params))


def first_far(near, other, params, held):
    rows = 128
    plain = pl.BlockSpec((rows, D), lambda i: (i, 0))
    return pl.pallas_call(
        first_far_kernel,
        grid=(TOK // rows,),
        in_specs=[
            pl.BlockSpec((1, rows, D), lambda i: (0, lax.min(i, 1), 0)),
            pl.BlockSpec((1, rows, D), lambda i: (0, lax.max(i - 2, 0), 0)),
        ]
        + [whole((1, D))] * 4
        + [pl.BlockSpec(memory_space=pl.ANY)] * 2,
        out_specs=[plain] * 2
        + [pl.BlockSpec((16, 2, 64, rows), lambda i: (0, 0, 0, i + TOK // rows))] * 2,
        out_shape=[jax.ShapeDtypeStruct((TOK, D), BF16)] * 2
        + [jax.ShapeDtypeStruct(TURNED, BF16)] * 2,
        input_output_aliases={6: 2, 7: 3},
        compiler_params=pltpu.CompilerParams(vmem_limit_bytes=VMEM),
        cost_estimate=COST,
    )(near, other, *(p.reshape(1, D) for p in params), *held)


def phi(upward):
    return 0.5 * (1.0 + lax.erf(upward * math.sqrt(0.5)))


def gelu_slope(upward, below):
    return below + upward * (jnp.exp(-0.5 * upward * upward) * (1.0 / math.sqrt(2.0 * math.pi)))


def as_row(block):
    return jnp.concatenate([block[i : i + 1, :] for i in range(block.shape[0])], axis=1)


def feed_kernel(second, cot_turned, weight, bias, act_out, slope_out, down_grad):
    upward = plain_dot(second[...], weight[...]) + as_row(bias[0])
    below = phi(upward)
    act = (upward * below).astype(BF16)
    act_out[...] = act
    slope_out[...] = gelu_slope(upward, below)
    down_grad[...] = plain_dot(cot_turned[...].reshape(D, TOK), act).reshape(16, 128, -1)


def feed(second, cot_turned, weight, bias):
    units, width = weight.shape[1], 512
    column = pl.BlockSpec((TOK, width), lambda j: (0, j))
    return pl.pallas_call(
        feed_kernel,
        grid=(units // width,),
        in_specs=[
            whole((TOK, D)),
            whole((16, 2, 64, TOK)),
            pl.BlockSpec((D, width), lambda j: (0, j)),
            pl.BlockSpec((1, width // 128, 128), lambda j: (j, 0, 0)),
        ],
        out_specs=[column, column, pl.BlockSpec((16, 128, width), lambda j: (0, 0, j))],
        out_shape=[
            jax.ShapeDtypeStruct((TOK, units), BF16),
            jax.ShapeDtypeStruct((TOK, units), F32),
            jax.ShapeDtypeStruct((16, 128, units), F32),
        ],
        compiler_params=pltpu.CompilerParams(vmem_limit_bytes=VMEM),
        cost_estimate=COST,
    )(second, cot_turned, weight, bias.reshape(-1, width // 128, 128))


def feed_back_kernel(cot, weight, slope, up_grad):
    up_grad[...] = (contract_cols(cot[...], weight[...]) * slope[...]).astype(BF16)


def feed_back(cot, weight, slope):
    units, width = slope.shape[1], 512
    column = pl.BlockSpec((TOK, width), lambda j: (0, j))
    return pl.pallas_call(
        feed_back_kernel,
        grid=(units // width,),
        in_specs=[whole((TOK, D)), pl.BlockSpec((width, D), lambda j: (j, 0)), column],
        out_specs=column,
        out_shape=jax.ShapeDtypeStruct((TOK, units), BF16),
        compiler_params=pltpu.CompilerParams(vmem_limit_bytes=VMEM),
        cost_estimate=COST,
    )(cot, weight, slope)


def cot_far_kernel(n, m, side, rows, weight, slope, dense, *refs):
    sums, (up_grad, grad_mixed, cot_turned), totals, low = (
        refs[:m],
        refs[m + n : m + n + 3],
        refs[m + n + 3 : -1],
        refs[-1],
    )

    @pl.when(pl.program_id(0) == 0)
    def _():
        low[...] = rows[...].astype(BF16)
        put_turned(cot_turned, rows[...])
        grad_mixed[...] = contract_cols(low[...], dense[...]).astype(BF16)

    up_grad[...] = (contract_cols(low[...], weight[...]) * slope[...]).astype(BF16)
    for k, total in enumerate(totals):
        total[...] = sums[2 * k][...] + sums[2 * k + 1][...]


def cot_far_half(k, side, rows, weight, slope, dense, held, sums=()):
    half, width = TOK // 2, 256
    steps = slope.shape[1] // width
    shapes = [
        jax.ShapeDtypeStruct((TOK, slope.shape[1]), BF16),
        jax.ShapeDtypeStruct((TOK, HD), BF16),
        jax.ShapeDtypeStruct(TURNED, BF16),
    ]
    piece = pl.BlockSpec((half, D // steps), lambda j, s: (0, j))
    first = 5 + len(sums)
    return pl.pallas_call(
        partial(cot_far_kernel, len(held), len(sums)),
        grid_spec=pltpu.PrefetchScalarGridSpec(
            num_scalar_prefetch=1,
            grid=(steps,),
            in_specs=[
                whole((half, D)),
                pl.BlockSpec((width, D), lambda j, s: (s[0] * steps + j, 0)),
                pl.BlockSpec((half, width), lambda j, s: (k, j)),
                pl.BlockSpec((HD, D), lambda j, s: (s[0], 0)),
            ]
            + [piece] * len(sums)
            + [pl.BlockSpec(memory_space=pl.ANY)] * len(held),
            out_specs=[
                pl.BlockSpec((half, width), lambda j, s: (k, j)),
                pl.BlockSpec((half, HD), lambda j, s: (k, 0)),
                pl.BlockSpec((16, 2, 64, half), lambda j, s: (0, 0, 0, 2 + k)),
            ]
            + [piece] * (len(sums) // 2),
            scratch_shapes=[pltpu.VMEM((half, D), BF16)],
        ),
        out_shape=shapes + [jax.ShapeDtypeStruct((half, D), F32)] * (len(sums) // 2),
        input_output_aliases={first: 2} if len(held) == 1 else {first + i: i for i in range(3)},
        compiler_params=pltpu.CompilerParams(vmem_limit_bytes=VMEM),
        cost_estimate=COST,
    )(side, rows, weight, slope, dense, *sums, *held)


def slope_far_kernel(side, second, weight, bias, slope):
    upward = plain_dot(second[...], weight[...]) + as_row(bias[0])
    slope[...] = gelu_slope(upward, phi(upward))


def slope_far(side, second, weight, bias):
    units, width = weight.shape[1] // 2, 512
    steps = units // width
    return pl.pallas_call(
        slope_far_kernel,
        grid_spec=pltpu.PrefetchScalarGridSpec(
            num_scalar_prefetch=1,
            grid=(steps,),
            in_specs=[
                whole((TOK, D)),
                pl.BlockSpec((D, width), lambda j, s: (0, s[0] * steps + j)),
                pl.BlockSpec((1, width // 128, 128), lambda j, s: (s[0] * steps + j, 0, 0)),
            ],
            out_specs=pl.BlockSpec((TOK, width), lambda j, s: (0, j)),
        ),
        out_shape=jax.ShapeDtypeStruct((TOK, units), F32),
        compiler_params=pltpu.CompilerParams(vmem_limit_bytes=VMEM),
        cost_estimate=COST,
    )(side, second, weight, bias.reshape(-1, width // 128, 128))


def turn(values, tables, sign):
    first = values[:, :128]
    cosine, rising, falling = tables
    first = (
        first * cosine[...]
        + (pltpu.roll(first, 32, 1) * rising[...] + pltpu.roll(first, 96, 1) * falling[...]) * sign
    )
    return jnp.concatenate([first, values[:, 128:]], axis=1)


def as_column(row):
    return jnp.broadcast_to(row, (8, row.shape[1])).T[:, 0:1]


def cosine_and_sine(angles):
    turns = jnp.floor(angles * (2.0 / math.pi) + 0.5)
    rest = ((angles - turns * 1.5703125) - turns * 4.837512969970703e-4) - turns * 7.549789954891882e-8
    square = rest * rest
    sine = ((-1.9515295891e-4 * square + 8.3321608736e-3) * square - 1.6666654611e-1) * square
    sine = sine * rest + rest
    cosine = (2.443315711809948e-5 * square - 1.388731625493765e-3) * square + 4.166664568298827e-2
    cosine = cosine * (square * square) - 0.5 * square + 1.0
    quarter = turns.astype(jnp.int32) & 3
    odd = (quarter & 1) == 1
    flipped = jnp.where(odd, sine, cosine), jnp.where(odd, cosine, sine)
    return (
        jnp.where((quarter == 1) | (quarter == 2), -flipped[0], flipped[0]),
        jnp.where(quarter >= 2, -flipped[1], flipped[1]),
    )


def project_kernel(place, first, weight, bias, marks, inverse, queries, keys, values, *tables):
    @pl.when(pl.program_id(0) == 0)
    def _():
        angles = inverse[...] * marks[1:2, :]
        cosine, sine = cosine_and_sine(angles)
        none, rest = jnp.zeros_like(sine), jnp.zeros((64, TOK), F32)
        tables[0][...] = jnp.concatenate([cosine, cosine, rest + 1.0], axis=0).T
        tables[1][...] = jnp.concatenate([none, sine, rest], axis=0).T
        tables[2][...] = jnp.concatenate([-sine, none, rest], axis=0).T

    head = pl.program_id(0) + place[0] * (2 - pl.num_programs(0))
    packed = plain_dot(first[...], weight[...]) + bias[pl.ds(head, 1), :]
    queries[...] = turn(packed[:, :HD], tables, 1.0).astype(BF16)
    keys[...] = turn(packed[:, HD : 2 * HD], tables, 1.0).astype(BF16)
    values[...] = packed[:, 2 * HD :].astype(BF16)


def project(place, heads, first, weight, bias, marks):
    inverse = jnp.asarray((10000.0 ** (-2.0 * np.arange(32) / ROT)).astype(np.float32).reshape(32, 1))
    at = (lambda h, s: h) if heads == 2 else (lambda h, s: s[0])
    column = pl.BlockSpec((TOK, HD), lambda h, s: (0, h))
    return pl.pallas_call(
        project_kernel,
        grid_spec=pltpu.PrefetchScalarGridSpec(
            num_scalar_prefetch=1,
            grid=(heads,),
            in_specs=[
                whole((TOK, D)),
                pl.BlockSpec((D, 3 * HD), lambda h, s: (0, at(h, s))),
                whole((2, 3 * HD)),
                whole((2, TOK)),
                whole((32, 1)),
            ],
            out_specs=[column] * 3 + [pl.BlockSpec((TOK, 128), lambda h, s: (0, 0))] * 3,
        ),
        out_shape=[jax.ShapeDtypeStruct((TOK, heads * HD), BF16)] * 3
        + [jax.ShapeDtypeStruct((TOK, 128), F32)] * 3,
        compiler_params=pltpu.CompilerParams(vmem_limit_bytes=VMEM),
        cost_estimate=COST,
    )(place, first, weight, bias, marks, inverse)


def attend_kernel(place, queries, keys, values, cosine, rising, falling, marks, *refs):
    given, (mixed_out, grad_out) = refs[:-2], refs[-2:]
    tables = (cosine, rising, falling)
    scale = 1.0 / math.sqrt(HD)
    queries, keys, values = queries[...], keys[...], values[...]
    segments = marks[0:1, :]

    def order(axis):
        return lax.rem(lax.broadcasted_iota(jnp.int32, (TOK, TOK), axis) + place[1], TOK)

    allowed = (as_column(segments) == segments) & (order(0) >= order(1))
    scores = jnp.where(allowed, contract_cols(queries, keys) * scale, NEGATIVE)
    top = jnp.max(scores, axis=-1, keepdims=True)
    weights = jnp.exp(scores - top)
    probs = weights / jnp.sum(weights, axis=-1, keepdims=True)
    probs_low = probs.astype(BF16)
    mixed_out[...] = plain_dot(probs_low, values).astype(BF16)
    grad_mixed = given[0][...]
    if len(given) == 2:
        grad_mixed = contract_cols(grad_mixed, given[1][...]).astype(BF16)
    grad_probs = contract_cols(grad_mixed, values)
    along = jnp.sum(probs * grad_probs, axis=-1, keepdims=True)
    grad_scores = (probs * (grad_probs - along)).astype(BF16)
    grad_query = plain_dot(grad_scores, keys) * scale
    grad_key = plain_dot(grad_scores.T, queries) * scale
    grad_value = plain_dot(probs_low.T, grad_mixed)
    grad_out[:, :HD] = turn(grad_query, tables, -1.0).astype(BF16)
    grad_out[:, HD : 2 * HD] = turn(grad_key, tables, -1.0).astype(BF16)
    grad_out[:, 2 * HD :] = grad_value.astype(BF16)


def attend(place, heads, projected, given, marks):
    column = pl.BlockSpec((TOK, HD), lambda h, s: (0, h))
    return pl.pallas_call(
        attend_kernel,
        grid_spec=pltpu.PrefetchScalarGridSpec(
            num_scalar_prefetch=1,
            grid=(heads,),
            in_specs=[column] * 3
            + [whole((TOK, 128))] * 3
            + [whole((2, TOK))]
            + ([column] if len(given) == 1 else [whole((TOK, D)), pl.BlockSpec((HD, D), lambda h, s: (h, 0))]),
            out_specs=[column, pl.BlockSpec((TOK, 3 * HD), lambda h, s: (0, h))],
        ),
        out_shape=[
            jax.ShapeDtypeStruct((TOK, heads * HD), BF16),
            jax.ShapeDtypeStruct((TOK, heads * 3 * HD), BF16),
        ],
        compiler_params=pltpu.CompilerParams(vmem_limit_bytes=VMEM),
        cost_estimate=COST,
    )(place, *projected, marks, *given)


def put_halves(core, values, scratch, mine, other):
    scratch[...] = values
    half = TOK // 2
    mine[...] = scratch[pl.ds(pl.multiple_of(core[0] * half, half), half), :]
    other[...] = scratch[pl.ds(pl.multiple_of((1 - core[0]) * half, half), half), :]


def branch_kernel(core, mixed, act, dense, down, mine, other, scratch):
    total = plain_dot(act[...], down[...]) + plain_dot(mixed[...], dense[...])
    put_halves(core, total, scratch, mine, other)


def back_kernel(
    core, packed, up_grad, qkv, up, hidden, stats, gain, gain_two, mine, other, sums, scratch
):
    first = contract_cols(packed[...], qkv[...])
    second = contract_cols(up_grad[...], up[...])
    put_halves(core, first * gain[...] + second * gain_two[...], scratch, mine, other)
    normed = (hidden[...].astype(F32) - stats[:, 0:1]) * stats[:, 64:65]
    rows = [
        jnp.sum(v, axis=0, keepdims=True) for v in (first * normed, first, second * normed, second)
    ]
    sums[...] = jnp.concatenate(rows + [jnp.zeros((4, first.shape[1]), F32)], axis=0)


def halves_call(kernel, core, operands, specs, with_sums):
    width = 512
    half = pl.BlockSpec((TOK // 2, width), lambda j, s: (0, j))
    return pl.pallas_call(
        kernel,
        grid_spec=pltpu.PrefetchScalarGridSpec(
            num_scalar_prefetch=1,
            grid=(D // width,),
            in_specs=specs,
            out_specs=[half, half] + [pl.BlockSpec((8, width), lambda j, s: (0, j))] * with_sums,
            scratch_shapes=[pltpu.VMEM((TOK, width), F32)],
        ),
        out_shape=[jax.ShapeDtypeStruct((TOK // 2, D), F32)] * 2
        + [jax.ShapeDtypeStruct((8, D), F32)] * with_sums,
        compiler_params=pltpu.CompilerParams(vmem_limit_bytes=VMEM),
        cost_estimate=COST,
    )(core, *operands)


def branch_halves(core, mixed, act, dense, down):
    specs = [whole(mixed.shape), whole(act.shape)]
    specs += [pl.BlockSpec((w.shape[0], 512), lambda j, s: (0, j)) for w in (dense, down)]
    return halves_call(branch_kernel, core, (mixed, act, dense, down), specs, False)


def back_halves(core, packed, up_grad, qkv, up, hidden, stats, gain, gain_two):
    specs = [whole(packed.shape), whole(up_grad.shape)]
    specs += [pl.BlockSpec((512, w.shape[1]), lambda j, s: (j, 0)) for w in (qkv, up)]
    specs += [pl.BlockSpec((TOK, 512), lambda j, s: (0, j)), whole((TOK, 128))]
    specs += [pl.BlockSpec((1, 512), lambda j, s: (0, j))] * 2
    operands = (packed, up_grad, qkv, up, hidden, stats, gain.reshape(1, D), gain_two.reshape(1, D))
    return halves_call(back_kernel, core, operands, specs, True)


def final_kernel(n, half, branch, combined, hidden, cot, stats, bias, bias_too, *refs):
    output, input_grad = refs[n:]
    rows = hidden[...].astype(F32)
    output[...] = rows + branch[...] + bias[...] + bias_too[...]
    e = combined[...]
    inv_std = stats[:, 64:65]
    normed = (rows - stats[:, 0:1]) * inv_std
    input_grad[...] = cot[...].astype(F32) + inv_std * (
        e
        - jnp.mean(e, axis=-1, keepdims=True)
        - normed * jnp.mean(e * normed, axis=-1, keepdims=True)
    )


def final_half(half, branch, combined, hidden, cot, stats, biases, held):
    rows = 128
    steps = TOK // 2 // rows
    given = pl.BlockSpec((rows, D), lambda i, s: (i, 0))
    placed = pl.BlockSpec((rows, D), lambda i, s: (s[0] * steps + i, 0))
    return pl.pallas_call(
        partial(final_kernel, len(held)),
        grid_spec=pltpu.PrefetchScalarGridSpec(
            num_scalar_prefetch=1,
            grid=(steps,),
            in_specs=[given, given, placed, placed]
            + [pl.BlockSpec((rows, 128), lambda i, s: (s[0] * steps + i, 0))]
            + [whole((1, D))] * 2
            + [pl.BlockSpec(memory_space=pl.ANY)] * len(held),
            out_specs=[placed, placed],
        ),
        out_shape=[jax.ShapeDtypeStruct((TOK, D), F32)] * 2,
        input_output_aliases={8: 0, 9: 1} if held else {},
        compiler_params=pltpu.CompilerParams(vmem_limit_bytes=VMEM),
        cost_estimate=COST,
    )(half, branch, combined, hidden, cot, stats, *(b.reshape(1, D) for b in biases), *held)


def joint_kernel(side, *refs):
    lefts, rights, target, held, arrived = refs[:3], refs[3:9], refs[9], refs[10:13], refs[13]
    step = pl.program_id(0)
    copies = [pltpu.make_async_copy(lefts[k], held[k], arrived.at[k]) for k in range(3)]

    @pl.when(step == 0)
    def _():
        for copy in copies:
            copy.start()

    for k, (start, stop) in enumerate(((0, 4), (4, 5), (5, 8))):

        @pl.when(step == start)
        def _(k=k):
            copies[k].wait()

        @pl.when((step >= start) & (step < stop))
        def _(k=k):
            right = jnp.concatenate([rights[2 * k][...], rights[2 * k + 1][...]], axis=0)
            total = plain_dot(held[k][...].reshape(D, 2 * TOK), right)
            target[...] = total.reshape(16, 128, -1)


def joint(side, lefts, rights):
    width = 256
    specs = [pl.BlockSpec(memory_space=pl.ANY)] * 3
    for start, n in ((0, 4), (4, 1), (5, 3)):

        def near(j, s, start=start, n=n):
            return (0, s[0] * n + jnp.clip(j - start, 0, n - 1))

        def far(j, s, start=start, n=n):
            return (0, jnp.clip(j - start, 0, n - 1))

        specs += [pl.BlockSpec((TOK, width), near), pl.BlockSpec((TOK, width), far)]
    return pl.pallas_call(
        joint_kernel,
        grid_spec=pltpu.PrefetchScalarGridSpec(
            num_scalar_prefetch=1,
            grid=(8,),
            in_specs=specs,
            out_specs=pl.BlockSpec((16, 128, width), lambda j, s: (0, 0, j)),
            scratch_shapes=[pltpu.VMEM(TURNED, BF16)] * 3 + [pltpu.SemaphoreType.DMA((3,))],
        ),
        out_shape=jax.ShapeDtypeStruct((16, 128, 8 * width), F32),
        compiler_params=pltpu.CompilerParams(vmem_limit_bytes=VMEM),
        cost_estimate=COST,
    )(side, *lefts, *rights)


def assemble_kernel(side, near, far, up, dense, qkv):
    def put(low, high):
        up[...] = jnp.concatenate([low[:, :1024], high[:, :1024]], axis=1)
        dense[...] = jnp.concatenate([low[:, 1024:1280], high[:, 1024:1280]], axis=1)
        qkv[...] = jnp.concatenate([low[:, 1280:], high[:, 1280:]], axis=1)

    @pl.when(side[0] == 0)
    def _():
        put(near[0], far[...])

    @pl.when(side[0] != 0)
    def _():
        put(far[...], near[0])


def assemble(side, near, far):
    shapes = ((64, 2048), (64, 512), (64, 1536))
    return pl.pallas_call(
        assemble_kernel,
        grid_spec=pltpu.PrefetchScalarGridSpec(
            num_scalar_prefetch=1,
            grid=(1,),
            in_specs=[
                pl.BlockSpec((1, 64, 2048), lambda i, s: (0, s[0], 0)),
                pl.BlockSpec((64, 2048), lambda i, s: (0, 0)),
            ],
            out_specs=[pl.BlockSpec(shape, lambda i, s: (0, 0)) for shape in shapes],
        ),
        out_shape=[jax.ShapeDtypeStruct(shape, F32) for shape in shapes],
        compiler_params=pltpu.CompilerParams(vmem_limit_bytes=VMEM),
        cost_estimate=COST,
    )(side, near, far)


def body(
    hidden_in,
    segment_ids,
    positions,
    ln1_gain,
    ln1_bias,
    qkv_weight,
    qkv_bias,
    dense_weight,
    dense_bias,
    ln2_gain,
    ln2_bias,
    fc1_weight,
    fc1_bias,
    fc2_weight,
    fc2_bias,
    cotangent,
):
    core = lax.axis_index("c")
    side = lax.axis_index("zl")
    half_rows = TOK // 2
    at_side = side.astype(jnp.int32).reshape(1)
    at_core = core.astype(jnp.int32).reshape(1)
    own_place = jnp.zeros((2,), jnp.int32)
    far_place = jnp.stack([side, core * half_rows]).astype(jnp.int32)
    after = lax.optimization_barrier
    params = (ln1_gain, ln1_bias, ln2_gain, ln2_bias)

    def of_core(values, which):
        return lax.dynamic_slice_in_dim(values, which * half_rows, half_rows, 0)

    marks = jnp.concatenate([segment_ids, positions]).astype(F32).reshape(1, 2 * TOK)
    hidden_sent = jnp.concatenate(
        [of_core(hidden_in, core).astype(F32), jnp.pad(marks, ((0, 7), (0, D - 2 * TOK)))], axis=0
    )
    hidden_pair = lax.all_gather(hidden_sent, "zl")

    second_in, cot_turned, stats = norm_call(
        second_kernel, 256, (hidden_in, cotangent), 1, 1, (ln2_gain, ln2_bias), stats=True
    )
    act_low, slope, down_grad = feed(second_in, cot_turned, fc1_weight, fc1_bias)
    down_sum = after(lax.psum_scatter(down_grad, ("x", "y"), scatter_dimension=0, tiled=True))
    _, cotangent, hidden_in = after((down_grad, cotangent, hidden_in))

    own_marks = marks.reshape(2, TOK)
    first_in, first_turned, second_turned = norm_call(first_kernel, 256, (hidden_in,), 1, 2, params)
    projected = project(own_place, 2, first_in, qkv_weight, qkv_bias, own_marks)
    mixed_low, grad_packed = attend(
        own_place, 2, projected, (cotangent, dense_weight), own_marks
    )
    branch, branch_other = branch_halves(at_core, mixed_low, act_low, dense_weight, fc2_weight)
    branch = branch + send(branch_other, "c")
    branch, cot_sent = after((branch, of_core(cotangent, core).astype(F32)))

    hidden_pair, branch, cot_sent = after((hidden_pair, branch, cot_sent))
    cot_got = send(cot_sent, "zl")
    hidden_got = lax.dynamic_slice_in_dim(hidden_pair, 1 - side, 1, 0)
    hidden_too = send(hidden_got, "c")

    def beside(hidden_got, hidden_too, first_turned, second_turned, slope, grad_packed):
        first_in, second_in, first_turned, second_turned = first_far(
            hidden_got, hidden_too, params, (first_turned, second_turned)
        )
        slope_side = slope_far(at_side, second_in, fc1_weight, fc1_bias)
        marks_got = hidden_got[0, half_rows, : 2 * TOK].reshape(2, 2, half_rows)
        marks_far = jnp.where(core == 0, marks_got, marks_got[:, ::-1]).reshape(2, TOK)
        projected_far = project(far_place, 1, first_in, qkv_weight, qkv_bias, marks_far)
        grad_up = feed_back(cotangent, fc2_weight, slope)
        backs = back_halves(
            at_core,
            grad_packed,
            grad_up,
            qkv_weight,
            fc1_weight,
            hidden_in,
            stats,
            ln1_gain,
            ln2_gain,
        )
        return first_turned, second_turned, slope_side, marks_far, grad_up, *backs, *projected_far

    (
        first_turned,
        second_turned,
        slope_side,
        marks_far,
        grad_up,
        combined,
        combined_other,
        norms,
        *projected_far,
    ) = lax.cond(
        core > 1,
        beside,
        beside,
        hidden_got,
        hidden_too,
        first_turned,
        second_turned,
        slope,
        grad_packed,
    )

    slope_side, cot_got, combined_other = after((slope_side, cot_got, combined_other))
    cot_too = send(cot_got, "c")
    combined_too = send(combined_other, "c")
    held = cot_far_half(0, at_side, cot_got, fc2_weight, slope_side, dense_weight, (cot_turned,))
    *held, cot_too, combined_too = after((*held, cot_too, combined_too))
    grad_up_far, grad_mixed_far, cot_turned, combined = cot_far_half(
        1,
        at_side,
        cot_too,
        fc2_weight,
        slope_side,
        dense_weight,
        held,
        (combined, combined_too),
    )
    branch, combined = after((branch, combined))
    branch = lax.psum(branch, "zh")
    combined = lax.psum(combined, "zh")
    mixed_far, grad_packed_far = attend(far_place, 1, projected_far, (grad_mixed_far,), marks_far)
    joint_grad = joint(
        at_side,
        (second_turned, cot_turned, first_turned),
        (grad_up, grad_up_far, mixed_low, mixed_far, grad_packed, grad_packed_far),
    )
    joint_grad, down_sum = after((joint_grad, down_sum))
    joint_sum = after(lax.psum_scatter(joint_grad, ("x", "y"), scatter_dimension=0, tiled=True))
    _, norms, grad_packed, grad_up, cotangent, down_sum = after(
        (joint_grad, norms, grad_packed, grad_up, cotangent, down_sum)
    )

    norms = norms[:4].reshape(4, 32, 64).transpose(1, 0, 2).reshape(32, 256)
    grad_out = cotangent.astype(F32)
    bias_sum = jnp.sum(grad_out, axis=0)
    qkv_bias_sum = jnp.sum(grad_packed.astype(F32), axis=0)
    up_bias_grad = jnp.sum(grad_up.astype(F32), axis=0)
    small = jnp.concatenate(
        [
            norms,
            bias_sum.reshape(32, 64),
            qkv_bias_sum.reshape(2, 32, 24).transpose(1, 0, 2).reshape(32, 48),
            up_bias_grad.reshape(16, 32, 4).transpose(1, 0, 2).reshape(32, 64),
            jnp.zeros((32, 80), F32),
        ],
        axis=1,
    )
    def of_side(values, which):
        return lax.dynamic_slice_in_dim(values[0], which * 64, 64, 0)

    down_far = send(of_side(down_sum, 1 - side), "zl")
    for axis in ("x", "y"):
        small = small + swap(small, axis, 1)
        small = small + swap(small, axis, 2)
        small, down_far = after((small, down_far))
    block = lax.axis_index("x") * 4 + lax.axis_index("y")
    own_small = lax.dynamic_slice_in_dim(small, side * 16 + block, 1, 0)
    far_small = lax.dynamic_slice_in_dim(small, (1 - side) * 16 + block, 1, 0)
    small = (own_small + send(far_small, "zl")).reshape(-1)

    norms = small[:256]
    norms = norms + send(norms, "c")
    norms = norms + send(norms, "zh")
    norms, branch, combined = after((norms, branch, combined))
    norms = norms.reshape(4, 64)
    bias_total = small[256:320]
    biases = (dense_bias, fc2_bias)
    own = (hidden_in, cotangent, stats, biases)
    branch_too, combined_too = send(branch, "c"), send(combined, "c")
    *finals, joint_sum = after((*final_half(at_core, branch, combined, *own, ()), joint_sum))
    output, input_grad = final_half(1 - at_core, branch_too, combined_too, *own, finals)

    down_sum = of_side(down_sum, side) + down_far
    joint_far = send(of_side(joint_sum, 1 - side), "zl")
    up_sum, dense_sum, qkv_sum = assemble(at_side, joint_sum, joint_far)
    return (
        output,
        input_grad,
        norms[0],
        norms[1],
        qkv_sum,
        small[320:368].reshape(2, 24),
        dense_sum.T,
        bias_total,
        norms[2],
        norms[3],
        up_sum,
        small[368:432].reshape(16, 4),
        down_sum.T,
        bias_total,
    )


def solution(mesh):
    fine = Mesh(mesh.devices.reshape(tuple(SIZES.values())), tuple(SIZES))
    return jax.shard_map(
        body,
        mesh=fine,
        in_specs=(
            P(DP, None),
            P(DP),
            P(DP),
            P(),
            P(),
            P(None, TENSOR),
            P(TENSOR, None),
            P(TENSOR, None),
            P(),
            P(),
            P(),
            P(None, TENSOR),
            P(TENSOR, None),
            P(TENSOR, None),
            P(),
            P(DP, None),
        ),
        out_specs=(
            P(DP, None),
            P(DP, None),
            P(DP),
            P(DP),
            P(DP, TENSOR),
            P(TENSOR, DP),
            P(TENSOR, DP),
            P(DP),
            P(DP),
            P(DP),
            P(DP, TENSOR),
            P(TENSOR, DP),
            P(TENSOR, DP),
            P(DP),
        ),
        check_vma=False,
    )
```

```python
from functools import partial
import math

import jax
import jax.numpy as jnp
import numpy as np
from jax import lax
from jax.experimental import pallas as pl
from jax.experimental.pallas import tpu as pltpu
from jax.sharding import Mesh, PartitionSpec as P

HD = 256
ROT = 64
TOK = 512
D = 2048
EPSILON = 1e-05
NEGATIVE = -1000000000.0
SIZES = {"zl": 2, "x": 4, "y": 4, "zh": 2, "c": 2}
DP = ("zl", "x", "y")
TENSOR = ("zh", "c")
F32 = jnp.float32
BF16 = jnp.bfloat16


def send(value, axis, step=1):
    n = SIZES[axis]
    return lax.ppermute(value, axis, [(i, (i + step) % n) for i in range(n)])


def swap(value, axis, bit):
    return lax.ppermute(value, axis, [(i, i ^ bit) for i in range(SIZES[axis])])


def plain_dot(left, right):
    return jnp.dot(left, right, preferred_element_type=F32)


def contract_cols(left, right):
    return lax.dot_general(left, right, (((1,), (1,)), ((), ())), preferred_element_type=F32)


VMEM = 56 * 1024 * 1024
COST = pl.CostEstimate(flops=1000000, bytes_accessed=1000000, transcendentals=0)


def whole(shape):
    return pl.BlockSpec(shape, lambda *_: (0,) * len(shape), pipeline_mode=pl.Buffered(1))


def put_turned(target, rows):
    for z in range(2):
        for pair in range(8):
            start = z * 1024 + pair * 128
            block = rows[:, start : start + 128].T.astype(BF16)
            target[2 * pair, z] = block[:64]
            target[2 * pair + 1, z] = block[64:]


def normalise(hidden):
    average = jnp.mean(hidden, axis=-1, keepdims=True)
    centred = hidden - average
    inv_std = lax.rsqrt(jnp.mean(centred * centred, axis=-1, keepdims=True) + EPSILON)
    return centred * inv_std, inv_std


def second_kernel(hidden, cot, gain, shift, second_out, cot_turned, stats):
    rows = hidden[...].astype(F32)
    average = jnp.mean(rows, axis=-1, keepdims=True)
    centred = rows - average
    inv_std = lax.rsqrt(jnp.mean(centred * centred, axis=-1, keepdims=True) + EPSILON)
    second_out[...] = (centred * inv_std * gain[...] + shift[...]).astype(BF16)
    put_turned(cot_turned, cot[...].astype(F32))
    lane = lax.broadcasted_iota(jnp.int32, (rows.shape[0], 128), 1)
    stats[...] = jnp.where(lane < 64, average, inv_std)


def first_kernel(hidden, gain, shift, gain_two, shift_two, first_out, first_turned, second_turned):
    normed, _ = normalise(hidden[...].astype(F32))
    first = normed * gain[...] + shift[...]
    first_out[...] = first.astype(BF16)
    put_turned(first_turned, first)
    put_turned(second_turned, normed * gain_two[...] + shift_two[...])


def first_far_kernel(near, other, gain, shift, gain_two, shift_two, *refs):
    first_out, second_out, first_turned, second_turned = refs[2:]

    def step(rows):
        normed, _ = normalise(rows)
        first = normed * gain[...] + shift[...]
        second = normed * gain_two[...] + shift_two[...]
        first_out[...] = first.astype(BF16)
        second_out[...] = second.astype(BF16)
        put_turned(first_turned, first)
        put_turned(second_turned, second)

    @pl.when(pl.program_id(0) < 2)
    def _():
        step(near[0])

    @pl.when(pl.program_id(0) >= 2)
    def _():
        step(other[0])


TURNED = (16, 2, 64, 2 * TOK)


def norm_call(kernel, rows, n_rows, n_plain, n_turned, params, stats=False):
    plain = pl.BlockSpec((rows, D), lambda i: (i, 0))
    return pl.pallas_call(
        kernel,
        grid=(TOK // rows,),
        in_specs=[plain] * len(n_rows) + [whole((1, D))] * len(params),
        out_specs=[plain] * n_plain
        + [pl.BlockSpec((16, 2, 64, rows), lambda i: (0, 0, 0, i))] * n_turned
        + [pl.BlockSpec((rows, 128), lambda i: (i, 0))] * stats,
        out_shape=[jax.ShapeDtypeStruct((TOK, D), BF16)] * n_plain
        + [jax.ShapeDtypeStruct(TURNED, BF16)] * n_turned
        + [jax.ShapeDtypeStruct((TOK, 128), F32)] * stats,
        compiler_params=pltpu.CompilerParams(vmem_limit_bytes=VMEM),
        cost_estimate=COST,
    )(*n_rows, *(p.reshape(1, D) for p in params))


def first_far(near, other, params, held):
    rows = 128
    plain = pl.BlockSpec((rows, D), lambda i: (i, 0))
    return pl.pallas_call(
        first_far_kernel,
        grid=(TOK // rows,),
        in_specs=[
            pl.BlockSpec((1, rows, D), lambda i: (0, lax.min(i, 1), 0)),
            pl.BlockSpec((1, rows, D), lambda i: (0, lax.max(i - 2, 0), 0)),
        ]
        + [whole((1, D))] * 4
        + [pl.BlockSpec(memory_space=pl.ANY)] * 2,
        out_specs=[plain] * 2
        + [pl.BlockSpec((16, 2, 64, rows), lambda i: (0, 0, 0, i + TOK // rows))] * 2,
        out_shape=[jax.ShapeDtypeStruct((TOK, D), BF16)] * 2
        + [jax.ShapeDtypeStruct(TURNED, BF16)] * 2,
        input_output_aliases={6: 2, 7: 3},
        compiler_params=pltpu.CompilerParams(vmem_limit_bytes=VMEM),
        cost_estimate=COST,
    )(near, other, *(p.reshape(1, D) for p in params), *held)


def phi(upward):
    return 0.5 * (1.0 + lax.erf(upward * math.sqrt(0.5)))


def gelu_slope(upward, below):
    return below + upward * (jnp.exp(-0.5 * upward * upward) * (1.0 / math.sqrt(2.0 * math.pi)))


def as_row(block):
    return jnp.concatenate([block[i : i + 1, :] for i in range(block.shape[0])], axis=1)


def feed_kernel(second, cot_turned, weight, bias, act_out, slope_out, down_grad):
    upward = plain_dot(second[...], weight[...]) + as_row(bias[0])
    below = phi(upward)
    act = (upward * below).astype(BF16)
    act_out[...] = act
    slope_out[...] = gelu_slope(upward, below)
    down_grad[...] = plain_dot(cot_turned[...].reshape(D, TOK), act).reshape(16, 128, -1)


def feed(second, cot_turned, weight, bias):
    units, width = weight.shape[1], 512
    column = pl.BlockSpec((TOK, width), lambda j: (0, j))
    return pl.pallas_call(
        feed_kernel,
        grid=(units // width,),
        in_specs=[
            whole((TOK, D)),
            whole((16, 2, 64, TOK)),
            pl.BlockSpec((D, width), lambda j: (0, j)),
            pl.BlockSpec((1, width // 128, 128), lambda j: (j, 0, 0)),
        ],
        out_specs=[column, column, pl.BlockSpec((16, 128, width), lambda j: (0, 0, j))],
        out_shape=[
            jax.ShapeDtypeStruct((TOK, units), BF16),
            jax.ShapeDtypeStruct((TOK, units), F32),
            jax.ShapeDtypeStruct((16, 128, units), F32),
        ],
        compiler_params=pltpu.CompilerParams(vmem_limit_bytes=VMEM),
        cost_estimate=COST,
    )(second, cot_turned, weight, bias.reshape(-1, width // 128, 128))


def feed_back_kernel(cot, weight, slope, up_grad):
    up_grad[...] = (contract_cols(cot[...], weight[...]) * slope[...]).astype(BF16)


def feed_back(cot, weight, slope):
    units, width = slope.shape[1], 512
    column = pl.BlockSpec((TOK, width), lambda j: (0, j))
    return pl.pallas_call(
        feed_back_kernel,
        grid=(units // width,),
        in_specs=[whole((TOK, D)), pl.BlockSpec((width, D), lambda j: (j, 0)), column],
        out_specs=column,
        out_shape=jax.ShapeDtypeStruct((TOK, units), BF16),
        compiler_params=pltpu.CompilerParams(vmem_limit_bytes=VMEM),
        cost_estimate=COST,
    )(cot, weight, slope)


def cot_far_kernel(side, near, other, weight, slope, dense, held, up_grad, grad_mixed, cot_turned, low):
    half = TOK // 2

    @pl.when(pl.program_id(0) == 0)
    def _():
        for k, rows in enumerate((near, other)):
            low[k * half : k * half + half] = rows[...].astype(BF16)
            put_turned(cot_turned.at[:, :, :, k * half : k * half + half], rows[...])
        grad_mixed[...] = contract_cols(low[...], dense[...]).astype(BF16)

    up_grad[...] = (contract_cols(low[...], weight[...]) * slope[...]).astype(BF16)


def cot_far(side, near, other, weight, slope, dense, held):
    width = 256
    steps = slope.shape[1] // width
    column = pl.BlockSpec((TOK, width), lambda j, s: (0, j))
    return pl.pallas_call(
        cot_far_kernel,
        grid_spec=pltpu.PrefetchScalarGridSpec(
            num_scalar_prefetch=1,
            grid=(steps,),
            in_specs=[
                whole((TOK // 2, D)),
                whole((TOK // 2, D)),
                pl.BlockSpec((width, D), lambda j, s: (s[0] * steps + j, 0)),
                column,
                pl.BlockSpec((HD, D), lambda j, s: (s[0], 0)),
                pl.BlockSpec(memory_space=pl.ANY),
            ],
            out_specs=[
                column,
                pl.BlockSpec((TOK, HD), lambda j, s: (0, 0)),
                pl.BlockSpec((16, 2, 64, TOK), lambda j, s: (0, 0, 0, 1)),
            ],
            scratch_shapes=[pltpu.VMEM((TOK, D), BF16)],
        ),
        out_shape=[
            jax.ShapeDtypeStruct((TOK, slope.shape[1]), BF16),
            jax.ShapeDtypeStruct((TOK, HD), BF16),
            jax.ShapeDtypeStruct(TURNED, BF16),
        ],
        input_output_aliases={6: 2},
        compiler_params=pltpu.CompilerParams(vmem_limit_bytes=VMEM),
        cost_estimate=COST,
    )(side, near, other, weight, slope, dense, held)


def slope_far_kernel(side, second, weight, bias, slope):
    upward = plain_dot(second[...], weight[...]) + as_row(bias[0])
    slope[...] = gelu_slope(upward, phi(upward))


def slope_far(side, second, weight, bias):
    units, width = weight.shape[1] // 2, 512
    steps = units // width
    return pl.pallas_call(
        slope_far_kernel,
        grid_spec=pltpu.PrefetchScalarGridSpec(
            num_scalar_prefetch=1,
            grid=(steps,),
            in_specs=[
                whole((TOK, D)),
                pl.BlockSpec((D, width), lambda j, s: (0, s[0] * steps + j)),
                pl.BlockSpec((1, width // 128, 128), lambda j, s: (s[0] * steps + j, 0, 0)),
            ],
            out_specs=pl.BlockSpec((TOK, width), lambda j, s: (0, j)),
        ),
        out_shape=jax.ShapeDtypeStruct((TOK, units), F32),
        compiler_params=pltpu.CompilerParams(vmem_limit_bytes=VMEM),
        cost_estimate=COST,
    )(side, second, weight, bias.reshape(-1, width // 128, 128))


def turn(values, tables, sign):
    first = values[:, :128]
    cosine, rising, falling = tables
    first = (
        first * cosine[...]
        + (pltpu.roll(first, 32, 1) * rising[...] + pltpu.roll(first, 96, 1) * falling[...]) * sign
    )
    return jnp.concatenate([first, values[:, 128:]], axis=1)


def as_column(row):
    return jnp.broadcast_to(row, (8, row.shape[1])).T[:, 0:1]


def cosine_and_sine(angles):
    turns = jnp.floor(angles * (2.0 / math.pi) + 0.5)
    rest = ((angles - turns * 1.5703125) - turns * 4.837512969970703e-4) - turns * 7.549789954891882e-8
    square = rest * rest
    sine = ((-1.9515295891e-4 * square + 8.3321608736e-3) * square - 1.6666654611e-1) * square
    sine = sine * rest + rest
    cosine = (2.443315711809948e-5 * square - 1.388731625493765e-3) * square + 4.166664568298827e-2
    cosine = cosine * (square * square) - 0.5 * square + 1.0
    quarter = turns.astype(jnp.int32) & 3
    odd = (quarter & 1) == 1
    flipped = jnp.where(odd, sine, cosine), jnp.where(odd, cosine, sine)
    return (
        jnp.where((quarter == 1) | (quarter == 2), -flipped[0], flipped[0]),
        jnp.where(quarter >= 2, -flipped[1], flipped[1]),
    )


def project_kernel(place, first, weight, bias, marks, inverse, queries, keys, values, *tables):
    @pl.when(pl.program_id(0) == 0)
    def _():
        angles = inverse[...] * marks[1:2, :]
        cosine, sine = cosine_and_sine(angles)
        none, rest = jnp.zeros_like(sine), jnp.zeros((64, TOK), F32)
        tables[0][...] = jnp.concatenate([cosine, cosine, rest + 1.0], axis=0).T
        tables[1][...] = jnp.concatenate([none, sine, rest], axis=0).T
        tables[2][...] = jnp.concatenate([-sine, none, rest], axis=0).T

    head = pl.program_id(0) + place[0] * (2 - pl.num_programs(0))
    packed = plain_dot(first[...], weight[...]) + bias[pl.ds(head, 1), :]
    queries[...] = turn(packed[:, :HD], tables, 1.0).astype(BF16)
    keys[...] = turn(packed[:, HD : 2 * HD], tables, 1.0).astype(BF16)
    values[...] = packed[:, 2 * HD :].astype(BF16)


def project(place, heads, first, weight, bias, marks):
    inverse = jnp.asarray((10000.0 ** (-2.0 * np.arange(32) / ROT)).astype(np.float32).reshape(32, 1))
    at = (lambda h, s: h) if heads == 2 else (lambda h, s: s[0])
    column = pl.BlockSpec((TOK, HD), lambda h, s: (0, h))
    return pl.pallas_call(
        project_kernel,
        grid_spec=pltpu.PrefetchScalarGridSpec(
            num_scalar_prefetch=1,
            grid=(heads,),
            in_specs=[
                whole((TOK, D)),
                pl.BlockSpec((D, 3 * HD), lambda h, s: (0, at(h, s))),
                whole((2, 3 * HD)),
                whole((2, TOK)),
                whole((32, 1)),
            ],
            out_specs=[column] * 3 + [pl.BlockSpec((TOK, 128), lambda h, s: (0, 0))] * 3,
        ),
        out_shape=[jax.ShapeDtypeStruct((TOK, heads * HD), BF16)] * 3
        + [jax.ShapeDtypeStruct((TOK, 128), F32)] * 3,
        compiler_params=pltpu.CompilerParams(vmem_limit_bytes=VMEM),
        cost_estimate=COST,
    )(place, first, weight, bias, marks, inverse)


def attend_kernel(place, queries, keys, values, cosine, rising, falling, marks, *refs):
    given, (mixed_out, grad_out) = refs[:-2], refs[-2:]
    tables = (cosine, rising, falling)
    scale = 1.0 / math.sqrt(HD)
    queries, keys, values = queries[...], keys[...], values[...]
    segments = marks[0:1, :]

    def order(axis):
        return lax.rem(lax.broadcasted_iota(jnp.int32, (TOK, TOK), axis) + place[1], TOK)

    allowed = (as_column(segments) == segments) & (order(0) >= order(1))
    scores = jnp.where(allowed, contract_cols(queries, keys) * scale, NEGATIVE)
    top = jnp.max(scores, axis=-1, keepdims=True)
    weights = jnp.exp(scores - top)
    probs = weights / jnp.sum(weights, axis=-1, keepdims=True)
    probs_low = probs.astype(BF16)
    mixed_out[...] = plain_dot(probs_low, values).astype(BF16)
    grad_mixed = given[0][...]
    if len(given) == 2:
        grad_mixed = contract_cols(grad_mixed, given[1][...]).astype(BF16)
    grad_probs = contract_cols(grad_mixed, values)
    along = jnp.sum(probs * grad_probs, axis=-1, keepdims=True)
    grad_scores = (probs * (grad_probs - along)).astype(BF16)
    grad_query = plain_dot(grad_scores, keys) * scale
    grad_key = plain_dot(grad_scores.T, queries) * scale
    grad_value = plain_dot(probs_low.T, grad_mixed)
    grad_out[:, :HD] = turn(grad_query, tables, -1.0).astype(BF16)
    grad_out[:, HD : 2 * HD] = turn(grad_key, tables, -1.0).astype(BF16)
    grad_out[:, 2 * HD :] = grad_value.astype(BF16)


def attend(place, heads, projected, given, marks):
    column = pl.BlockSpec((TOK, HD), lambda h, s: (0, h))
    return pl.pallas_call(
        attend_kernel,
        grid_spec=pltpu.PrefetchScalarGridSpec(
            num_scalar_prefetch=1,
            grid=(heads,),
            in_specs=[column] * 3
            + [whole((TOK, 128))] * 3
            + [whole((2, TOK))]
            + ([column] if len(given) == 1 else [whole((TOK, D)), pl.BlockSpec((HD, D), lambda h, s: (h, 0))]),
            out_specs=[column, pl.BlockSpec((TOK, 3 * HD), lambda h, s: (0, h))],
        ),
        out_shape=[
            jax.ShapeDtypeStruct((TOK, heads * HD), BF16),
            jax.ShapeDtypeStruct((TOK, heads * 3 * HD), BF16),
        ],
        compiler_params=pltpu.CompilerParams(vmem_limit_bytes=VMEM),
        cost_estimate=COST,
    )(place, *projected, marks, *given)


def put_halves(core, values, scratch, mine, other):
    scratch[...] = values
    half = TOK // 2
    mine[...] = scratch[pl.ds(pl.multiple_of(core[0] * half, half), half), :]
    other[...] = scratch[pl.ds(pl.multiple_of((1 - core[0]) * half, half), half), :]


def branch_kernel(core, mixed, act, dense, down, mine, other, scratch):
    total = plain_dot(act[...], down[...]) + plain_dot(mixed[...], dense[...])
    put_halves(core, total, scratch, mine, other)


def back_kernel(
    core, packed, up_grad, qkv, up, hidden, stats, gain, gain_two, mine, other, sums, scratch
):
    first = contract_cols(packed[...], qkv[...])
    second = contract_cols(up_grad[...], up[...])
    put_halves(core, first * gain[...] + second * gain_two[...], scratch, mine, other)
    normed = (hidden[...].astype(F32) - stats[:, 0:1]) * stats[:, 64:65]
    rows = [
        jnp.sum(v, axis=0, keepdims=True) for v in (first * normed, first, second * normed, second)
    ]
    sums[...] = jnp.concatenate(rows + [jnp.zeros((4, first.shape[1]), F32)], axis=0)


def halves_call(kernel, core, operands, specs, with_sums):
    width = 512
    half = pl.BlockSpec((TOK // 2, width), lambda j, s: (0, j))
    return pl.pallas_call(
        kernel,
        grid_spec=pltpu.PrefetchScalarGridSpec(
            num_scalar_prefetch=1,
            grid=(D // width,),
            in_specs=specs,
            out_specs=[half, half] + [pl.BlockSpec((8, width), lambda j, s: (0, j))] * with_sums,
            scratch_shapes=[pltpu.VMEM((TOK, width), F32)],
        ),
        out_shape=[jax.ShapeDtypeStruct((TOK // 2, D), F32)] * 2
        + [jax.ShapeDtypeStruct((8, D), F32)] * with_sums,
        compiler_params=pltpu.CompilerParams(vmem_limit_bytes=VMEM),
        cost_estimate=COST,
    )(core, *operands)


def branch_halves(core, mixed, act, dense, down):
    specs = [whole(mixed.shape), whole(act.shape)]
    specs += [pl.BlockSpec((w.shape[0], 512), lambda j, s: (0, j)) for w in (dense, down)]
    return halves_call(branch_kernel, core, (mixed, act, dense, down), specs, False)


def back_halves(core, packed, up_grad, qkv, up, hidden, stats, gain, gain_two):
    specs = [whole(packed.shape), whole(up_grad.shape)]
    specs += [pl.BlockSpec((512, w.shape[1]), lambda j, s: (j, 0)) for w in (qkv, up)]
    specs += [pl.BlockSpec((TOK, 512), lambda j, s: (0, j)), whole((TOK, 128))]
    specs += [pl.BlockSpec((1, 512), lambda j, s: (0, j))] * 2
    operands = (packed, up_grad, qkv, up, hidden, stats, gain.reshape(1, D), gain_two.reshape(1, D))
    return halves_call(back_kernel, core, operands, specs, True)


def final_kernel(n, half, branch, combined, hidden, cot, stats, bias, bias_too, *refs):
    output, input_grad = refs[n:]
    rows = hidden[...].astype(F32)
    output[...] = rows + branch[...] + bias[...] + bias_too[...]
    e = combined[...]
    inv_std = stats[:, 64:65]
    normed = (rows - stats[:, 0:1]) * inv_std
    input_grad[...] = cot[...].astype(F32) + inv_std * (
        e
        - jnp.mean(e, axis=-1, keepdims=True)
        - normed * jnp.mean(e * normed, axis=-1, keepdims=True)
    )


def final_half(half, branch, combined, hidden, cot, stats, biases, held):
    rows = 128
    steps = TOK // 2 // rows
    given = pl.BlockSpec((rows, D), lambda i, s: (i, 0))
    placed = pl.BlockSpec((rows, D), lambda i, s: (s[0] * steps + i, 0))
    return pl.pallas_call(
        partial(final_kernel, len(held)),
        grid_spec=pltpu.PrefetchScalarGridSpec(
            num_scalar_prefetch=1,
            grid=(steps,),
            in_specs=[given, given, placed, placed]
            + [pl.BlockSpec((rows, 128), lambda i, s: (s[0] * steps + i, 0))]
            + [whole((1, D))] * 2
            + [pl.BlockSpec(memory_space=pl.ANY)] * len(held),
            out_specs=[placed, placed],
        ),
        out_shape=[jax.ShapeDtypeStruct((TOK, D), F32)] * 2,
        input_output_aliases={8: 0, 9: 1} if held else {},
        compiler_params=pltpu.CompilerParams(vmem_limit_bytes=VMEM),
        cost_estimate=COST,
    )(half, branch, combined, hidden, cot, stats, *(b.reshape(1, D) for b in biases), *held)


def joint_kernel(side, *refs):
    lefts, rights, target, held, arrived = refs[:3], refs[3:9], refs[9], refs[10:13], refs[13]
    step = pl.program_id(0)
    copies = [pltpu.make_async_copy(lefts[k], held[k], arrived.at[k]) for k in range(3)]

    @pl.when(step == 0)
    def _():
        for copy in copies:
            copy.start()

    for k, (start, stop) in enumerate(((0, 4), (4, 5), (5, 8))):

        @pl.when(step == start)
        def _(k=k):
            copies[k].wait()

        @pl.when((step >= start) & (step < stop))
        def _(k=k):
            right = jnp.concatenate([rights[2 * k][...], rights[2 * k + 1][...]], axis=0)
            total = plain_dot(held[k][...].reshape(D, 2 * TOK), right)
            target[...] = total.reshape(16, 128, -1)


def joint(side, lefts, rights):
    width = 256
    specs = [pl.BlockSpec(memory_space=pl.ANY)] * 3
    for start, n in ((0, 4), (4, 1), (5, 3)):

        def near(j, s, start=start, n=n):
            return (0, s[0] * n + jnp.clip(j - start, 0, n - 1))

        def far(j, s, start=start, n=n):
            return (0, jnp.clip(j - start, 0, n - 1))

        specs += [pl.BlockSpec((TOK, width), near), pl.BlockSpec((TOK, width), far)]
    return pl.pallas_call(
        joint_kernel,
        grid_spec=pltpu.PrefetchScalarGridSpec(
            num_scalar_prefetch=1,
            grid=(8,),
            in_specs=specs,
            out_specs=pl.BlockSpec((16, 128, width), lambda j, s: (0, 0, j)),
            scratch_shapes=[pltpu.VMEM(TURNED, BF16)] * 3 + [pltpu.SemaphoreType.DMA((3,))],
        ),
        out_shape=jax.ShapeDtypeStruct((16, 128, 8 * width), F32),
        compiler_params=pltpu.CompilerParams(vmem_limit_bytes=VMEM),
        cost_estimate=COST,
    )(side, *lefts, *rights)


def assemble_kernel(side, near, far, up, dense, qkv):
    def put(low, high):
        up[...] = jnp.concatenate([low[:, :1024], high[:, :1024]], axis=1)
        dense[...] = jnp.concatenate([low[:, 1024:1280], high[:, 1024:1280]], axis=1)
        qkv[...] = jnp.concatenate([low[:, 1280:], high[:, 1280:]], axis=1)

    @pl.when(side[0] == 0)
    def _():
        put(near[0], far[...])

    @pl.when(side[0] != 0)
    def _():
        put(far[...], near[0])


def assemble(side, near, far):
    shapes = ((64, 2048), (64, 512), (64, 1536))
    return pl.pallas_call(
        assemble_kernel,
        grid_spec=pltpu.PrefetchScalarGridSpec(
            num_scalar_prefetch=1,
            grid=(1,),
            in_specs=[
                pl.BlockSpec((1, 64, 2048), lambda i, s: (0, s[0], 0)),
                pl.BlockSpec((64, 2048), lambda i, s: (0, 0)),
            ],
            out_specs=[pl.BlockSpec(shape, lambda i, s: (0, 0)) for shape in shapes],
        ),
        out_shape=[jax.ShapeDtypeStruct(shape, F32) for shape in shapes],
        compiler_params=pltpu.CompilerParams(vmem_limit_bytes=VMEM),
        cost_estimate=COST,
    )(side, near, far)


def body(
    hidden_in,
    segment_ids,
    positions,
    ln1_gain,
    ln1_bias,
    qkv_weight,
    qkv_bias,
    dense_weight,
    dense_bias,
    ln2_gain,
    ln2_bias,
    fc1_weight,
    fc1_bias,
    fc2_weight,
    fc2_bias,
    cotangent,
):
    core = lax.axis_index("c")
    side = lax.axis_index("zl")
    half_rows = TOK // 2
    at_side = side.astype(jnp.int32).reshape(1)
    at_core = core.astype(jnp.int32).reshape(1)
    own_place = jnp.zeros((2,), jnp.int32)
    far_place = jnp.stack([side, core * half_rows]).astype(jnp.int32)
    after = lax.optimization_barrier
    params = (ln1_gain, ln1_bias, ln2_gain, ln2_bias)

    def of_core(values, which):
        return lax.dynamic_slice_in_dim(values, which * half_rows, half_rows, 0)

    marks = jnp.concatenate([segment_ids, positions]).astype(F32).reshape(1, 2 * TOK)
    hidden_sent = jnp.concatenate(
        [of_core(hidden_in, core).astype(F32), jnp.pad(marks, ((0, 7), (0, D - 2 * TOK)))], axis=0
    )
    hidden_pair = lax.all_gather(hidden_sent, "zl")

    second_in, cot_turned, stats = norm_call(
        second_kernel, 256, (hidden_in, cotangent), 1, 1, (ln2_gain, ln2_bias), stats=True
    )
    act_low, slope, down_grad = feed(second_in, cot_turned, fc1_weight, fc1_bias)
    down_sum = after(lax.psum_scatter(down_grad, ("x", "y"), scatter_dimension=0, tiled=True))
    _, cotangent, hidden_in = after((down_grad, cotangent, hidden_in))

    cot_got = lax.ppermute(
        of_core(cotangent, core).astype(F32), ("zl", "zh"), [(i, 3 - i) for i in range(4)]
    )

    own_marks = marks.reshape(2, TOK)

    def own_step(hidden_in, cotangent, slope):
        first_in, first_turned, second_turned = norm_call(
            first_kernel, 256, (hidden_in,), 1, 2, params
        )
        projected = project(own_place, 2, first_in, qkv_weight, qkv_bias, own_marks)
        mixed_low, grad_packed = attend(
            own_place, 2, projected, (cotangent, dense_weight), own_marks
        )
        grad_up = feed_back(cotangent, fc2_weight, slope)
        return first_turned, second_turned, mixed_low, grad_packed, grad_up

    first_turned, second_turned, mixed_low, grad_packed, grad_up = lax.cond(
        core > 1, own_step, own_step, hidden_in, cotangent, slope
    )
    hidden_pair, cot_got, mixed_low = after((hidden_pair, cot_got, mixed_low))
    hidden_got = lax.dynamic_slice_in_dim(hidden_pair, 1 - side, 1, 0)
    hidden_too, cot_too = send(hidden_got, "c"), send(cot_got, "c")
    branch, branch_other = branch_halves(at_core, mixed_low, act_low, dense_weight, fc2_weight)
    hidden_too, branch_other = after((hidden_too, branch_other))
    branch_too = send(branch_other, "c")

    first_far_in, second_far_in, first_turned, second_turned = first_far(
        hidden_got, hidden_too, params, (first_turned, second_turned)
    )
    second_far_in, branch_too = after((second_far_in, branch_too))
    branch = lax.psum(branch + branch_too, "zh")
    slope_side = slope_far(at_side, second_far_in, fc1_weight, fc1_bias)
    marks_got = hidden_got[0, half_rows, : 2 * TOK].reshape(2, 2, half_rows)
    marks_far = jnp.where(core == 0, marks_got, marks_got[:, ::-1]).reshape(2, TOK)
    projected_far = project(far_place, 1, first_far_in, qkv_weight, qkv_bias, marks_far)
    grad_up_far, grad_mixed_far, cot_turned = cot_far(
        at_side, cot_got, cot_too, fc2_weight, slope_side, dense_weight, cot_turned
    )
    mixed_far, grad_packed_far = attend(
        far_place, 1, projected_far, (grad_mixed_far,), marks_far
    )
    joint_grad = joint(
        at_side,
        (second_turned, cot_turned, first_turned),
        (grad_up, grad_up_far, mixed_low, mixed_far, grad_packed, grad_packed_far),
    )
    joint_grad, down_sum = after((joint_grad, down_sum))
    joint_sum = after(lax.psum_scatter(joint_grad, ("x", "y"), scatter_dimension=0, tiled=True))
    _, grad_packed, grad_up, cotangent, down_sum = after(
        (joint_grad, grad_packed, grad_up, cotangent, down_sum)
    )

    combined, combined_other, norms = back_halves(
        at_core, grad_packed, grad_up, qkv_weight, fc1_weight, hidden_in, stats, ln1_gain, ln2_gain
    )
    combined = combined + send(combined_other, "c")
    combined_too = send(combined, "zh")

    norms = norms[:4].reshape(4, 32, 64).transpose(1, 0, 2).reshape(32, 256)
    grad_out = cotangent.astype(F32)
    bias_sum = jnp.sum(grad_out, axis=0)
    qkv_bias_sum = jnp.sum(grad_packed.astype(F32), axis=0)
    up_bias_grad = jnp.sum(grad_up.astype(F32), axis=0)
    small = jnp.concatenate(
        [
            norms,
            bias_sum.reshape(32, 64),
            qkv_bias_sum.reshape(2, 32, 24).transpose(1, 0, 2).reshape(32, 48),
            up_bias_grad.reshape(16, 32, 4).transpose(1, 0, 2).reshape(32, 64),
            jnp.zeros((32, 80), F32),
        ],
        axis=1,
    )
    def of_side(values, which):
        return lax.dynamic_slice_in_dim(values[0], which * 64, 64, 0)

    down_far = send(of_side(down_sum, 1 - side), "zl")
    for axis in ("x", "y"):
        small = small + swap(small, axis, 1)
        small = small + swap(small, axis, 2)
        small, down_far = after((small, down_far))
    block = lax.axis_index("x") * 4 + lax.axis_index("y")
    own_small = lax.dynamic_slice_in_dim(small, side * 16 + block, 1, 0)
    far_small = lax.dynamic_slice_in_dim(small, (1 - side) * 16 + block, 1, 0)
    small = (own_small + send(far_small, "zl")).reshape(-1)

    norms = small[:256]
    norms = norms + send(norms, "c")
    norms = norms + send(norms, "zh")
    norms, branch, combined_too = after((norms, branch, combined_too))
    combined = combined + combined_too
    norms = norms.reshape(4, 64)
    bias_total = small[256:320]
    biases = (dense_bias, fc2_bias)
    own = (hidden_in, cotangent, stats, biases)
    branch_too, combined_too = send(branch, "c"), send(combined, "c")
    finals = final_half(at_core, branch, combined, *own, ())
    finals = final_half(1 - at_core, branch_too, combined_too, *own, finals)
    output, input_grad, joint_sum = after((*finals, joint_sum))

    down_sum = of_side(down_sum, side) + down_far
    joint_far = send(of_side(joint_sum, 1 - side), "zl")
    up_sum, dense_sum, qkv_sum = assemble(at_side, joint_sum, joint_far)
    return (
        output,
        input_grad,
        norms[0],
        norms[1],
        qkv_sum,
        small[320:368].reshape(2, 24),
        dense_sum.T,
        bias_total,
        norms[2],
        norms[3],
        up_sum,
        small[368:432].reshape(16, 4),
        down_sum.T,
        bias_total,
    )


def solution(mesh):
    fine = Mesh(mesh.devices.reshape(tuple(SIZES.values())), tuple(SIZES))
    return jax.shard_map(
        body,
        mesh=fine,
        in_specs=(
            P(DP, None),
            P(DP),
            P(DP),
            P(),
            P(),
            P(None, TENSOR),
            P(TENSOR, None),
            P(TENSOR, None),
            P(),
            P(),
            P(),
            P(None, TENSOR),
            P(TENSOR, None),
            P(TENSOR, None),
            P(),
            P(DP, None),
        ),
        out_specs=(
            P(DP, None),
            P(DP, None),
            P(DP),
            P(DP),
            P(DP, TENSOR),
            P(TENSOR, DP),
            P(TENSOR, DP),
            P(DP),
            P(DP),
            P(DP),
            P(DP, TENSOR),
            P(TENSOR, DP),
            P(TENSOR, DP),
            P(DP),
        ),
        check_vma=False,
    )
```

```python
from functools import partial
import math

import jax
import jax.numpy as jnp
import numpy as np
from jax import lax
from jax.experimental import pallas as pl
from jax.experimental.pallas import tpu as pltpu
from jax.sharding import Mesh, PartitionSpec as P

HD = 256
ROT = 64
TOK = 512
D = 2048
EPSILON = 1e-05
NEGATIVE = -1000000000.0
SIZES = {"zl": 2, "x": 4, "y": 4, "zh": 2, "c": 2}
DP = ("zl", "x", "y")
TENSOR = ("zh", "c")
F32 = jnp.float32
BF16 = jnp.bfloat16


def send(value, axis, step=1):
    n = SIZES[axis]
    return lax.ppermute(value, axis, [(i, (i + step) % n) for i in range(n)])


def swap(value, axis, bit):
    return lax.ppermute(value, axis, [(i, i ^ bit) for i in range(SIZES[axis])])


def plain_dot(left, right):
    return jnp.dot(left, right, preferred_element_type=F32)


def contract_cols(left, right):
    return lax.dot_general(left, right, (((1,), (1,)), ((), ())), preferred_element_type=F32)


VMEM = 56 * 1024 * 1024
COST = pl.CostEstimate(flops=1000000, bytes_accessed=1000000, transcendentals=0)


def whole(shape):
    return pl.BlockSpec(shape, lambda *_: (0,) * len(shape), pipeline_mode=pl.Buffered(1))


def put_turned(target, rows):
    for z in range(2):
        for pair in range(8):
            start = z * 1024 + pair * 128
            block = rows[:, start : start + 128].T.astype(BF16)
            target[2 * pair, z] = block[:64]
            target[2 * pair + 1, z] = block[64:]


def normalise(hidden):
    average = jnp.mean(hidden, axis=-1, keepdims=True)
    centred = hidden - average
    inv_std = lax.rsqrt(jnp.mean(centred * centred, axis=-1, keepdims=True) + EPSILON)
    return centred * inv_std, inv_std


def second_kernel(core, hidden, cot, gain, shift, second_out, cot_turned, stats, sent):
    rows = hidden[...].astype(F32)

    @pl.when(pl.program_id(0) == core[0])
    def _():
        sent[...] = rows

    average = jnp.mean(rows, axis=-1, keepdims=True)
    centred = rows - average
    inv_std = lax.rsqrt(jnp.mean(centred * centred, axis=-1, keepdims=True) + EPSILON)
    second_out[...] = (centred * inv_std * gain[...] + shift[...]).astype(BF16)
    put_turned(cot_turned, cot[...].astype(F32))
    lane = lax.broadcasted_iota(jnp.int32, (rows.shape[0], 128), 1)
    stats[...] = jnp.where(lane < 64, average, inv_std)


def second(core, hidden, cot, gain, shift):
    rows = TOK // 2
    plain = pl.BlockSpec((rows, D), lambda i, s: (i, 0))
    return pl.pallas_call(
        second_kernel,
        grid_spec=pltpu.PrefetchScalarGridSpec(
            num_scalar_prefetch=1,
            grid=(2,),
            in_specs=[plain] * 2 + [whole((1, D))] * 2,
            out_specs=[
                plain,
                pl.BlockSpec((16, 2, 64, rows), lambda i, s: (0, 0, 0, i)),
                pl.BlockSpec((rows, 128), lambda i, s: (i, 0)),
                pl.BlockSpec((rows, D), lambda i, s: (0, 0)),
            ],
        ),
        out_shape=[
            jax.ShapeDtypeStruct((TOK, D), BF16),
            jax.ShapeDtypeStruct(TURNED, BF16),
            jax.ShapeDtypeStruct((TOK, 128), F32),
            jax.ShapeDtypeStruct((rows, D), F32),
        ],
        compiler_params=pltpu.CompilerParams(vmem_limit_bytes=VMEM),
        cost_estimate=COST,
    )(core, hidden, cot, gain.reshape(1, D), shift.reshape(1, D))


def first_kernel(hidden, gain, shift, gain_two, shift_two, first_out, first_turned, second_turned):
    normed, _ = normalise(hidden[...].astype(F32))
    first = normed * gain[...] + shift[...]
    first_out[...] = first.astype(BF16)
    put_turned(first_turned, first)
    put_turned(second_turned, normed * gain_two[...] + shift_two[...])


def first_far_kernel(near, other, gain, shift, gain_two, shift_two, *refs):
    first_out, second_out, first_turned, second_turned = refs[2:]

    def step(rows):
        normed, _ = normalise(rows)
        first = normed * gain[...] + shift[...]
        second = normed * gain_two[...] + shift_two[...]
        first_out[...] = first.astype(BF16)
        second_out[...] = second.astype(BF16)
        put_turned(first_turned, first)
        put_turned(second_turned, second)

    @pl.when(pl.program_id(0) < 2)
    def _():
        step(near[0])

    @pl.when(pl.program_id(0) >= 2)
    def _():
        step(other[0])


TURNED = (16, 2, 64, 2 * TOK)


def norm_call(kernel, rows, n_rows, n_plain, n_turned, params):
    plain = pl.BlockSpec((rows, D), lambda i: (i, 0))
    return pl.pallas_call(
        kernel,
        grid=(TOK // rows,),
        in_specs=[plain] * len(n_rows) + [whole((1, D))] * len(params),
        out_specs=[plain] * n_plain
        + [pl.BlockSpec((16, 2, 64, rows), lambda i: (0, 0, 0, i))] * n_turned,
        out_shape=[jax.ShapeDtypeStruct((TOK, D), BF16)] * n_plain
        + [jax.ShapeDtypeStruct(TURNED, BF16)] * n_turned,
        compiler_params=pltpu.CompilerParams(vmem_limit_bytes=VMEM),
        cost_estimate=COST,
    )(*n_rows, *(p.reshape(1, D) for p in params))


def first_far(near, other, params, held):
    rows = 128
    plain = pl.BlockSpec((rows, D), lambda i: (i, 0))
    return pl.pallas_call(
        first_far_kernel,
        grid=(TOK // rows,),
        in_specs=[
            pl.BlockSpec((1, rows, D), lambda i: (0, lax.min(i, 1), 0)),
            pl.BlockSpec((1, rows, D), lambda i: (0, lax.max(i - 2, 0), 0)),
        ]
        + [whole((1, D))] * 4
        + [pl.BlockSpec(memory_space=pl.ANY)] * 2,
        out_specs=[plain] * 2
        + [pl.BlockSpec((16, 2, 64, rows), lambda i: (0, 0, 0, i + TOK // rows))] * 2,
        out_shape=[jax.ShapeDtypeStruct((TOK, D), BF16)] * 2
        + [jax.ShapeDtypeStruct(TURNED, BF16)] * 2,
        input_output_aliases={6: 2, 7: 3},
        compiler_params=pltpu.CompilerParams(vmem_limit_bytes=VMEM),
        cost_estimate=COST,
    )(near, other, *(p.reshape(1, D) for p in params), *held)


def phi(upward):
    return 0.5 * (1.0 + lax.erf(upward * math.sqrt(0.5)))


def gelu_slope(upward, below):
    return below + upward * (jnp.exp(-0.5 * upward * upward) * (1.0 / math.sqrt(2.0 * math.pi)))


def as_row(block):
    return jnp.concatenate([block[i : i + 1, :] for i in range(block.shape[0])], axis=1)


def feed_kernel(second, cot_turned, weight, bias, act_out, slope_out, down_grad):
    upward = plain_dot(second[...], weight[...]) + as_row(bias[0])
    below = phi(upward)
    act = (upward * below).astype(BF16)
    act_out[...] = act
    slope_out[...] = gelu_slope(upward, below)
    down_grad[...] = plain_dot(cot_turned[...].reshape(D, TOK), act).reshape(16, 128, -1)


def feed(second, cot_turned, weight, bias):
    units, width = weight.shape[1], 512
    column = pl.BlockSpec((TOK, width), lambda j: (0, j))
    return pl.pallas_call(
        feed_kernel,
        grid=(units // width,),
        in_specs=[
            whole((TOK, D)),
            whole((16, 2, 64, TOK)),
            pl.BlockSpec((D, width), lambda j: (0, j)),
            pl.BlockSpec((1, width // 128, 128), lambda j: (j, 0, 0)),
        ],
        out_specs=[column, column, pl.BlockSpec((16, 128, width), lambda j: (0, 0, j))],
        out_shape=[
            jax.ShapeDtypeStruct((TOK, units), BF16),
            jax.ShapeDtypeStruct((TOK, units), F32),
            jax.ShapeDtypeStruct((16, 128, units), F32),
        ],
        compiler_params=pltpu.CompilerParams(vmem_limit_bytes=VMEM),
        cost_estimate=COST,
    )(second, cot_turned, weight, bias.reshape(-1, width // 128, 128))


def feed_back_kernel(cot, weight, slope, up_grad):
    up_grad[...] = (contract_cols(cot[...], weight[...]) * slope[...]).astype(BF16)


def feed_back(cot, weight, slope):
    units, width = slope.shape[1], 512
    column = pl.BlockSpec((TOK, width), lambda j: (0, j))
    return pl.pallas_call(
        feed_back_kernel,
        grid=(units // width,),
        in_specs=[whole((TOK, D)), pl.BlockSpec((width, D), lambda j: (j, 0)), column],
        out_specs=column,
        out_shape=jax.ShapeDtypeStruct((TOK, units), BF16),
        compiler_params=pltpu.CompilerParams(vmem_limit_bytes=VMEM),
        cost_estimate=COST,
    )(cot, weight, slope)


def cot_far_kernel(side, near, other, weight, slope, dense, held, up_grad, grad_mixed, cot_turned, low):
    half = TOK // 2

    @pl.when(pl.program_id(0) == 0)
    def _():
        for k, rows in enumerate((near, other)):
            low[k * half : k * half + half] = rows[...].astype(BF16)
            put_turned(cot_turned.at[:, :, :, k * half : k * half + half], rows[...])
        grad_mixed[...] = contract_cols(low[...], dense[...]).astype(BF16)

    up_grad[...] = (contract_cols(low[...], weight[...]) * slope[...]).astype(BF16)


def cot_far(side, near, other, weight, slope, dense, held):
    width = 256
    steps = slope.shape[1] // width
    column = pl.BlockSpec((TOK, width), lambda j, s: (0, j))
    return pl.pallas_call(
        cot_far_kernel,
        grid_spec=pltpu.PrefetchScalarGridSpec(
            num_scalar_prefetch=1,
            grid=(steps,),
            in_specs=[
                whole((TOK // 2, D)),
                whole((TOK // 2, D)),
                pl.BlockSpec((width, D), lambda j, s: (s[0] * steps + j, 0)),
                column,
                pl.BlockSpec((HD, D), lambda j, s: (s[0], 0)),
                pl.BlockSpec(memory_space=pl.ANY),
            ],
            out_specs=[
                column,
                pl.BlockSpec((TOK, HD), lambda j, s: (0, 0)),
                pl.BlockSpec((16, 2, 64, TOK), lambda j, s: (0, 0, 0, 1)),
            ],
            scratch_shapes=[pltpu.VMEM((TOK, D), BF16)],
        ),
        out_shape=[
            jax.ShapeDtypeStruct((TOK, slope.shape[1]), BF16),
            jax.ShapeDtypeStruct((TOK, HD), BF16),
            jax.ShapeDtypeStruct(TURNED, BF16),
        ],
        input_output_aliases={6: 2},
        compiler_params=pltpu.CompilerParams(vmem_limit_bytes=VMEM),
        cost_estimate=COST,
    )(side, near, other, weight, slope, dense, held)


def slope_far_kernel(side, second, weight, bias, slope):
    upward = plain_dot(second[...], weight[...]) + as_row(bias[0])
    slope[...] = gelu_slope(upward, phi(upward))


def slope_far(side, second, weight, bias):
    units, width = weight.shape[1] // 2, 512
    steps = units // width
    return pl.pallas_call(
        slope_far_kernel,
        grid_spec=pltpu.PrefetchScalarGridSpec(
            num_scalar_prefetch=1,
            grid=(steps,),
            in_specs=[
                whole((TOK, D)),
                pl.BlockSpec((D, width), lambda j, s: (0, s[0] * steps + j)),
                pl.BlockSpec((1, width // 128, 128), lambda j, s: (s[0] * steps + j, 0, 0)),
            ],
            out_specs=pl.BlockSpec((TOK, width), lambda j, s: (0, j)),
        ),
        out_shape=jax.ShapeDtypeStruct((TOK, units), F32),
        compiler_params=pltpu.CompilerParams(vmem_limit_bytes=VMEM),
        cost_estimate=COST,
    )(side, second, weight, bias.reshape(-1, width // 128, 128))


def turn(values, tables, sign):
    first = values[:, :128]
    cosine, rising, falling = tables
    first = (
        first * cosine[...]
        + (pltpu.roll(first, 32, 1) * rising[...] + pltpu.roll(first, 96, 1) * falling[...]) * sign
    )
    return jnp.concatenate([first, values[:, 128:]], axis=1)


def as_column(row):
    return jnp.broadcast_to(row, (8, row.shape[1])).T[:, 0:1]


def cosine_and_sine(angles):
    turns = jnp.floor(angles * (2.0 / math.pi) + 0.5)
    rest = ((angles - turns * 1.5703125) - turns * 4.837512969970703e-4) - turns * 7.549789954891882e-8
    square = rest * rest
    sine = ((-1.9515295891e-4 * square + 8.3321608736e-3) * square - 1.6666654611e-1) * square
    sine = sine * rest + rest
    cosine = (2.443315711809948e-5 * square - 1.388731625493765e-3) * square + 4.166664568298827e-2
    cosine = cosine * (square * square) - 0.5 * square + 1.0
    quarter = turns.astype(jnp.int32) & 3
    odd = (quarter & 1) == 1
    flipped = jnp.where(odd, sine, cosine), jnp.where(odd, cosine, sine)
    return (
        jnp.where((quarter == 1) | (quarter == 2), -flipped[0], flipped[0]),
        jnp.where(quarter >= 2, -flipped[1], flipped[1]),
    )


def project_kernel(place, first, weight, bias, marks, inverse, queries, keys, values, *tables):
    @pl.when(pl.program_id(0) == 0)
    def _():
        angles = inverse[...] * marks[1:2, :]
        cosine, sine = cosine_and_sine(angles)
        none, rest = jnp.zeros_like(sine), jnp.zeros((64, TOK), F32)
        tables[0][...] = jnp.concatenate([cosine, cosine, rest + 1.0], axis=0).T
        tables[1][...] = jnp.concatenate([none, sine, rest], axis=0).T
        tables[2][...] = jnp.concatenate([-sine, none, rest], axis=0).T

    head = pl.program_id(0) + place[0] * (2 - pl.num_programs(0))
    packed = plain_dot(first[...], weight[...]) + bias[pl.ds(head, 1), :]
    queries[...] = turn(packed[:, :HD], tables, 1.0).astype(BF16)
    keys[...] = turn(packed[:, HD : 2 * HD], tables, 1.0).astype(BF16)
    values[...] = packed[:, 2 * HD :].astype(BF16)


def project(place, heads, first, weight, bias, marks):
    inverse = jnp.asarray((10000.0 ** (-2.0 * np.arange(32) / ROT)).astype(np.float32).reshape(32, 1))
    at = (lambda h, s: h) if heads == 2 else (lambda h, s: s[0])
    column = pl.BlockSpec((TOK, HD), lambda h, s: (0, h))
    return pl.pallas_call(
        project_kernel,
        grid_spec=pltpu.PrefetchScalarGridSpec(
            num_scalar_prefetch=1,
            grid=(heads,),
            in_specs=[
                whole((TOK, D)),
                pl.BlockSpec((D, 3 * HD), lambda h, s: (0, at(h, s))),
                whole((2, 3 * HD)),
                whole((2, TOK)),
                whole((32, 1)),
            ],
            out_specs=[column] * 3 + [pl.BlockSpec((TOK, 128), lambda h, s: (0, 0))] * 3,
        ),
        out_shape=[jax.ShapeDtypeStruct((TOK, heads * HD), BF16)] * 3
        + [jax.ShapeDtypeStruct((TOK, 128), F32)] * 3,
        compiler_params=pltpu.CompilerParams(vmem_limit_bytes=VMEM),
        cost_estimate=COST,
    )(place, first, weight, bias, marks, inverse)


def attend_kernel(place, queries, keys, values, cosine, rising, falling, marks, *refs):
    given, (mixed_out, grad_out) = refs[:-2], refs[-2:]
    tables = (cosine, rising, falling)
    scale = 1.0 / math.sqrt(HD)
    queries, keys, values = queries[...], keys[...], values[...]
    segments = marks[0:1, :]

    def order(axis):
        return lax.rem(lax.broadcasted_iota(jnp.int32, (TOK, TOK), axis) + place[1], TOK)

    allowed = (as_column(segments) == segments) & (order(0) >= order(1))
    scores = jnp.where(allowed, contract_cols(queries, keys) * scale, NEGATIVE)
    top = jnp.max(scores, axis=-1, keepdims=True)
    weights = jnp.exp(scores - top)
    probs = weights / jnp.sum(weights, axis=-1, keepdims=True)
    probs_low = probs.astype(BF16)
    mixed_out[...] = plain_dot(probs_low, values).astype(BF16)
    grad_mixed = given[0][...]
    if len(given) == 2:
        grad_mixed = contract_cols(grad_mixed, given[1][...]).astype(BF16)
    grad_probs = contract_cols(grad_mixed, values)
    along = jnp.sum(probs * grad_probs, axis=-1, keepdims=True)
    grad_scores = (probs * (grad_probs - along)).astype(BF16)
    grad_query = plain_dot(grad_scores, keys) * scale
    grad_key = plain_dot(grad_scores.T, queries) * scale
    grad_value = plain_dot(probs_low.T, grad_mixed)
    grad_out[:, :HD] = turn(grad_query, tables, -1.0).astype(BF16)
    grad_out[:, HD : 2 * HD] = turn(grad_key, tables, -1.0).astype(BF16)
    grad_out[:, 2 * HD :] = grad_value.astype(BF16)


def attend(place, heads, projected, given, marks):
    column = pl.BlockSpec((TOK, HD), lambda h, s: (0, h))
    return pl.pallas_call(
        attend_kernel,
        grid_spec=pltpu.PrefetchScalarGridSpec(
            num_scalar_prefetch=1,
            grid=(heads,),
            in_specs=[column] * 3
            + [whole((TOK, 128))] * 3
            + [whole((2, TOK))]
            + ([column] if len(given) == 1 else [whole((TOK, D)), pl.BlockSpec((HD, D), lambda h, s: (h, 0))]),
            out_specs=[column, pl.BlockSpec((TOK, 3 * HD), lambda h, s: (0, h))],
        ),
        out_shape=[
            jax.ShapeDtypeStruct((TOK, heads * HD), BF16),
            jax.ShapeDtypeStruct((TOK, heads * 3 * HD), BF16),
        ],
        compiler_params=pltpu.CompilerParams(vmem_limit_bytes=VMEM),
        cost_estimate=COST,
    )(place, *projected, marks, *given)


def put_halves(core, values, scratch, mine, other):
    scratch[...] = values
    half = TOK // 2
    mine[...] = scratch[pl.ds(pl.multiple_of(core[0] * half, half), half), :]
    other[...] = scratch[pl.ds(pl.multiple_of((1 - core[0]) * half, half), half), :]


def branch_kernel(core, mixed, act, dense, down, mine, other, scratch):
    total = plain_dot(act[...], down[...]) + plain_dot(mixed[...], dense[...])
    put_halves(core, total, scratch, mine, other)


def back_kernel(
    core, packed, up_grad, qkv, up, hidden, stats, gain, gain_two, mine, other, sums, scratch
):
    first = contract_cols(packed[...], qkv[...])
    second = contract_cols(up_grad[...], up[...])
    put_halves(core, first * gain[...] + second * gain_two[...], scratch, mine, other)
    normed = (hidden[...].astype(F32) - stats[:, 0:1]) * stats[:, 64:65]
    rows = [
        jnp.sum(v, axis=0, keepdims=True) for v in (first * normed, first, second * normed, second)
    ]
    sums[...] = jnp.concatenate(rows + [jnp.zeros((4, first.shape[1]), F32)], axis=0)


def halves_call(kernel, core, operands, specs, with_sums):
    width = 512
    half = pl.BlockSpec((TOK // 2, width), lambda j, s: (0, j))
    return pl.pallas_call(
        kernel,
        grid_spec=pltpu.PrefetchScalarGridSpec(
            num_scalar_prefetch=1,
            grid=(D // width,),
            in_specs=specs,
            out_specs=[half, half] + [pl.BlockSpec((8, width), lambda j, s: (0, j))] * with_sums,
            scratch_shapes=[pltpu.VMEM((TOK, width), F32)],
        ),
        out_shape=[jax.ShapeDtypeStruct((TOK // 2, D), F32)] * 2
        + [jax.ShapeDtypeStruct((8, D), F32)] * with_sums,
        compiler_params=pltpu.CompilerParams(vmem_limit_bytes=VMEM),
        cost_estimate=COST,
    )(core, *operands)


def branch_halves(core, mixed, act, dense, down):
    specs = [whole(mixed.shape), whole(act.shape)]
    specs += [pl.BlockSpec((w.shape[0], 512), lambda j, s: (0, j)) for w in (dense, down)]
    return halves_call(branch_kernel, core, (mixed, act, dense, down), specs, False)


def back_halves(core, packed, up_grad, qkv, up, hidden, stats, gain, gain_two):
    specs = [whole(packed.shape), whole(up_grad.shape)]
    specs += [pl.BlockSpec((512, w.shape[1]), lambda j, s: (j, 0)) for w in (qkv, up)]
    specs += [pl.BlockSpec((TOK, 512), lambda j, s: (0, j)), whole((TOK, 128))]
    specs += [pl.BlockSpec((1, 512), lambda j, s: (0, j))] * 2
    operands = (packed, up_grad, qkv, up, hidden, stats, gain.reshape(1, D), gain_two.reshape(1, D))
    return halves_call(back_kernel, core, operands, specs, True)


def final_kernel(n, half, branch, combined, hidden, cot, stats, bias, bias_too, *refs):
    output, input_grad = refs[n:]
    rows = hidden[...].astype(F32)
    output[...] = rows + branch[...] + bias[...] + bias_too[...]
    e = combined[...]
    inv_std = stats[:, 64:65]
    normed = (rows - stats[:, 0:1]) * inv_std
    input_grad[...] = cot[...].astype(F32) + inv_std * (
        e
        - jnp.mean(e, axis=-1, keepdims=True)
        - normed * jnp.mean(e * normed, axis=-1, keepdims=True)
    )


def final_half(half, branch, combined, hidden, cot, stats, biases, held):
    rows = 128
    steps = TOK // 2 // rows
    given = pl.BlockSpec((rows, D), lambda i, s: (i, 0))
    placed = pl.BlockSpec((rows, D), lambda i, s: (s[0] * steps + i, 0))
    return pl.pallas_call(
        partial(final_kernel, len(held)),
        grid_spec=pltpu.PrefetchScalarGridSpec(
            num_scalar_prefetch=1,
            grid=(steps,),
            in_specs=[given, given, placed, placed]
            + [pl.BlockSpec((rows, 128), lambda i, s: (s[0] * steps + i, 0))]
            + [whole((1, D))] * 2
            + [pl.BlockSpec(memory_space=pl.ANY)] * len(held),
            out_specs=[placed, placed],
        ),
        out_shape=[jax.ShapeDtypeStruct((TOK, D), F32)] * 2,
        input_output_aliases={8: 0, 9: 1} if held else {},
        compiler_params=pltpu.CompilerParams(vmem_limit_bytes=VMEM),
        cost_estimate=COST,
    )(half, branch, combined, hidden, cot, stats, *(b.reshape(1, D) for b in biases), *held)


def joint_kernel(side, *refs):
    lefts, rights, target, held, arrived = refs[:3], refs[3:9], refs[9], refs[10:13], refs[13]
    step = pl.program_id(0)
    copies = [pltpu.make_async_copy(lefts[k], held[k], arrived.at[k]) for k in range(3)]

    @pl.when(step == 0)
    def _():
        for copy in copies:
            copy.start()

    for k, (start, stop) in enumerate(((0, 4), (4, 5), (5, 8))):

        @pl.when(step == start)
        def _(k=k):
            copies[k].wait()

        @pl.when((step >= start) & (step < stop))
        def _(k=k):
            right = jnp.concatenate([rights[2 * k][...], rights[2 * k + 1][...]], axis=0)
            total = plain_dot(held[k][...].reshape(D, 2 * TOK), right)
            target[...] = total.reshape(16, 128, -1)


def joint(side, lefts, rights):
    width = 256
    specs = [pl.BlockSpec(memory_space=pl.ANY)] * 3
    for start, n in ((0, 4), (4, 1), (5, 3)):

        def near(j, s, start=start, n=n):
            return (0, s[0] * n + jnp.clip(j - start, 0, n - 1))

        def far(j, s, start=start, n=n):
            return (0, jnp.clip(j - start, 0, n - 1))

        specs += [pl.BlockSpec((TOK, width), near), pl.BlockSpec((TOK, width), far)]
    return pl.pallas_call(
        joint_kernel,
        grid_spec=pltpu.PrefetchScalarGridSpec(
            num_scalar_prefetch=1,
            grid=(8,),
            in_specs=specs,
            out_specs=pl.BlockSpec((16, 128, width), lambda j, s: (0, 0, j)),
            scratch_shapes=[pltpu.VMEM(TURNED, BF16)] * 3 + [pltpu.SemaphoreType.DMA((3,))],
        ),
        out_shape=jax.ShapeDtypeStruct((16, 128, 8 * width), F32),
        compiler_params=pltpu.CompilerParams(vmem_limit_bytes=VMEM),
        cost_estimate=COST,
    )(side, *lefts, *rights)


def assemble_kernel(side, near, far, up, dense, qkv):
    def put(low, high):
        up[...] = jnp.concatenate([low[:, :1024], high[:, :1024]], axis=1)
        dense[...] = jnp.concatenate([low[:, 1024:1280], high[:, 1024:1280]], axis=1)
        qkv[...] = jnp.concatenate([low[:, 1280:], high[:, 1280:]], axis=1)

    @pl.when(side[0] == 0)
    def _():
        put(near[0], far[...])

    @pl.when(side[0] != 0)
    def _():
        put(far[...], near[0])


def assemble(side, near, far):
    shapes = ((64, 2048), (64, 512), (64, 1536))
    return pl.pallas_call(
        assemble_kernel,
        grid_spec=pltpu.PrefetchScalarGridSpec(
            num_scalar_prefetch=1,
            grid=(1,),
            in_specs=[
                pl.BlockSpec((1, 64, 2048), lambda i, s: (0, s[0], 0)),
                pl.BlockSpec((64, 2048), lambda i, s: (0, 0)),
            ],
            out_specs=[pl.BlockSpec(shape, lambda i, s: (0, 0)) for shape in shapes],
        ),
        out_shape=[jax.ShapeDtypeStruct(shape, F32) for shape in shapes],
        compiler_params=pltpu.CompilerParams(vmem_limit_bytes=VMEM),
        cost_estimate=COST,
    )(side, near, far)


def body(
    hidden_in,
    segment_ids,
    positions,
    ln1_gain,
    ln1_bias,
    qkv_weight,
    qkv_bias,
    dense_weight,
    dense_bias,
    ln2_gain,
    ln2_bias,
    fc1_weight,
    fc1_bias,
    fc2_weight,
    fc2_bias,
    cotangent,
):
    core = lax.axis_index("c")
    side = lax.axis_index("zl")
    half_rows = TOK // 2
    at_side = side.astype(jnp.int32).reshape(1)
    at_core = core.astype(jnp.int32).reshape(1)
    own_place = jnp.zeros((2,), jnp.int32)
    far_place = jnp.stack([side, core * half_rows]).astype(jnp.int32)
    after = lax.optimization_barrier
    params = (ln1_gain, ln1_bias, ln2_gain, ln2_bias)

    def of_core(values, which):
        return lax.dynamic_slice_in_dim(values, which * half_rows, half_rows, 0)

    second_in, cot_turned, stats, hidden_sent = second(
        at_core, hidden_in, cotangent, ln2_gain, ln2_bias
    )
    hidden_pair = lax.all_gather(hidden_sent, "zl")
    act_low, slope, down_grad = feed(second_in, cot_turned, fc1_weight, fc1_bias)
    down_sum = after(lax.psum_scatter(down_grad, ("x", "y"), scatter_dimension=0, tiled=True))
    _, cotangent, hidden_in = after((down_grad, cotangent, hidden_in))

    marks = jnp.concatenate([segment_ids, positions]).astype(F32).reshape(1, 2 * TOK)
    cot_sent = jnp.concatenate(
        [of_core(cotangent, core).astype(F32), jnp.pad(marks, ((0, 7), (0, D - 2 * TOK)))], axis=0
    )
    cot_got = lax.ppermute(cot_sent, ("zl", "zh"), [(i, 3 - i) for i in range(4)])

    own_marks = marks.reshape(2, TOK)

    def own_step(hidden_in, cotangent, act_low, slope):
        first_in, first_turned, second_turned = norm_call(
            first_kernel, 256, (hidden_in,), 1, 2, params
        )
        projected = project(own_place, 2, first_in, qkv_weight, qkv_bias, own_marks)
        mixed_low, grad_packed = attend(
            own_place, 2, projected, (cotangent, dense_weight), own_marks
        )
        grad_up = feed_back(cotangent, fc2_weight, slope)
        branches = branch_halves(at_core, mixed_low, act_low, dense_weight, fc2_weight)
        return first_turned, second_turned, mixed_low, grad_packed, grad_up, *branches

    (
        first_turned,
        second_turned,
        mixed_low,
        grad_packed,
        grad_up,
        branch,
        branch_other,
    ) = lax.cond(core > 1, own_step, own_step, hidden_in, cotangent, act_low, slope)
    hidden_pair, mixed_low = after((hidden_pair, mixed_low))
    hidden_got = lax.dynamic_slice_in_dim(hidden_pair, 1 - side, 1, 0)
    hidden_too, branch_too = send(hidden_got, "c"), send(branch_other, "c")
    hidden_too, cot_got = after((hidden_too, cot_got))
    cot_too = send(cot_got, "c")

    first_far_in, second_far_in, first_turned, second_turned = first_far(
        hidden_got, hidden_too, params, (first_turned, second_turned)
    )
    second_far_in, branch_too = after((second_far_in, branch_too))
    branch = lax.psum(branch + branch_too, "zh")
    slope_side = slope_far(at_side, second_far_in, fc1_weight, fc1_bias)
    marks_got = cot_got[half_rows, : 2 * TOK].reshape(2, 2, half_rows)
    marks_far = jnp.where(core == 0, marks_got, marks_got[:, ::-1]).reshape(2, TOK)
    projected_far = project(far_place, 1, first_far_in, qkv_weight, qkv_bias, marks_far)
    grad_up_far, grad_mixed_far, cot_turned = cot_far(
        at_side, cot_got, cot_too, fc2_weight, slope_side, dense_weight, cot_turned
    )
    mixed_far, grad_packed_far = attend(
        far_place, 1, projected_far, (grad_mixed_far,), marks_far
    )
    joint_grad = joint(
        at_side,
        (second_turned, cot_turned, first_turned),
        (grad_up, grad_up_far, mixed_low, mixed_far, grad_packed, grad_packed_far),
    )
    joint_grad, down_sum = after((joint_grad, down_sum))
    joint_sum = after(lax.psum_scatter(joint_grad, ("x", "y"), scatter_dimension=0, tiled=True))
    _, grad_packed, grad_up, cotangent, down_sum = after(
        (joint_grad, grad_packed, grad_up, cotangent, down_sum)
    )

    combined, combined_other, norms = back_halves(
        at_core, grad_packed, grad_up, qkv_weight, fc1_weight, hidden_in, stats, ln1_gain, ln2_gain
    )
    combined = combined + send(combined_other, "c")
    combined_too = send(combined, "zh")

    norms = norms[:4].reshape(4, 32, 64).transpose(1, 0, 2).reshape(32, 256)
    grad_out = cotangent.astype(F32)
    bias_sum = jnp.sum(grad_out, axis=0)
    qkv_bias_sum = jnp.sum(grad_packed.astype(F32), axis=0)
    up_bias_grad = jnp.sum(grad_up.astype(F32), axis=0)
    small = jnp.concatenate(
        [
            norms,
            bias_sum.reshape(32, 64),
            qkv_bias_sum.reshape(2, 32, 24).transpose(1, 0, 2).reshape(32, 48),
            up_bias_grad.reshape(16, 32, 4).transpose(1, 0, 2).reshape(32, 64),
            jnp.zeros((32, 80), F32),
        ],
        axis=1,
    )
    def of_side(values, which):
        return lax.dynamic_slice_in_dim(values[0], which * 64, 64, 0)

    down_far = send(of_side(down_sum, 1 - side), "zl")
    for axis in ("x", "y"):
        small = small + swap(small, axis, 1)
        small = small + swap(small, axis, 2)
    block = lax.axis_index("x") * 4 + lax.axis_index("y")
    own_small = lax.dynamic_slice_in_dim(small, side * 16 + block, 1, 0)
    far_small = lax.dynamic_slice_in_dim(small, (1 - side) * 16 + block, 1, 0)
    small = (own_small + send(far_small, "zl")).reshape(-1)

    norms = small[:256]
    norms = norms + send(norms, "c")
    norms = norms + send(norms, "zh")
    norms, branch, combined_too, down_far = after((norms, branch, combined_too, down_far))
    combined = combined + combined_too
    norms = norms.reshape(4, 64)
    bias_total = small[256:320]
    biases = (dense_bias, fc2_bias)
    own = (hidden_in, cotangent, stats, biases)
    branch_too, combined_too = send(branch, "c"), send(combined, "c")
    finals = final_half(at_core, branch, combined, *own, ())
    finals = final_half(1 - at_core, branch_too, combined_too, *own, finals)
    output, input_grad, joint_sum = after((*finals, joint_sum))

    down_sum = of_side(down_sum, side) + down_far
    joint_far = send(of_side(joint_sum, 1 - side), "zl")
    up_sum, dense_sum, qkv_sum = assemble(at_side, joint_sum, joint_far)
    return (
        output,
        input_grad,
        norms[0],
        norms[1],
        qkv_sum,
        small[320:368].reshape(2, 24),
        dense_sum.T,
        bias_total,
        norms[2],
        norms[3],
        up_sum,
        small[368:432].reshape(16, 4),
        down_sum.T,
        bias_total,
    )


def solution(mesh):
    fine = Mesh(mesh.devices.reshape(tuple(SIZES.values())), tuple(SIZES))
    return jax.shard_map(
        body,
        mesh=fine,
        in_specs=(
            P(DP, None),
            P(DP),
            P(DP),
            P(),
            P(),
            P(None, TENSOR),
            P(TENSOR, None),
            P(TENSOR, None),
            P(),
            P(),
            P(),
            P(None, TENSOR),
            P(TENSOR, None),
            P(TENSOR, None),
            P(),
            P(DP, None),
        ),
        out_specs=(
            P(DP, None),
            P(DP, None),
            P(DP),
            P(DP),
            P(DP, TENSOR),
            P(TENSOR, DP),
            P(TENSOR, DP),
            P(DP),
            P(DP),
            P(DP),
            P(DP, TENSOR),
            P(TENSOR, DP),
            P(TENSOR, DP),
            P(DP),
        ),
        check_vma=False,
    )
```

```python
from functools import partial
import math

import jax
import jax.numpy as jnp
import numpy as np
from jax import lax
from jax.experimental import pallas as pl
from jax.experimental.pallas import tpu as pltpu
from jax.sharding import Mesh, PartitionSpec as P

HD = 256
ROT = 64
TOK = 512
D = 2048
EPSILON = 1e-05
NEGATIVE = -1000000000.0
SIZES = {"zl": 2, "x": 4, "y": 4, "zh": 2, "c": 2}
DP = ("zl", "x", "y")
TENSOR = ("zh", "c")
F32 = jnp.float32
BF16 = jnp.bfloat16


def send(value, axis, step=1):
    n = SIZES[axis]
    return lax.ppermute(value, axis, [(i, (i + step) % n) for i in range(n)])


def swap(value, axis, bit):
    return lax.ppermute(value, axis, [(i, i ^ bit) for i in range(SIZES[axis])])


def plain_dot(left, right):
    return jnp.dot(left, right, preferred_element_type=F32)


def contract_cols(left, right):
    return lax.dot_general(left, right, (((1,), (1,)), ((), ())), preferred_element_type=F32)


VMEM = 56 * 1024 * 1024
VMEM_LESS = 24 * 1024 * 1024
COST = pl.CostEstimate(flops=1000000, bytes_accessed=1000000, transcendentals=0)


def whole(shape):
    return pl.BlockSpec(shape, lambda *_: (0,) * len(shape), pipeline_mode=pl.Buffered(1))


def put_turned(target, rows):
    for z in range(2):
        for pair in range(8):
            start = z * 1024 + pair * 128
            block = rows[:, start : start + 128].T.astype(BF16)
            target[2 * pair, z] = block[:64]
            target[2 * pair + 1, z] = block[64:]


def normalise(hidden):
    average = jnp.mean(hidden, axis=-1, keepdims=True)
    centred = hidden - average
    inv_std = lax.rsqrt(jnp.mean(centred * centred, axis=-1, keepdims=True) + EPSILON)
    return centred * inv_std, inv_std


def second_kernel(core, hidden, gain, shift, second_out, stats, sent):
    rows = hidden[...].astype(F32)

    @pl.when(pl.program_id(0) == core[0])
    def _():
        sent[...] = rows

    average = jnp.mean(rows, axis=-1, keepdims=True)
    centred = rows - average
    inv_std = lax.rsqrt(jnp.mean(centred * centred, axis=-1, keepdims=True) + EPSILON)
    second_out[...] = (centred * inv_std * gain[...] + shift[...]).astype(BF16)
    lane = lax.broadcasted_iota(jnp.int32, (rows.shape[0], 128), 1)
    stats[...] = jnp.where(lane < 64, average, inv_std)


def second(core, hidden, gain, shift):
    rows = TOK // 2
    plain = pl.BlockSpec((rows, D), lambda i, s: (i, 0))
    return pl.pallas_call(
        second_kernel,
        grid_spec=pltpu.PrefetchScalarGridSpec(
            num_scalar_prefetch=1,
            grid=(2,),
            in_specs=[plain] + [whole((1, D))] * 2,
            out_specs=[
                plain,
                pl.BlockSpec((rows, 128), lambda i, s: (i, 0)),
                pl.BlockSpec((rows, D), lambda i, s: (0, 0)),
            ],
        ),
        out_shape=[
            jax.ShapeDtypeStruct((TOK, D), BF16),
            jax.ShapeDtypeStruct((TOK, 128), F32),
            jax.ShapeDtypeStruct((rows, D), F32),
        ],
        compiler_params=pltpu.CompilerParams(vmem_limit_bytes=VMEM),
        cost_estimate=COST,
    )(core, hidden, gain.reshape(1, D), shift.reshape(1, D))


def first_kernel(
    hidden, cot, gain, shift, gain_two, shift_two, first_out, first_turned, second_turned, cot_turned
):
    normed, _ = normalise(hidden[...].astype(F32))
    first = normed * gain[...] + shift[...]
    first_out[...] = first.astype(BF16)
    put_turned(first_turned, first)
    put_turned(second_turned, normed * gain_two[...] + shift_two[...])
    put_turned(cot_turned, cot[...].astype(F32))


def first_far_kernel(near, other, gain, shift, gain_two, shift_two, *refs):
    first_out, second_out, first_turned, second_turned = refs[2:]

    def step(rows):
        normed, _ = normalise(rows)
        first = normed * gain[...] + shift[...]
        second = normed * gain_two[...] + shift_two[...]
        first_out[...] = first.astype(BF16)
        second_out[...] = second.astype(BF16)
        put_turned(first_turned, first)
        put_turned(second_turned, second)

    @pl.when(pl.program_id(0) < 2)
    def _():
        step(near[0])

    @pl.when(pl.program_id(0) >= 2)
    def _():
        step(other[0])


TURNED = (16, 2, 64, 2 * TOK)


def norm_call(kernel, rows, n_rows, n_plain, n_turned, params):
    plain = pl.BlockSpec((rows, D), lambda i: (i, 0))
    return pl.pallas_call(
        kernel,
        grid=(TOK // rows,),
        in_specs=[plain] * len(n_rows) + [whole((1, D))] * len(params),
        out_specs=[plain] * n_plain
        + [pl.BlockSpec((16, 2, 64, rows), lambda i: (0, 0, 0, i))] * n_turned,
        out_shape=[jax.ShapeDtypeStruct((TOK, D), BF16)] * n_plain
        + [jax.ShapeDtypeStruct(TURNED, BF16)] * n_turned,
        compiler_params=pltpu.CompilerParams(vmem_limit_bytes=VMEM),
        cost_estimate=COST,
    )(*n_rows, *(p.reshape(1, D) for p in params))


def first_far(near, other, params, held):
    rows = 128
    plain = pl.BlockSpec((rows, D), lambda i: (i, 0))
    return pl.pallas_call(
        first_far_kernel,
        grid=(TOK // rows,),
        in_specs=[
            pl.BlockSpec((1, rows, D), lambda i: (0, lax.min(i, 1), 0)),
            pl.BlockSpec((1, rows, D), lambda i: (0, lax.max(i - 2, 0), 0)),
        ]
        + [whole((1, D))] * 4
        + [pl.BlockSpec(memory_space=pl.ANY)] * 2,
        out_specs=[plain] * 2
        + [pl.BlockSpec((16, 2, 64, rows), lambda i: (0, 0, 0, i + TOK // rows))] * 2,
        out_shape=[jax.ShapeDtypeStruct((TOK, D), BF16)] * 2
        + [jax.ShapeDtypeStruct(TURNED, BF16)] * 2,
        input_output_aliases={6: 2, 7: 3},
        compiler_params=pltpu.CompilerParams(vmem_limit_bytes=VMEM),
        cost_estimate=COST,
    )(near, other, *(p.reshape(1, D) for p in params), *held)


def phi(upward):
    return 0.5 * (1.0 + lax.erf(upward * math.sqrt(0.5)))


def gelu_slope(upward, below):
    return below + upward * (jnp.exp(-0.5 * upward * upward) * (1.0 / math.sqrt(2.0 * math.pi)))


def as_row(block):
    return jnp.concatenate([block[i : i + 1, :] for i in range(block.shape[0])], axis=1)


def feed_kernel(second, cot, weight, bias, act_out, slope_out, down_grad):
    upward = plain_dot(second[...], weight[...]) + as_row(bias[0])
    below = phi(upward)
    act = (upward * below).astype(BF16)
    act_out[...] = act
    slope_out[...] = gelu_slope(upward, below)
    total = lax.dot_general(cot[...], act, (((0,), (0,)), ((), ())), preferred_element_type=F32)
    for z in range(2):
        rows = total[z * 1024 : z * 1024 + 1024]
        down_grad[:, z * 64 : z * 64 + 64] = rows.reshape(16, 64, -1)


def feed(second, cot, weight, bias):
    units, width = weight.shape[1], 512
    column = pl.BlockSpec((TOK, width), lambda j: (0, j))
    return pl.pallas_call(
        feed_kernel,
        grid=(units // width,),
        in_specs=[
            whole((TOK, D)),
            whole((TOK, D)),
            pl.BlockSpec((D, width), lambda j: (0, j)),
            pl.BlockSpec((1, width // 128, 128), lambda j: (j, 0, 0)),
        ],
        out_specs=[column, column, pl.BlockSpec((16, 128, width), lambda j: (0, 0, j))],
        out_shape=[
            jax.ShapeDtypeStruct((TOK, units), BF16),
            jax.ShapeDtypeStruct((TOK, units), F32),
            jax.ShapeDtypeStruct((16, 128, units), F32),
        ],
        compiler_params=pltpu.CompilerParams(vmem_limit_bytes=VMEM),
        cost_estimate=COST,
    )(second, cot, weight, bias.reshape(-1, width // 128, 128))


def feed_back_kernel(cot, weight, slope, up_grad):
    up_grad[...] = (contract_cols(cot[...], weight[...]) * slope[...]).astype(BF16)


def feed_back(cot, weight, slope):
    units, width = slope.shape[1], 512
    column = pl.BlockSpec((TOK, width), lambda j: (0, j))
    return pl.pallas_call(
        feed_back_kernel,
        grid=(units // width,),
        in_specs=[whole((TOK, D)), pl.BlockSpec((width, D), lambda j: (j, 0)), column],
        out_specs=column,
        out_shape=jax.ShapeDtypeStruct((TOK, units), BF16),
        compiler_params=pltpu.CompilerParams(vmem_limit_bytes=VMEM),
        cost_estimate=COST,
    )(cot, weight, slope)


def cot_far_kernel(side, near, other, weight, slope, dense, held, up_grad, grad_mixed, cot_turned, low):
    half = TOK // 2

    @pl.when(pl.program_id(0) == 0)
    def _():
        for k, rows in enumerate((near, other)):
            low[k * half : k * half + half] = rows[...].astype(BF16)
            put_turned(cot_turned.at[:, :, :, k * half : k * half + half], rows[...])
        grad_mixed[...] = contract_cols(low[...], dense[...]).astype(BF16)

    up_grad[...] = (contract_cols(low[...], weight[...]) * slope[...]).astype(BF16)


def cot_far(side, near, other, weight, slope, dense, held):
    width = 256
    steps = slope.shape[1] // width
    column = pl.BlockSpec((TOK, width), lambda j, s: (0, j))
    return pl.pallas_call(
        cot_far_kernel,
        grid_spec=pltpu.PrefetchScalarGridSpec(
            num_scalar_prefetch=1,
            grid=(steps,),
            in_specs=[
                whole((TOK // 2, D)),
                whole((TOK // 2, D)),
                pl.BlockSpec((width, D), lambda j, s: (s[0] * steps + j, 0)),
                column,
                pl.BlockSpec((HD, D), lambda j, s: (s[0], 0)),
                pl.BlockSpec(memory_space=pl.ANY),
            ],
            out_specs=[
                column,
                pl.BlockSpec((TOK, HD), lambda j, s: (0, 0)),
                pl.BlockSpec((16, 2, 64, TOK), lambda j, s: (0, 0, 0, 1)),
            ],
            scratch_shapes=[pltpu.VMEM((TOK, D), BF16)],
        ),
        out_shape=[
            jax.ShapeDtypeStruct((TOK, slope.shape[1]), BF16),
            jax.ShapeDtypeStruct((TOK, HD), BF16),
            jax.ShapeDtypeStruct(TURNED, BF16),
        ],
        input_output_aliases={6: 2},
        compiler_params=pltpu.CompilerParams(vmem_limit_bytes=VMEM),
        cost_estimate=COST,
    )(side, near, other, weight, slope, dense, held)


def slope_far_kernel(side, second, weight, bias, sums, sums_too, slope, total):
    upward = plain_dot(second[...], weight[...]) + as_row(bias[0])
    slope[...] = gelu_slope(upward, phi(upward))
    total[...] = sums[...] + sums_too[...]


def slope_far(side, second, weight, bias, sums, sums_too):
    units, width = weight.shape[1] // 2, 512
    steps = units // width
    piece = pl.BlockSpec((TOK // 2 // steps, D), lambda j, s: (j, 0))
    return pl.pallas_call(
        slope_far_kernel,
        grid_spec=pltpu.PrefetchScalarGridSpec(
            num_scalar_prefetch=1,
            grid=(steps,),
            in_specs=[
                whole((TOK, D)),
                pl.BlockSpec((D, width), lambda j, s: (0, s[0] * steps + j)),
                pl.BlockSpec((1, width // 128, 128), lambda j, s: (s[0] * steps + j, 0, 0)),
                piece,
                piece,
            ],
            out_specs=[pl.BlockSpec((TOK, width), lambda j, s: (0, j)), piece],
        ),
        out_shape=[
            jax.ShapeDtypeStruct((TOK, units), F32),
            jax.ShapeDtypeStruct((TOK // 2, D), F32),
        ],
        compiler_params=pltpu.CompilerParams(vmem_limit_bytes=VMEM),
        cost_estimate=COST,
    )(side, second, weight, bias.reshape(-1, width // 128, 128), sums, sums_too)


def turn(values, tables, sign):
    first = values[:, :128]
    cosine, rising, falling = tables
    first = (
        first * cosine[...]
        + (pltpu.roll(first, 32, 1) * rising[...] + pltpu.roll(first, 96, 1) * falling[...]) * sign
    )
    return jnp.concatenate([first, values[:, 128:]], axis=1)


def as_column(row):
    return jnp.broadcast_to(row, (8, row.shape[1])).T[:, 0:1]


def cosine_and_sine(angles):
    turns = jnp.floor(angles * (2.0 / math.pi) + 0.5)
    rest = ((angles - turns * 1.5703125) - turns * 4.837512969970703e-4) - turns * 7.549789954891882e-8
    square = rest * rest
    sine = ((-1.9515295891e-4 * square + 8.3321608736e-3) * square - 1.6666654611e-1) * square
    sine = sine * rest + rest
    cosine = (2.443315711809948e-5 * square - 1.388731625493765e-3) * square + 4.166664568298827e-2
    cosine = cosine * (square * square) - 0.5 * square + 1.0
    quarter = turns.astype(jnp.int32) & 3
    odd = (quarter & 1) == 1
    flipped = jnp.where(odd, sine, cosine), jnp.where(odd, cosine, sine)
    return (
        jnp.where((quarter == 1) | (quarter == 2), -flipped[0], flipped[0]),
        jnp.where(quarter >= 2, -flipped[1], flipped[1]),
    )


def project_kernel(place, first, weight, bias, marks, inverse, queries, keys, values, *tables):
    @pl.when(pl.program_id(0) == 0)
    def _():
        angles = inverse[...] * marks[1:2, :]
        cosine, sine = cosine_and_sine(angles)
        none, rest = jnp.zeros_like(sine), jnp.zeros((64, TOK), F32)
        tables[0][...] = jnp.concatenate([cosine, cosine, rest + 1.0], axis=0).T
        tables[1][...] = jnp.concatenate([none, sine, rest], axis=0).T
        tables[2][...] = jnp.concatenate([-sine, none, rest], axis=0).T

    head = pl.program_id(0) + place[0] * (2 - pl.num_programs(0))
    packed = plain_dot(first[...], weight[...]) + bias[pl.ds(head, 1), :]
    queries[...] = turn(packed[:, :HD], tables, 1.0).astype(BF16)
    keys[...] = turn(packed[:, HD : 2 * HD], tables, 1.0).astype(BF16)
    values[...] = packed[:, 2 * HD :].astype(BF16)


def project(place, heads, first, weight, bias, marks):
    inverse = jnp.asarray((10000.0 ** (-2.0 * np.arange(32) / ROT)).astype(np.float32).reshape(32, 1))
    at = (lambda h, s: h) if heads == 2 else (lambda h, s: s[0])
    column = pl.BlockSpec((TOK, HD), lambda h, s: (0, h))
    return pl.pallas_call(
        project_kernel,
        grid_spec=pltpu.PrefetchScalarGridSpec(
            num_scalar_prefetch=1,
            grid=(heads,),
            in_specs=[
                whole((TOK, D)),
                pl.BlockSpec((D, 3 * HD), lambda h, s: (0, at(h, s))),
                whole((2, 3 * HD)),
                whole((2, TOK)),
                whole((32, 1)),
            ],
            out_specs=[column] * 3 + [pl.BlockSpec((TOK, 128), lambda h, s: (0, 0))] * 3,
        ),
        out_shape=[jax.ShapeDtypeStruct((TOK, heads * HD), BF16)] * 3
        + [jax.ShapeDtypeStruct((TOK, 128), F32)] * 3,
        compiler_params=pltpu.CompilerParams(vmem_limit_bytes=VMEM),
        cost_estimate=COST,
    )(place, first, weight, bias, marks, inverse)


def attend_kernel(place, queries, keys, values, cosine, rising, falling, marks, *refs):
    given, (mixed_out, grad_out) = refs[:-2], refs[-2:]
    tables = (cosine, rising, falling)
    scale = 1.0 / math.sqrt(HD)
    queries, keys, values = queries[...], keys[...], values[...]
    segments = marks[0:1, :]

    def order(axis):
        return lax.rem(lax.broadcasted_iota(jnp.int32, (TOK, TOK), axis) + place[1], TOK)

    allowed = (as_column(segments) == segments) & (order(0) >= order(1))
    scores = jnp.where(allowed, contract_cols(queries, keys) * scale, NEGATIVE)
    top = jnp.max(scores, axis=-1, keepdims=True)
    weights = jnp.exp(scores - top)
    probs = weights / jnp.sum(weights, axis=-1, keepdims=True)
    probs_low = probs.astype(BF16)
    mixed_out[...] = plain_dot(probs_low, values).astype(BF16)
    grad_mixed = given[0][...]
    if len(given) == 2:
        grad_mixed = contract_cols(grad_mixed, given[1][...]).astype(BF16)
    grad_probs = contract_cols(grad_mixed, values)
    along = jnp.sum(probs * grad_probs, axis=-1, keepdims=True)
    grad_scores = (probs * (grad_probs - along)).astype(BF16)
    grad_query = plain_dot(grad_scores, keys) * scale
    grad_key = plain_dot(grad_scores.T, queries) * scale
    grad_value = plain_dot(probs_low.T, grad_mixed)
    grad_out[:, :HD] = turn(grad_query, tables, -1.0).astype(BF16)
    grad_out[:, HD : 2 * HD] = turn(grad_key, tables, -1.0).astype(BF16)
    grad_out[:, 2 * HD :] = grad_value.astype(BF16)


def attend(place, heads, projected, given, marks):
    column = pl.BlockSpec((TOK, HD), lambda h, s: (0, h))
    return pl.pallas_call(
        attend_kernel,
        grid_spec=pltpu.PrefetchScalarGridSpec(
            num_scalar_prefetch=1,
            grid=(heads,),
            in_specs=[column] * 3
            + [whole((TOK, 128))] * 3
            + [whole((2, TOK))]
            + ([column] if len(given) == 1 else [whole((TOK, D)), pl.BlockSpec((HD, D), lambda h, s: (h, 0))]),
            out_specs=[column, pl.BlockSpec((TOK, 3 * HD), lambda h, s: (0, h))],
        ),
        out_shape=[
            jax.ShapeDtypeStruct((TOK, heads * HD), BF16),
            jax.ShapeDtypeStruct((TOK, heads * 3 * HD), BF16),
        ],
        compiler_params=pltpu.CompilerParams(vmem_limit_bytes=VMEM),
        cost_estimate=COST,
    )(place, *projected, marks, *given)


def put_halves(core, values, scratch, mine, other):
    scratch[...] = values
    half = TOK // 2
    mine[...] = scratch[pl.ds(pl.multiple_of(core[0] * half, half), half), :]
    other[...] = scratch[pl.ds(pl.multiple_of((1 - core[0]) * half, half), half), :]


def branch_kernel(core, mixed, act, dense, down, mine, other, scratch):
    total = plain_dot(act[...], down[...]) + plain_dot(mixed[...], dense[...])
    put_halves(core, total, scratch, mine, other)


def back_kernel(
    core, packed, up_grad, qkv, up, hidden, stats, gain, gain_two, mine, other, sums, scratch
):
    first = contract_cols(packed[...], qkv[...])
    second = contract_cols(up_grad[...], up[...])
    put_halves(core, first * gain[...] + second * gain_two[...], scratch, mine, other)
    normed = (hidden[...].astype(F32) - stats[:, 0:1]) * stats[:, 64:65]
    rows = [
        jnp.sum(v, axis=0, keepdims=True) for v in (first * normed, first, second * normed, second)
    ]
    sums[...] = jnp.concatenate(rows + [jnp.zeros((4, first.shape[1]), F32)], axis=0)


def halves_call(kernel, core, operands, specs, with_sums):
    width = 512
    half = pl.BlockSpec((TOK // 2, width), lambda j, s: (0, j))
    return pl.pallas_call(
        kernel,
        grid_spec=pltpu.PrefetchScalarGridSpec(
            num_scalar_prefetch=1,
            grid=(D // width,),
            in_specs=specs,
            out_specs=[half, half] + [pl.BlockSpec((8, width), lambda j, s: (0, j))] * with_sums,
            scratch_shapes=[pltpu.VMEM((TOK, width), F32)],
        ),
        out_shape=[jax.ShapeDtypeStruct((TOK // 2, D), F32)] * 2
        + [jax.ShapeDtypeStruct((8, D), F32)] * with_sums,
        compiler_params=pltpu.CompilerParams(vmem_limit_bytes=VMEM),
        cost_estimate=COST,
    )(core, *operands)


def branch_halves(core, mixed, act, dense, down):
    specs = [whole(mixed.shape), whole(act.shape)]
    specs += [pl.BlockSpec((w.shape[0], 512), lambda j, s: (0, j)) for w in (dense, down)]
    return halves_call(branch_kernel, core, (mixed, act, dense, down), specs, False)


def back_halves(core, packed, up_grad, qkv, up, hidden, stats, gain, gain_two):
    specs = [whole(packed.shape), whole(up_grad.shape)]
    specs += [pl.BlockSpec((512, w.shape[1]), lambda j, s: (j, 0)) for w in (qkv, up)]
    specs += [pl.BlockSpec((TOK, 512), lambda j, s: (0, j)), whole((TOK, 128))]
    specs += [pl.BlockSpec((1, 512), lambda j, s: (0, j))] * 2
    operands = (packed, up_grad, qkv, up, hidden, stats, gain.reshape(1, D), gain_two.reshape(1, D))
    return halves_call(back_kernel, core, operands, specs, True)


def final_kernel(n, half, branch, combined, hidden, cot, stats, bias, bias_too, *refs):
    output, input_grad = refs[n:]
    rows = hidden[...].astype(F32)
    output[...] = rows + branch[...] + bias[...] + bias_too[...]
    e = combined[...]
    inv_std = stats[:, 64:65]
    normed = (rows - stats[:, 0:1]) * inv_std
    input_grad[...] = cot[...].astype(F32) + inv_std * (
        e
        - jnp.mean(e, axis=-1, keepdims=True)
        - normed * jnp.mean(e * normed, axis=-1, keepdims=True)
    )


def final_half(half, branch, combined, hidden, cot, stats, biases, held):
    rows = 128
    steps = TOK // 2 // rows
    given = pl.BlockSpec((rows, D), lambda i, s: (i, 0))
    placed = pl.BlockSpec((rows, D), lambda i, s: (s[0] * steps + i, 0))
    return pl.pallas_call(
        partial(final_kernel, len(held)),
        grid_spec=pltpu.PrefetchScalarGridSpec(
            num_scalar_prefetch=1,
            grid=(steps,),
            in_specs=[given, given, placed, placed]
            + [pl.BlockSpec((rows, 128), lambda i, s: (s[0] * steps + i, 0))]
            + [whole((1, D))] * 2
            + [pl.BlockSpec(memory_space=pl.ANY)] * len(held),
            out_specs=[placed, placed],
        ),
        out_shape=[jax.ShapeDtypeStruct((TOK, D), F32)] * 2,
        input_output_aliases={8: 0, 9: 1} if held else {},
        compiler_params=pltpu.CompilerParams(vmem_limit_bytes=VMEM_LESS),
        cost_estimate=COST,
    )(half, branch, combined, hidden, cot, stats, *(b.reshape(1, D) for b in biases), *held)


def joint_kernel(side, *refs):
    lefts, rights, target, held, arrived = refs[:3], refs[3:9], refs[9], refs[10:13], refs[13]
    step = pl.program_id(0)
    copies = [pltpu.make_async_copy(lefts[k], held[k], arrived.at[k]) for k in range(3)]

    @pl.when(step == 0)
    def _():
        for copy in copies:
            copy.start()

    for k, (start, stop) in enumerate(((0, 4), (4, 5), (5, 8))):

        @pl.when(step == start)
        def _(k=k):
            copies[k].wait()

        @pl.when((step >= start) & (step < stop))
        def _(k=k):
            right = jnp.concatenate([rights[2 * k][...], rights[2 * k + 1][...]], axis=0)
            total = plain_dot(held[k][...].reshape(D, 2 * TOK), right)
            target[...] = total.reshape(16, 128, -1)


def joint(side, lefts, rights):
    width = 256
    specs = [pl.BlockSpec(memory_space=pl.ANY)] * 3
    for start, n in ((0, 4), (4, 1), (5, 3)):

        def near(j, s, start=start, n=n):
            return (0, s[0] * n + jnp.clip(j - start, 0, n - 1))

        def far(j, s, start=start, n=n):
            return (0, jnp.clip(j - start, 0, n - 1))

        specs += [pl.BlockSpec((TOK, width), near), pl.BlockSpec((TOK, width), far)]
    return pl.pallas_call(
        joint_kernel,
        grid_spec=pltpu.PrefetchScalarGridSpec(
            num_scalar_prefetch=1,
            grid=(8,),
            in_specs=specs,
            out_specs=pl.BlockSpec((16, 128, width), lambda j, s: (0, 0, j)),
            scratch_shapes=[pltpu.VMEM(TURNED, BF16)] * 3 + [pltpu.SemaphoreType.DMA((3,))],
        ),
        out_shape=jax.ShapeDtypeStruct((16, 128, 8 * width), F32),
        compiler_params=pltpu.CompilerParams(vmem_limit_bytes=VMEM),
        cost_estimate=COST,
    )(side, *lefts, *rights)


def assemble_kernel(side, near, far, up, dense, qkv):
    def put(low, high):
        up[...] = jnp.concatenate([low[:, :1024], high[:, :1024]], axis=1)
        dense[...] = jnp.concatenate([low[:, 1024:1280], high[:, 1024:1280]], axis=1)
        qkv[...] = jnp.concatenate([low[:, 1280:], high[:, 1280:]], axis=1)

    @pl.when(side[0] == 0)
    def _():
        put(near[0], far[...])

    @pl.when(side[0] != 0)
    def _():
        put(far[...], near[0])


def assemble(side, near, far):
    shapes = ((64, 2048), (64, 512), (64, 1536))
    return pl.pallas_call(
        assemble_kernel,
        grid_spec=pltpu.PrefetchScalarGridSpec(
            num_scalar_prefetch=1,
            grid=(1,),
            in_specs=[
                pl.BlockSpec((1, 64, 2048), lambda i, s: (0, s[0], 0)),
                pl.BlockSpec((64, 2048), lambda i, s: (0, 0)),
            ],
            out_specs=[pl.BlockSpec(shape, lambda i, s: (0, 0)) for shape in shapes],
        ),
        out_shape=[jax.ShapeDtypeStruct(shape, F32) for shape in shapes],
        compiler_params=pltpu.CompilerParams(vmem_limit_bytes=VMEM_LESS),
        cost_estimate=COST,
    )(side, near, far)


def body(
    hidden_in,
    segment_ids,
    positions,
    ln1_gain,
    ln1_bias,
    qkv_weight,
    qkv_bias,
    dense_weight,
    dense_bias,
    ln2_gain,
    ln2_bias,
    fc1_weight,
    fc1_bias,
    fc2_weight,
    fc2_bias,
    cotangent,
):
    core = lax.axis_index("c")
    side = lax.axis_index("zl")
    half_rows = TOK // 2
    at_side = side.astype(jnp.int32).reshape(1)
    at_core = core.astype(jnp.int32).reshape(1)
    own_place = jnp.zeros((2,), jnp.int32)
    far_place = jnp.stack([side, core * half_rows]).astype(jnp.int32)
    after = lax.optimization_barrier
    params = (ln1_gain, ln1_bias, ln2_gain, ln2_bias)

    def of_core(values, which):
        return lax.dynamic_slice_in_dim(values, which * half_rows, half_rows, 0)

    second_in, stats, hidden_sent = second(at_core, hidden_in, ln2_gain, ln2_bias)
    hidden_pair = lax.all_gather(hidden_sent, "zl")
    act_low, slope, down_grad = feed(second_in, cotangent, fc1_weight, fc1_bias)
    down_sum = after(lax.psum_scatter(down_grad, ("x", "y"), scatter_dimension=0, tiled=True))
    _, cotangent, hidden_in = after((down_grad, cotangent, hidden_in))

    marks = jnp.concatenate([segment_ids, positions]).astype(F32).reshape(1, 2 * TOK)
    cot_sent = jnp.concatenate(
        [of_core(cotangent, core).astype(F32), jnp.pad(marks, ((0, 7), (0, D - 2 * TOK)))], axis=0
    )
    cot_got = lax.ppermute(cot_sent, ("zl", "zh"), [(i, 3 - i) for i in range(4)])

    own_marks = marks.reshape(2, TOK)

    def own_step(hidden_in, cotangent, act_low, slope):
        first_in, first_turned, second_turned, cot_turned = norm_call(
            first_kernel, 256, (hidden_in, cotangent), 1, 3, params
        )
        projected = project(own_place, 2, first_in, qkv_weight, qkv_bias, own_marks)
        mixed_low, grad_packed = attend(
            own_place, 2, projected, (cotangent, dense_weight), own_marks
        )
        grad_up = feed_back(cotangent, fc2_weight, slope)
        branches = branch_halves(at_core, mixed_low, act_low, dense_weight, fc2_weight)
        return first_turned, second_turned, cot_turned, mixed_low, grad_packed, grad_up, *branches

    (
        first_turned,
        second_turned,
        cot_turned,
        mixed_low,
        grad_packed,
        grad_up,
        branch,
        branch_other,
    ) = lax.cond(core > 1, own_step, own_step, hidden_in, cotangent, act_low, slope)
    hidden_pair, mixed_low = after((hidden_pair, mixed_low))
    hidden_got = lax.dynamic_slice_in_dim(hidden_pair, 1 - side, 1, 0)
    hidden_too, branch_too = send(hidden_got, "c"), send(branch_other, "c")
    hidden_too, cot_got = after((hidden_too, cot_got))
    cot_too = send(cot_got, "c")

    first_far_in, second_far_in, first_turned, second_turned = first_far(
        hidden_got, hidden_too, params, (first_turned, second_turned)
    )
    slope_side, branch = slope_far(
        at_side, second_far_in, fc1_weight, fc1_bias, branch, branch_too
    )
    branch = lax.psum(branch, "zh")
    marks_got = cot_got[half_rows, : 2 * TOK].reshape(2, 2, half_rows)
    marks_far = jnp.where(core == 0, marks_got, marks_got[:, ::-1]).reshape(2, TOK)
    projected_far = project(far_place, 1, first_far_in, qkv_weight, qkv_bias, marks_far)
    grad_up_far, grad_mixed_far, cot_turned = cot_far(
        at_side, cot_got, cot_too, fc2_weight, slope_side, dense_weight, cot_turned
    )
    mixed_far, grad_packed_far = attend(
        far_place, 1, projected_far, (grad_mixed_far,), marks_far
    )
    joint_grad = joint(
        at_side,
        (second_turned, cot_turned, first_turned),
        (grad_up, grad_up_far, mixed_low, mixed_far, grad_packed, grad_packed_far),
    )
    joint_grad, down_sum = after((joint_grad, down_sum))
    joint_sum = after(lax.psum_scatter(joint_grad, ("x", "y"), scatter_dimension=0, tiled=True))
    _, grad_packed, grad_up, cotangent, down_sum = after(
        (joint_grad, grad_packed, grad_up, cotangent, down_sum)
    )

    combined, combined_other, norms = back_halves(
        at_core, grad_packed, grad_up, qkv_weight, fc1_weight, hidden_in, stats, ln1_gain, ln2_gain
    )
    combined = combined + send(combined_other, "c")
    combined_too = send(combined, "zh")

    norms = norms[:4].reshape(4, 32, 64).transpose(1, 0, 2).reshape(32, 256)
    grad_out = cotangent.astype(F32)
    bias_sum = jnp.sum(grad_out, axis=0)
    qkv_bias_sum = jnp.sum(grad_packed.astype(F32), axis=0)
    up_bias_grad = jnp.sum(grad_up.astype(F32), axis=0)
    small = jnp.concatenate(
        [
            norms,
            bias_sum.reshape(32, 64),
            qkv_bias_sum.reshape(2, 32, 24).transpose(1, 0, 2).reshape(32, 48),
            up_bias_grad.reshape(16, 32, 4).transpose(1, 0, 2).reshape(32, 64),
            jnp.zeros((32, 80), F32),
        ],
        axis=1,
    )
    def of_side(values, which):
        return lax.dynamic_slice_in_dim(values[0], which * 64, 64, 0)

    down_far = send(of_side(down_sum, 1 - side), "zl")
    for axis in ("x", "y"):
        small = small + swap(small, axis, 1)
        small = small + swap(small, axis, 2)
    block = lax.axis_index("x") * 4 + lax.axis_index("y")
    own_small = lax.dynamic_slice_in_dim(small, side * 16 + block, 1, 0)
    far_small = lax.dynamic_slice_in_dim(small, (1 - side) * 16 + block, 1, 0)
    small = (own_small + send(far_small, "zl")).reshape(-1)

    norms = small[:256]
    norms = norms + send(norms, "c")
    norms = norms + send(norms, "zh")
    norms, branch, combined_too, down_far = after((norms, branch, combined_too, down_far))
    combined = combined + combined_too
    norms = norms.reshape(4, 64)
    bias_total = small[256:320]
    biases = (dense_bias, fc2_bias)
    own = (hidden_in, cotangent, stats, biases)
    branch_too, combined_too = send(branch, "c"), send(combined, "c")
    finals = final_half(at_core, branch, combined, *own, ())
    finals = final_half(1 - at_core, branch_too, combined_too, *own, finals)
    output, input_grad, joint_sum = after((*finals, joint_sum))

    down_sum = of_side(down_sum, side) + down_far
    joint_far = send(of_side(joint_sum, 1 - side), "zl")
    up_sum, dense_sum, qkv_sum = assemble(at_side, joint_sum, joint_far)
    return (
        output,
        input_grad,
        norms[0],
        norms[1],
        qkv_sum,
        small[320:368].reshape(2, 24),
        dense_sum.T,
        bias_total,
        norms[2],
        norms[3],
        up_sum,
        small[368:432].reshape(16, 4),
        down_sum.T,
        bias_total,
    )


def solution(mesh):
    fine = Mesh(mesh.devices.reshape(tuple(SIZES.values())), tuple(SIZES))
    return jax.shard_map(
        body,
        mesh=fine,
        in_specs=(
            P(DP, None),
            P(DP),
            P(DP),
            P(),
            P(),
            P(None, TENSOR),
            P(TENSOR, None),
            P(TENSOR, None),
            P(),
            P(),
            P(),
            P(None, TENSOR),
            P(TENSOR, None),
            P(TENSOR, None),
            P(),
            P(DP, None),
        ),
        out_specs=(
            P(DP, None),
            P(DP, None),
            P(DP),
            P(DP),
            P(DP, TENSOR),
            P(TENSOR, DP),
            P(TENSOR, DP),
            P(DP),
            P(DP),
            P(DP),
            P(DP, TENSOR),
            P(TENSOR, DP),
            P(TENSOR, DP),
            P(DP),
        ),
        check_vma=False,
    )
```

```python
from functools import partial
import math

import jax
import jax.numpy as jnp
import numpy as np
from jax import lax
from jax.experimental import pallas as pl
from jax.experimental.pallas import tpu as pltpu
from jax.sharding import Mesh, PartitionSpec as P

HD = 256
ROT = 64
TOK = 512
D = 2048
EPSILON = 1e-05
NEGATIVE = -1000000000.0
SIZES = {"zl": 2, "x": 4, "y": 4, "zh": 2, "c": 2}
DP = ("zl", "x", "y")
TENSOR = ("zh", "c")
F32 = jnp.float32
BF16 = jnp.bfloat16


def send(value, axis, step=1):
    n = SIZES[axis]
    return lax.ppermute(value, axis, [(i, (i + step) % n) for i in range(n)])


def swap(value, axis, bit):
    return lax.ppermute(value, axis, [(i, i ^ bit) for i in range(SIZES[axis])])


def plain_dot(left, right):
    return jnp.dot(left, right, preferred_element_type=F32)


def contract_cols(left, right):
    return lax.dot_general(left, right, (((1,), (1,)), ((), ())), preferred_element_type=F32)


VMEM = 56 * 1024 * 1024
VMEM_LESS = 24 * 1024 * 1024
COST = pl.CostEstimate(flops=1000000, bytes_accessed=1000000, transcendentals=0)


def whole(shape):
    return pl.BlockSpec(shape, lambda *_: (0,) * len(shape), pipeline_mode=pl.Buffered(1))


def put_turned(target, rows):
    for z in range(2):
        for pair in range(8):
            start = z * 1024 + pair * 128
            block = rows[:, start : start + 128].T.astype(BF16)
            target[2 * pair, z] = block[:64]
            target[2 * pair + 1, z] = block[64:]


def normalise(hidden):
    average = jnp.mean(hidden, axis=-1, keepdims=True)
    centred = hidden - average
    inv_std = lax.rsqrt(jnp.mean(centred * centred, axis=-1, keepdims=True) + EPSILON)
    return centred * inv_std, average, inv_std


def first_kernel(
    hidden,
    cot,
    gain,
    shift,
    gain_two,
    shift_two,
    first_out,
    first_turned,
    second_turned,
    cot_turned,
    stats,
):
    normed, average, inv_std = normalise(hidden[...].astype(F32))
    first = normed * gain[...] + shift[...]
    first_out[...] = first.astype(BF16)
    put_turned(first_turned, first)
    put_turned(second_turned, normed * gain_two[...] + shift_two[...])
    put_turned(cot_turned, cot[...].astype(F32))
    lane = lax.broadcasted_iota(jnp.int32, (normed.shape[0], 128), 1)
    stats[...] = jnp.where(lane < 64, average, inv_std)


def first_far_kernel(near, other, gain, shift, gain_two, shift_two, *refs):
    first_out, second_out, first_turned, second_turned = refs[2:]

    def step(rows):
        normed, _, _ = normalise(rows)
        first = normed * gain[...] + shift[...]
        second = normed * gain_two[...] + shift_two[...]
        first_out[...] = first.astype(BF16)
        second_out[...] = second.astype(BF16)
        put_turned(first_turned, first)
        put_turned(second_turned, second)

    @pl.when(pl.program_id(0) < 2)
    def _():
        step(near[...])

    @pl.when(pl.program_id(0) >= 2)
    def _():
        step(other[...])


TURNED = (16, 2, 64, 2 * TOK)


def first(hidden, cot, params):
    rows = TOK // 2
    plain = pl.BlockSpec((rows, D), lambda i: (i, 0))
    return pl.pallas_call(
        first_kernel,
        grid=(2,),
        in_specs=[plain] * 2 + [whole((1, D))] * 4,
        out_specs=[plain]
        + [pl.BlockSpec((16, 2, 64, rows), lambda i: (0, 0, 0, i))] * 3
        + [pl.BlockSpec((rows, 128), lambda i: (i, 0))],
        out_shape=[jax.ShapeDtypeStruct((TOK, D), BF16)]
        + [jax.ShapeDtypeStruct(TURNED, BF16)] * 3
        + [jax.ShapeDtypeStruct((TOK, 128), F32)],
        compiler_params=pltpu.CompilerParams(vmem_limit_bytes=VMEM),
        cost_estimate=COST,
    )(hidden, cot, *(p.reshape(1, D) for p in params))


def first_far(near, other, params, held):
    rows = 128
    plain = pl.BlockSpec((rows, D), lambda i: (i, 0))
    return pl.pallas_call(
        first_far_kernel,
        grid=(TOK // rows,),
        in_specs=[
            pl.BlockSpec((rows, D), lambda i: (lax.min(i, 1), 0)),
            pl.BlockSpec((rows, D), lambda i: (lax.max(i - 2, 0), 0)),
        ]
        + [whole((1, D))] * 4
        + [pl.BlockSpec(memory_space=pl.ANY)] * 2,
        out_specs=[plain] * 2
        + [pl.BlockSpec((16, 2, 64, rows), lambda i: (0, 0, 0, i + TOK // rows))] * 2,
        out_shape=[jax.ShapeDtypeStruct((TOK, D), BF16)] * 2
        + [jax.ShapeDtypeStruct(TURNED, BF16)] * 2,
        input_output_aliases={6: 2, 7: 3},
        compiler_params=pltpu.CompilerParams(vmem_limit_bytes=VMEM),
        cost_estimate=COST,
    )(near, other, *(p.reshape(1, D) for p in params), *held)


def phi(upward):
    return 0.5 * (1.0 + lax.erf(upward * math.sqrt(0.5)))


def gelu_slope(upward, below):
    return below + upward * (jnp.exp(-0.5 * upward * upward) * (1.0 / math.sqrt(2.0 * math.pi)))


def as_row(block):
    return jnp.concatenate([block[i : i + 1, :] for i in range(block.shape[0])], axis=1)


def feed_kernel(hidden, gain, shift, cot, weight, bias, act_out, slope_out, down_grad, second):
    @pl.when(pl.program_id(0) == 0)
    def _():
        for start in (0, TOK // 2):
            rows = slice(start, start + TOK // 2)
            normed, _, _ = normalise(hidden[rows].astype(F32))
            second[rows] = (normed * gain[...] + shift[...]).astype(BF16)

    upward = plain_dot(second[...], weight[...]) + as_row(bias[0])
    below = phi(upward)
    act = (upward * below).astype(BF16)
    act_out[...] = act
    slope_out[...] = gelu_slope(upward, below)
    total = lax.dot_general(cot[...], act, (((0,), (0,)), ((), ())), preferred_element_type=F32)
    for z in range(2):
        rows = total[z * 1024 : z * 1024 + 1024]
        down_grad[:, z * 64 : z * 64 + 64] = rows.reshape(16, 64, -1)


def feed(hidden, gain, shift, cot, weight, bias):
    units, width = weight.shape[1], 512
    column = pl.BlockSpec((TOK, width), lambda j: (0, j))
    return pl.pallas_call(
        feed_kernel,
        grid=(units // width,),
        in_specs=[
            whole((TOK, D)),
            whole((1, D)),
            whole((1, D)),
            whole((TOK, D)),
            pl.BlockSpec((D, width), lambda j: (0, j)),
            pl.BlockSpec((1, width // 128, 128), lambda j: (j, 0, 0)),
        ],
        out_specs=[column, column, pl.BlockSpec((16, 128, width), lambda j: (0, 0, j))],
        out_shape=[
            jax.ShapeDtypeStruct((TOK, units), BF16),
            jax.ShapeDtypeStruct((TOK, units), F32),
            jax.ShapeDtypeStruct((16, 128, units), F32),
        ],
        scratch_shapes=[pltpu.VMEM((TOK, D), BF16)],
        compiler_params=pltpu.CompilerParams(vmem_limit_bytes=VMEM),
        cost_estimate=COST,
    )(
        hidden,
        gain.reshape(1, D),
        shift.reshape(1, D),
        cot,
        weight,
        bias.reshape(-1, width // 128, 128),
    )


def feed_back_kernel(cot, weight, slope, up_grad):
    up_grad[...] = (contract_cols(cot[...], weight[...]) * slope[...]).astype(BF16)


def feed_back(cot, weight, slope):
    units, width = slope.shape[1], 512
    column = pl.BlockSpec((TOK, width), lambda j: (0, j))
    return pl.pallas_call(
        feed_back_kernel,
        grid=(units // width,),
        in_specs=[whole((TOK, D)), pl.BlockSpec((width, D), lambda j: (j, 0)), column],
        out_specs=column,
        out_shape=jax.ShapeDtypeStruct((TOK, units), BF16),
        compiler_params=pltpu.CompilerParams(vmem_limit_bytes=VMEM),
        cost_estimate=COST,
    )(cot, weight, slope)


def cot_far_kernel(side, near, other, weight, slope, dense, held, up_grad, grad_mixed, cot_turned, low):
    half = TOK // 2

    @pl.when(pl.program_id(0) == 0)
    def _():
        for k, rows in enumerate((near, other)):
            low[k * half : k * half + half] = rows[...].astype(BF16)
            put_turned(cot_turned.at[:, :, :, k * half : k * half + half], rows[...])
        grad_mixed[...] = contract_cols(low[...], dense[...]).astype(BF16)

    up_grad[...] = (contract_cols(low[...], weight[...]) * slope[...]).astype(BF16)


def cot_far(side, near, other, weight, slope, dense, held):
    width = 256
    steps = slope.shape[1] // width
    column = pl.BlockSpec((TOK, width), lambda j, s: (0, j))
    return pl.pallas_call(
        cot_far_kernel,
        grid_spec=pltpu.PrefetchScalarGridSpec(
            num_scalar_prefetch=1,
            grid=(steps,),
            in_specs=[
                whole((TOK // 2, D)),
                whole((TOK // 2, D)),
                pl.BlockSpec((width, D), lambda j, s: (s[0] * steps + j, 0)),
                column,
                pl.BlockSpec((HD, D), lambda j, s: (s[0], 0)),
                pl.BlockSpec(memory_space=pl.ANY),
            ],
            out_specs=[
                column,
                pl.BlockSpec((TOK, HD), lambda j, s: (0, 0)),
                pl.BlockSpec((16, 2, 64, TOK), lambda j, s: (0, 0, 0, 1)),
            ],
            scratch_shapes=[pltpu.VMEM((TOK, D), BF16)],
        ),
        out_shape=[
            jax.ShapeDtypeStruct((TOK, slope.shape[1]), BF16),
            jax.ShapeDtypeStruct((TOK, HD), BF16),
            jax.ShapeDtypeStruct(TURNED, BF16),
        ],
        input_output_aliases={6: 2},
        compiler_params=pltpu.CompilerParams(vmem_limit_bytes=VMEM),
        cost_estimate=COST,
    )(side, near, other, weight, slope, dense, held)


def slope_far_kernel(side, second, weight, bias, slope):
    upward = plain_dot(second[...], weight[...]) + as_row(bias[0])
    slope[...] = gelu_slope(upward, phi(upward))


def slope_far(side, second, weight, bias):
    units, width = weight.shape[1] // 2, 512
    steps = units // width
    return pl.pallas_call(
        slope_far_kernel,
        grid_spec=pltpu.PrefetchScalarGridSpec(
            num_scalar_prefetch=1,
            grid=(steps,),
            in_specs=[
                whole((TOK, D)),
                pl.BlockSpec((D, width), lambda j, s: (0, s[0] * steps + j)),
                pl.BlockSpec((1, width // 128, 128), lambda j, s: (s[0] * steps + j, 0, 0)),
            ],
            out_specs=pl.BlockSpec((TOK, width), lambda j, s: (0, j)),
        ),
        out_shape=jax.ShapeDtypeStruct((TOK, units), F32),
        compiler_params=pltpu.CompilerParams(vmem_limit_bytes=VMEM),
        cost_estimate=COST,
    )(side, second, weight, bias.reshape(-1, width // 128, 128))


def turn(values, tables, sign):
    first = values[:, :128]
    cosine, rising, falling = tables
    first = (
        first * cosine[...]
        + (pltpu.roll(first, 32, 1) * rising[...] + pltpu.roll(first, 96, 1) * falling[...]) * sign
    )
    return jnp.concatenate([first, values[:, 128:]], axis=1)


def as_column(row):
    return jnp.broadcast_to(row, (8, row.shape[1])).T[:, 0:1]


def cosine_and_sine(angles):
    turns = jnp.floor(angles * (2.0 / math.pi) + 0.5)
    rest = ((angles - turns * 1.5703125) - turns * 4.837512969970703e-4) - turns * 7.549789954891882e-8
    square = rest * rest
    sine = ((-1.9515295891e-4 * square + 8.3321608736e-3) * square - 1.6666654611e-1) * square
    sine = sine * rest + rest
    cosine = (2.443315711809948e-5 * square - 1.388731625493765e-3) * square + 4.166664568298827e-2
    cosine = cosine * (square * square) - 0.5 * square + 1.0
    quarter = turns.astype(jnp.int32) & 3
    odd = (quarter & 1) == 1
    flipped = jnp.where(odd, sine, cosine), jnp.where(odd, cosine, sine)
    return (
        jnp.where((quarter == 1) | (quarter == 2), -flipped[0], flipped[0]),
        jnp.where(quarter >= 2, -flipped[1], flipped[1]),
    )


def project_kernel(place, first, weight, bias, marks, inverse, queries, keys, values, *tables):
    @pl.when(pl.program_id(0) == 0)
    def _():
        angles = inverse[...] * marks[1:2, :]
        cosine, sine = cosine_and_sine(angles)
        none, rest = jnp.zeros_like(sine), jnp.zeros((64, TOK), F32)
        tables[0][...] = jnp.concatenate([cosine, cosine, rest + 1.0], axis=0).T
        tables[1][...] = jnp.concatenate([none, sine, rest], axis=0).T
        tables[2][...] = jnp.concatenate([-sine, none, rest], axis=0).T

    head = pl.program_id(0) + place[0] * (2 - pl.num_programs(0))
    packed = plain_dot(first[...], weight[...]) + bias[pl.ds(head, 1), :]
    queries[...] = turn(packed[:, :HD], tables, 1.0).astype(BF16)
    keys[...] = turn(packed[:, HD : 2 * HD], tables, 1.0).astype(BF16)
    values[...] = packed[:, 2 * HD :].astype(BF16)


def project(place, heads, first, weight, bias, marks):
    inverse = jnp.asarray((10000.0 ** (-2.0 * np.arange(32) / ROT)).astype(np.float32).reshape(32, 1))
    at = (lambda h, s: h) if heads == 2 else (lambda h, s: s[0])
    column = pl.BlockSpec((TOK, HD), lambda h, s: (0, h))
    return pl.pallas_call(
        project_kernel,
        grid_spec=pltpu.PrefetchScalarGridSpec(
            num_scalar_prefetch=1,
            grid=(heads,),
            in_specs=[
                whole((TOK, D)),
                pl.BlockSpec((D, 3 * HD), lambda h, s: (0, at(h, s))),
                whole((2, 3 * HD)),
                whole((2, TOK)),
                whole((32, 1)),
            ],
            out_specs=[column] * 3 + [pl.BlockSpec((TOK, 128), lambda h, s: (0, 0))] * 3,
        ),
        out_shape=[jax.ShapeDtypeStruct((TOK, heads * HD), BF16)] * 3
        + [jax.ShapeDtypeStruct((TOK, 128), F32)] * 3,
        compiler_params=pltpu.CompilerParams(vmem_limit_bytes=VMEM),
        cost_estimate=COST,
    )(place, first, weight, bias, marks, inverse)


def attend_kernel(place, queries, keys, values, cosine, rising, falling, marks, *refs):
    given, (mixed_out, grad_out) = refs[:-2], refs[-2:]
    tables = (cosine, rising, falling)
    scale = 1.0 / math.sqrt(HD)
    queries, keys, values = queries[...], keys[...], values[...]
    segments = marks[0:1, :]

    def order(axis):
        return lax.rem(lax.broadcasted_iota(jnp.int32, (TOK, TOK), axis) + place[1], TOK)

    allowed = (as_column(segments) == segments) & (order(0) >= order(1))
    scores = jnp.where(allowed, contract_cols(queries, keys) * scale, NEGATIVE)
    top = jnp.max(scores, axis=-1, keepdims=True)
    weights = jnp.exp(scores - top)
    probs = weights / jnp.sum(weights, axis=-1, keepdims=True)
    probs_low = probs.astype(BF16)
    mixed_out[...] = plain_dot(probs_low, values).astype(BF16)
    grad_mixed = given[0][...]
    if len(given) == 2:
        grad_mixed = contract_cols(grad_mixed, given[1][...]).astype(BF16)
    grad_probs = contract_cols(grad_mixed, values)
    along = jnp.sum(probs * grad_probs, axis=-1, keepdims=True)
    grad_scores = (probs * (grad_probs - along)).astype(BF16)
    grad_query = plain_dot(grad_scores, keys) * scale
    grad_key = plain_dot(grad_scores.T, queries) * scale
    grad_value = plain_dot(probs_low.T, grad_mixed)
    grad_out[:, :HD] = turn(grad_query, tables, -1.0).astype(BF16)
    grad_out[:, HD : 2 * HD] = turn(grad_key, tables, -1.0).astype(BF16)
    grad_out[:, 2 * HD :] = grad_value.astype(BF16)


def attend(place, heads, projected, given, marks):
    column = pl.BlockSpec((TOK, HD), lambda h, s: (0, h))
    return pl.pallas_call(
        attend_kernel,
        grid_spec=pltpu.PrefetchScalarGridSpec(
            num_scalar_prefetch=1,
            grid=(heads,),
            in_specs=[column] * 3
            + [whole((TOK, 128))] * 3
            + [whole((2, TOK))]
            + ([column] if len(given) == 1 else [whole((TOK, D)), pl.BlockSpec((HD, D), lambda h, s: (h, 0))]),
            out_specs=[column, pl.BlockSpec((TOK, 3 * HD), lambda h, s: (0, h))],
        ),
        out_shape=[
            jax.ShapeDtypeStruct((TOK, heads * HD), BF16),
            jax.ShapeDtypeStruct((TOK, heads * 3 * HD), BF16),
        ],
        compiler_params=pltpu.CompilerParams(vmem_limit_bytes=VMEM),
        cost_estimate=COST,
    )(place, *projected, marks, *given)


def put_halves(core, values, scratch, mine, other):
    scratch[...] = values
    half = TOK // 2
    mine[...] = scratch[pl.ds(pl.multiple_of(core[0] * half, half), half), :]
    other[...] = scratch[pl.ds(pl.multiple_of((1 - core[0]) * half, half), half), :]


def branch_kernel(core, mixed, act, dense, down, mine, other, scratch):
    total = plain_dot(act[...], down[...]) + plain_dot(mixed[...], dense[...])
    put_halves(core, total, scratch, mine, other)


def back_kernel(
    core, packed, up_grad, qkv, up, hidden, stats, gain, gain_two, mine, other, sums, scratch
):
    first = contract_cols(packed[...], qkv[...])
    second = contract_cols(up_grad[...], up[...])
    put_halves(core, first * gain[...] + second * gain_two[...], scratch, mine, other)
    normed = (hidden[...].astype(F32) - stats[:, 0:1]) * stats[:, 64:65]
    rows = [
        jnp.sum(v, axis=0, keepdims=True) for v in (first * normed, first, second * normed, second)
    ]
    sums[...] = jnp.concatenate(rows + [jnp.zeros((4, first.shape[1]), F32)], axis=0)


def halves_call(kernel, core, operands, specs, with_sums):
    width = 512
    half = pl.BlockSpec((TOK // 2, width), lambda j, s: (0, j))
    return pl.pallas_call(
        kernel,
        grid_spec=pltpu.PrefetchScalarGridSpec(
            num_scalar_prefetch=1,
            grid=(D // width,),
            in_specs=specs,
            out_specs=[half, half] + [pl.BlockSpec((8, width), lambda j, s: (0, j))] * with_sums,
            scratch_shapes=[pltpu.VMEM((TOK, width), F32)],
        ),
        out_shape=[jax.ShapeDtypeStruct((TOK // 2, D), F32)] * 2
        + [jax.ShapeDtypeStruct((8, D), F32)] * with_sums,
        compiler_params=pltpu.CompilerParams(vmem_limit_bytes=VMEM),
        cost_estimate=COST,
    )(core, *operands)


def branch_halves(core, mixed, act, dense, down):
    specs = [whole(mixed.shape), whole(act.shape)]
    specs += [pl.BlockSpec((w.shape[0], 512), lambda j, s: (0, j)) for w in (dense, down)]
    return halves_call(branch_kernel, core, (mixed, act, dense, down), specs, False)


def back_halves(core, packed, up_grad, qkv, up, hidden, stats, gain, gain_two):
    specs = [whole(packed.shape), whole(up_grad.shape)]
    specs += [pl.BlockSpec((512, w.shape[1]), lambda j, s: (j, 0)) for w in (qkv, up)]
    specs += [pl.BlockSpec((TOK, 512), lambda j, s: (0, j)), whole((TOK, 128))]
    specs += [pl.BlockSpec((1, 512), lambda j, s: (0, j))] * 2
    operands = (packed, up_grad, qkv, up, hidden, stats, gain.reshape(1, D), gain_two.reshape(1, D))
    return halves_call(back_kernel, core, operands, specs, True)


def final_kernel(n, half, branch, combined, hidden, cot, stats, bias, bias_too, *refs):
    output, input_grad = refs[n:]
    rows = hidden[...].astype(F32)
    output[...] = rows + branch[...] + bias[...] + bias_too[...]
    e = combined[...]
    inv_std = stats[:, 64:65]
    normed = (rows - stats[:, 0:1]) * inv_std
    input_grad[...] = cot[...].astype(F32) + inv_std * (
        e
        - jnp.mean(e, axis=-1, keepdims=True)
        - normed * jnp.mean(e * normed, axis=-1, keepdims=True)
    )


def final_half(half, branch, combined, hidden, cot, stats, biases, held):
    rows = 128
    steps = TOK // 2 // rows
    given = pl.BlockSpec((rows, D), lambda i, s: (i, 0))
    placed = pl.BlockSpec((rows, D), lambda i, s: (s[0] * steps + i, 0))
    return pl.pallas_call(
        partial(final_kernel, len(held)),
        grid_spec=pltpu.PrefetchScalarGridSpec(
            num_scalar_prefetch=1,
            grid=(steps,),
            in_specs=[given, given, placed, placed]
            + [pl.BlockSpec((rows, 128), lambda i, s: (s[0] * steps + i, 0))]
            + [whole((1, D))] * 2
            + [pl.BlockSpec(memory_space=pl.ANY)] * len(held),
            out_specs=[placed, placed],
        ),
        out_shape=[jax.ShapeDtypeStruct((TOK, D), F32)] * 2,
        input_output_aliases={8: 0, 9: 1} if held else {},
        compiler_params=pltpu.CompilerParams(vmem_limit_bytes=VMEM_LESS),
        cost_estimate=COST,
    )(half, branch, combined, hidden, cot, stats, *(b.reshape(1, D) for b in biases), *held)


def joint_kernel(side, *refs):
    lefts, rights, target, held, arrived = refs[:3], refs[3:9], refs[9], refs[10:13], refs[13]
    step = pl.program_id(0)
    copies = [pltpu.make_async_copy(lefts[k], held[k], arrived.at[k]) for k in range(3)]

    def put(columns, k, given):
        right = jnp.concatenate([rights[2 * k][:, given], rights[2 * k + 1][:, given]], axis=0)
        total = plain_dot(held[k][...].reshape(D, 2 * TOK), right)
        target[:, :, columns] = total.reshape(16, 128, -1)

    @pl.when(step == 0)
    def _():
        for copy in copies:
            copy.start()
        copies[0].wait()

    @pl.when(step < 2)
    def _():
        put(slice(0, 512), 0, slice(0, 512))

    @pl.when(step == 2)
    def _():
        copies[1].wait()
        copies[2].wait()
        put(slice(0, HD), 1, slice(0, HD))
        put(slice(HD, 512), 2, slice(0, 512 - HD))

    @pl.when(step == 3)
    def _():
        put(slice(0, 512), 2, slice(512 - HD, 3 * HD))


def joint(side, lefts, rights):
    specs = [pl.BlockSpec(memory_space=pl.ANY)] * 3
    for width, n in ((512, 2), (HD, 1), (3 * HD, 1)):

        def near(j, s, n=n):
            return (0, s[0] * n + jnp.clip(j, 0, n - 1))

        def far(j, s, n=n):
            return (0, jnp.clip(j, 0, n - 1))

        specs += [pl.BlockSpec((TOK, width), near), pl.BlockSpec((TOK, width), far)]
    return pl.pallas_call(
        joint_kernel,
        grid_spec=pltpu.PrefetchScalarGridSpec(
            num_scalar_prefetch=1,
            grid=(4,),
            in_specs=specs,
            out_specs=pl.BlockSpec((16, 128, 512), lambda j, s: (0, 0, j)),
            scratch_shapes=[pltpu.VMEM(TURNED, BF16)] * 3 + [pltpu.SemaphoreType.DMA((3,))],
        ),
        out_shape=jax.ShapeDtypeStruct((16, 128, 2048), F32),
        compiler_params=pltpu.CompilerParams(vmem_limit_bytes=VMEM),
        cost_estimate=COST,
    )(side, *lefts, *rights)


def assemble_kernel(side, near, far, up, dense, qkv):
    def put(low, high):
        up[...] = jnp.concatenate([low[:, :1024], high[:, :1024]], axis=1)
        dense[...] = jnp.concatenate([low[:, 1024:1280], high[:, 1024:1280]], axis=1)
        qkv[...] = jnp.concatenate([low[:, 1280:], high[:, 1280:]], axis=1)

    @pl.when(side[0] == 0)
    def _():
        put(near[0], far[...])

    @pl.when(side[0] != 0)
    def _():
        put(far[...], near[0])


def assemble(side, near, far):
    shapes = ((64, 2048), (64, 512), (64, 1536))
    return pl.pallas_call(
        assemble_kernel,
        grid_spec=pltpu.PrefetchScalarGridSpec(
            num_scalar_prefetch=1,
            grid=(1,),
            in_specs=[
                pl.BlockSpec((1, 64, 2048), lambda i, s: (0, s[0], 0)),
                pl.BlockSpec((64, 2048), lambda i, s: (0, 0)),
            ],
            out_specs=[pl.BlockSpec(shape, lambda i, s: (0, 0)) for shape in shapes],
        ),
        out_shape=[jax.ShapeDtypeStruct(shape, F32) for shape in shapes],
        compiler_params=pltpu.CompilerParams(vmem_limit_bytes=VMEM_LESS),
        cost_estimate=COST,
    )(side, near, far)


def body(
    hidden_in,
    segment_ids,
    positions,
    ln1_gain,
    ln1_bias,
    qkv_weight,
    qkv_bias,
    dense_weight,
    dense_bias,
    ln2_gain,
    ln2_bias,
    fc1_weight,
    fc1_bias,
    fc2_weight,
    fc2_bias,
    cotangent,
):
    core = lax.axis_index("c")
    side = lax.axis_index("zl")
    half_rows = TOK // 2
    at_side = side.astype(jnp.int32).reshape(1)
    at_core = core.astype(jnp.int32).reshape(1)
    own_place = jnp.zeros((2,), jnp.int32)
    far_place = jnp.stack([side, core * half_rows]).astype(jnp.int32)
    after = lax.optimization_barrier
    params = (ln1_gain, ln1_bias, ln2_gain, ln2_bias)

    def of_core(values, which):
        return lax.dynamic_slice_in_dim(values, which * half_rows, half_rows, 0)

    act_low, slope, down_grad = feed(
        hidden_in, ln2_gain, ln2_bias, cotangent, fc1_weight, fc1_bias
    )
    down_sum = after(lax.psum_scatter(down_grad, ("x", "y"), scatter_dimension=0, tiled=True))
    _, cotangent, hidden_in = after((down_grad, cotangent, hidden_in))

    hidden_got = send(of_core(hidden_in, core).astype(F32), "zl")
    marks = jnp.concatenate([segment_ids, positions]).astype(F32).reshape(1, 2 * TOK)
    cot_sent = jnp.concatenate(
        [of_core(cotangent, core).astype(F32), jnp.pad(marks, ((0, 7), (0, D - 2 * TOK)))], axis=0
    )
    cot_got = lax.ppermute(cot_sent, ("zl", "zh"), [(i, 3 - i) for i in range(4)])

    own_marks = marks.reshape(2, TOK)

    def own_step(hidden_in, cotangent, act_low, slope):
        first_in, *turned, stats = first(hidden_in, cotangent, params)
        projected = project(own_place, 2, first_in, qkv_weight, qkv_bias, own_marks)
        mixed_low, grad_packed = attend(
            own_place, 2, projected, (cotangent, dense_weight), own_marks
        )
        grad_up = feed_back(cotangent, fc2_weight, slope)
        branches = branch_halves(at_core, mixed_low, act_low, dense_weight, fc2_weight)
        return *turned, stats, mixed_low, grad_packed, grad_up, *branches

    (
        first_turned,
        second_turned,
        cot_turned,
        stats,
        mixed_low,
        grad_packed,
        grad_up,
        branch,
        branch_other,
    ) = lax.cond(core > 1, own_step, own_step, hidden_in, cotangent, act_low, slope)
    branch_too = send(branch_other, "c")
    hidden_got, cot_got, branch_too = after((hidden_got, cot_got, branch_too))
    hidden_too = send(hidden_got, "c")
    branch = lax.psum(branch + branch_too, "zh")
    hidden_too, cot_got = after((hidden_too, cot_got))
    cot_too = send(cot_got, "c")

    first_far_in, second_far_in, first_turned, second_turned = first_far(
        hidden_got, hidden_too, params, (first_turned, second_turned)
    )
    slope_side = slope_far(at_side, second_far_in, fc1_weight, fc1_bias)
    marks_got = cot_got[half_rows, : 2 * TOK].reshape(2, 2, half_rows)
    marks_far = jnp.where(core == 0, marks_got, marks_got[:, ::-1]).reshape(2, TOK)
    projected_far = project(far_place, 1, first_far_in, qkv_weight, qkv_bias, marks_far)
    grad_up_far, grad_mixed_far, cot_turned = cot_far(
        at_side, cot_got, cot_too, fc2_weight, slope_side, dense_weight, cot_turned
    )
    mixed_far, grad_packed_far = attend(
        far_place, 1, projected_far, (grad_mixed_far,), marks_far
    )
    joint_grad = joint(
        at_side,
        (second_turned, cot_turned, first_turned),
        (grad_up, grad_up_far, mixed_low, mixed_far, grad_packed, grad_packed_far),
    )
    joint_grad, down_sum = after((joint_grad, down_sum))
    joint_sum = after(lax.psum_scatter(joint_grad, ("x", "y"), scatter_dimension=0, tiled=True))
    _, grad_packed, grad_up, cotangent, down_sum = after(
        (joint_grad, grad_packed, grad_up, cotangent, down_sum)
    )

    combined, combined_other, norms = back_halves(
        at_core, grad_packed, grad_up, qkv_weight, fc1_weight, hidden_in, stats, ln1_gain, ln2_gain
    )
    combined = combined + send(combined_other, "c")
    combined_too = send(combined, "zh")

    norms = norms[:4].reshape(4, 32, 64).transpose(1, 0, 2).reshape(32, 256)
    grad_out = cotangent.astype(F32)
    bias_sum = jnp.sum(grad_out, axis=0)
    qkv_bias_sum = jnp.sum(grad_packed.astype(F32), axis=0)
    up_bias_grad = jnp.sum(grad_up.astype(F32), axis=0)
    small = jnp.concatenate(
        [
            norms,
            bias_sum.reshape(32, 64),
            qkv_bias_sum.reshape(2, 32, 24).transpose(1, 0, 2).reshape(32, 48),
            up_bias_grad.reshape(16, 32, 4).transpose(1, 0, 2).reshape(32, 64),
            jnp.zeros((32, 80), F32),
        ],
        axis=1,
    )
    def of_side(values, which):
        return lax.dynamic_slice_in_dim(values[0], which * 64, 64, 0)

    down_far = send(of_side(down_sum, 1 - side), "zl")
    for axis in ("x", "y"):
        small = small + swap(small, axis, 1)
        small = small + swap(small, axis, 2)
    block = lax.axis_index("x") * 4 + lax.axis_index("y")
    own_small = lax.dynamic_slice_in_dim(small, side * 16 + block, 1, 0)
    far_small = lax.dynamic_slice_in_dim(small, (1 - side) * 16 + block, 1, 0)
    small = (own_small + send(far_small, "zl")).reshape(-1)

    norms = small[:256]
    norms = norms + send(norms, "c")
    norms = norms + send(norms, "zh")
    norms, branch, combined_too, down_far = after((norms, branch, combined_too, down_far))
    combined = combined + combined_too
    norms = norms.reshape(4, 64)
    bias_total = small[256:320]
    biases = (dense_bias, fc2_bias)
    own = (hidden_in, cotangent, stats, biases)
    branch_too, combined_too = send(branch, "c"), send(combined, "c")
    finals = final_half(at_core, branch, combined, *own, ())
    finals = final_half(1 - at_core, branch_too, combined_too, *own, finals)
    output, input_grad, joint_sum = after((*finals, joint_sum))

    down_sum = of_side(down_sum, side) + down_far
    joint_far = send(of_side(joint_sum, 1 - side), "zl")
    up_sum, dense_sum, qkv_sum = assemble(at_side, joint_sum, joint_far)
    return (
        output,
        input_grad,
        norms[0],
        norms[1],
        qkv_sum,
        small[320:368].reshape(2, 24),
        dense_sum.T,
        bias_total,
        norms[2],
        norms[3],
        up_sum,
        small[368:432].reshape(16, 4),
        down_sum.T,
        bias_total,
    )


def solution(mesh):
    fine = Mesh(mesh.devices.reshape(tuple(SIZES.values())), tuple(SIZES))
    return jax.shard_map(
        body,
        mesh=fine,
        in_specs=(
            P(DP, None),
            P(DP),
            P(DP),
            P(),
            P(),
            P(None, TENSOR),
            P(TENSOR, None),
            P(TENSOR, None),
            P(),
            P(),
            P(),
            P(None, TENSOR),
            P(TENSOR, None),
            P(TENSOR, None),
            P(),
            P(DP, None),
        ),
        out_specs=(
            P(DP, None),
            P(DP, None),
            P(DP),
            P(DP),
            P(DP, TENSOR),
            P(TENSOR, DP),
            P(TENSOR, DP),
            P(DP),
            P(DP),
            P(DP),
            P(DP, TENSOR),
            P(TENSOR, DP),
            P(TENSOR, DP),
            P(DP),
        ),
        check_vma=False,
    )
```

```python
from functools import partial
import math

import jax
import jax.numpy as jnp
import numpy as np
from jax import lax
from jax.experimental import pallas as pl
from jax.experimental.pallas import tpu as pltpu
from jax.sharding import Mesh, PartitionSpec as P

HD = 256
ROT = 64
TOK = 512
D = 2048
EPSILON = 1e-05
NEGATIVE = -1000000000.0
SIZES = {"zl": 2, "x": 4, "y": 4, "zh": 2, "c": 2}
DP = ("zl", "x", "y")
TENSOR = ("zh", "c")
F32 = jnp.float32
BF16 = jnp.bfloat16


def send(value, axis, step=1):
    n = SIZES[axis]
    return lax.ppermute(value, axis, [(i, (i + step) % n) for i in range(n)])


def swap(value, axis, bit):
    return lax.ppermute(value, axis, [(i, i ^ bit) for i in range(SIZES[axis])])


def plain_dot(left, right):
    return jnp.dot(left, right, preferred_element_type=F32)


def contract_cols(left, right):
    return lax.dot_general(left, right, (((1,), (1,)), ((), ())), preferred_element_type=F32)


VMEM = 56 * 1024 * 1024
VMEM_LESS = 24 * 1024 * 1024
WHOLE = 896
COST = pl.CostEstimate(flops=1000000, bytes_accessed=1000000, transcendentals=0)


def whole(shape):
    return pl.BlockSpec(shape, lambda *_: (0,) * len(shape), pipeline_mode=pl.Buffered(1))


def put_turned(target, rows):
    for z in range(2):
        for pair in range(8):
            start = z * 1024 + pair * 128
            block = rows[:, start : start + 128].T.astype(BF16)
            target[2 * pair, z] = block[:64]
            target[2 * pair + 1, z] = block[64:]


def normalise(hidden):
    average = jnp.mean(hidden, axis=-1, keepdims=True)
    centred = hidden - average
    inv_std = lax.rsqrt(jnp.mean(centred * centred, axis=-1, keepdims=True) + EPSILON)
    return centred * inv_std, average, inv_std


def first_kernel(
    hidden,
    cot,
    gain,
    shift,
    gain_two,
    shift_two,
    first_out,
    first_turned,
    second_turned,
    cot_turned,
    stats,
):
    normed, average, inv_std = normalise(hidden[...].astype(F32))
    first = normed * gain[...] + shift[...]
    first_out[...] = first.astype(BF16)
    put_turned(first_turned, first)
    put_turned(second_turned, normed * gain_two[...] + shift_two[...])
    put_turned(cot_turned, cot[...].astype(F32))
    lane = lax.broadcasted_iota(jnp.int32, (normed.shape[0], 128), 1)
    stats[...] = jnp.where(lane < 64, average, inv_std)


def first_far_kernel(near, other, gain, shift, gain_two, shift_two, *refs):
    first_out, second_out, first_turned, second_turned = refs[2:]

    def step(rows):
        normed, _, _ = normalise(rows)
        first = normed * gain[...] + shift[...]
        second = normed * gain_two[...] + shift_two[...]
        first_out[...] = first.astype(BF16)
        second_out[...] = second.astype(BF16)
        put_turned(first_turned, first)
        put_turned(second_turned, second)

    @pl.when(pl.program_id(0) < 2)
    def _():
        step(near[...])

    @pl.when(pl.program_id(0) >= 2)
    def _():
        step(other[...])


TURNED = (16, 2, 64, 2 * TOK)


def first(hidden, cot, params):
    rows = TOK // 2
    plain = pl.BlockSpec((rows, D), lambda i: (i, 0))
    return pl.pallas_call(
        first_kernel,
        grid=(2,),
        in_specs=[plain] * 2 + [whole((1, D))] * 4,
        out_specs=[plain]
        + [pl.BlockSpec((16, 2, 64, rows), lambda i: (0, 0, 0, i))] * 3
        + [pl.BlockSpec((rows, 128), lambda i: (i, 0))],
        out_shape=[jax.ShapeDtypeStruct((TOK, D), BF16)]
        + [jax.ShapeDtypeStruct(TURNED, BF16)] * 3
        + [jax.ShapeDtypeStruct((TOK, 128), F32)],
        compiler_params=pltpu.CompilerParams(vmem_limit_bytes=VMEM),
        cost_estimate=COST,
    )(hidden, cot, *(p.reshape(1, D) for p in params))


def first_far(near, other, params, held):
    rows = 128
    plain = pl.BlockSpec((rows, D), lambda i: (i, 0))
    return pl.pallas_call(
        first_far_kernel,
        grid=(TOK // rows,),
        in_specs=[
            pl.BlockSpec((rows, D), lambda i: (lax.min(i, 1), 0)),
            pl.BlockSpec((rows, D), lambda i: (lax.max(i - 2, 0), 0)),
        ]
        + [whole((1, D))] * 4
        + [pl.BlockSpec(memory_space=pl.ANY)] * 2,
        out_specs=[plain] * 2
        + [pl.BlockSpec((16, 2, 64, rows), lambda i: (0, 0, 0, i + TOK // rows))] * 2,
        out_shape=[jax.ShapeDtypeStruct((TOK, D), BF16)] * 2
        + [jax.ShapeDtypeStruct(TURNED, BF16)] * 2,
        input_output_aliases={6: 2, 7: 3},
        compiler_params=pltpu.CompilerParams(vmem_limit_bytes=VMEM),
        cost_estimate=COST,
    )(near, other, *(p.reshape(1, D) for p in params), *held)


def phi(upward):
    return 0.5 * (1.0 + lax.erf(upward * math.sqrt(0.5)))


def gelu_slope(upward, below):
    return below + upward * (jnp.exp(-0.5 * upward * upward) * (1.0 / math.sqrt(2.0 * math.pi)))


def as_row(block):
    return jnp.concatenate([block[i : i + 1, :] for i in range(block.shape[0])], axis=1)


def feed_kernel(hidden, gain, shift, cot, weight, bias, act_out, slope_out, down_grad, second):
    @pl.when(pl.program_id(0) == 0)
    def _():
        for start in (0, TOK // 2):
            rows = slice(start, start + TOK // 2)
            normed, _, _ = normalise(hidden[rows].astype(F32))
            second[rows] = (normed * gain[...] + shift[...]).astype(BF16)

    upward = plain_dot(second[...], weight[...]) + as_row(bias[0])
    below = phi(upward)
    act = (upward * below).astype(BF16)
    act_out[...] = act
    slope_out[...] = gelu_slope(upward, below)
    total = lax.dot_general(
        cot[...], act[:, :WHOLE], (((0,), (0,)), ((), ())), preferred_element_type=F32
    )
    for z in range(2):
        rows = total[z * 1024 : z * 1024 + 1024]
        down_grad[:, z * 64 : z * 64 + 64] = rows.reshape(16, 64, -1)


def feed(hidden, gain, shift, cot, weight, bias):
    units, width = weight.shape[1], 1024
    column = pl.BlockSpec((TOK, width), lambda j: (0, j))
    return pl.pallas_call(
        feed_kernel,
        grid=(units // width,),
        in_specs=[
            whole((TOK, D)),
            whole((1, D)),
            whole((1, D)),
            whole((TOK, D)),
            pl.BlockSpec((D, width), lambda j: (0, j)),
            pl.BlockSpec((1, width // 128, 128), lambda j: (j, 0, 0)),
        ],
        out_specs=[column, column, pl.BlockSpec((16, 128, WHOLE), lambda j: (0, 0, j))],
        out_shape=[
            jax.ShapeDtypeStruct((TOK, units), BF16),
            jax.ShapeDtypeStruct((TOK, units), F32),
            jax.ShapeDtypeStruct((16, 128, 2 * WHOLE), F32),
        ],
        scratch_shapes=[pltpu.VMEM((TOK, D), BF16)],
        compiler_params=pltpu.CompilerParams(vmem_limit_bytes=VMEM),
        cost_estimate=COST,
    )(
        hidden,
        gain.reshape(1, D),
        shift.reshape(1, D),
        cot,
        weight,
        bias.reshape(-1, width // 128, 128),
    )


def feed_back_kernel(cot, weight, slope, up_grad):
    up_grad[...] = (contract_cols(cot[...], weight[...]) * slope[...]).astype(BF16)


def feed_back(cot, weight, slope):
    units, width = slope.shape[1], 512
    column = pl.BlockSpec((TOK, width), lambda j: (0, j))
    return pl.pallas_call(
        feed_back_kernel,
        grid=(units // width,),
        in_specs=[whole((TOK, D)), pl.BlockSpec((width, D), lambda j: (j, 0)), column],
        out_specs=column,
        out_shape=jax.ShapeDtypeStruct((TOK, units), BF16),
        compiler_params=pltpu.CompilerParams(vmem_limit_bytes=VMEM),
        cost_estimate=COST,
    )(cot, weight, slope)


def cot_far_kernel(side, near, other, weight, slope, dense, held, up_grad, grad_mixed, cot_turned, low):
    half = TOK // 2

    @pl.when(pl.program_id(0) == 0)
    def _():
        for k, rows in enumerate((near, other)):
            low[k * half : k * half + half] = rows[...].astype(BF16)
            put_turned(cot_turned.at[:, :, :, k * half : k * half + half], rows[...])
        grad_mixed[...] = contract_cols(low[...], dense[...]).astype(BF16)

    up_grad[...] = (contract_cols(low[...], weight[...]) * slope[...]).astype(BF16)


def cot_far(side, near, other, weight, slope, dense, held):
    width = 256
    steps = slope.shape[1] // width
    column = pl.BlockSpec((TOK, width), lambda j, s: (0, j))
    return pl.pallas_call(
        cot_far_kernel,
        grid_spec=pltpu.PrefetchScalarGridSpec(
            num_scalar_prefetch=1,
            grid=(steps,),
            in_specs=[
                whole((TOK // 2, D)),
                whole((TOK // 2, D)),
                pl.BlockSpec((width, D), lambda j, s: (s[0] * steps + j, 0)),
                column,
                pl.BlockSpec((HD, D), lambda j, s: (s[0], 0)),
                pl.BlockSpec(memory_space=pl.ANY),
            ],
            out_specs=[
                column,
                pl.BlockSpec((TOK, HD), lambda j, s: (0, 0)),
                pl.BlockSpec((16, 2, 64, TOK), lambda j, s: (0, 0, 0, 1)),
            ],
            scratch_shapes=[pltpu.VMEM((TOK, D), BF16)],
        ),
        out_shape=[
            jax.ShapeDtypeStruct((TOK, slope.shape[1]), BF16),
            jax.ShapeDtypeStruct((TOK, HD), BF16),
            jax.ShapeDtypeStruct(TURNED, BF16),
        ],
        input_output_aliases={6: 2},
        compiler_params=pltpu.CompilerParams(vmem_limit_bytes=VMEM),
        cost_estimate=COST,
    )(side, near, other, weight, slope, dense, held)


def slope_far_kernel(side, second, weight, bias, slope, act_out):
    upward = plain_dot(second[...], weight[...]) + as_row(bias[0])
    below = phi(upward)
    slope[...] = gelu_slope(upward, below)

    @pl.when(pl.program_id(0) == pl.num_programs(0) - 1)
    def _():
        shared = act_out.shape[1]
        act_out[...] = (upward[:, -shared:] * below[:, -shared:]).astype(BF16)


def slope_far(side, second, weight, bias):
    units, width = weight.shape[1] // 2, 512
    steps = units // width
    return pl.pallas_call(
        slope_far_kernel,
        grid_spec=pltpu.PrefetchScalarGridSpec(
            num_scalar_prefetch=1,
            grid=(steps,),
            in_specs=[
                whole((TOK, D)),
                pl.BlockSpec((D, width), lambda j, s: (0, s[0] * steps + j)),
                pl.BlockSpec((1, width // 128, 128), lambda j, s: (s[0] * steps + j, 0, 0)),
            ],
            out_specs=[
                pl.BlockSpec((TOK, width), lambda j, s: (0, j)),
                pl.BlockSpec((TOK, units - WHOLE), lambda j, s: (0, 0)),
            ],
        ),
        out_shape=[
            jax.ShapeDtypeStruct((TOK, units), F32),
            jax.ShapeDtypeStruct((TOK, units - WHOLE), BF16),
        ],
        compiler_params=pltpu.CompilerParams(vmem_limit_bytes=VMEM),
        cost_estimate=COST,
    )(side, second, weight, bias.reshape(-1, width // 128, 128))


def turn(values, tables, sign):
    first = values[:, :128]
    cosine, rising, falling = tables
    first = (
        first * cosine[...]
        + (pltpu.roll(first, 32, 1) * rising[...] + pltpu.roll(first, 96, 1) * falling[...]) * sign
    )
    return jnp.concatenate([first, values[:, 128:]], axis=1)


def as_column(row):
    return jnp.broadcast_to(row, (8, row.shape[1])).T[:, 0:1]


def cosine_and_sine(angles):
    turns = jnp.floor(angles * (2.0 / math.pi) + 0.5)
    rest = ((angles - turns * 1.5703125) - turns * 4.837512969970703e-4) - turns * 7.549789954891882e-8
    square = rest * rest
    sine = ((-1.9515295891e-4 * square + 8.3321608736e-3) * square - 1.6666654611e-1) * square
    sine = sine * rest + rest
    cosine = (2.443315711809948e-5 * square - 1.388731625493765e-3) * square + 4.166664568298827e-2
    cosine = cosine * (square * square) - 0.5 * square + 1.0
    quarter = turns.astype(jnp.int32) & 3
    odd = (quarter & 1) == 1
    flipped = jnp.where(odd, sine, cosine), jnp.where(odd, cosine, sine)
    return (
        jnp.where((quarter == 1) | (quarter == 2), -flipped[0], flipped[0]),
        jnp.where(quarter >= 2, -flipped[1], flipped[1]),
    )


def project_kernel(place, first, weight, bias, marks, inverse, queries, keys, values, *tables):
    @pl.when(pl.program_id(0) == 0)
    def _():
        angles = inverse[...] * marks[1:2, :]
        cosine, sine = cosine_and_sine(angles)
        none, rest = jnp.zeros_like(sine), jnp.zeros((64, TOK), F32)
        tables[0][...] = jnp.concatenate([cosine, cosine, rest + 1.0], axis=0).T
        tables[1][...] = jnp.concatenate([none, sine, rest], axis=0).T
        tables[2][...] = jnp.concatenate([-sine, none, rest], axis=0).T

    head = pl.program_id(0) + place[0] * (2 - pl.num_programs(0))
    packed = plain_dot(first[...], weight[...]) + bias[pl.ds(head, 1), :]
    queries[...] = turn(packed[:, :HD], tables, 1.0).astype(BF16)
    keys[...] = turn(packed[:, HD : 2 * HD], tables, 1.0).astype(BF16)
    values[...] = packed[:, 2 * HD :].astype(BF16)


def project(place, heads, first, weight, bias, marks):
    inverse = jnp.asarray((10000.0 ** (-2.0 * np.arange(32) / ROT)).astype(np.float32).reshape(32, 1))
    at = (lambda h, s: h) if heads == 2 else (lambda h, s: s[0])
    column = pl.BlockSpec((TOK, HD), lambda h, s: (0, h))
    return pl.pallas_call(
        project_kernel,
        grid_spec=pltpu.PrefetchScalarGridSpec(
            num_scalar_prefetch=1,
            grid=(heads,),
            in_specs=[
                whole((TOK, D)),
                pl.BlockSpec((D, 3 * HD), lambda h, s: (0, at(h, s))),
                whole((2, 3 * HD)),
                whole((2, TOK)),
                whole((32, 1)),
            ],
            out_specs=[column] * 3 + [pl.BlockSpec((TOK, 128), lambda h, s: (0, 0))] * 3,
        ),
        out_shape=[jax.ShapeDtypeStruct((TOK, heads * HD), BF16)] * 3
        + [jax.ShapeDtypeStruct((TOK, 128), F32)] * 3,
        compiler_params=pltpu.CompilerParams(vmem_limit_bytes=VMEM),
        cost_estimate=COST,
    )(place, first, weight, bias, marks, inverse)


def attend_kernel(place, queries, keys, values, cosine, rising, falling, marks, *refs):
    given, (mixed_out, grad_out) = refs[:-2], refs[-2:]
    tables = (cosine, rising, falling)
    scale = 1.0 / math.sqrt(HD)
    queries, keys, values = queries[...], keys[...], values[...]
    segments = marks[0:1, :]

    def order(axis):
        return lax.rem(lax.broadcasted_iota(jnp.int32, (TOK, TOK), axis) + place[1], TOK)

    allowed = (as_column(segments) == segments) & (order(0) >= order(1))
    scores = jnp.where(allowed, contract_cols(queries, keys) * scale, NEGATIVE)
    top = jnp.max(scores, axis=-1, keepdims=True)
    weights = jnp.exp(scores - top)
    probs = weights / jnp.sum(weights, axis=-1, keepdims=True)
    probs_low = probs.astype(BF16)
    mixed_out[...] = plain_dot(probs_low, values).astype(BF16)
    grad_mixed = given[0][...]
    if len(given) == 2:
        grad_mixed = contract_cols(grad_mixed, given[1][...]).astype(BF16)
    grad_probs = contract_cols(grad_mixed, values)
    along = jnp.sum(probs * grad_probs, axis=-1, keepdims=True)
    grad_scores = (probs * (grad_probs - along)).astype(BF16)
    grad_query = plain_dot(grad_scores, keys) * scale
    grad_key = plain_dot(grad_scores.T, queries) * scale
    grad_value = plain_dot(probs_low.T, grad_mixed)
    grad_out[:, :HD] = turn(grad_query, tables, -1.0).astype(BF16)
    grad_out[:, HD : 2 * HD] = turn(grad_key, tables, -1.0).astype(BF16)
    grad_out[:, 2 * HD :] = grad_value.astype(BF16)


def attend(place, heads, projected, given, marks):
    column = pl.BlockSpec((TOK, HD), lambda h, s: (0, h))
    return pl.pallas_call(
        attend_kernel,
        grid_spec=pltpu.PrefetchScalarGridSpec(
            num_scalar_prefetch=1,
            grid=(heads,),
            in_specs=[column] * 3
            + [whole((TOK, 128))] * 3
            + [whole((2, TOK))]
            + ([column] if len(given) == 1 else [whole((TOK, D)), pl.BlockSpec((HD, D), lambda h, s: (h, 0))]),
            out_specs=[column, pl.BlockSpec((TOK, 3 * HD), lambda h, s: (0, h))],
        ),
        out_shape=[
            jax.ShapeDtypeStruct((TOK, heads * HD), BF16),
            jax.ShapeDtypeStruct((TOK, heads * 3 * HD), BF16),
        ],
        compiler_params=pltpu.CompilerParams(vmem_limit_bytes=VMEM),
        cost_estimate=COST,
    )(place, *projected, marks, *given)


def put_halves(core, values, scratch, mine, other):
    scratch[...] = values
    half = TOK // 2
    mine[...] = scratch[pl.ds(pl.multiple_of(core[0] * half, half), half), :]
    other[...] = scratch[pl.ds(pl.multiple_of((1 - core[0]) * half, half), half), :]


def branch_kernel(mixed, act, dense, down, total):
    total[...] = plain_dot(act[...], down[...]) + plain_dot(mixed[...], dense[...])


def back_kernel(
    core, packed, up_grad, qkv, up, hidden, stats, gain, gain_two, mine, other, sums, scratch
):
    first = contract_cols(packed[...], qkv[...])
    second = contract_cols(up_grad[...], up[...])
    put_halves(core, first * gain[...] + second * gain_two[...], scratch, mine, other)
    normed = (hidden[...].astype(F32) - stats[:, 0:1]) * stats[:, 64:65]
    rows = [
        jnp.sum(v, axis=0, keepdims=True) for v in (first * normed, first, second * normed, second)
    ]
    sums[...] = jnp.concatenate(rows + [jnp.zeros((4, first.shape[1]), F32)], axis=0)


def halves_call(kernel, core, operands, specs, with_sums):
    width = 512
    half = pl.BlockSpec((TOK // 2, width), lambda j, s: (0, j))
    return pl.pallas_call(
        kernel,
        grid_spec=pltpu.PrefetchScalarGridSpec(
            num_scalar_prefetch=1,
            grid=(D // width,),
            in_specs=specs,
            out_specs=[half, half] + [pl.BlockSpec((8, width), lambda j, s: (0, j))] * with_sums,
            scratch_shapes=[pltpu.VMEM((TOK, width), F32)],
        ),
        out_shape=[jax.ShapeDtypeStruct((TOK // 2, D), F32)] * 2
        + [jax.ShapeDtypeStruct((8, D), F32)] * with_sums,
        compiler_params=pltpu.CompilerParams(vmem_limit_bytes=VMEM),
        cost_estimate=COST,
    )(core, *operands)


def branches(mixed, act, dense, down):
    width = 512
    return pl.pallas_call(
        branch_kernel,
        grid=(D // width,),
        in_specs=[whole(mixed.shape), whole(act.shape)]
        + [pl.BlockSpec((w.shape[0], width), lambda j: (0, j)) for w in (dense, down)],
        out_specs=pl.BlockSpec((TOK, width), lambda j: (0, j)),
        out_shape=jax.ShapeDtypeStruct((TOK, D), F32),
        compiler_params=pltpu.CompilerParams(vmem_limit_bytes=VMEM),
        cost_estimate=COST,
    )(mixed, act, dense, down)


def back_halves(core, packed, up_grad, qkv, up, hidden, stats, gain, gain_two):
    specs = [whole(packed.shape), whole(up_grad.shape)]
    specs += [pl.BlockSpec((512, w.shape[1]), lambda j, s: (j, 0)) for w in (qkv, up)]
    specs += [pl.BlockSpec((TOK, 512), lambda j, s: (0, j)), whole((TOK, 128))]
    specs += [pl.BlockSpec((1, 512), lambda j, s: (0, j))] * 2
    operands = (packed, up_grad, qkv, up, hidden, stats, gain.reshape(1, D), gain_two.reshape(1, D))
    return halves_call(back_kernel, core, operands, specs, True)


def final_kernel(n, half, branch, combined, hidden, cot, stats, bias, bias_too, *refs):
    output, input_grad = refs[n:]
    rows = hidden[...].astype(F32)
    output[...] = rows + branch[...] + bias[...] + bias_too[...]
    e = combined[...]
    inv_std = stats[:, 64:65]
    normed = (rows - stats[:, 0:1]) * inv_std
    input_grad[...] = cot[...].astype(F32) + inv_std * (
        e
        - jnp.mean(e, axis=-1, keepdims=True)
        - normed * jnp.mean(e * normed, axis=-1, keepdims=True)
    )


def final_half(half, branch, combined, hidden, cot, stats, biases, held):
    rows = 128
    steps = TOK // 2 // rows
    given = pl.BlockSpec((rows, D), lambda i, s: (i, 0))
    placed = pl.BlockSpec((rows, D), lambda i, s: (s[0] * steps + i, 0))
    return pl.pallas_call(
        partial(final_kernel, len(held)),
        grid_spec=pltpu.PrefetchScalarGridSpec(
            num_scalar_prefetch=1,
            grid=(steps,),
            in_specs=[placed, given, placed, placed]
            + [pl.BlockSpec((rows, 128), lambda i, s: (s[0] * steps + i, 0))]
            + [whole((1, D))] * 2
            + [pl.BlockSpec(memory_space=pl.ANY)] * len(held),
            out_specs=[placed, placed],
        ),
        out_shape=[jax.ShapeDtypeStruct((TOK, D), F32)] * 2,
        input_output_aliases={8: 0, 9: 1} if held else {},
        compiler_params=pltpu.CompilerParams(vmem_limit_bytes=VMEM_LESS),
        cost_estimate=COST,
    )(half, branch, combined, hidden, cot, stats, *(b.reshape(1, D) for b in biases), *held)


def joint_kernel(side, *refs):
    lefts, rights, target, held, arrived = refs[:3], refs[3:11], refs[11], refs[12:15], refs[15]
    step = pl.program_id(0)
    copies = [pltpu.make_async_copy(lefts[k], held[k], arrived.at[k]) for k in range(3)]

    def put(columns, k, n, given):
        right = jnp.concatenate([rights[2 * n][:, given], rights[2 * n + 1][:, given]], axis=0)
        total = plain_dot(held[k][...].reshape(D, 2 * TOK), right)
        target[:, :, columns] = total.reshape(16, 128, -1)

    @pl.when(step == 0)
    def _():
        for copy in copies:
            copy.start()
        copies[0].wait()

    @pl.when(step < 2)
    def _():
        put(slice(0, 512), 0, 0, slice(0, 512))

    @pl.when(step == 2)
    def _():
        copies[1].wait()
        copies[2].wait()
        put(slice(0, HD), 1, 1, slice(0, HD))
        put(slice(HD, 512), 2, 2, slice(0, 512 - HD))

    @pl.when(step == 3)
    def _():
        put(slice(0, 512), 2, 2, slice(512 - HD, 3 * HD))

    @pl.when(step == 4)
    def _():
        put(slice(0, 1024 - WHOLE), 1, 3, slice(0, 1024 - WHOLE))


def joint(side, lefts, rights):
    specs = [pl.BlockSpec(memory_space=pl.ANY)] * 3
    for width, n in ((512, 2), (HD, 1), (3 * HD, 1)):

        def near(j, s, n=n):
            return (0, s[0] * n + jnp.clip(j, 0, n - 1))

        def far(j, s, n=n):
            return (0, jnp.clip(j, 0, n - 1))

        specs += [pl.BlockSpec((TOK, width), near), pl.BlockSpec((TOK, width), far)]
    shared = 1024 - WHOLE
    specs += [
        pl.BlockSpec((TOK, shared), lambda j, s: (0, (s[0] + 1) * (1024 // shared) - 1)),
        pl.BlockSpec((TOK, shared), lambda j, s: (0, 0)),
    ]
    return pl.pallas_call(
        joint_kernel,
        grid_spec=pltpu.PrefetchScalarGridSpec(
            num_scalar_prefetch=1,
            grid=(5,),
            in_specs=specs,
            out_specs=pl.BlockSpec((16, 128, 512), lambda j, s: (0, 0, j)),
            scratch_shapes=[pltpu.VMEM(TURNED, BF16)] * 3 + [pltpu.SemaphoreType.DMA((3,))],
        ),
        out_shape=jax.ShapeDtypeStruct((16, 128, 2048 + shared), F32),
        compiler_params=pltpu.CompilerParams(vmem_limit_bytes=VMEM),
        cost_estimate=COST,
    )(side, *lefts, *rights)


def assemble_kernel(side, near, far, part, up, dense, qkv, down):
    def put(low, high):
        up[...] = jnp.concatenate([low[:, :1024], high[:, :1024]], axis=1)
        dense[...] = jnp.concatenate([low[:, 1024:1280], high[:, 1024:1280]], axis=1)
        qkv[...] = jnp.concatenate([low[:, 1280:2048], high[:, 1280:2048]], axis=1)
        down[...] = jnp.concatenate(
            [part[:, :WHOLE], low[:, 2048:], part[:, WHOLE:], high[:, 2048:]], axis=1
        )

    @pl.when(side[0] == 0)
    def _():
        put(near[0], far[...])

    @pl.when(side[0] != 0)
    def _():
        put(far[...], near[0])


def assemble(side, near, far, part):
    shapes = ((64, 2048), (64, 512), (64, 1536), (64, 2048))
    columns = far.shape[1]
    return pl.pallas_call(
        assemble_kernel,
        grid_spec=pltpu.PrefetchScalarGridSpec(
            num_scalar_prefetch=1,
            grid=(1,),
            in_specs=[
                pl.BlockSpec((1, 64, columns), lambda i, s: (0, s[0], 0)),
                pl.BlockSpec((64, columns), lambda i, s: (0, 0)),
                pl.BlockSpec((64, 2 * WHOLE), lambda i, s: (0, 0)),
            ],
            out_specs=[pl.BlockSpec(shape, lambda i, s: (0, 0)) for shape in shapes],
        ),
        out_shape=[jax.ShapeDtypeStruct(shape, F32) for shape in shapes],
        compiler_params=pltpu.CompilerParams(vmem_limit_bytes=VMEM_LESS),
        cost_estimate=COST,
    )(side, near, far, part)


def body(
    hidden_in,
    segment_ids,
    positions,
    ln1_gain,
    ln1_bias,
    qkv_weight,
    qkv_bias,
    dense_weight,
    dense_bias,
    ln2_gain,
    ln2_bias,
    fc1_weight,
    fc1_bias,
    fc2_weight,
    fc2_bias,
    cotangent,
):
    core = lax.axis_index("c")
    side = lax.axis_index("zl")
    half_rows = TOK // 2
    at_side = side.astype(jnp.int32).reshape(1)
    at_core = core.astype(jnp.int32).reshape(1)
    own_place = jnp.zeros((2,), jnp.int32)
    far_place = jnp.stack([side, core * half_rows]).astype(jnp.int32)
    after = lax.optimization_barrier
    params = (ln1_gain, ln1_bias, ln2_gain, ln2_bias)

    def of_core(values, which):
        return lax.dynamic_slice_in_dim(values, which * half_rows, half_rows, 0)

    act_low, slope, down_grad = feed(
        hidden_in, ln2_gain, ln2_bias, cotangent, fc1_weight, fc1_bias
    )
    down_sum = after(lax.psum_scatter(down_grad, ("x", "y"), scatter_dimension=0, tiled=True))
    _, cotangent, hidden_in = after((down_grad, cotangent, hidden_in))

    hidden_got = send(of_core(hidden_in, core).astype(F32), "zl")
    marks = jnp.concatenate([segment_ids, positions]).astype(F32).reshape(1, 2 * TOK)
    cot_sent = jnp.concatenate(
        [of_core(cotangent, core).astype(F32), jnp.pad(marks, ((0, 7), (0, D - 2 * TOK)))], axis=0
    )
    cot_got = lax.ppermute(cot_sent, ("zl", "zh"), [(i, 3 - i) for i in range(4)])

    own_marks = marks.reshape(2, TOK)

    def own_step(hidden_in, cotangent, act_low, slope):
        first_in, *turned, stats = first(hidden_in, cotangent, params)
        projected = project(own_place, 2, first_in, qkv_weight, qkv_bias, own_marks)
        mixed_low, grad_packed = attend(
            own_place, 2, projected, (cotangent, dense_weight), own_marks
        )
        grad_up = feed_back(cotangent, fc2_weight, slope)
        branch = branches(mixed_low, act_low, dense_weight, fc2_weight)
        return *turned, stats, mixed_low, grad_packed, grad_up, branch

    (
        first_turned,
        second_turned,
        cot_turned,
        stats,
        mixed_low,
        grad_packed,
        grad_up,
        branch,
    ) = lax.cond(core > 1, own_step, own_step, hidden_in, cotangent, act_low, slope)
    branch = lax.psum(branch, TENSOR)
    hidden_got, mixed_low = after((hidden_got, mixed_low))
    hidden_too = send(hidden_got, "c")
    hidden_too, cot_got = after((hidden_too, cot_got))
    cot_too = send(cot_got, "c")

    first_far_in, second_far_in, first_turned, second_turned = first_far(
        hidden_got, hidden_too, params, (first_turned, second_turned)
    )
    slope_side, act_far = slope_far(at_side, second_far_in, fc1_weight, fc1_bias)
    marks_got = cot_got[half_rows, : 2 * TOK].reshape(2, 2, half_rows)
    marks_far = jnp.where(core == 0, marks_got, marks_got[:, ::-1]).reshape(2, TOK)
    projected_far = project(far_place, 1, first_far_in, qkv_weight, qkv_bias, marks_far)
    grad_up_far, grad_mixed_far, cot_turned = cot_far(
        at_side, cot_got, cot_too, fc2_weight, slope_side, dense_weight, cot_turned
    )
    mixed_far, grad_packed_far = attend(
        far_place, 1, projected_far, (grad_mixed_far,), marks_far
    )
    joint_grad = joint(
        at_side,
        (second_turned, cot_turned, first_turned),
        (
            grad_up,
            grad_up_far,
            mixed_low,
            mixed_far,
            grad_packed,
            grad_packed_far,
            act_low,
            act_far,
        ),
    )
    joint_grad, down_sum = after((joint_grad, down_sum))
    joint_sum = after(lax.psum_scatter(joint_grad, ("x", "y"), scatter_dimension=0, tiled=True))
    _, grad_packed, grad_up, cotangent, down_sum = after(
        (joint_grad, grad_packed, grad_up, cotangent, down_sum)
    )

    combined, combined_other, norms = back_halves(
        at_core, grad_packed, grad_up, qkv_weight, fc1_weight, hidden_in, stats, ln1_gain, ln2_gain
    )
    combined = combined + send(combined_other, "c")
    combined_too = send(combined, "zh")

    norms = norms[:4].reshape(4, 32, 64).transpose(1, 0, 2).reshape(32, 256)
    grad_out = cotangent.astype(F32)
    bias_sum = jnp.sum(grad_out, axis=0)
    qkv_bias_sum = jnp.sum(grad_packed.astype(F32), axis=0)
    up_bias_grad = jnp.sum(grad_up.astype(F32), axis=0)
    small = jnp.concatenate(
        [
            norms,
            bias_sum.reshape(32, 64),
            qkv_bias_sum.reshape(2, 32, 24).transpose(1, 0, 2).reshape(32, 48),
            up_bias_grad.reshape(16, 32, 4).transpose(1, 0, 2).reshape(32, 64),
            jnp.zeros((32, 80), F32),
        ],
        axis=1,
    )
    def of_side(values, which):
        return lax.dynamic_slice_in_dim(values[0], which * 64, 64, 0)

    down_far = send(of_side(down_sum, 1 - side), "zl")
    for axis in ("x", "y"):
        small = small + swap(small, axis, 1)
        small = small + swap(small, axis, 2)
    block = lax.axis_index("x") * 4 + lax.axis_index("y")
    own_small = lax.dynamic_slice_in_dim(small, side * 16 + block, 1, 0)
    far_small = lax.dynamic_slice_in_dim(small, (1 - side) * 16 + block, 1, 0)
    small = (own_small + send(far_small, "zl")).reshape(-1)

    norms = small[:256]
    norms = norms + send(norms, "c")
    norms = norms + send(norms, "zh")
    norms, branch, combined_too, down_far = after((norms, branch, combined_too, down_far))
    combined = combined + combined_too
    norms = norms.reshape(4, 64)
    bias_total = small[256:320]
    biases = (dense_bias, fc2_bias)
    own = (hidden_in, cotangent, stats, biases)
    combined_too = send(combined, "c")
    finals = final_half(at_core, branch, combined, *own, ())
    finals = final_half(1 - at_core, branch, combined_too, *own, finals)
    output, input_grad, joint_sum = after((*finals, joint_sum))

    down_sum = of_side(down_sum, side) + down_far
    joint_far = send(of_side(joint_sum, 1 - side), "zl")
    up_sum, dense_sum, qkv_sum, down_sum = assemble(at_side, joint_sum, joint_far, down_sum)
    return (
        output,
        input_grad,
        norms[0],
        norms[1],
        qkv_sum,
        small[320:368].reshape(2, 24),
        dense_sum.T,
        bias_total,
        norms[2],
        norms[3],
        up_sum,
        small[368:432].reshape(16, 4),
        down_sum.T,
        bias_total,
    )


def solution(mesh):
    fine = Mesh(mesh.devices.reshape(tuple(SIZES.values())), tuple(SIZES))
    return jax.shard_map(
        body,
        mesh=fine,
        in_specs=(
            P(DP, None),
            P(DP),
            P(DP),
            P(),
            P(),
            P(None, TENSOR),
            P(TENSOR, None),
            P(TENSOR, None),
            P(),
            P(),
            P(),
            P(None, TENSOR),
            P(TENSOR, None),
            P(TENSOR, None),
            P(),
            P(DP, None),
        ),
        out_specs=(
            P(DP, None),
            P(DP, None),
            P(DP),
            P(DP),
            P(DP, TENSOR),
            P(TENSOR, DP),
            P(TENSOR, DP),
            P(DP),
            P(DP),
            P(DP),
            P(DP, TENSOR),
            P(TENSOR, DP),
            P(TENSOR, DP),
            P(DP),
        ),
        check_vma=False,
    )
```

```python
from functools import partial
import math

import jax
import jax.numpy as jnp
import numpy as np
from jax import lax
from jax.experimental import pallas as pl
from jax.experimental.pallas import tpu as pltpu
from jax.sharding import Mesh, PartitionSpec as P

HD = 256
ROT = 64
TOK = 512
D = 2048
EPSILON = 1e-05
NEGATIVE = -1000000000.0
SIZES = {"zl": 2, "x": 4, "y": 4, "zh": 2, "c": 2}
DP = ("zl", "x", "y")
TENSOR = ("zh", "c")
F32 = jnp.float32
BF16 = jnp.bfloat16


def send(value, axis, step=1):
    n = SIZES[axis]
    return lax.ppermute(value, axis, [(i, (i + step) % n) for i in range(n)])


def swap(value, axis, bit):
    return lax.ppermute(value, axis, [(i, i ^ bit) for i in range(SIZES[axis])])


def plain_dot(left, right):
    return jnp.dot(left, right, preferred_element_type=F32)


def contract_cols(left, right):
    return lax.dot_general(left, right, (((1,), (1,)), ((), ())), preferred_element_type=F32)


VMEM = 56 * 1024 * 1024
VMEM_LESS = 24 * 1024 * 1024
WHOLE = 896
COST = pl.CostEstimate(flops=1000000, bytes_accessed=1000000, transcendentals=0)


def whole(shape):
    return pl.BlockSpec(shape, lambda *_: (0,) * len(shape), pipeline_mode=pl.Buffered(1))


def put_turned(target, rows):
    for z in range(2):
        for pair in range(8):
            start = z * 1024 + pair * 128
            block = rows[:, start : start + 128].T.astype(BF16)
            target[2 * pair, z] = block[:64]
            target[2 * pair + 1, z] = block[64:]


def normalise(hidden):
    average = jnp.mean(hidden, axis=-1, keepdims=True)
    centred = hidden - average
    inv_std = lax.rsqrt(jnp.mean(centred * centred, axis=-1, keepdims=True) + EPSILON)
    return centred * inv_std, average, inv_std


def first_kernel(
    hidden,
    cot,
    gain,
    shift,
    gain_two,
    shift_two,
    first_out,
    first_turned,
    second_turned,
    cot_turned,
    stats,
):
    normed, average, inv_std = normalise(hidden[...].astype(F32))
    first = normed * gain[...] + shift[...]
    first_out[...] = first.astype(BF16)
    put_turned(first_turned, first)
    put_turned(second_turned, normed * gain_two[...] + shift_two[...])
    put_turned(cot_turned, cot[...].astype(F32))
    lane = lax.broadcasted_iota(jnp.int32, (normed.shape[0], 128), 1)
    stats[...] = jnp.where(lane < 64, average, inv_std)


def first_far_kernel(near, other, gain, shift, gain_two, shift_two, *refs):
    first_out, second_out, first_turned, second_turned = refs[2:]

    def step(rows):
        normed, _, _ = normalise(rows)
        first = normed * gain[...] + shift[...]
        second = normed * gain_two[...] + shift_two[...]
        first_out[...] = first.astype(BF16)
        second_out[...] = second.astype(BF16)
        put_turned(first_turned, first)
        put_turned(second_turned, second)

    @pl.when(pl.program_id(0) < 2)
    def _():
        step(near[...])

    @pl.when(pl.program_id(0) >= 2)
    def _():
        step(other[...])


TURNED = (16, 2, 64, 2 * TOK)


def first(hidden, cot, params):
    rows = TOK // 2
    plain = pl.BlockSpec((rows, D), lambda i: (i, 0))
    return pl.pallas_call(
        first_kernel,
        grid=(2,),
        in_specs=[plain] * 2 + [whole((1, D))] * 4,
        out_specs=[plain]
        + [pl.BlockSpec((16, 2, 64, rows), lambda i: (0, 0, 0, i))] * 3
        + [pl.BlockSpec((rows, 128), lambda i: (i, 0))],
        out_shape=[jax.ShapeDtypeStruct((TOK, D), BF16)]
        + [jax.ShapeDtypeStruct(TURNED, BF16)] * 3
        + [jax.ShapeDtypeStruct((TOK, 128), F32)],
        compiler_params=pltpu.CompilerParams(vmem_limit_bytes=VMEM),
        cost_estimate=COST,
    )(hidden, cot, *(p.reshape(1, D) for p in params))


def first_far(near, other, params, held):
    rows = 128
    plain = pl.BlockSpec((rows, D), lambda i: (i, 0))
    return pl.pallas_call(
        first_far_kernel,
        grid=(TOK // rows,),
        in_specs=[
            pl.BlockSpec((rows, D), lambda i: (lax.min(i, 1), 0)),
            pl.BlockSpec((rows, D), lambda i: (lax.max(i - 2, 0), 0)),
        ]
        + [whole((1, D))] * 4
        + [pl.BlockSpec(memory_space=pl.ANY)] * 2,
        out_specs=[plain] * 2
        + [pl.BlockSpec((16, 2, 64, rows), lambda i: (0, 0, 0, i + TOK // rows))] * 2,
        out_shape=[jax.ShapeDtypeStruct((TOK, D), BF16)] * 2
        + [jax.ShapeDtypeStruct(TURNED, BF16)] * 2,
        input_output_aliases={6: 2, 7: 3},
        compiler_params=pltpu.CompilerParams(vmem_limit_bytes=VMEM),
        cost_estimate=COST,
    )(near, other, *(p.reshape(1, D) for p in params), *held)


def phi(upward):
    return 0.5 * (1.0 + lax.erf(upward * math.sqrt(0.5)))


def gelu_slope(upward, below):
    return below + upward * (jnp.exp(-0.5 * upward * upward) * (1.0 / math.sqrt(2.0 * math.pi)))


def as_row(block):
    return jnp.concatenate([block[i : i + 1, :] for i in range(block.shape[0])], axis=1)


def feed_kernel(hidden, gain, shift, cot, weight, bias, act_out, slope_out, down_grad, second):
    @pl.when(pl.program_id(0) == 0)
    def _():
        for start in (0, TOK // 2):
            rows = slice(start, start + TOK // 2)
            normed, _, _ = normalise(hidden[rows].astype(F32))
            second[rows] = (normed * gain[...] + shift[...]).astype(BF16)

    upward = plain_dot(second[...], weight[...]) + as_row(bias[0])
    below = phi(upward)
    act = (upward * below).astype(BF16)
    act_out[...] = act
    slope_out[...] = gelu_slope(upward, below)
    total = lax.dot_general(
        cot[...], act[:, :WHOLE], (((0,), (0,)), ((), ())), preferred_element_type=F32
    )
    for z in range(2):
        rows = total[z * 1024 : z * 1024 + 1024]
        down_grad[:, z * 64 : z * 64 + 64] = rows.reshape(16, 64, -1)


def feed(hidden, gain, shift, cot, weight, bias):
    units, width = weight.shape[1], 1024
    column = pl.BlockSpec((TOK, width), lambda j: (0, j))
    return pl.pallas_call(
        feed_kernel,
        grid=(units // width,),
        in_specs=[
            whole((TOK, D)),
            whole((1, D)),
            whole((1, D)),
            whole((TOK, D)),
            pl.BlockSpec((D, width), lambda j: (0, j)),
            pl.BlockSpec((1, width // 128, 128), lambda j: (j, 0, 0)),
        ],
        out_specs=[column, column, pl.BlockSpec((16, 128, WHOLE), lambda j: (0, 0, j))],
        out_shape=[
            jax.ShapeDtypeStruct((TOK, units), BF16),
            jax.ShapeDtypeStruct((TOK, units), F32),
            jax.ShapeDtypeStruct((16, 128, 2 * WHOLE), F32),
        ],
        scratch_shapes=[pltpu.VMEM((TOK, D), BF16)],
        compiler_params=pltpu.CompilerParams(vmem_limit_bytes=VMEM),
        cost_estimate=COST,
    )(
        hidden,
        gain.reshape(1, D),
        shift.reshape(1, D),
        cot,
        weight,
        bias.reshape(-1, width // 128, 128),
    )


def feed_back_kernel(cot, weight, slope, up_grad):
    up_grad[...] = (contract_cols(cot[...], weight[...]) * slope[...]).astype(BF16)


def feed_back(cot, weight, slope):
    units, width = slope.shape[1], 512
    column = pl.BlockSpec((TOK, width), lambda j: (0, j))
    return pl.pallas_call(
        feed_back_kernel,
        grid=(units // width,),
        in_specs=[whole((TOK, D)), pl.BlockSpec((width, D), lambda j: (j, 0)), column],
        out_specs=column,
        out_shape=jax.ShapeDtypeStruct((TOK, units), BF16),
        compiler_params=pltpu.CompilerParams(vmem_limit_bytes=VMEM),
        cost_estimate=COST,
    )(cot, weight, slope)


def cot_far_kernel(side, near, other, weight, slope, dense, held, up_grad, grad_mixed, cot_turned, low):
    half = TOK // 2

    @pl.when(pl.program_id(0) == 0)
    def _():
        for k, rows in enumerate((near, other)):
            low[k * half : k * half + half] = rows[...].astype(BF16)
            put_turned(cot_turned.at[:, :, :, k * half : k * half + half], rows[...])
        grad_mixed[...] = contract_cols(low[...], dense[...]).astype(BF16)

    up_grad[...] = (contract_cols(low[...], weight[...]) * slope[...]).astype(BF16)


def cot_far(side, near, other, weight, slope, dense, held):
    width = 256
    steps = slope.shape[1] // width
    column = pl.BlockSpec((TOK, width), lambda j, s: (0, j))
    return pl.pallas_call(
        cot_far_kernel,
        grid_spec=pltpu.PrefetchScalarGridSpec(
            num_scalar_prefetch=1,
            grid=(steps,),
            in_specs=[
                whole((TOK // 2, D)),
                whole((TOK // 2, D)),
                pl.BlockSpec((width, D), lambda j, s: (s[0] * steps + j, 0)),
                column,
                pl.BlockSpec((HD, D), lambda j, s: (s[0], 0)),
                pl.BlockSpec(memory_space=pl.ANY),
            ],
            out_specs=[
                column,
                pl.BlockSpec((TOK, HD), lambda j, s: (0, 0)),
                pl.BlockSpec((16, 2, 64, TOK), lambda j, s: (0, 0, 0, 1)),
            ],
            scratch_shapes=[pltpu.VMEM((TOK, D), BF16)],
        ),
        out_shape=[
            jax.ShapeDtypeStruct((TOK, slope.shape[1]), BF16),
            jax.ShapeDtypeStruct((TOK, HD), BF16),
            jax.ShapeDtypeStruct(TURNED, BF16),
        ],
        input_output_aliases={6: 2},
        compiler_params=pltpu.CompilerParams(vmem_limit_bytes=VMEM),
        cost_estimate=COST,
    )(side, near, other, weight, slope, dense, held)


def slope_far_kernel(side, second, weight, bias, slope, act_out):
    upward = plain_dot(second[...], weight[...]) + as_row(bias[0])
    below = phi(upward)
    slope[...] = gelu_slope(upward, below)

    @pl.when(pl.program_id(0) == pl.num_programs(0) - 1)
    def _():
        shared = act_out.shape[1]
        act_out[...] = (upward[:, -shared:] * below[:, -shared:]).astype(BF16)


def slope_far(side, second, weight, bias):
    units, width = weight.shape[1] // 2, 512
    steps = units // width
    return pl.pallas_call(
        slope_far_kernel,
        grid_spec=pltpu.PrefetchScalarGridSpec(
            num_scalar_prefetch=1,
            grid=(steps,),
            in_specs=[
                whole((TOK, D)),
                pl.BlockSpec((D, width), lambda j, s: (0, s[0] * steps + j)),
                pl.BlockSpec((1, width // 128, 128), lambda j, s: (s[0] * steps + j, 0, 0)),
            ],
            out_specs=[
                pl.BlockSpec((TOK, width), lambda j, s: (0, j)),
                pl.BlockSpec((TOK, units - WHOLE), lambda j, s: (0, 0)),
            ],
        ),
        out_shape=[
            jax.ShapeDtypeStruct((TOK, units), F32),
            jax.ShapeDtypeStruct((TOK, units - WHOLE), BF16),
        ],
        compiler_params=pltpu.CompilerParams(vmem_limit_bytes=VMEM),
        cost_estimate=COST,
    )(side, second, weight, bias.reshape(-1, width // 128, 128))


def turn(values, tables, sign):
    first = values[:, :128]
    cosine, rising, falling = tables
    first = (
        first * cosine[...]
        + (pltpu.roll(first, 32, 1) * rising[...] + pltpu.roll(first, 96, 1) * falling[...]) * sign
    )
    return jnp.concatenate([first, values[:, 128:]], axis=1)


def as_column(row):
    return jnp.broadcast_to(row, (8, row.shape[1])).T[:, 0:1]


def cosine_and_sine(angles):
    turns = jnp.floor(angles * (2.0 / math.pi) + 0.5)
    rest = ((angles - turns * 1.5703125) - turns * 4.837512969970703e-4) - turns * 7.549789954891882e-8
    square = rest * rest
    sine = ((-1.9515295891e-4 * square + 8.3321608736e-3) * square - 1.6666654611e-1) * square
    sine = sine * rest + rest
    cosine = (2.443315711809948e-5 * square - 1.388731625493765e-3) * square + 4.166664568298827e-2
    cosine = cosine * (square * square) - 0.5 * square + 1.0
    quarter = turns.astype(jnp.int32) & 3
    odd = (quarter & 1) == 1
    flipped = jnp.where(odd, sine, cosine), jnp.where(odd, cosine, sine)
    return (
        jnp.where((quarter == 1) | (quarter == 2), -flipped[0], flipped[0]),
        jnp.where(quarter >= 2, -flipped[1], flipped[1]),
    )


def project_kernel(place, first, weight, bias, marks, inverse, queries, keys, values, *tables):
    @pl.when(pl.program_id(0) == 0)
    def _():
        angles = inverse[...] * marks[1:2, :]
        cosine, sine = cosine_and_sine(angles)
        none, rest = jnp.zeros_like(sine), jnp.zeros((64, TOK), F32)
        tables[0][...] = jnp.concatenate([cosine, cosine, rest + 1.0], axis=0).T
        tables[1][...] = jnp.concatenate([none, sine, rest], axis=0).T
        tables[2][...] = jnp.concatenate([-sine, none, rest], axis=0).T

    head = pl.program_id(0) + place[0] * (2 - pl.num_programs(0))
    packed = plain_dot(first[...], weight[...]) + bias[pl.ds(head, 1), :]
    queries[...] = turn(packed[:, :HD], tables, 1.0).astype(BF16)
    keys[...] = turn(packed[:, HD : 2 * HD], tables, 1.0).astype(BF16)
    values[...] = packed[:, 2 * HD :].astype(BF16)


def project(place, heads, first, weight, bias, marks):
    inverse = jnp.asarray((10000.0 ** (-2.0 * np.arange(32) / ROT)).astype(np.float32).reshape(32, 1))
    at = (lambda h, s: h) if heads == 2 else (lambda h, s: s[0])
    column = pl.BlockSpec((TOK, HD), lambda h, s: (0, h))
    return pl.pallas_call(
        project_kernel,
        grid_spec=pltpu.PrefetchScalarGridSpec(
            num_scalar_prefetch=1,
            grid=(heads,),
            in_specs=[
                whole((TOK, D)),
                pl.BlockSpec((D, 3 * HD), lambda h, s: (0, at(h, s))),
                whole((2, 3 * HD)),
                whole((2, TOK)),
                whole((32, 1)),
            ],
            out_specs=[column] * 3 + [pl.BlockSpec((TOK, 128), lambda h, s: (0, 0))] * 3,
        ),
        out_shape=[jax.ShapeDtypeStruct((TOK, heads * HD), BF16)] * 3
        + [jax.ShapeDtypeStruct((TOK, 128), F32)] * 3,
        compiler_params=pltpu.CompilerParams(vmem_limit_bytes=VMEM),
        cost_estimate=COST,
    )(place, first, weight, bias, marks, inverse)


def attend_kernel(place, queries, keys, values, cosine, rising, falling, marks, *refs):
    given, (mixed_out, grad_out) = refs[:-2], refs[-2:]
    tables = (cosine, rising, falling)
    scale = 1.0 / math.sqrt(HD)
    queries, keys, values = queries[...], keys[...], values[...]
    segments = marks[0:1, :]

    def order(axis):
        return lax.rem(lax.broadcasted_iota(jnp.int32, (TOK, TOK), axis) + place[1], TOK)

    allowed = (as_column(segments) == segments) & (order(0) >= order(1))
    scores = jnp.where(allowed, contract_cols(queries, keys) * scale, NEGATIVE)
    top = jnp.max(scores, axis=-1, keepdims=True)
    weights = jnp.exp(scores - top)
    probs = weights / jnp.sum(weights, axis=-1, keepdims=True)
    probs_low = probs.astype(BF16)
    mixed_out[...] = plain_dot(probs_low, values).astype(BF16)
    grad_mixed = given[0][...]
    if len(given) == 2:
        grad_mixed = contract_cols(grad_mixed, given[1][...]).astype(BF16)
    grad_probs = contract_cols(grad_mixed, values)
    along = jnp.sum(probs * grad_probs, axis=-1, keepdims=True)
    grad_scores = (probs * (grad_probs - along)).astype(BF16)
    grad_query = plain_dot(grad_scores, keys) * scale
    grad_key = plain_dot(grad_scores.T, queries) * scale
    grad_value = plain_dot(probs_low.T, grad_mixed)
    grad_out[:, :HD] = turn(grad_query, tables, -1.0).astype(BF16)
    grad_out[:, HD : 2 * HD] = turn(grad_key, tables, -1.0).astype(BF16)
    grad_out[:, 2 * HD :] = grad_value.astype(BF16)


def attend(place, heads, projected, given, marks):
    column = pl.BlockSpec((TOK, HD), lambda h, s: (0, h))
    return pl.pallas_call(
        attend_kernel,
        grid_spec=pltpu.PrefetchScalarGridSpec(
            num_scalar_prefetch=1,
            grid=(heads,),
            in_specs=[column] * 3
            + [whole((TOK, 128))] * 3
            + [whole((2, TOK))]
            + ([column] if len(given) == 1 else [whole((TOK, D)), pl.BlockSpec((HD, D), lambda h, s: (h, 0))]),
            out_specs=[column, pl.BlockSpec((TOK, 3 * HD), lambda h, s: (0, h))],
        ),
        out_shape=[
            jax.ShapeDtypeStruct((TOK, heads * HD), BF16),
            jax.ShapeDtypeStruct((TOK, heads * 3 * HD), BF16),
        ],
        compiler_params=pltpu.CompilerParams(vmem_limit_bytes=VMEM),
        cost_estimate=COST,
    )(place, *projected, marks, *given)


def put_halves(core, values, scratch, mine, other):
    scratch[...] = values
    half = TOK // 2
    mine[...] = scratch[pl.ds(pl.multiple_of(core[0] * half, half), half), :]
    other[...] = scratch[pl.ds(pl.multiple_of((1 - core[0]) * half, half), half), :]


def branch_kernel(mixed, act, dense, down, total):
    total[...] = plain_dot(act[...], down[...]) + plain_dot(mixed[...], dense[...])


def back_kernel(
    core, packed, up_grad, qkv, up, hidden, stats, gain, gain_two, mine, other, sums, scratch
):
    first = contract_cols(packed[...], qkv[...])
    second = contract_cols(up_grad[...], up[...])
    put_halves(core, first * gain[...] + second * gain_two[...], scratch, mine, other)
    normed = (hidden[...].astype(F32) - stats[:, 0:1]) * stats[:, 64:65]
    rows = [
        jnp.sum(v, axis=0, keepdims=True) for v in (first * normed, first, second * normed, second)
    ]
    sums[...] = jnp.concatenate(rows + [jnp.zeros((4, first.shape[1]), F32)], axis=0)


def halves_call(kernel, core, operands, specs, with_sums):
    width = 512
    half = pl.BlockSpec((TOK // 2, width), lambda j, s: (0, j))
    return pl.pallas_call(
        kernel,
        grid_spec=pltpu.PrefetchScalarGridSpec(
            num_scalar_prefetch=1,
            grid=(D // width,),
            in_specs=specs,
            out_specs=[half, half] + [pl.BlockSpec((8, width), lambda j, s: (0, j))] * with_sums,
            scratch_shapes=[pltpu.VMEM((TOK, width), F32)],
        ),
        out_shape=[jax.ShapeDtypeStruct((TOK // 2, D), F32)] * 2
        + [jax.ShapeDtypeStruct((8, D), F32)] * with_sums,
        compiler_params=pltpu.CompilerParams(vmem_limit_bytes=VMEM),
        cost_estimate=COST,
    )(core, *operands)


def branches(mixed, act, dense, down):
    width = 512
    return pl.pallas_call(
        branch_kernel,
        grid=(D // width,),
        in_specs=[whole(mixed.shape), whole(act.shape)]
        + [pl.BlockSpec((w.shape[0], width), lambda j: (0, j)) for w in (dense, down)],
        out_specs=pl.BlockSpec((TOK, width), lambda j: (0, j)),
        out_shape=jax.ShapeDtypeStruct((TOK, D), F32),
        compiler_params=pltpu.CompilerParams(vmem_limit_bytes=VMEM),
        cost_estimate=COST,
    )(mixed, act, dense, down)


def back_halves(core, packed, up_grad, qkv, up, hidden, stats, gain, gain_two):
    specs = [whole(packed.shape), whole(up_grad.shape)]
    specs += [pl.BlockSpec((512, w.shape[1]), lambda j, s: (j, 0)) for w in (qkv, up)]
    specs += [pl.BlockSpec((TOK, 512), lambda j, s: (0, j)), whole((TOK, 128))]
    specs += [pl.BlockSpec((1, 512), lambda j, s: (0, j))] * 2
    operands = (packed, up_grad, qkv, up, hidden, stats, gain.reshape(1, D), gain_two.reshape(1, D))
    return halves_call(back_kernel, core, operands, specs, True)


def final_kernel(n, half, branch, combined, hidden, cot, stats, bias, bias_too, *refs):
    output, input_grad = refs[n:]
    rows = hidden[...].astype(F32)
    output[...] = rows + branch[...] + bias[...] + bias_too[...]
    e = combined[...]
    inv_std = stats[:, 64:65]
    normed = (rows - stats[:, 0:1]) * inv_std
    input_grad[...] = cot[...].astype(F32) + inv_std * (
        e
        - jnp.mean(e, axis=-1, keepdims=True)
        - normed * jnp.mean(e * normed, axis=-1, keepdims=True)
    )


def final_half(half, branch, combined, hidden, cot, stats, biases, held):
    rows = 128
    steps = TOK // 2 // rows
    given = pl.BlockSpec((rows, D), lambda i, s: (i, 0))
    placed = pl.BlockSpec((rows, D), lambda i, s: (s[0] * steps + i, 0))
    return pl.pallas_call(
        partial(final_kernel, len(held)),
        grid_spec=pltpu.PrefetchScalarGridSpec(
            num_scalar_prefetch=1,
            grid=(steps,),
            in_specs=[placed, given, placed, placed]
            + [pl.BlockSpec((rows, 128), lambda i, s: (s[0] * steps + i, 0))]
            + [whole((1, D))] * 2
            + [pl.BlockSpec(memory_space=pl.ANY)] * len(held),
            out_specs=[placed, placed],
        ),
        out_shape=[jax.ShapeDtypeStruct((TOK, D), F32)] * 2,
        input_output_aliases={8: 0, 9: 1} if held else {},
        compiler_params=pltpu.CompilerParams(vmem_limit_bytes=VMEM_LESS),
        cost_estimate=COST,
    )(half, branch, combined, hidden, cot, stats, *(b.reshape(1, D) for b in biases), *held)


def joint_kernel(side, *refs):
    lefts, rights, target, held, right, arrived = (
        refs[:3],
        refs[3:11],
        refs[11],
        refs[12],
        refs[13],
        refs[14],
    )
    step = pl.program_id(0)
    copies = [pltpu.make_async_copy(lefts[k], held.at[k], arrived.at[k]) for k in range(3)]

    @pl.when(step == 0)
    def _():
        for copy in copies:
            copy.start()
        copies[0].wait()

    @pl.when(step == 4)
    def _():
        copies[1].wait()
        copies[2].wait()

    for n, (start, stop) in enumerate(((0, 4), (4, 5), (5, 8), (8, 9))):

        @pl.when((step >= start) & (step < stop))
        def _(n=n):
            for k in range(2):
                given = rights[2 * n + k]
                right[k * TOK : k * TOK + TOK, : given.shape[1]] = given[...]

    k = jnp.where(step < 4, 0, jnp.where((step >= 5) & (step < 8), 2, 1))
    target[...] = plain_dot(held[k].reshape(D, 2 * TOK), right[...]).reshape(16, 128, -1)


def joint(side, lefts, rights):
    width, shared = 256, 1024 - WHOLE
    specs = [pl.BlockSpec(memory_space=pl.ANY)] * 3
    for start, n in ((0, 4), (4, 1), (5, 3)):

        def near(j, s, start=start, n=n):
            return (0, s[0] * n + jnp.clip(j - start, 0, n - 1))

        def far(j, s, start=start, n=n):
            return (0, jnp.clip(j - start, 0, n - 1))

        specs += [pl.BlockSpec((TOK, width), near), pl.BlockSpec((TOK, width), far)]
    specs += [
        pl.BlockSpec((TOK, shared), lambda j, s: (0, (s[0] + 1) * (1024 // shared) - 1)),
        pl.BlockSpec((TOK, shared), lambda j, s: (0, 0)),
    ]
    return pl.pallas_call(
        joint_kernel,
        grid_spec=pltpu.PrefetchScalarGridSpec(
            num_scalar_prefetch=1,
            grid=(9,),
            in_specs=specs,
            out_specs=pl.BlockSpec((16, 128, width), lambda j, s: (0, 0, j)),
            scratch_shapes=[
                pltpu.VMEM((3,) + TURNED, BF16),
                pltpu.VMEM((2 * TOK, width), BF16),
                pltpu.SemaphoreType.DMA((3,)),
            ],
        ),
        out_shape=jax.ShapeDtypeStruct((16, 128, 2048 + shared), F32),
        compiler_params=pltpu.CompilerParams(vmem_limit_bytes=VMEM),
        cost_estimate=COST,
    )(side, *lefts, *rights)


def assemble_kernel(side, near, far, part, up, dense, qkv, down):
    def put(low, high):
        up[...] = jnp.concatenate([low[:, :1024], high[:, :1024]], axis=1)
        dense[...] = jnp.concatenate([low[:, 1024:1280], high[:, 1024:1280]], axis=1)
        qkv[...] = jnp.concatenate([low[:, 1280:2048], high[:, 1280:2048]], axis=1)
        down[...] = jnp.concatenate(
            [part[:, :WHOLE], low[:, 2048:], part[:, WHOLE:], high[:, 2048:]], axis=1
        )

    @pl.when(side[0] == 0)
    def _():
        put(near[0], far[...])

    @pl.when(side[0] != 0)
    def _():
        put(far[...], near[0])


def assemble(side, near, far, part):
    shapes = ((64, 2048), (64, 512), (64, 1536), (64, 2048))
    columns = far.shape[1]
    return pl.pallas_call(
        assemble_kernel,
        grid_spec=pltpu.PrefetchScalarGridSpec(
            num_scalar_prefetch=1,
            grid=(1,),
            in_specs=[
                pl.BlockSpec((1, 64, columns), lambda i, s: (0, s[0], 0)),
                pl.BlockSpec((64, columns), lambda i, s: (0, 0)),
                pl.BlockSpec((64, 2 * WHOLE), lambda i, s: (0, 0)),
            ],
            out_specs=[pl.BlockSpec(shape, lambda i, s: (0, 0)) for shape in shapes],
        ),
        out_shape=[jax.ShapeDtypeStruct(shape, F32) for shape in shapes],
        compiler_params=pltpu.CompilerParams(vmem_limit_bytes=VMEM_LESS),
        cost_estimate=COST,
    )(side, near, far, part)


def body(
    hidden_in,
    segment_ids,
    positions,
    ln1_gain,
    ln1_bias,
    qkv_weight,
    qkv_bias,
    dense_weight,
    dense_bias,
    ln2_gain,
    ln2_bias,
    fc1_weight,
    fc1_bias,
    fc2_weight,
    fc2_bias,
    cotangent,
):
    core = lax.axis_index("c")
    side = lax.axis_index("zl")
    half_rows = TOK // 2
    at_side = side.astype(jnp.int32).reshape(1)
    at_core = core.astype(jnp.int32).reshape(1)
    own_place = jnp.zeros((2,), jnp.int32)
    far_place = jnp.stack([side, core * half_rows]).astype(jnp.int32)
    after = lax.optimization_barrier
    params = (ln1_gain, ln1_bias, ln2_gain, ln2_bias)

    def of_core(values, which):
        return lax.dynamic_slice_in_dim(values, which * half_rows, half_rows, 0)

    act_low, slope, down_grad = feed(
        hidden_in, ln2_gain, ln2_bias, cotangent, fc1_weight, fc1_bias
    )
    down_sum = after(lax.psum_scatter(down_grad, ("x", "y"), scatter_dimension=0, tiled=True))
    _, cotangent, hidden_in = after((down_grad, cotangent, hidden_in))

    hidden_got = send(of_core(hidden_in, core).astype(F32), "zl")
    marks = jnp.concatenate([segment_ids, positions]).astype(F32).reshape(1, 2 * TOK)
    cot_sent = jnp.concatenate(
        [of_core(cotangent, core).astype(F32), jnp.pad(marks, ((0, 7), (0, D - 2 * TOK)))], axis=0
    )
    cot_got = lax.ppermute(cot_sent, ("zl", "zh"), [(i, 3 - i) for i in range(4)])

    own_marks = marks.reshape(2, TOK)

    def own_step(hidden_in, cotangent, act_low, slope):
        first_in, *turned, stats = first(hidden_in, cotangent, params)
        projected = project(own_place, 2, first_in, qkv_weight, qkv_bias, own_marks)
        mixed_low, grad_packed = attend(
            own_place, 2, projected, (cotangent, dense_weight), own_marks
        )
        grad_up = feed_back(cotangent, fc2_weight, slope)
        branch = branches(mixed_low, act_low, dense_weight, fc2_weight)
        return *turned, stats, mixed_low, grad_packed, grad_up, branch

    (
        first_turned,
        second_turned,
        cot_turned,
        stats,
        mixed_low,
        grad_packed,
        grad_up,
        branch,
    ) = lax.cond(core > 1, own_step, own_step, hidden_in, cotangent, act_low, slope)
    branch = lax.psum(branch, TENSOR)
    hidden_got, mixed_low = after((hidden_got, mixed_low))
    hidden_too = send(hidden_got, "c")
    hidden_too, cot_got = after((hidden_too, cot_got))
    cot_too = send(cot_got, "c")

    first_far_in, second_far_in, first_turned, second_turned = first_far(
        hidden_got, hidden_too, params, (first_turned, second_turned)
    )
    slope_side, act_far = slope_far(at_side, second_far_in, fc1_weight, fc1_bias)
    marks_got = cot_got[half_rows, : 2 * TOK].reshape(2, 2, half_rows)
    marks_far = jnp.where(core == 0, marks_got, marks_got[:, ::-1]).reshape(2, TOK)
    projected_far = project(far_place, 1, first_far_in, qkv_weight, qkv_bias, marks_far)
    grad_up_far, grad_mixed_far, cot_turned = cot_far(
        at_side, cot_got, cot_too, fc2_weight, slope_side, dense_weight, cot_turned
    )
    mixed_far, grad_packed_far = attend(
        far_place, 1, projected_far, (grad_mixed_far,), marks_far
    )
    joint_grad = joint(
        at_side,
        (second_turned, cot_turned, first_turned),
        (
            grad_up,
            grad_up_far,
            mixed_low,
            mixed_far,
            grad_packed,
            grad_packed_far,
            act_low,
            act_far,
        ),
    )
    joint_grad, down_sum = after((joint_grad, down_sum))
    joint_sum = after(lax.psum_scatter(joint_grad, ("x", "y"), scatter_dimension=0, tiled=True))
    _, grad_packed, grad_up, cotangent, down_sum = after(
        (joint_grad, grad_packed, grad_up, cotangent, down_sum)
    )

    combined, combined_other, norms = back_halves(
        at_core, grad_packed, grad_up, qkv_weight, fc1_weight, hidden_in, stats, ln1_gain, ln2_gain
    )
    combined = combined + send(combined_other, "c")
    combined_too = send(combined, "zh")

    norms = norms[:4].reshape(4, 32, 64).transpose(1, 0, 2).reshape(32, 256)
    grad_out = cotangent.astype(F32)
    bias_sum = jnp.sum(grad_out, axis=0)
    qkv_bias_sum = jnp.sum(grad_packed.astype(F32), axis=0)
    up_bias_grad = jnp.sum(grad_up.astype(F32), axis=0)
    small = jnp.concatenate(
        [
            norms,
            bias_sum.reshape(32, 64),
            qkv_bias_sum.reshape(2, 32, 24).transpose(1, 0, 2).reshape(32, 48),
            up_bias_grad.reshape(16, 32, 4).transpose(1, 0, 2).reshape(32, 64),
            jnp.zeros((32, 80), F32),
        ],
        axis=1,
    )
    def of_side(values, which):
        return lax.dynamic_slice_in_dim(values[0], which * 64, 64, 0)

    down_far = send(of_side(down_sum, 1 - side), "zl")
    for axis in ("x", "y"):
        small = small + swap(small, axis, 1)
        small = small + swap(small, axis, 2)
    block = lax.axis_index("x") * 4 + lax.axis_index("y")
    own_small = lax.dynamic_slice_in_dim(small, side * 16 + block, 1, 0)
    far_small = lax.dynamic_slice_in_dim(small, (1 - side) * 16 + block, 1, 0)
    small = (own_small + send(far_small, "zl")).reshape(-1)

    norms = small[:256]
    norms = norms + send(norms, "c")
    norms = norms + send(norms, "zh")
    norms, branch, combined_too, down_far = after((norms, branch, combined_too, down_far))
    combined = combined + combined_too
    norms = norms.reshape(4, 64)
    bias_total = small[256:320]
    biases = (dense_bias, fc2_bias)
    own = (hidden_in, cotangent, stats, biases)
    combined_too = send(combined, "c")
    finals = final_half(at_core, branch, combined, *own, ())
    finals = final_half(1 - at_core, branch, combined_too, *own, finals)
    output, input_grad, joint_sum = after((*finals, joint_sum))

    down_sum = of_side(down_sum, side) + down_far
    joint_far = send(of_side(joint_sum, 1 - side), "zl")
    up_sum, dense_sum, qkv_sum, down_sum = assemble(at_side, joint_sum, joint_far, down_sum)
    return (
        output,
        input_grad,
        norms[0],
        norms[1],
        qkv_sum,
        small[320:368].reshape(2, 24),
        dense_sum.T,
        bias_total,
        norms[2],
        norms[3],
        up_sum,
        small[368:432].reshape(16, 4),
        down_sum.T,
        bias_total,
    )


def solution(mesh):
    fine = Mesh(mesh.devices.reshape(tuple(SIZES.values())), tuple(SIZES))
    return jax.shard_map(
        body,
        mesh=fine,
        in_specs=(
            P(DP, None),
            P(DP),
            P(DP),
            P(),
            P(),
            P(None, TENSOR),
            P(TENSOR, None),
            P(TENSOR, None),
            P(),
            P(),
            P(),
            P(None, TENSOR),
            P(TENSOR, None),
            P(TENSOR, None),
            P(),
            P(DP, None),
        ),
        out_specs=(
            P(DP, None),
            P(DP, None),
            P(DP),
            P(DP),
            P(DP, TENSOR),
            P(TENSOR, DP),
            P(TENSOR, DP),
            P(DP),
            P(DP),
            P(DP),
            P(DP, TENSOR),
            P(TENSOR, DP),
            P(TENSOR, DP),
            P(DP),
        ),
        check_vma=False,
    )
```

```python
from functools import partial
import math

import jax
import jax.numpy as jnp
import numpy as np
from jax import lax
from jax.experimental import pallas as pl
from jax.experimental.pallas import tpu as pltpu
from jax.sharding import Mesh, PartitionSpec as P

HD = 256
ROT = 64
TOK = 512
D = 2048
EPSILON = 1e-05
NEGATIVE = -1000000000.0
SIZES = {"zl": 2, "x": 4, "y": 4, "zh": 2, "c": 2}
DP = ("zl", "x", "y")
TENSOR = ("zh", "c")
F32 = jnp.float32
BF16 = jnp.bfloat16


def send(value, axis, step=1):
    n = SIZES[axis]
    return lax.ppermute(value, axis, [(i, (i + step) % n) for i in range(n)])


def swap(value, axis, bit):
    return lax.ppermute(value, axis, [(i, i ^ bit) for i in range(SIZES[axis])])


def plain_dot(left, right):
    return jnp.dot(left, right, preferred_element_type=F32)


def contract_cols(left, right):
    return lax.dot_general(left, right, (((1,), (1,)), ((), ())), preferred_element_type=F32)


VMEM = 56 * 1024 * 1024
VMEM_LESS = 24 * 1024 * 1024
WHOLE = 896
COST = pl.CostEstimate(flops=1000000, bytes_accessed=1000000, transcendentals=0)


def whole(shape):
    return pl.BlockSpec(shape, lambda *_: (0,) * len(shape), pipeline_mode=pl.Buffered(1))


def put_turned(target, rows):
    for z in range(2):
        for pair in range(8):
            start = z * 1024 + pair * 128
            block = rows[:, start : start + 128].T.astype(BF16)
            target[2 * pair, z] = block[:64]
            target[2 * pair + 1, z] = block[64:]


def normalise(hidden):
    average = jnp.mean(hidden, axis=-1, keepdims=True)
    centred = hidden - average
    inv_std = lax.rsqrt(jnp.mean(centred * centred, axis=-1, keepdims=True) + EPSILON)
    return centred * inv_std, average, inv_std


def sent_kernel(core, hidden, cot, marks, hidden_out, cot_out):
    half = TOK // 2
    hidden_out[...] = hidden[...].astype(F32)
    cot_out[:half] = cot[...].astype(F32)
    row = jnp.concatenate([marks[...], jnp.zeros((1, D - 2 * TOK), F32)], axis=1)
    cot_out[half : half + 8] = jnp.broadcast_to(row, (8, D))


def sent(core, hidden, cot, marks):
    half = TOK // 2
    rows = pl.BlockSpec((half, D), lambda i, s: (s[0], 0))
    return pl.pallas_call(
        sent_kernel,
        grid_spec=pltpu.PrefetchScalarGridSpec(
            num_scalar_prefetch=1,
            grid=(1,),
            in_specs=[rows, rows, pl.BlockSpec((1, 2 * TOK), lambda i, s: (0, 0))],
            out_specs=[
                pl.BlockSpec((half, D), lambda i, s: (0, 0)),
                pl.BlockSpec((half + 8, D), lambda i, s: (0, 0)),
            ],
        ),
        out_shape=[
            jax.ShapeDtypeStruct((half, D), F32),
            jax.ShapeDtypeStruct((half + 8, D), F32),
        ],
        compiler_params=pltpu.CompilerParams(vmem_limit_bytes=VMEM),
        cost_estimate=COST,
    )(core, hidden, cot, marks)


def first_kernel(
    hidden,
    cot,
    gain,
    shift,
    gain_two,
    shift_two,
    first_out,
    first_turned,
    second_turned,
    cot_turned,
    stats,
):
    normed, average, inv_std = normalise(hidden[...].astype(F32))
    first = normed * gain[...] + shift[...]
    first_out[...] = first.astype(BF16)
    put_turned(first_turned, first)
    put_turned(second_turned, normed * gain_two[...] + shift_two[...])
    put_turned(cot_turned, cot[...].astype(F32))
    lane = lax.broadcasted_iota(jnp.int32, (normed.shape[0], 128), 1)
    stats[...] = jnp.where(lane < 64, average, inv_std)


def first_far_kernel(near, other, gain, shift, gain_two, shift_two, *refs):
    first_out, second_out, first_turned, second_turned = refs[2:]

    def step(rows):
        normed, _, _ = normalise(rows)
        first = normed * gain[...] + shift[...]
        second = normed * gain_two[...] + shift_two[...]
        first_out[...] = first.astype(BF16)
        second_out[...] = second.astype(BF16)
        put_turned(first_turned, first)
        put_turned(second_turned, second)

    @pl.when(pl.program_id(0) < 2)
    def _():
        step(near[...])

    @pl.when(pl.program_id(0) >= 2)
    def _():
        step(other[...])


TURNED = (16, 2, 64, 2 * TOK)


def first(hidden, cot, params):
    rows = TOK // 2
    plain = pl.BlockSpec((rows, D), lambda i: (i, 0))
    return pl.pallas_call(
        first_kernel,
        grid=(2,),
        in_specs=[plain] * 2 + [whole((1, D))] * 4,
        out_specs=[plain]
        + [pl.BlockSpec((16, 2, 64, rows), lambda i: (0, 0, 0, i))] * 3
        + [pl.BlockSpec((rows, 128), lambda i: (i, 0))],
        out_shape=[jax.ShapeDtypeStruct((TOK, D), BF16)]
        + [jax.ShapeDtypeStruct(TURNED, BF16)] * 3
        + [jax.ShapeDtypeStruct((TOK, 128), F32)],
        compiler_params=pltpu.CompilerParams(vmem_limit_bytes=VMEM),
        cost_estimate=COST,
    )(hidden, cot, *(p.reshape(1, D) for p in params))


def first_far(near, other, params, held):
    rows = 128
    plain = pl.BlockSpec((rows, D), lambda i: (i, 0))
    return pl.pallas_call(
        first_far_kernel,
        grid=(TOK // rows,),
        in_specs=[
            pl.BlockSpec((rows, D), lambda i: (lax.min(i, 1), 0)),
            pl.BlockSpec((rows, D), lambda i: (lax.max(i - 2, 0), 0)),
        ]
        + [whole((1, D))] * 4
        + [pl.BlockSpec(memory_space=pl.ANY)] * 2,
        out_specs=[plain] * 2
        + [pl.BlockSpec((16, 2, 64, rows), lambda i: (0, 0, 0, i + TOK // rows))] * 2,
        out_shape=[jax.ShapeDtypeStruct((TOK, D), BF16)] * 2
        + [jax.ShapeDtypeStruct(TURNED, BF16)] * 2,
        input_output_aliases={6: 2, 7: 3},
        compiler_params=pltpu.CompilerParams(vmem_limit_bytes=VMEM),
        cost_estimate=COST,
    )(near, other, *(p.reshape(1, D) for p in params), *held)


def phi(upward):
    return 0.5 * (1.0 + lax.erf(upward * math.sqrt(0.5)))


def gelu_slope(upward, below):
    return below + upward * (jnp.exp(-0.5 * upward * upward) * (1.0 / math.sqrt(2.0 * math.pi)))


def as_row(block):
    return jnp.concatenate([block[i : i + 1, :] for i in range(block.shape[0])], axis=1)


def feed_kernel(hidden, gain, shift, cot, weight, bias, act_out, slope_out, down_grad, second):
    @pl.when(pl.program_id(0) == 0)
    def _():
        for start in (0, TOK // 2):
            rows = slice(start, start + TOK // 2)
            normed, _, _ = normalise(hidden[rows].astype(F32))
            second[rows] = (normed * gain[...] + shift[...]).astype(BF16)

    upward = plain_dot(second[...], weight[...]) + as_row(bias[0])
    below = phi(upward)
    act = (upward * below).astype(BF16)
    act_out[...] = act
    slope_out[...] = gelu_slope(upward, below)
    total = lax.dot_general(
        cot[...], act[:, :WHOLE], (((0,), (0,)), ((), ())), preferred_element_type=F32
    )
    for z in range(2):
        rows = total[z * 1024 : z * 1024 + 1024]
        down_grad[:, z * 64 : z * 64 + 64] = rows.reshape(16, 64, -1)


def feed(hidden, gain, shift, cot, weight, bias):
    units, width = weight.shape[1], 1024
    column = pl.BlockSpec((TOK, width), lambda j: (0, j))
    return pl.pallas_call(
        feed_kernel,
        grid=(units // width,),
        in_specs=[
            whole((TOK, D)),
            whole((1, D)),
            whole((1, D)),
            whole((TOK, D)),
            pl.BlockSpec((D, width), lambda j: (0, j)),
            pl.BlockSpec((1, width // 128, 128), lambda j: (j, 0, 0)),
        ],
        out_specs=[column, column, pl.BlockSpec((16, 128, WHOLE), lambda j: (0, 0, j))],
        out_shape=[
            jax.ShapeDtypeStruct((TOK, units), BF16),
            jax.ShapeDtypeStruct((TOK, units), F32),
            jax.ShapeDtypeStruct((16, 128, 2 * WHOLE), F32),
        ],
        scratch_shapes=[pltpu.VMEM((TOK, D), BF16)],
        compiler_params=pltpu.CompilerParams(vmem_limit_bytes=VMEM),
        cost_estimate=COST,
    )(
        hidden,
        gain.reshape(1, D),
        shift.reshape(1, D),
        cot,
        weight,
        bias.reshape(-1, width // 128, 128),
    )


def feed_back_kernel(cot, weight, slope, up_grad):
    up_grad[...] = (contract_cols(cot[...], weight[...]) * slope[...]).astype(BF16)


def feed_back(cot, weight, slope):
    units, width = slope.shape[1], 512
    column = pl.BlockSpec((TOK, width), lambda j: (0, j))
    return pl.pallas_call(
        feed_back_kernel,
        grid=(units // width,),
        in_specs=[whole((TOK, D)), pl.BlockSpec((width, D), lambda j: (j, 0)), column],
        out_specs=column,
        out_shape=jax.ShapeDtypeStruct((TOK, units), BF16),
        compiler_params=pltpu.CompilerParams(vmem_limit_bytes=VMEM),
        cost_estimate=COST,
    )(cot, weight, slope)


def cot_far_kernel(side, near, other, weight, slope, dense, held, up_grad, grad_mixed, cot_turned, low):
    half = TOK // 2

    @pl.when(pl.program_id(0) == 0)
    def _():
        for k, rows in enumerate((near, other)):
            low[k * half : k * half + half] = rows[...].astype(BF16)
            put_turned(cot_turned.at[:, :, :, k * half : k * half + half], rows[...])
        grad_mixed[...] = contract_cols(low[...], dense[...]).astype(BF16)

    up_grad[...] = (contract_cols(low[...], weight[...]) * slope[...]).astype(BF16)


def cot_far(side, near, other, weight, slope, dense, held):
    width = 256
    steps = slope.shape[1] // width
    column = pl.BlockSpec((TOK, width), lambda j, s: (0, j))
    return pl.pallas_call(
        cot_far_kernel,
        grid_spec=pltpu.PrefetchScalarGridSpec(
            num_scalar_prefetch=1,
            grid=(steps,),
            in_specs=[
                whole((TOK // 2, D)),
                whole((TOK // 2, D)),
                pl.BlockSpec((width, D), lambda j, s: (s[0] * steps + j, 0)),
                column,
                pl.BlockSpec((HD, D), lambda j, s: (s[0], 0)),
                pl.BlockSpec(memory_space=pl.ANY),
            ],
            out_specs=[
                column,
                pl.BlockSpec((TOK, HD), lambda j, s: (0, 0)),
                pl.BlockSpec((16, 2, 64, TOK), lambda j, s: (0, 0, 0, 1)),
            ],
            scratch_shapes=[pltpu.VMEM((TOK, D), BF16)],
        ),
        out_shape=[
            jax.ShapeDtypeStruct((TOK, slope.shape[1]), BF16),
            jax.ShapeDtypeStruct((TOK, HD), BF16),
            jax.ShapeDtypeStruct(TURNED, BF16),
        ],
        input_output_aliases={6: 2},
        compiler_params=pltpu.CompilerParams(vmem_limit_bytes=VMEM),
        cost_estimate=COST,
    )(side, near, other, weight, slope, dense, held)


def slope_far_kernel(side, second, weight, bias, slope, act_out):
    upward = plain_dot(second[...], weight[...]) + as_row(bias[0])
    below = phi(upward)
    slope[...] = gelu_slope(upward, below)

    @pl.when(pl.program_id(0) == pl.num_programs(0) - 1)
    def _():
        shared = act_out.shape[1]
        act_out[...] = (upward[:, -shared:] * below[:, -shared:]).astype(BF16)


def slope_far(side, second, weight, bias):
    units, width = weight.shape[1] // 2, 512
    steps = units // width
    return pl.pallas_call(
        slope_far_kernel,
        grid_spec=pltpu.PrefetchScalarGridSpec(
            num_scalar_prefetch=1,
            grid=(steps,),
            in_specs=[
                whole((TOK, D)),
                pl.BlockSpec((D, width), lambda j, s: (0, s[0] * steps + j)),
                pl.BlockSpec((1, width // 128, 128), lambda j, s: (s[0] * steps + j, 0, 0)),
            ],
            out_specs=[
                pl.BlockSpec((TOK, width), lambda j, s: (0, j)),
                pl.BlockSpec((TOK, units - WHOLE), lambda j, s: (0, 0)),
            ],
        ),
        out_shape=[
            jax.ShapeDtypeStruct((TOK, units), F32),
            jax.ShapeDtypeStruct((TOK, units - WHOLE), BF16),
        ],
        compiler_params=pltpu.CompilerParams(vmem_limit_bytes=VMEM),
        cost_estimate=COST,
    )(side, second, weight, bias.reshape(-1, width // 128, 128))


def turn(values, tables, sign):
    first = values[:, :128]
    cosine, rising, falling = tables
    first = (
        first * cosine[...]
        + (pltpu.roll(first, 32, 1) * rising[...] + pltpu.roll(first, 96, 1) * falling[...]) * sign
    )
    return jnp.concatenate([first, values[:, 128:]], axis=1)


def as_column(row):
    return jnp.broadcast_to(row, (8, row.shape[1])).T[:, 0:1]


def cosine_and_sine(angles):
    turns = jnp.floor(angles * (2.0 / math.pi) + 0.5)
    rest = ((angles - turns * 1.5703125) - turns * 4.837512969970703e-4) - turns * 7.549789954891882e-8
    square = rest * rest
    sine = ((-1.9515295891e-4 * square + 8.3321608736e-3) * square - 1.6666654611e-1) * square
    sine = sine * rest + rest
    cosine = (2.443315711809948e-5 * square - 1.388731625493765e-3) * square + 4.166664568298827e-2
    cosine = cosine * (square * square) - 0.5 * square + 1.0
    quarter = turns.astype(jnp.int32) & 3
    odd = (quarter & 1) == 1
    flipped = jnp.where(odd, sine, cosine), jnp.where(odd, cosine, sine)
    return (
        jnp.where((quarter == 1) | (quarter == 2), -flipped[0], flipped[0]),
        jnp.where(quarter >= 2, -flipped[1], flipped[1]),
    )


def project_kernel(place, first, weight, bias, marks, inverse, queries, keys, values, *tables):
    @pl.when(pl.program_id(0) == 0)
    def _():
        angles = inverse[...] * marks[1:2, :]
        cosine, sine = cosine_and_sine(angles)
        none, rest = jnp.zeros_like(sine), jnp.zeros((64, TOK), F32)
        tables[0][...] = jnp.concatenate([cosine, cosine, rest + 1.0], axis=0).T
        tables[1][...] = jnp.concatenate([none, sine, rest], axis=0).T
        tables[2][...] = jnp.concatenate([-sine, none, rest], axis=0).T

    head = pl.program_id(0) + place[0] * (2 - pl.num_programs(0))
    packed = plain_dot(first[...], weight[...]) + bias[pl.ds(head, 1), :]
    queries[...] = turn(packed[:, :HD], tables, 1.0).astype(BF16)
    keys[...] = turn(packed[:, HD : 2 * HD], tables, 1.0).astype(BF16)
    values[...] = packed[:, 2 * HD :].astype(BF16)


def project(place, heads, first, weight, bias, marks):
    inverse = jnp.asarray((10000.0 ** (-2.0 * np.arange(32) / ROT)).astype(np.float32).reshape(32, 1))
    at = (lambda h, s: h) if heads == 2 else (lambda h, s: s[0])
    column = pl.BlockSpec((TOK, HD), lambda h, s: (0, h))
    return pl.pallas_call(
        project_kernel,
        grid_spec=pltpu.PrefetchScalarGridSpec(
            num_scalar_prefetch=1,
            grid=(heads,),
            in_specs=[
                whole((TOK, D)),
                pl.BlockSpec((D, 3 * HD), lambda h, s: (0, at(h, s))),
                whole((2, 3 * HD)),
                whole((2, TOK)),
                whole((32, 1)),
            ],
            out_specs=[column] * 3 + [pl.BlockSpec((TOK, 128), lambda h, s: (0, 0))] * 3,
        ),
        out_shape=[jax.ShapeDtypeStruct((TOK, heads * HD), BF16)] * 3
        + [jax.ShapeDtypeStruct((TOK, 128), F32)] * 3,
        compiler_params=pltpu.CompilerParams(vmem_limit_bytes=VMEM),
        cost_estimate=COST,
    )(place, first, weight, bias, marks, inverse)


def attend_kernel(place, queries, keys, values, cosine, rising, falling, marks, *refs):
    given, (mixed_out, grad_out) = refs[:-2], refs[-2:]
    tables = (cosine, rising, falling)
    scale = 1.0 / math.sqrt(HD)
    queries, keys, values = queries[...], keys[...], values[...]
    segments = marks[0:1, :]

    def order(axis):
        return lax.rem(lax.broadcasted_iota(jnp.int32, (TOK, TOK), axis) + place[1], TOK)

    allowed = (as_column(segments) == segments) & (order(0) >= order(1))
    scores = jnp.where(allowed, contract_cols(queries, keys) * scale, NEGATIVE)
    top = jnp.max(scores, axis=-1, keepdims=True)
    weights = jnp.exp(scores - top)
    probs = weights / jnp.sum(weights, axis=-1, keepdims=True)
    probs_low = probs.astype(BF16)
    mixed_out[...] = plain_dot(probs_low, values).astype(BF16)
    grad_mixed = given[0][...]
    if len(given) == 2:
        grad_mixed = contract_cols(grad_mixed, given[1][...]).astype(BF16)
    grad_probs = contract_cols(grad_mixed, values)
    along = jnp.sum(probs * grad_probs, axis=-1, keepdims=True)
    grad_scores = (probs * (grad_probs - along)).astype(BF16)
    grad_query = plain_dot(grad_scores, keys) * scale
    grad_key = plain_dot(grad_scores.T, queries) * scale
    grad_value = plain_dot(probs_low.T, grad_mixed)
    grad_out[:, :HD] = turn(grad_query, tables, -1.0).astype(BF16)
    grad_out[:, HD : 2 * HD] = turn(grad_key, tables, -1.0).astype(BF16)
    grad_out[:, 2 * HD :] = grad_value.astype(BF16)


def attend(place, heads, projected, given, marks):
    column = pl.BlockSpec((TOK, HD), lambda h, s: (0, h))
    return pl.pallas_call(
        attend_kernel,
        grid_spec=pltpu.PrefetchScalarGridSpec(
            num_scalar_prefetch=1,
            grid=(heads,),
            in_specs=[column] * 3
            + [whole((TOK, 128))] * 3
            + [whole((2, TOK))]
            + ([column] if len(given) == 1 else [whole((TOK, D)), pl.BlockSpec((HD, D), lambda h, s: (h, 0))]),
            out_specs=[column, pl.BlockSpec((TOK, 3 * HD), lambda h, s: (0, h))],
        ),
        out_shape=[
            jax.ShapeDtypeStruct((TOK, heads * HD), BF16),
            jax.ShapeDtypeStruct((TOK, heads * 3 * HD), BF16),
        ],
        compiler_params=pltpu.CompilerParams(vmem_limit_bytes=VMEM),
        cost_estimate=COST,
    )(place, *projected, marks, *given)


def put_halves(core, values, scratch, mine, other):
    scratch[...] = values
    half = TOK // 2
    mine[...] = scratch[pl.ds(pl.multiple_of(core[0] * half, half), half), :]
    other[...] = scratch[pl.ds(pl.multiple_of((1 - core[0]) * half, half), half), :]


def branch_kernel(mixed, act, dense, down, total):
    total[...] = plain_dot(act[...], down[...]) + plain_dot(mixed[...], dense[...])


def back_kernel(
    core, packed, up_grad, qkv, up, hidden, stats, gain, gain_two, mine, other, sums, scratch
):
    first = contract_cols(packed[...], qkv[...])
    second = contract_cols(up_grad[...], up[...])
    put_halves(core, first * gain[...] + second * gain_two[...], scratch, mine, other)
    normed = (hidden[...].astype(F32) - stats[:, 0:1]) * stats[:, 64:65]
    rows = [
        jnp.sum(v, axis=0, keepdims=True) for v in (first * normed, first, second * normed, second)
    ]
    sums[...] = jnp.concatenate(rows + [jnp.zeros((4, first.shape[1]), F32)], axis=0)


def halves_call(kernel, core, operands, specs, with_sums):
    width = 512
    half = pl.BlockSpec((TOK // 2, width), lambda j, s: (0, j))
    return pl.pallas_call(
        kernel,
        grid_spec=pltpu.PrefetchScalarGridSpec(
            num_scalar_prefetch=1,
            grid=(D // width,),
            in_specs=specs,
            out_specs=[half, half] + [pl.BlockSpec((8, width), lambda j, s: (0, j))] * with_sums,
            scratch_shapes=[pltpu.VMEM((TOK, width), F32)],
        ),
        out_shape=[jax.ShapeDtypeStruct((TOK // 2, D), F32)] * 2
        + [jax.ShapeDtypeStruct((8, D), F32)] * with_sums,
        compiler_params=pltpu.CompilerParams(vmem_limit_bytes=VMEM),
        cost_estimate=COST,
    )(core, *operands)


def branches(mixed, act, dense, down):
    width = 512
    return pl.pallas_call(
        branch_kernel,
        grid=(D // width,),
        in_specs=[whole(mixed.shape), whole(act.shape)]
        + [pl.BlockSpec((w.shape[0], width), lambda j: (0, j)) for w in (dense, down)],
        out_specs=pl.BlockSpec((TOK, width), lambda j: (0, j)),
        out_shape=jax.ShapeDtypeStruct((TOK, D), F32),
        compiler_params=pltpu.CompilerParams(vmem_limit_bytes=VMEM),
        cost_estimate=COST,
    )(mixed, act, dense, down)


def back_halves(core, packed, up_grad, qkv, up, hidden, stats, gain, gain_two):
    specs = [whole(packed.shape), whole(up_grad.shape)]
    specs += [pl.BlockSpec((512, w.shape[1]), lambda j, s: (j, 0)) for w in (qkv, up)]
    specs += [pl.BlockSpec((TOK, 512), lambda j, s: (0, j)), whole((TOK, 128))]
    specs += [pl.BlockSpec((1, 512), lambda j, s: (0, j))] * 2
    operands = (packed, up_grad, qkv, up, hidden, stats, gain.reshape(1, D), gain_two.reshape(1, D))
    return halves_call(back_kernel, core, operands, specs, True)


def final_kernel(n, half, branch, combined, hidden, cot, stats, bias, bias_too, *refs):
    output, input_grad = refs[n:]
    rows = hidden[...].astype(F32)
    output[...] = rows + branch[...] + bias[...] + bias_too[...]
    e = combined[...]
    inv_std = stats[:, 64:65]
    normed = (rows - stats[:, 0:1]) * inv_std
    input_grad[...] = cot[...].astype(F32) + inv_std * (
        e
        - jnp.mean(e, axis=-1, keepdims=True)
        - normed * jnp.mean(e * normed, axis=-1, keepdims=True)
    )


def final_half(half, branch, combined, hidden, cot, stats, biases, held):
    rows = 128
    steps = TOK // 2 // rows
    given = pl.BlockSpec((rows, D), lambda i, s: (i, 0))
    placed = pl.BlockSpec((rows, D), lambda i, s: (s[0] * steps + i, 0))
    return pl.pallas_call(
        partial(final_kernel, len(held)),
        grid_spec=pltpu.PrefetchScalarGridSpec(
            num_scalar_prefetch=1,
            grid=(steps,),
            in_specs=[placed, given, placed, placed]
            + [pl.BlockSpec((rows, 128), lambda i, s: (s[0] * steps + i, 0))]
            + [whole((1, D))] * 2
            + [pl.BlockSpec(memory_space=pl.ANY)] * len(held),
            out_specs=[placed, placed],
        ),
        out_shape=[jax.ShapeDtypeStruct((TOK, D), F32)] * 2,
        input_output_aliases={8: 0, 9: 1} if held else {},
        compiler_params=pltpu.CompilerParams(vmem_limit_bytes=VMEM_LESS),
        cost_estimate=COST,
    )(half, branch, combined, hidden, cot, stats, *(b.reshape(1, D) for b in biases), *held)


def joint_kernel(side, *refs):
    lefts, rights, target, held, right, arrived = (
        refs[:3],
        refs[3:11],
        refs[11],
        refs[12],
        refs[13],
        refs[14],
    )
    step = pl.program_id(0)
    copies = [pltpu.make_async_copy(lefts[k], held.at[k], arrived.at[k]) for k in range(3)]

    @pl.when(step == 0)
    def _():
        for copy in copies:
            copy.start()
        copies[0].wait()

    @pl.when(step == 4)
    def _():
        copies[1].wait()
        copies[2].wait()

    for n, (start, stop) in enumerate(((0, 4), (4, 5), (5, 8), (8, 9))):

        @pl.when((step >= start) & (step < stop))
        def _(n=n):
            for k in range(2):
                given = rights[2 * n + k]
                right[k * TOK : k * TOK + TOK, : given.shape[1]] = given[...]

    k = jnp.where(step < 4, 0, jnp.where((step >= 5) & (step < 8), 2, 1))
    target[...] = plain_dot(held[k].reshape(D, 2 * TOK), right[...]).reshape(16, 128, -1)


def joint(side, lefts, rights):
    width, shared = 256, 1024 - WHOLE
    specs = [pl.BlockSpec(memory_space=pl.ANY)] * 3
    for start, n in ((0, 4), (4, 1), (5, 3)):

        def near(j, s, start=start, n=n):
            return (0, s[0] * n + jnp.clip(j - start, 0, n - 1))

        def far(j, s, start=start, n=n):
            return (0, jnp.clip(j - start, 0, n - 1))

        specs += [pl.BlockSpec((TOK, width), near), pl.BlockSpec((TOK, width), far)]
    specs += [
        pl.BlockSpec((TOK, shared), lambda j, s: (0, (s[0] + 1) * (1024 // shared) - 1)),
        pl.BlockSpec((TOK, shared), lambda j, s: (0, 0)),
    ]
    return pl.pallas_call(
        joint_kernel,
        grid_spec=pltpu.PrefetchScalarGridSpec(
            num_scalar_prefetch=1,
            grid=(9,),
            in_specs=specs,
            out_specs=pl.BlockSpec((16, 128, width), lambda j, s: (0, 0, j)),
            scratch_shapes=[
                pltpu.VMEM((3,) + TURNED, BF16),
                pltpu.VMEM((2 * TOK, width), BF16),
                pltpu.SemaphoreType.DMA((3,)),
            ],
        ),
        out_shape=jax.ShapeDtypeStruct((16, 128, 2048 + shared), F32),
        compiler_params=pltpu.CompilerParams(vmem_limit_bytes=VMEM),
        cost_estimate=COST,
    )(side, *lefts, *rights)


def assemble_kernel(side, near, far, part, up, dense, qkv, down):
    def put(low, high):
        up[...] = jnp.concatenate([low[:, :1024], high[:, :1024]], axis=1)
        dense[...] = jnp.concatenate([low[:, 1024:1280], high[:, 1024:1280]], axis=1)
        qkv[...] = jnp.concatenate([low[:, 1280:2048], high[:, 1280:2048]], axis=1)
        down[...] = jnp.concatenate(
            [part[:, :WHOLE], low[:, 2048:], part[:, WHOLE:], high[:, 2048:]], axis=1
        )

    @pl.when(side[0] == 0)
    def _():
        put(near[0], far[...])

    @pl.when(side[0] != 0)
    def _():
        put(far[...], near[0])


def assemble(side, near, far, part):
    shapes = ((64, 2048), (64, 512), (64, 1536), (64, 2048))
    columns = far.shape[1]
    return pl.pallas_call(
        assemble_kernel,
        grid_spec=pltpu.PrefetchScalarGridSpec(
            num_scalar_prefetch=1,
            grid=(1,),
            in_specs=[
                pl.BlockSpec((1, 64, columns), lambda i, s: (0, s[0], 0)),
                pl.BlockSpec((64, columns), lambda i, s: (0, 0)),
                pl.BlockSpec((64, 2 * WHOLE), lambda i, s: (0, 0)),
            ],
            out_specs=[pl.BlockSpec(shape, lambda i, s: (0, 0)) for shape in shapes],
        ),
        out_shape=[jax.ShapeDtypeStruct(shape, F32) for shape in shapes],
        compiler_params=pltpu.CompilerParams(vmem_limit_bytes=VMEM_LESS),
        cost_estimate=COST,
    )(side, near, far, part)


def body(
    hidden_in,
    segment_ids,
    positions,
    ln1_gain,
    ln1_bias,
    qkv_weight,
    qkv_bias,
    dense_weight,
    dense_bias,
    ln2_gain,
    ln2_bias,
    fc1_weight,
    fc1_bias,
    fc2_weight,
    fc2_bias,
    cotangent,
):
    core = lax.axis_index("c")
    side = lax.axis_index("zl")
    half_rows = TOK // 2
    at_side = side.astype(jnp.int32).reshape(1)
    at_core = core.astype(jnp.int32).reshape(1)
    own_place = jnp.zeros((2,), jnp.int32)
    far_place = jnp.stack([side, core * half_rows]).astype(jnp.int32)
    after = lax.optimization_barrier
    params = (ln1_gain, ln1_bias, ln2_gain, ln2_bias)

    def of_core(values, which):
        return lax.dynamic_slice_in_dim(values, which * half_rows, half_rows, 0)

    act_low, slope, down_grad = feed(
        hidden_in, ln2_gain, ln2_bias, cotangent, fc1_weight, fc1_bias
    )
    down_sum = after(lax.psum_scatter(down_grad, ("x", "y"), scatter_dimension=0, tiled=True))
    _, cotangent, hidden_in = after((down_grad, cotangent, hidden_in))

    marks = jnp.concatenate([segment_ids, positions]).astype(F32).reshape(1, 2 * TOK)
    hidden_sent, cot_sent = sent(at_core, hidden_in, cotangent, marks)
    hidden_got = send(hidden_sent, "zl")
    cot_got = lax.ppermute(cot_sent, ("zl", "zh"), [(i, 3 - i) for i in range(4)])

    own_marks = marks.reshape(2, TOK)

    def own_step(hidden_in, cotangent, act_low, slope):
        first_in, *turned, stats = first(hidden_in, cotangent, params)
        projected = project(own_place, 2, first_in, qkv_weight, qkv_bias, own_marks)
        mixed_low, grad_packed = attend(
            own_place, 2, projected, (cotangent, dense_weight), own_marks
        )
        grad_up = feed_back(cotangent, fc2_weight, slope)
        branch = branches(mixed_low, act_low, dense_weight, fc2_weight)
        return *turned, stats, mixed_low, grad_packed, grad_up, branch

    (
        first_turned,
        second_turned,
        cot_turned,
        stats,
        mixed_low,
        grad_packed,
        grad_up,
        branch,
    ) = lax.cond(core > 1, own_step, own_step, hidden_in, cotangent, act_low, slope)
    branch = lax.psum(branch, TENSOR)
    hidden_got, mixed_low = after((hidden_got, mixed_low))
    hidden_too = send(hidden_got, "c")
    hidden_too, cot_got = after((hidden_too, cot_got))
    cot_too = send(cot_got, "c")

    first_far_in, second_far_in, first_turned, second_turned = first_far(
        hidden_got, hidden_too, params, (first_turned, second_turned)
    )
    slope_side, act_far = slope_far(at_side, second_far_in, fc1_weight, fc1_bias)
    marks_got = cot_got[half_rows, : 2 * TOK].reshape(2, 2, half_rows)
    marks_far = jnp.where(core == 0, marks_got, marks_got[:, ::-1]).reshape(2, TOK)
    projected_far = project(far_place, 1, first_far_in, qkv_weight, qkv_bias, marks_far)
    grad_up_far, grad_mixed_far, cot_turned = cot_far(
        at_side, cot_got, cot_too, fc2_weight, slope_side, dense_weight, cot_turned
    )
    mixed_far, grad_packed_far = attend(
        far_place, 1, projected_far, (grad_mixed_far,), marks_far
    )
    joint_grad = joint(
        at_side,
        (second_turned, cot_turned, first_turned),
        (
            grad_up,
            grad_up_far,
            mixed_low,
            mixed_far,
            grad_packed,
            grad_packed_far,
            act_low,
            act_far,
        ),
    )
    joint_grad, down_sum = after((joint_grad, down_sum))
    joint_sum = after(lax.psum_scatter(joint_grad, ("x", "y"), scatter_dimension=0, tiled=True))
    _, grad_packed, grad_up, cotangent, down_sum = after(
        (joint_grad, grad_packed, grad_up, cotangent, down_sum)
    )

    combined, combined_other, norms = back_halves(
        at_core, grad_packed, grad_up, qkv_weight, fc1_weight, hidden_in, stats, ln1_gain, ln2_gain
    )
    combined = combined + send(combined_other, "c")
    combined_too = send(combined, "zh")

    norms = norms[:4].reshape(4, 32, 64).transpose(1, 0, 2).reshape(32, 256)
    grad_out = cotangent.astype(F32)
    bias_sum = jnp.sum(grad_out, axis=0)
    qkv_bias_sum = jnp.sum(grad_packed.astype(F32), axis=0)
    up_bias_grad = jnp.sum(grad_up.astype(F32), axis=0)
    small = jnp.concatenate(
        [
            norms,
            bias_sum.reshape(32, 64),
            qkv_bias_sum.reshape(2, 32, 24).transpose(1, 0, 2).reshape(32, 48),
            up_bias_grad.reshape(16, 32, 4).transpose(1, 0, 2).reshape(32, 64),
            jnp.zeros((32, 80), F32),
        ],
        axis=1,
    )
    def of_side(values, which):
        return lax.dynamic_slice_in_dim(values[0], which * 64, 64, 0)

    down_far = send(of_side(down_sum, 1 - side), "zl")
    for axis in ("x", "y"):
        small = small + swap(small, axis, 1)
        small = small + swap(small, axis, 2)
    block = lax.axis_index("x") * 4 + lax.axis_index("y")
    own_small = lax.dynamic_slice_in_dim(small, side * 16 + block, 1, 0)
    far_small = lax.dynamic_slice_in_dim(small, (1 - side) * 16 + block, 1, 0)
    small = (own_small + send(far_small, "zl")).reshape(-1)

    norms = small[:256]
    norms = norms + send(norms, "c")
    norms = norms + send(norms, "zh")
    norms, branch, combined_too, down_far = after((norms, branch, combined_too, down_far))
    combined = combined + combined_too
    norms = norms.reshape(4, 64)
    bias_total = small[256:320]
    biases = (dense_bias, fc2_bias)
    own = (hidden_in, cotangent, stats, biases)
    combined_too = send(combined, "c")
    finals = final_half(at_core, branch, combined, *own, ())
    finals = final_half(1 - at_core, branch, combined_too, *own, finals)
    output, input_grad, joint_sum = after((*finals, joint_sum))

    down_sum = of_side(down_sum, side) + down_far
    joint_far = send(of_side(joint_sum, 1 - side), "zl")
    up_sum, dense_sum, qkv_sum, down_sum = assemble(at_side, joint_sum, joint_far, down_sum)
    return (
        output,
        input_grad,
        norms[0],
        norms[1],
        qkv_sum,
        small[320:368].reshape(2, 24),
        dense_sum.T,
        bias_total,
        norms[2],
        norms[3],
        up_sum,
        small[368:432].reshape(16, 4),
        down_sum.T,
        bias_total,
    )


def solution(mesh):
    fine = Mesh(mesh.devices.reshape(tuple(SIZES.values())), tuple(SIZES))
    return jax.shard_map(
        body,
        mesh=fine,
        in_specs=(
            P(DP, None),
            P(DP),
            P(DP),
            P(),
            P(),
            P(None, TENSOR),
            P(TENSOR, None),
            P(TENSOR, None),
            P(),
            P(),
            P(),
            P(None, TENSOR),
            P(TENSOR, None),
            P(TENSOR, None),
            P(),
            P(DP, None),
        ),
        out_specs=(
            P(DP, None),
            P(DP, None),
            P(DP),
            P(DP),
            P(DP, TENSOR),
            P(TENSOR, DP),
            P(TENSOR, DP),
            P(DP),
            P(DP),
            P(DP),
            P(DP, TENSOR),
            P(TENSOR, DP),
            P(TENSOR, DP),
            P(DP),
        ),
        check_vma=False,
    )
```
